32 devices in a mesh: section: 2 (over x), gy: 4 (over z), gz: 4 (over y, core).
Axes of the slice: x: 2, y: 2, z: 4, core: 2. Of those that a mesh axis runs over, the one named last changes fastest.
Arguments:
- inflow: float32 [2, 64, 2, 8, 512], P(None, None, None, 'gy', 'gz'), may hold values from -6 to 6
- weights: float32 [4, 27, 64, 64], P('section'), may hold values from -0.15625 to 0.15625
- biases: float32 [4, 64], P('section'), may hold values from -3 to 3
- cotangent: float32 [2, 64, 2, 8, 512], P(None, None, None, 'gy', 'gz'), may hold values from -6 to 6
Outputs:
- section_out: float32 [2, 2, 64, 2, 8, 512], P('section', None, None, None, 'gy', 'gz')
- section_grad: float32 [2, 2, 64, 2, 8, 512], P('section', None, None, None, 'gy', 'gz')
- weight_grad: float32 [4, 27, 64, 64], P('section')
- bias_grad: float32 [4, 64], P('section')
The draws below stay inside these ranges and needn't reach their ends.
All inputs are finite; a program needn't handle non-finite values.
Results may differ from the reference program's by a relative error of at most 0.0001.
Values sent between devices are 32-bit elements; how exact they have to be, the bound alone decides.
No kernel may reach another device: no remote copies, remote signals or barrier semaphores. Data moves between devices by JAX's collectives and lax.ppermute only.
A program may use at most 128 MiB of HBM per device.

```python
import math
import jax
import jax.numpy as jnp
from jax import lax

C = 64
LAYERS_DEV = 2
MB = 2
LAYERS = 4
NX = 2
NY = 8
NZ = 512


def block_levels(stream_key, shape, cuts, smallest, largest):
    factor_of, own = 1.0, jax.random.fold_in(stream_key, 6)
    for axis_at, parts in cuts:
        heights = jnp.exp(jax.random.uniform(jax.random.fold_in(own, axis_at), (parts,), jnp.float32, smallest / len(cuts), largest / len(cuts)))
        factor_of = factor_of * jnp.repeat(heights, shape[axis_at] // parts).reshape([-1 if axis == axis_at else 1 for axis in range(len(shape))])
    return factor_of


def bell_draw(key, shape, deviation, most, split=(), kind=jnp.bfloat16):
    level = block_levels(key, shape, split, -0.22, 0.18) if split else 1.0
    drawn = jax.random.normal(key, shape, jnp.float32) * deviation * level
    return jnp.minimum(jnp.maximum(drawn, -most), most).astype(kind)


def setup_inputs(seed: int = 0) -> dict:
    seeds = jax.random.split(jax.random.key(seed), 5)
    inflow = bell_draw(seeds[0], (MB, C, NX, NY, NZ), 1.0, 6.0, ((3, 4), (4, 4)), jnp.float32)
    weights = bell_draw(seeds[1], (LAYERS, 27, C, C), (27 * C) ** -0.5, 0.15625, ((0, 2),), jnp.float32)
    biases = bell_draw(seeds[2], (LAYERS, C), 0.5, 3.0, ((0, 2),), jnp.float32)
    cotangent = bell_draw(seeds[3], (MB, C, NX, NY, NZ), 1.0, 6.0, ((3, 4), (4, 4)), jnp.float32)
    return dict(inflow=inflow, weights=weights, biases=biases, cotangent=cotangent)


def stacked_taps(padded, out_sizes, flipped):
    size_x, size_y, size_z = out_sizes
    pieces = []
    for offset in range(27):
        start_x, start_y, start_z = (offset // 9, offset // 3 % 3, offset % 3)
        if flipped:
            start_x, start_y, start_z = (2 - start_x, 2 - start_y, 2 - start_z)
        pieces.append(padded[:, start_x:start_x + size_x, start_y:start_y + size_y, start_z:start_z + size_z])
    return jnp.stack(pieces)

def zero_rim(values):
    return jnp.pad(values, ((0, 0), (1, 1), (1, 1), (1, 1)))

def reference(inflow, weights, biases, cotangent):
    highest = lax.Precision.HIGHEST
    grad_scale = 1.0 / math.sqrt(MB * NX * NY * NZ)
    extents = inflow.shape[2:]
    weight_grads = jnp.zeros(weights.shape, jnp.float32)
    bias_grads = jnp.zeros(biases.shape, jnp.float32)
    middles, finals, inflow_grads, middle_grads = ([], [], [], [])
    for micro in range(MB):
        current = inflow[micro]
        stored = []
        for layer_index in range(LAYERS):
            padded = zero_rim(current)
            pre_act = jnp.einsum('toc,tcxyz->oxyz', weights[layer_index], stacked_taps(padded, extents, False), precision=highest)
            pre_act = pre_act + biases[layer_index][:, None, None, None]
            current = jax.nn.silu(pre_act)
            stored.append((padded, pre_act))
            if layer_index == LAYERS_DEV - 1:
                middles.append(current)
        finals.append(current)
        gradient = cotangent[micro]
        for layer_index in reversed(range(LAYERS)):
            padded, pre_act = stored[layer_index]
            sigmoid_value = jax.nn.sigmoid(pre_act)
            slope_grad = gradient * sigmoid_value * (1.0 + pre_act * (1.0 - sigmoid_value))
            weight_grads = weight_grads.at[layer_index].add(jnp.einsum('oxyz,tcxyz->toc', slope_grad, stacked_taps(padded, extents, False), precision=highest))
            bias_grads = bias_grads.at[layer_index].add(lax.optimization_barrier(jnp.sum(slope_grad, axis=(1, 2, 3))))
            gradient = jnp.einsum('toc,toxyz->cxyz', weights[layer_index], stacked_taps(zero_rim(slope_grad), extents, True), precision=highest)
            if layer_index == LAYERS_DEV:
                middle_grads.append(gradient)
        inflow_grads.append(gradient)
    section_out = jnp.stack([jnp.stack(middles), jnp.stack(finals)])
    section_grad = jnp.stack([jnp.stack(inflow_grads), jnp.stack(middle_grads)])
    return (section_out, section_grad, weight_grads * grad_scale, bias_grads * grad_scale)
```

```python
import functools
import math

import jax
import jax.numpy as jnp
from jax import lax
from jax.experimental import pallas as pl
from jax.experimental.pallas import tpu as pltpu
from jax.sharding import PartitionSpec as P

HALO = 8
LANES = 128
BF16 = jnp.bfloat16
F32 = jnp.float32


def shifted(block, axis, distance):
    count = lax.axis_size(axis)
    route = [(i, i + distance) for i in range(count) if 0 <= i + distance < count]
    return lax.ppermute(block, axis, route)


def split_terms(values):
    high = values.astype(BF16)
    return high, (values - high.astype(F32)).astype(BF16)


def slab_kernel(dims, place, own, other, cells, outs, sums, fwd, bwd, acts, rim, kept, slopes, acc):
    micros, rows_y, depth, width, chunk_y, chans, limit_z, scale = dims
    section = place[0]
    origin = place[1]
    chunk = chunk_y * depth
    chunks = rows_y // chunk_y
    per_owner = rows_y // cells.shape[0]
    zs = lax.broadcasted_iota(jnp.int32, (depth, LANES), 0)
    in_grid = ((zs + origin >= 0) & (zs + origin < limit_z)).astype(F32)[None]
    mine = ((zs >= HALO) & (zs < HALO + width)).astype(F32)[None]

    def prepare(pair, carry):
        for half in range(2):
            layer = 2 * pair + half
            for b in range(3):
                for c in range(3):
                    taps = []
                    for a in range(3):
                        tap = 9 * a + 3 * b + c
                        both = jnp.where(pair == section, own[tap], other[tap])
                        taps.append(both[:, half * chans : (half + 1) * chans])
                    top = jnp.concatenate([taps[1], taps[2]], axis=1)
                    low = jnp.concatenate([taps[0], taps[1]], axis=1)
                    block = jnp.concatenate([top, low], axis=0)
                    for target, value, row, col in (
                        (fwd, block.T, b, c),
                        (bwd, block, 2 - b, 2 - c),
                    ):
                        hi, lo = split_terms(value)
                        at = slice(col * LANES, (col + 1) * LANES)
                        target[layer, 2 * row * LANES : (2 * row + 1) * LANES, at] = hi
                        target[layer, (2 * row + 1) * LANES : (2 * row + 2) * LANES, at] = hi
                        target[layer, (6 + row) * LANES : (7 + row) * LANES, at] = lo
        return carry

    lax.fori_loop(0, 2, prepare, 0)

    def over_chunks(body):
        if chunks == 1:
            for micro in range(micros):
                body(micro, 0, 0)
        else:

            def step(index, carry):
                part = index % chunks
                body(index // chunks, part, pl.multiple_of(part * chunk, 16))
                return carry

            lax.fori_loop(0, micros * chunks, step, 0)

    def put_rows(target, lead, start, values):
        hi, lo = split_terms(values)
        at = pl.ds(start + depth, chunk)
        target[(*lead, at, slice(0, LANES))] = hi
        target[(*lead, at, slice(LANES, 2 * LANES))] = lo

    def pieces_of(source, lead, start):
        return [source[(*lead, pl.ds(start + b * depth, chunk), slice(None))] for b in range(3)]

    def conv(source, lead, start, table):
        pieces = pieces_of(source, lead, start)
        left = jnp.concatenate(pieces + [piece[:, :LANES] for piece in pieces], axis=1)
        out = jnp.dot(left, table[...], preferred_element_type=F32)
        before = pltpu.roll(out[:, :LANES], 1, 0)
        after = pltpu.roll(out[:, 2 * LANES :], chunk - 1, 0)
        return before + out[:, LANES : 2 * LANES] + after

    def masked(values, mask):
        return (values.reshape(chunk_y, depth, LANES) * mask).reshape(chunk, LANES)

    blank = jnp.zeros((depth, 2 * LANES), BF16)
    for micro in range(micros):
        for edge in (0, rows_y + 1):
            at = slice(edge * depth, (edge + 1) * depth)
            for layer in range(4):
                acts[layer, micro, at, :] = blank
            for side in range(2):
                rim[side, micro, at, :] = blank

    def load(micro, part, which):
        rows = [part * chunk_y + y for y in range(chunk_y)]
        pieces = [cells[row // per_owner, which, micro, row % per_owner] for row in rows]
        return jnp.concatenate(pieces, axis=0)

    def emit(slot, micro, part, values):
        inner = values.reshape(chunk_y, depth, LANES)[:, HALO : HALO + width, :]
        outs[slot, micro, pl.ds(part * chunk_y, chunk_y)] = inner

    over_chunks(lambda micro, part, start: put_rows(acts, (0, micro), start, load(micro, part, 0)))

    for layer in range(4):
        source = own if layer < 2 else other
        half = layer % 2

        def forward(micro, part, start):
            row = jnp.where(section == layer // 2, own[27, 0:1, :], other[27, 0:1, :])
            bias = row[:, half * chans : (half + 1) * chans]
            bias = jnp.concatenate([bias, bias], axis=1)
            pre = conv(acts, (layer, micro), start, fwd.at[layer]) + bias
            grown = 1.0 + jnp.exp(-pre)
            sigma = 1.0 / grown
            kept[layer, micro, pl.ds(start, chunk), :] = sigma * (1.0 + pre * (1.0 - sigma))
            out = masked(pre / grown, in_grid)
            if layer < 3:
                put_rows(acts, (layer + 1, micro), start, out)
            if half == 1:
                pl.when(section == layer // 2)(lambda: emit(0, micro, part, out))

        over_chunks(forward)

    def take_gradient(layer, micro, start, gradient):
        slope = masked(gradient * kept[layer, micro, pl.ds(start, chunk), :], in_grid)
        slopes[layer, micro, pl.ds(start, chunk), :] = masked(slope, mine)
        put_rows(rim, (layer % 2, micro), start, slope)

    over_chunks(lambda micro, part, start: take_gradient(3, micro, start, load(micro, part, 1)))

    def backward(layer):
        def pull(micro, part, start):
            gradient = conv(rim, (layer % 2, micro), start, bwd.at[layer])
            if layer > 0:
                take_gradient(layer - 1, micro, start, gradient)
            if layer % 2 == 0:
                pl.when(section == layer // 2)(lambda: emit(1, micro, part, gradient))

        over_chunks(pull)

    backward(3)
    backward(2)

    @pl.when(section == 0)
    def _():
        backward(1)
        backward(0)

    sums[27] = jnp.zeros((chans, LANES), F32)
    for slot in range(2):
        layer = 2 * section + slot
        acc[...] = jnp.zeros(acc.shape, F32)

        def gather(micro, part, start):
            slope = slopes[layer, micro, pl.ds(start, chunk), :]
            moved = [pltpu.roll(slope, 1 if c == 0 else chunk - 1, 0) if c != 1 else slope for c in (2, 1, 0)]
            terms = [split_terms(value) for value in moved]
            left_hi = jnp.concatenate([hi for hi, lo in terms], axis=1)
            left_lo = jnp.concatenate([lo for hi, lo in terms], axis=1)
            pieces = pieces_of(acts, (layer, micro), start)
            full = jnp.concatenate(pieces, axis=1)
            high = jnp.concatenate([piece[:, :LANES] for piece in pieces], axis=1)
            over_rows = (((0,), (0,)), ((), ()))
            one = lax.dot_general(left_hi, full, over_rows, preferred_element_type=F32)
            two = lax.dot_general(left_lo, high, over_rows, preferred_element_type=F32)
            for b in range(3):
                at = slice(b * LANES, (b + 1) * LANES)
                acc[0 : 3 * LANES, at] += (
                    one[:, 2 * b * LANES : (2 * b + 1) * LANES]
                    + one[:, (2 * b + 1) * LANES : (2 * b + 2) * LANES]
                    + two[:, at]
                )
            acc[3 * LANES : 3 * LANES + 1, 0:LANES] += jnp.sum(slope, axis=0, keepdims=True)

        over_chunks(gather)
        lanes = slice(slot * chans, (slot + 1) * chans)
        for b in range(3):
            for c in range(3):
                block = acc[c * LANES : (c + 1) * LANES, b * LANES : (b + 1) * LANES] * scale
                tap = 3 * b + c
                sums[tap, :, lanes] = block[chans:, :chans]
                sums[9 + tap, :, lanes] = block[:chans, :chans] + block[chans:, chans:]
                sums[18 + tap, :, lanes] = block[:chans, chans:]
        row = acc[3 * LANES : 3 * LANES + 1, 0:LANES] * scale
        sums[27, 0:1, lanes] = row[:, :chans] + row[:, chans:]


def packed(weights, biases):
    pair = jnp.concatenate([weights[0], weights[1]], axis=-1)
    row = jnp.concatenate([biases[0], biases[1]])[None, None, :]
    tail = jnp.pad(row, ((0, 0), (0, pair.shape[1] - 1), (0, 0)))
    return jnp.concatenate([pair, tail], axis=0)


def summed_over_grid(block):
    rows = block.shape[0]
    gy, gz = lax.axis_size("gy"), lax.axis_size("gz")
    even = -(-rows // (gy * gz * 8)) * gy * gz * 8
    block = jnp.pad(block, ((0, even - rows), (0, 0)))
    for axis, count in (("gz", gz), ("gy", gy)):
        parts = block.reshape(count, block.shape[0] // count, LANES)
        block = jnp.sum(lax.all_to_all(parts, axis, 0, 0), axis=0)
    for axis in ("gy", "gz"):
        block = lax.all_gather(block, axis, tiled=True)
    return block[:rows]


def per_device(inflow, weights, biases, cotangent):
    micros, chans, size_x, local_y, local_z = inflow.shape
    gy, gz = lax.axis_size("gy"), lax.axis_size("gz")
    rows_y = local_y * gy
    width = local_z // gy
    depth = -(-(width + 2 * HALO) // 16) * 16
    chunk_y = max(n for n in range(1, rows_y + 1) if rows_y % n == 0 and n * depth <= 384)
    scale = 1.0 / math.sqrt(micros * size_x * rows_y * local_z * gz)
    section = lax.axis_index("section")

    own = packed(weights, biases)
    other = lax.ppermute(own, "section", [(0, 1), (1, 0)])

    fields = jnp.stack([inflow, cotangent]).transpose(0, 1, 4, 5, 3, 2)
    fields = fields.reshape(2, micros, local_y, local_z, size_x * chans)
    before = shifted(fields[:, :, :, local_z - HALO :], "gz", 1)
    after = shifted(fields[:, :, :, :HALO], "gz", -1)
    span = width * (gy - 1) + depth
    fields = jnp.concatenate([before, fields, after], axis=3)
    fields = jnp.pad(fields, ((0, 0),) * 3 + ((0, max(0, span - fields.shape[3])), (0, 0)))
    windows = jnp.stack(
        [lax.slice_in_dim(fields, i * width, i * width + depth, axis=3) for i in range(gy)]
    )
    cells = lax.all_to_all(windows, "gy", 0, 0)

    origin = lax.axis_index("gz") * local_z + lax.axis_index("gy") * width - HALO
    place = jnp.stack([section, origin]).astype(jnp.int32)
    dims = (micros, rows_y, depth, width, chunk_y, chans, local_z * gz, scale)
    padded = (rows_y + 2) * depth
    full = rows_y * depth
    vmem = pl.BlockSpec(memory_space=pltpu.VMEM)
    outs, sums = pl.pallas_call(
        functools.partial(slab_kernel, dims),
        out_shape=(
            jax.ShapeDtypeStruct((2, micros, rows_y, width, LANES), F32),
            jax.ShapeDtypeStruct((28, chans, LANES), F32),
        ),
        in_specs=[pl.BlockSpec(memory_space=pltpu.SMEM), vmem, vmem, vmem],
        out_specs=(vmem, vmem),
        scratch_shapes=[
            pltpu.VMEM((4, 9 * LANES, 3 * LANES), BF16),
            pltpu.VMEM((4, 9 * LANES, 3 * LANES), BF16),
            pltpu.VMEM((4, micros, padded, 2 * LANES), BF16),
            pltpu.VMEM((2, micros, padded, 2 * LANES), BF16),
            pltpu.VMEM((4, micros, full, LANES), F32),
            pltpu.VMEM((4, micros, full, LANES), F32),
            pltpu.VMEM((3 * LANES + 8, 3 * LANES), F32),
        ],
        compiler_params=pltpu.CompilerParams(vmem_limit_bytes=56 * 1024 * 1024),
        name="slab",
    )(place, own, other, cells)

    total = summed_over_grid(sums.reshape(28 * chans, LANES)).reshape(28, chans, LANES)
    weight_total = jnp.stack([total[:27, :, :chans], total[:27, :, chans:]])
    bias_total = total[27, 0].reshape(2, chans)

    parts = outs.reshape(2, micros, gy, local_y, width, LANES).transpose(2, 0, 1, 3, 4, 5)
    parts = lax.all_to_all(parts, "gy", 0, 0)
    parts = parts.reshape(gy, 2, micros, local_y, width, size_x, chans)
    parts = parts.transpose(1, 2, 6, 5, 3, 0, 4)
    parts = parts.reshape(2, micros, chans, size_x, local_y, local_z)
    return (parts[0][None], parts[1][None], weight_total, bias_total)


def solution(mesh):
    grid = P(None, None, None, "gy", "gz")
    section_grid = P("section", None, None, None, "gy", "gz")
    return jax.shard_map(
        per_device,
        mesh=mesh,
        in_specs=(grid, P("section", None, None, None), P("section", None), grid),
        out_specs=(section_grid, section_grid, P("section", None, None, None), P("section", None)),
        check_vma=False,
    )
```

```python
import functools
import math

import jax
import jax.numpy as jnp
from jax import lax
from jax.experimental import pallas as pl
from jax.experimental.pallas import tpu as pltpu
from jax.sharding import PartitionSpec as P

HALO = 8
LANES = 128
BF16 = jnp.bfloat16
F32 = jnp.float32


def split_terms(values):
    high = values.astype(BF16)
    return high, (values - high.astype(F32)).astype(BF16)


def slab_kernel(dims, place, own, first, second, *rest):
    micros, rows_y, depth, width, chunk_y, chans, limit_z, scale, slabs, reach = dims
    windows, rest = rest[:slabs], rest[slabs:]
    edges, rest = rest[:-11], rest[-11:]
    front, back, sums, fwd, bwd, acts, rim, kept, slopes, field, acc = rest
    section, slab, swap = place[0], place[1], place[2]
    origin = place[3]
    chunk = chunk_y * depth
    chunks = rows_y // chunk_y
    per_owner = rows_y // slabs
    span = windows[0].shape[3]
    half_taps = first.shape[0]
    zs = lax.broadcasted_iota(jnp.int32, (depth, LANES), 0)
    in_grid = ((zs + origin >= 0) & (zs + origin < limit_z)).astype(F32)[None]
    mine = ((zs >= HALO) & (zs < HALO + width)).astype(F32)[None]

    def other(tap):
        index = tap % half_taps
        return jnp.where(swap // 2 == tap // half_taps, first[index], second[index])

    def prepare(pair, carry):
        for half in range(2):
            layer = 2 * pair + half
            for b in range(3):
                for c in range(3):
                    taps = []
                    for a in range(3):
                        tap = 9 * a + 3 * b + c
                        both = jnp.where(pair == section, own[tap], other(tap))
                        taps.append(both[:, half * chans : (half + 1) * chans])
                    top = jnp.concatenate([taps[1], taps[2]], axis=1)
                    low = jnp.concatenate([taps[0], taps[1]], axis=1)
                    block = jnp.concatenate([top, low], axis=0)
                    for target, value, row, col in (
                        (fwd, block.T, b, c),
                        (bwd, block, 2 - b, 2 - c),
                    ):
                        hi, lo = split_terms(value)
                        at = slice(col * LANES, (col + 1) * LANES)
                        target[layer, 2 * row * LANES : (2 * row + 1) * LANES, at] = hi
                        target[layer, (2 * row + 1) * LANES : (2 * row + 2) * LANES, at] = hi
                        target[layer, (6 + row) * LANES : (7 + row) * LANES, at] = lo
        return carry

    lax.fori_loop(0, 2, prepare, 0)

    def over_chunks(body):
        if chunks == 1:
            for micro in range(micros):
                body(micro, 0, 0)
        else:

            def step(index, carry):
                part = index % chunks
                body(index // chunks, part, pl.multiple_of(part * chunk, 16))
                return carry

            lax.fori_loop(0, micros * chunks, step, 0)

    def put_rows(target, lead, start, values):
        hi, lo = split_terms(values)
        at = pl.ds(start + depth, chunk)
        target[(*lead, at, slice(0, LANES))] = hi
        target[(*lead, at, slice(LANES, 2 * LANES))] = lo

    def pieces_of(source, lead, start):
        return [source[(*lead, pl.ds(start + b * depth, chunk), slice(None))] for b in range(3)]

    def conv(source, lead, start, table):
        pieces = pieces_of(source, lead, start)
        left = jnp.concatenate(pieces + [piece[:, :LANES] for piece in pieces], axis=1)
        out = jnp.dot(left, table[...], preferred_element_type=F32)
        before = pltpu.roll(out[:, :LANES], 1, 0)
        after = pltpu.roll(out[:, 2 * LANES :], chunk - 1, 0)
        return before + out[:, LANES : 2 * LANES] + after

    def masked(values, mask):
        return (values.reshape(chunk_y, depth, LANES) * mask).reshape(chunk, LANES)

    blank = jnp.zeros((depth, 2 * LANES), BF16)
    for micro in range(micros):
        for edge in (0, rows_y + 1):
            at = slice(edge * depth, (edge + 1) * depth)
            for layer in range(4):
                acts[layer, micro, at, :] = blank
            for side in range(2):
                rim[side, micro, at, :] = blank

    def emit(target, micro, part, values):
        inner = values.reshape(chunk_y, depth, LANES)[:, HALO : HALO + width, :]
        for y in range(chunk_y):
            row = part * chunk_y + y
            to = lax.rem(row // per_owner + slabs - slab, slabs)
            target[to, micro, row % per_owner] = inner[y]

    def place_cells(which, write):
        for micro in range(micros):
            for turn, window in enumerate(windows):
                owner = lax.rem(slab + slabs - turn, slabs)
                for y in range(per_owner):
                    value = window[which, micro, y]
                    if span < depth:
                        value = jnp.concatenate(
                            [value, jnp.zeros((depth - span, LANES), F32)], axis=0
                        )
                    row = owner * per_owner + y
                    write(micro, pl.multiple_of(row * depth, 16), value)

    def place_edges(which, add):
        left = slab < reach
        at = jnp.where(left, 0, HALO + width)

        @pl.when(left | (slab >= slabs - reach))
        def _():
            for m, edge in enumerate(edges):
                owner = jnp.where(left, m, (m + 1) % slabs)
                for micro in range(micros):
                    for y in range(per_owner):
                        start = (owner * per_owner + y) * depth + at
                        add(micro, pl.multiple_of(start, 8), edge[which, micro, y])

    def fill(which):
        def write(micro, start, value):
            field[micro, pl.ds(start, depth), :] = value

        def add(micro, start, value):
            field[micro, pl.ds(start, HALO), :] += value

        place_cells(which, write)
        place_edges(which, add)

    fill(0)
    over_chunks(
        lambda micro, part, start: put_rows(
            acts, (0, micro), start, field[micro, pl.ds(start, chunk), :]
        )
    )

    for layer in range(4):
        half = layer % 2

        def forward(micro, part, start):
            row = jnp.where(section == layer // 2, own[27, 0:1, :], other(27)[0:1, :])
            bias = row[:, half * chans : (half + 1) * chans]
            bias = jnp.concatenate([bias, bias], axis=1)
            pre = conv(acts, (layer, micro), start, fwd.at[layer]) + bias
            grown = 1.0 + jnp.exp(-pre)
            sigma = 1.0 / grown
            kept[layer, micro, pl.ds(start, chunk), :] = sigma * (1.0 + pre * (1.0 - sigma))
            out = masked(pre / grown, in_grid)
            if layer < 3:
                put_rows(acts, (layer + 1, micro), start, out)
            if half == 1:
                pl.when(section == layer // 2)(lambda: emit(front, micro, part, out))

        over_chunks(forward)

    def take_gradient(layer, micro, start, gradient):
        slope = masked(gradient * kept[layer, micro, pl.ds(start, chunk), :], in_grid)
        slopes[layer, micro, pl.ds(start, chunk), :] = masked(slope, mine)
        put_rows(rim, (layer % 2, micro), start, slope)

    fill(1)
    over_chunks(
        lambda micro, part, start: take_gradient(
            3, micro, start, field[micro, pl.ds(start, chunk), :]
        )
    )

    def backward(layer):
        def pull(micro, part, start):
            gradient = conv(rim, (layer % 2, micro), start, bwd.at[layer])
            if layer > 0:
                take_gradient(layer - 1, micro, start, gradient)
            if layer % 2 == 0:
                pl.when(section == layer // 2)(lambda: emit(back, micro, part, gradient))

        over_chunks(pull)

    backward(3)
    backward(2)

    @pl.when(section == 0)
    def _():
        backward(1)
        backward(0)

    def spot(tap):
        quarter = sums.shape[0] // 4
        return (tap // quarter ^ swap) * quarter + tap % quarter

    sums[spot(27)] = jnp.zeros((chans, LANES), F32)
    for slot in range(2):
        layer = 2 * section + slot
        acc[...] = jnp.zeros(acc.shape, F32)

        def gather(micro, part, start):
            slope = slopes[layer, micro, pl.ds(start, chunk), :]
            moved = [pltpu.roll(slope, 1 if c == 0 else chunk - 1, 0) if c != 1 else slope for c in (2, 1, 0)]
            terms = [split_terms(value) for value in moved]
            left_hi = jnp.concatenate([hi for hi, lo in terms], axis=1)
            left_lo = jnp.concatenate([lo for hi, lo in terms], axis=1)
            pieces = pieces_of(acts, (layer, micro), start)
            full = jnp.concatenate(pieces, axis=1)
            high = jnp.concatenate([piece[:, :LANES] for piece in pieces], axis=1)
            over_rows = (((0,), (0,)), ((), ()))
            one = lax.dot_general(left_hi, full, over_rows, preferred_element_type=F32)
            two = lax.dot_general(left_lo, high, over_rows, preferred_element_type=F32)
            for b in range(3):
                at = slice(b * LANES, (b + 1) * LANES)
                acc[0 : 3 * LANES, at] += (
                    one[:, 2 * b * LANES : (2 * b + 1) * LANES]
                    + one[:, (2 * b + 1) * LANES : (2 * b + 2) * LANES]
                    + two[:, at]
                )
            acc[3 * LANES : 3 * LANES + 1, 0:LANES] += jnp.sum(slope, axis=0, keepdims=True)

        over_chunks(gather)
        lanes = slice(slot * chans, (slot + 1) * chans)
        for b in range(3):
            for c in range(3):
                block = acc[c * LANES : (c + 1) * LANES, b * LANES : (b + 1) * LANES] * scale
                tap = 3 * b + c
                sums[spot(tap), :, lanes] = block[chans:, :chans]
                sums[spot(9 + tap), :, lanes] = block[:chans, :chans] + block[chans:, chans:]
                sums[spot(18 + tap), :, lanes] = block[:chans, chans:]
        row = acc[3 * LANES : 3 * LANES + 1, 0:LANES] * scale
        sums[spot(27), 0:1, lanes] = row[:, :chans] + row[:, chans:]


def packed(weights, biases):
    pair = jnp.concatenate([weights[0], weights[1]], axis=-1)
    row = jnp.concatenate([biases[0], biases[1]])[None, None, :]
    tail = jnp.pad(row, ((0, 0), (0, pair.shape[1] - 1), (0, 0)))
    return jnp.concatenate([pair, tail], axis=0)


def turned(block, distance):
    count = lax.axis_size("gy")
    return lax.ppermute(block, "gy", [(i, (i + distance) % count) for i in range(count)])


def spread(blocks):
    slabs = len(blocks)
    if slabs <= 8:
        return [blocks[0]] + [turned(blocks[turn], turn) for turn in range(1, slabs)]
    slab = lax.axis_index("gy")
    got = lax.all_to_all(jnp.roll(jnp.stack(blocks), slab, axis=0), "gy", 0, 0)
    got = jnp.roll(got[::-1], slab + 1, axis=0)
    return [got[turn] for turn in range(slabs)]


def swapped(block, bit):
    count = lax.axis_size("gz")
    return lax.ppermute(block, "gz", [(i, i ^ bit) for i in range(count)])


def unpack_kernel(chunk, place, *rest):
    slab, swap = place[1], place[2]
    near, rest = rest[:-5], rest[-5:]
    beside, across, weight, bias, whole = rest
    slabs = len(near)
    quarter = slabs * chunk
    chans = weight.shape[-1]

    def put(relative, turn, values):
        at = (relative ^ swap) * quarter + lax.rem(slab + slabs - turn, slabs) * chunk
        whole[pl.ds(pl.multiple_of(at, 8), chunk), :] = values

    for turn in range(slabs):
        rows = slice(turn * chunk, (turn + 1) * chunk)
        put(0, turn, near[turn][...])
        put(1, turn, beside[rows, :])
        for part in range(2):
            put(2 + part, turn, across[part * quarter + rows.start : part * quarter + rows.stop, :])
    for layer in range(2):
        lanes = slice(layer * chans, (layer + 1) * chans)
        for tap in range(28):
            at = tap // 7 * quarter + tap % 7 * chans
            if tap < 27:
                weight[layer, tap] = whole[at : at + chans, lanes]
            else:
                bias[layer : layer + 1, :] = whole[at : at + 1, lanes]


def summed_over_grid(block, place, chans):
    slabs = lax.axis_size("gy")
    slab = lax.axis_index("gy")
    for bit in (1, 2):
        rows = block.shape[0] // 2
        block = block[:rows] + swapped(block[rows:], bit)
    chunk = -(-block.shape[0] // (8 * slabs)) * 8
    block = jnp.pad(block, ((0, slabs * chunk - block.shape[0]), (0, 0)))
    parts = block.reshape(slabs, chunk, LANES)

    def part_for(turn):
        return lax.dynamic_index_in_dim(parts, (slab + turn) % slabs, 0, keepdims=False)

    mine = sum(spread([part_for(turn) for turn in range(slabs)]))
    near = spread([mine] * slabs)
    quarter = jnp.concatenate(near, axis=0)
    beside = swapped(quarter, 2)
    across = swapped(jnp.concatenate([quarter, beside], axis=0), 1)
    vmem = pl.BlockSpec(memory_space=pltpu.VMEM)
    return pl.pallas_call(
        functools.partial(unpack_kernel, chunk),
        out_shape=(
            jax.ShapeDtypeStruct((2, 27, chans, chans), F32),
            jax.ShapeDtypeStruct((2, chans), F32),
        ),
        in_specs=[pl.BlockSpec(memory_space=pltpu.SMEM)] + [vmem] * (slabs + 2),
        out_specs=(vmem, vmem),
        scratch_shapes=[pltpu.VMEM((4 * slabs * chunk, LANES), F32)],
        compiler_params=pltpu.CompilerParams(vmem_limit_bytes=16 * 1024 * 1024),
        name="unpack",
    )(place, *near, beside, across)


def restored(parts, size_x, chans):
    slabs, micros, local_y, width, _ = parts.shape
    slab = lax.axis_index("gy")
    got = spread([parts[turn] for turn in range(slabs)])
    twice = jnp.stack((got[::-1] * 2)[: 2 * slabs - 1])
    whole = lax.dynamic_slice_in_dim(twice, slabs - 1 - slab, slabs, 0)
    whole = whole.reshape(slabs, micros, local_y, width, size_x, chans)
    whole = whole.transpose(1, 5, 4, 2, 0, 3)
    return whole.reshape(1, micros, chans, size_x, local_y, slabs * width)


def edge_piece(fields, owner, reach):
    slabs, columns = lax.axis_size("gy"), lax.axis_size("gz")
    local_z = fields.shape[3]
    width = local_z // slabs
    follower = (owner + 1) % slabs
    whole = 0.0
    for r in range(reach):
        low = fields[:, :, :, local_z - HALO + r * width :]
        low = jnp.pad(low, ((0, 0),) * 3 + ((0, r * width), (0, 0)))
        high = fields[:, :, :, : HALO - r * width]
        high = jnp.pad(high, ((0, 0),) * 3 + ((r * width, 0), (0, 0)))
        route = [(owner * columns + g, r * columns + g + 1) for g in range(columns - 1)]
        last = (slabs - 1 - r) * columns
        route += [(follower * columns + g, last + g - 1) for g in range(1, columns)]
        sent = jnp.where(lax.axis_index("gy") == owner, low, high)
        whole = whole + lax.ppermute(sent, ("gy", "gz"), route) if r else lax.ppermute(sent, ("gy", "gz"), route)
    return whole


def per_device(inflow, weights, biases, cotangent):
    micros, chans, size_x, local_y, local_z = inflow.shape
    slabs, columns = lax.axis_size("gy"), lax.axis_size("gz")
    rows_y = local_y * slabs
    width = local_z // slabs
    span = width + 2 * HALO
    reach = -(-HALO // width)
    depth = -(-span // 16) * 16
    chunk_y = max(n for n in range(1, rows_y + 1) if rows_y % n == 0 and n * depth <= 384)
    scale = 1.0 / math.sqrt(micros * size_x * rows_y * local_z * columns)
    section = lax.axis_index("section")
    slab, column = lax.axis_index("gy"), lax.axis_index("gz")
    swap = 2 * (column % 2) + column // 2 % 2

    own = packed(weights, biases)
    half = own.shape[0] // 2
    sent = jnp.where(column % 2 == 1, own[half:], own[:half])
    first = lax.ppermute(sent, "section", [(0, 1), (1, 0)])
    second = swapped(first, 1)

    fields = jnp.stack([inflow, cotangent]).transpose(0, 1, 4, 5, 3, 2)
    fields = fields.reshape(2, micros, local_y, local_z, size_x * chans)
    wide = jnp.pad(fields, ((0, 0),) * 3 + ((HALO, HALO), (0, 0)))
    edges = []
    if slabs > 8:
        up = [(i, i + 1) for i in range(columns - 1)]
        down = [(i + 1, i) for i in range(columns - 1)]
        before = lax.ppermute(fields[:, :, :, local_z - HALO :], "gz", up)
        after = lax.ppermute(fields[:, :, :, :HALO], "gz", down)
        wide = jnp.concatenate([before, fields, after], axis=3)
    else:
        for m in range(slabs):
            edges.append(edge_piece(fields, m, reach))

    def window(turn):
        return lax.dynamic_slice_in_dim(wide, (slab + turn) % slabs * width, span, axis=3)

    windows = spread([window(turn) for turn in range(slabs)])

    origin = column * local_z + slab * width - HALO
    place = jnp.stack([section, slab, swap, origin]).astype(jnp.int32)
    dims = (
        (micros, rows_y, depth, width, chunk_y, chans, local_z * columns, scale, slabs, reach)
    )
    padded = (rows_y + 2) * depth
    full = rows_y * depth
    vmem = pl.BlockSpec(memory_space=pltpu.VMEM)
    piece = jax.ShapeDtypeStruct((slabs, micros, local_y, width, LANES), F32)
    scratch = [
        pltpu.VMEM((4, 9 * LANES, 3 * LANES), BF16),
        pltpu.VMEM((4, 9 * LANES, 3 * LANES), BF16),
        pltpu.VMEM((4, micros, padded, 2 * LANES), BF16),
        pltpu.VMEM((2, micros, padded, 2 * LANES), BF16),
        pltpu.VMEM((4, micros, full, LANES), F32),
        pltpu.VMEM((4, micros, full, LANES), F32),
        pltpu.VMEM((micros, full, LANES), F32),
        pltpu.VMEM((3 * LANES + 8, 3 * LANES), F32),
    ]
    held = sum(math.prod(item.shape) * item.dtype.itemsize for item in scratch)
    held += 4 * (2 * 28 * chans * LANES + 6 * micros * full * LANES)
    front, back, sums = pl.pallas_call(
        functools.partial(slab_kernel, dims),
        out_shape=(piece, piece, jax.ShapeDtypeStruct((28, chans, LANES), F32)),
        in_specs=[pl.BlockSpec(memory_space=pltpu.SMEM)] + [vmem] * (3 + slabs + len(edges)),
        out_specs=(vmem, vmem, vmem),
        scratch_shapes=scratch,
        compiler_params=pltpu.CompilerParams(vmem_limit_bytes=held + 8 * 1024 * 1024),
        name="slab",
    )(place, own, first, second, *windows, *edges)

    weight_total, bias_total = summed_over_grid(sums.reshape(28 * chans, LANES), place, chans)
    section_out = restored(front, size_x, chans)
    section_grad = restored(back, size_x, chans)
    return (section_out, section_grad, weight_total, bias_total)


def solution(mesh):
    grid = P(None, None, None, "gy", "gz")
    section_grid = P("section", None, None, None, "gy", "gz")
    return jax.shard_map(
        per_device,
        mesh=mesh,
        in_specs=(grid, P("section", None, None, None), P("section", None), grid),
        out_specs=(section_grid, section_grid, P("section", None, None, None), P("section", None)),
        check_vma=False,
    )
```

```python
import functools
import math

import jax
import jax.numpy as jnp
from jax import lax
from jax.experimental import pallas as pl
from jax.experimental.pallas import tpu as pltpu
from jax.sharding import PartitionSpec as P

HALO = 8
LANES = 128
TAPS = 27
BLOCKS = 28
BF16 = jnp.bfloat16
F32 = jnp.float32
SMEM = pl.BlockSpec(memory_space=pltpu.SMEM)
VMEM = pl.BlockSpec(memory_space=pltpu.VMEM)


def call(kernel, name, outs, args, scratch=(), flops=0):
    arrays = [jax.ShapeDtypeStruct(shape, kind) for shape, kind in outs]
    size = sum(math.prod(item.shape) * item.dtype.itemsize for item in [*arrays, *args[1:], *scratch])
    return pl.pallas_call(
        kernel,
        out_shape=arrays,
        in_specs=[SMEM] + [VMEM] * (len(args) - 1),
        out_specs=[VMEM] * len(arrays),
        scratch_shapes=list(scratch),
        compiler_params=pltpu.CompilerParams(vmem_limit_bytes=size + 6 * 1024 * 1024),
        cost_estimate=pl.CostEstimate(flops=flops, bytes_accessed=size, transcendentals=0),
        name=name,
    )(*args)


def split_terms(values):
    high = values.astype(BF16)
    return high, (values - high.astype(F32)).astype(BF16)


def pack_kernel(place, weights, biases, own, sent):
    chans = weights.shape[2]
    half = sent.shape[0]
    for tap in range(TAPS):
        own[tap] = jnp.concatenate([weights[0, tap], weights[1, tap]], axis=1)
    own[TAPS] = jnp.zeros((chans, LANES), F32)
    own[TAPS, 0:1, :] = jnp.concatenate([biases[0:1, :], biases[1:2, :]], axis=1)
    start = place[2] // 2 * half

    def copy(index, carry):
        sent[index] = own[start + index]
        return carry

    lax.fori_loop(0, half, copy, 0)


def table_kernel(place, *refs):
    parts, (fwd, bwd, row) = refs[:-3], refs[-3:]
    swap = place[2]
    count = parts[0].shape[0]
    chans = parts[0].shape[1]

    def block_of(tap):
        if len(parts) == 1:
            return parts[0][tap]
        index = tap % count
        return jnp.where(swap // 2 == tap // count, parts[0][index], parts[1][index])

    for b in range(3):
        for c in range(3):
            taps = [block_of(9 * a + 3 * b + c) for a in range(3)]
            for layer in range(2):
                lanes = slice(layer * chans, (layer + 1) * chans)
                below, level, above = [tap[:, lanes] for tap in taps]
                top = jnp.concatenate([level, above], axis=1)
                low = jnp.concatenate([below, level], axis=1)
                block = jnp.concatenate([top, low], axis=0)
                for target, value, r, at in ((fwd, block.T, b, c), (bwd, block, 2 - b, 2 - c)):
                    hi, lo = split_terms(value)
                    at = slice(at * LANES, (at + 1) * LANES)
                    target[layer, 2 * r * LANES : (2 * r + 1) * LANES, at] = hi
                    target[layer, (2 * r + 1) * LANES : (2 * r + 2) * LANES, at] = hi
                    target[layer, (6 + r) * LANES : (7 + r) * LANES, at] = lo
    last = block_of(TAPS)[0:1, :]
    for layer in range(2):
        part = last[:, layer * chans : (layer + 1) * chans]
        row[layer] = jnp.broadcast_to(jnp.concatenate([part, part], axis=1), (8, LANES))


def cut_kernel(dims, place, *refs):
    micros, chans, size_x, local_y, local_z, slabs, width, span, edged, fields = dims
    sources, refs = refs[:fields], refs[fields:]
    outs, wide = refs[:-1], refs[-1]
    slab = place[1]
    step = size_x * local_y
    for field, source in enumerate(sources):
        windows = outs[field * slabs : (field + 1) * slabs]
        edges = outs[fields * slabs :]
        for micro in range(micros):
            for y in range(local_y):
                first = micro * chans * step + y
                parts = [
                    source[pl.ds(first + x * local_y, chans, stride=step), :] for x in range(size_x)
                ]
                wide[field, micro, y, HALO : HALO + local_z] = jnp.concatenate(parts, axis=0).T
                wide[field, micro, y, :HALO] = jnp.zeros((HALO, LANES), F32)
                wide[field, micro, y, HALO + local_z :] = jnp.zeros((HALO, LANES), F32)
                if edged:
                    for turn in range(slabs):
                        start = lax.rem(slab + turn, slabs) * width
                        if width % 8 == 0:
                            start = pl.multiple_of(start, 8)
                        windows[turn][micro, y] = wide[field, micro, y, pl.ds(start, span)]
                    low = wide[field, micro, y, local_z : local_z + HALO]
                    high = wide[field, micro, y, HALO : 2 * HALO]
                    for m in range(slabs):
                        edges[m][field, micro, y] = jnp.where(slab == m, low, high)
                else:
                    windows[0][micro, y] = wide[field, micro, y, HALO : HALO + local_z]


class Slab:
    def __init__(self, dims, place):
        self.micros, self.rows_y, self.depth, self.width, self.chunk_y, self.slabs, limit_z = dims
        self.section, self.slab, self.swap, origin = place[0], place[1], place[2], place[3]
        self.chunk = self.chunk_y * self.depth
        self.chunks = self.rows_y // self.chunk_y
        self.per_owner = self.rows_y // self.slabs
        zs = lax.broadcasted_iota(jnp.int32, (self.depth, LANES), 0)
        inside = (zs + origin >= 0) & (zs + origin < limit_z)
        self.in_grid = inside.astype(F32)[None]
        self.mine = ((zs >= HALO) & (zs < HALO + self.width)).astype(F32)[None]

    def over_chunks(self, body):
        if self.chunks == 1:
            body(0, 0)
        else:

            def step(part, carry):
                body(part, pl.multiple_of(part * self.chunk, 16))
                return carry

            lax.fori_loop(0, self.chunks, step, 0)

    def masked(self, values, mask):
        cut = values.reshape(-1, self.depth, LANES) * mask
        return cut.reshape(values.shape)

    def put_rows(self, target, lead, start, values):
        hi, lo = split_terms(values)
        at = pl.ds(start + self.depth, self.chunk)
        for micro in range(self.micros):
            rows = slice(micro * self.chunk, (micro + 1) * self.chunk)
            target[lead, micro, at, slice(0, LANES)] = hi[rows]
            target[lead, micro, at, slice(LANES, 2 * LANES)] = lo[rows]

    def pieces_of(self, source, lead, start):
        pieces = []
        for b in range(3):
            at = pl.ds(start + b * self.depth, self.chunk)
            parts = [source[lead, micro, at, :] for micro in range(self.micros)]
            pieces.append(jnp.concatenate(parts, axis=0))
        return pieces

    def conv(self, source, lead, start, table):
        pieces = self.pieces_of(source, lead, start)
        left = jnp.concatenate(pieces + [piece[:, :LANES] for piece in pieces], axis=1)
        out = jnp.dot(left, table[...], preferred_element_type=F32)
        before = pltpu.roll(out[:, :LANES], 1, 0)
        after = pltpu.roll(out[:, 2 * LANES :], out.shape[0] - 1, 0)
        return before + out[:, LANES : 2 * LANES] + after

    def by_owner(self, layer, own, other, body):
        mine = layer // 2 == self.section
        pl.when(mine)(lambda: body(own, layer % 2))
        pl.when(jnp.logical_not(mine))(lambda: body(other, layer % 2))

    def blank_edges(self, target):
        blank = jnp.zeros((self.depth, 2 * LANES), BF16)
        for lead in range(target.shape[0]):
            for micro in range(self.micros):
                for edge in (0, self.rows_y + 1):
                    target[lead, micro, edge * self.depth : (edge + 1) * self.depth, :] = blank

    def read(self, source, lead, start):
        at = pl.ds(start, self.chunk)
        return jnp.concatenate([source[lead, micro, at, :] for micro in range(self.micros)], axis=0)

    def write(self, target, lead, start, values):
        for micro in range(self.micros):
            rows = slice(micro * self.chunk, (micro + 1) * self.chunk)
            target[lead, micro, pl.ds(start, self.chunk), :] = values[rows]

    def emit(self, target, part, values):
        inner = values.reshape(self.micros, self.chunk_y, self.depth, LANES)
        for y in range(self.chunk_y):
            row = part * self.chunk_y + y
            to = lax.rem(row // self.per_owner + self.slabs - self.slab, self.slabs)
            for micro in range(self.micros):
                value = inner[micro, y, HALO : HALO + self.width, :]
                target[to, micro, row % self.per_owner] = value

    def fill(self, field, windows, edges, which):
        span = windows[0].shape[2]
        for micro in range(self.micros):
            for turn, window in enumerate(windows):
                owner = lax.rem(self.slab + self.slabs - turn, self.slabs)
                for y in range(self.per_owner):
                    value = window[micro, y]
                    if span < self.depth:
                        extra = jnp.zeros((self.depth - span, LANES), F32)
                        value = jnp.concatenate([value, extra], axis=0)
                    start = pl.multiple_of((owner * self.per_owner + y) * self.depth, 16)
                    field[0, micro, pl.ds(start, self.depth), :] = value
        if not edges:
            return
        left = self.slab == 0
        at = jnp.where(left, 0, HALO + self.width)

        @pl.when(left | (self.slab == self.slabs - 1))
        def _():
            for m, edge in enumerate(edges):
                owner = jnp.where(left, m, (m + 1) % self.slabs)
                for micro in range(self.micros):
                    for y in range(self.per_owner):
                        start = pl.multiple_of((owner * self.per_owner + y) * self.depth + at, 8)
                        field[0, micro, pl.ds(start, HALO), :] = edge[which, micro, y]


def forward_kernel(dims, place, own, own_row, other, other_row, *refs):
    slab = Slab(dims, place)
    refs, (acts, kept, front, field) = refs[:-4], refs[-4:]
    slab.blank_edges(acts)
    slab.fill(field, refs[: slab.slabs], refs[slab.slabs :], 0)
    slab.over_chunks(
        lambda part, start: slab.put_rows(acts, 0, start, slab.read(field, 0, start))
    )

    def layer_step(layer, carry):
        def run(tables, half):
            table, row = tables

            def body(part, start):
                pre = slab.conv(acts, layer, start, table.at[half]) + row[half][0:1, :]
                grown = 1.0 + jnp.exp(-pre)
                sigma = 1.0 / grown
                slab.write(kept, layer, start, sigma * (1.0 + pre * (1.0 - sigma)))
                out = slab.masked(pre / grown, slab.in_grid)
                pl.when(layer < 3)(lambda: slab.put_rows(acts, layer + 1, start, out))
                pl.when(layer == 2 * slab.section + 1)(lambda: slab.emit(front, part, out))

            slab.over_chunks(body)

        slab.by_owner(layer, (own, own_row), (other, other_row), run)
        return carry

    lax.fori_loop(0, 4, layer_step, 0)


def backward_kernel(dims, scale, place, own, other, acts, kept, *refs):
    slab = Slab(dims, place)
    refs, (back, sums, rim, slopes, field, acc) = refs[:-6], refs[-6:]
    slab.blank_edges(rim)
    slab.fill(field, refs[: slab.slabs], refs[slab.slabs :], 1)

    def take_gradient(layer, start, gradient):
        slope = slab.masked(gradient * slab.read(kept, layer, start), slab.in_grid)
        slab.write(slopes, layer, start, slab.masked(slope, slab.mine))
        slab.put_rows(rim, layer % 2, start, slope)

    slab.over_chunks(lambda part, start: take_gradient(3, start, slab.read(field, 0, start)))

    def layer_step(index, carry):
        layer = 3 - index

        def run(table, half):
            def body(part, start):
                gradient = slab.conv(rim, layer % 2, start, table.at[half])
                pl.when(layer > 0)(lambda: take_gradient(layer - 1, start, gradient))
                pl.when(layer == 2 * slab.section)(lambda: slab.emit(back, part, gradient))

            slab.over_chunks(body)

        slab.by_owner(layer, own, other, run)
        return carry

    lax.fori_loop(0, jnp.where(slab.section == 0, 4, 2), layer_step, 0)

    quarter = BLOCKS // 4
    chans = LANES // 2

    def spot(tap):
        return (tap // quarter ^ slab.swap) * quarter + tap % quarter

    sums[spot(TAPS)] = jnp.zeros((chans, LANES), F32)
    for slot in range(2):
        layer = 2 * slab.section + slot
        acc[...] = jnp.zeros(acc.shape, F32)

        def gather(part, start):
            slope = slab.read(slopes, layer, start)
            moved = [pltpu.roll(slope, slope.shape[0] - 1, 0), slope, pltpu.roll(slope, 1, 0)]
            terms = [split_terms(value) for value in moved]
            left_hi = jnp.concatenate([hi for hi, lo in terms], axis=1)
            left_lo = jnp.concatenate([lo for hi, lo in terms], axis=1)
            pieces = slab.pieces_of(acts, layer, start)
            full = jnp.concatenate(pieces, axis=1)
            high = jnp.concatenate([piece[:, :LANES] for piece in pieces], axis=1)
            over_rows = (((0,), (0,)), ((), ()))
            one = lax.dot_general(left_hi, full, over_rows, preferred_element_type=F32)
            two = lax.dot_general(left_lo, high, over_rows, preferred_element_type=F32)
            for b in range(3):
                at = slice(b * LANES, (b + 1) * LANES)
                acc[0 : 3 * LANES, at] += (
                    one[:, 2 * b * LANES : (2 * b + 1) * LANES]
                    + one[:, (2 * b + 1) * LANES : (2 * b + 2) * LANES]
                    + two[:, at]
                )
            acc[3 * LANES : 3 * LANES + 1, 0:LANES] += jnp.sum(slope, axis=0, keepdims=True)

        slab.over_chunks(gather)
        lanes = slice(slot * chans, (slot + 1) * chans)
        for b in range(3):
            for c in range(3):
                block = acc[c * LANES : (c + 1) * LANES, b * LANES : (b + 1) * LANES] * scale
                tap = 3 * b + c
                sums[spot(tap), :, lanes] = block[chans:, :chans]
                sums[spot(9 + tap), :, lanes] = block[:chans, :chans] + block[chans:, chans:]
                sums[spot(18 + tap), :, lanes] = block[:chans, chans:]
        row = acc[3 * LANES : 3 * LANES + 1, 0:LANES] * scale
        sums[spot(TAPS), 0:1, lanes] = row[:, :chans] + row[:, chans:]


def unpack_kernel(chunk, place, *refs):
    slab, swap = place[1], place[2]
    near, (beside, across, weight, bias, whole) = refs[:-5], refs[-5:]
    slabs = len(near)
    quarter = slabs * chunk
    chans = weight.shape[-1]

    def put(relative, turn, values):
        at = (relative ^ swap) * quarter + lax.rem(slab + slabs - turn, slabs) * chunk
        whole[pl.ds(pl.multiple_of(at, 8), chunk), :] = values

    for turn in range(slabs):
        first = turn * chunk
        put(0, turn, near[turn][...])
        put(1, turn, beside[first : first + chunk, :])
        for part in range(2):
            start = part * quarter + first
            put(2 + part, turn, across[start : start + chunk, :])
    for layer in range(2):
        lanes = slice(layer * chans, (layer + 1) * chans)
        for tap in range(BLOCKS):
            at = tap // 7 * quarter + tap % 7 * chans
            if tap < TAPS:
                weight[layer, tap] = whole[at : at + chans, lanes]
            else:
                bias[layer : layer + 1, :] = whole[at : at + 1, lanes]


def restore_kernel(dims, place, *refs):
    micros, chans, size_x, local_y, width = dims
    pieces, (target, whole) = refs[:-2], refs[-2:]
    slab = place[1]
    slabs = len(pieces)
    step = size_x * local_y
    for micro in range(micros):
        for y in range(local_y):
            for turn in range(slabs):
                start = lax.rem(slab + slabs - turn, slabs) * width
                if width % 8 == 0:
                    start = pl.multiple_of(start, 8)
                whole[pl.ds(start, width), :] = pieces[turn][micro, y]
            block = whole[...].T
            for x in range(size_x):
                first = micro * chans * step + x * local_y + y
                part = block[x * chans : (x + 1) * chans]
                target[pl.ds(first, chans, stride=step), :] = part


def turned(block, distance):
    count = lax.axis_size("gy")
    return lax.ppermute(block, "gy", [(i, (i + distance) % count) for i in range(count)])


def spread(blocks):
    slabs = len(blocks)
    if slabs <= 8:
        return [blocks[0]] + [turned(blocks[turn], turn) for turn in range(1, slabs)]
    slab = lax.axis_index("gy")
    got = lax.all_to_all(jnp.roll(jnp.stack(blocks), slab, axis=0), "gy", 0, 0)
    got = jnp.roll(got[::-1], slab + 1, axis=0)
    return [got[turn] for turn in range(slabs)]


def swapped(block, bit):
    count = lax.axis_size("gz")
    return lax.ppermute(block, "gz", [(i, i ^ bit) for i in range(count)])


def edge_route(owner):
    slabs, columns = lax.axis_size("gy"), lax.axis_size("gz")
    follower = (owner + 1) % slabs
    route = [(owner * columns + g, g + 1) for g in range(columns - 1)]
    last = (slabs - 1) * columns
    return route + [(follower * columns + g, last + g - 1) for g in range(1, columns)]


def windows_of(inflow, cotangent, place, slabs, width, span):
    micros, chans, size_x, local_y, local_z = inflow.shape
    rows = micros * chans * size_x * local_y
    edged = width >= HALO and slabs > 1
    dims = (micros, chans, size_x, local_y, local_z, slabs if edged else 1, width, span, edged, 2)
    outs = [((micros, local_y, span if edged else local_z, LANES), F32)] * (2 * dims[5])
    if edged:
        outs += [((2, micros, local_y, HALO, LANES), F32)] * slabs
    wide = pltpu.VMEM((2, micros, local_y, local_z + 2 * HALO, LANES), F32)
    fields = [inflow.reshape(rows, local_z), cotangent.reshape(rows, local_z)]
    got = call(functools.partial(cut_kernel, dims), "cut", outs, [place, *fields], [wide])
    if edged:
        edges = [
            lax.ppermute(edge, ("gy", "gz"), edge_route(m))
            for m, edge in enumerate(got[2 * slabs :])
        ]
        return spread(got[:slabs]), spread(got[slabs : 2 * slabs]), edges
    columns = lax.axis_size("gz")
    slab = lax.axis_index("gy")
    results = []
    for field in got:
        up = [(i, i + 1) for i in range(columns - 1)]
        down = [(i + 1, i) for i in range(columns - 1)]
        before = lax.ppermute(field[:, :, local_z - HALO :], "gz", up)
        after = lax.ppermute(field[:, :, :HALO], "gz", down)
        wide = jnp.concatenate([before, field, after], axis=2)
        cuts = [
            lax.dynamic_slice_in_dim(wide, (slab + turn) % slabs * width, span, axis=2)
            for turn in range(slabs)
        ]
        results.append(spread(cuts))
    return results[0], results[1], []


def summed_over_grid(block):
    slabs = lax.axis_size("gy")
    slab = lax.axis_index("gy")
    for bit in (1, 2):
        rows = block.shape[0] // 2
        block = block[:rows] + swapped(block[rows:], bit)
    chunk = -(-block.shape[0] // (8 * slabs)) * 8
    block = jnp.pad(block, ((0, slabs * chunk - block.shape[0]), (0, 0)))
    parts = block.reshape(slabs, chunk, LANES)
    sent = [
        lax.dynamic_index_in_dim(parts, (slab + turn) % slabs, 0, keepdims=False)
        for turn in range(slabs)
    ]
    return sum(spread(sent))


def restored(pieces, shape, place):
    micros, chans, size_x, local_y, local_z = shape
    width = pieces[0].shape[2]
    dims = (micros, chans, size_x, local_y, width)
    rows = micros * chans * size_x * local_y
    kernel = functools.partial(restore_kernel, dims)
    scratch = [pltpu.VMEM((local_z, LANES), F32)]
    (whole,) = call(kernel, "restore", [((rows, local_z), F32)], [place, *pieces], scratch)
    return whole.reshape(1, *shape)


def per_device(inflow, weights, biases, cotangent):
    micros, chans, size_x, local_y, local_z = inflow.shape
    slabs, columns = lax.axis_size("gy"), lax.axis_size("gz")
    rows_y = local_y * slabs
    width = local_z // slabs
    span = width + 2 * HALO
    depth = -(-span // 16) * 16
    chunk_y = max(n for n in range(1, rows_y + 1) if rows_y % n == 0 and n * depth <= 384)
    scale = 1.0 / math.sqrt(micros * size_x * rows_y * local_z * columns)
    slab, column = lax.axis_index("gy"), lax.axis_index("gz")
    swap = 2 * (column % 2) + column // 2 % 2
    origin = column * local_z + slab * width - HALO
    place = jnp.stack([lax.axis_index("section"), slab, swap, origin]).astype(jnp.int32)

    half = BLOCKS // 2
    packs = [((BLOCKS, chans, LANES), F32), ((half, chans, LANES), F32)]
    own, sent = call(pack_kernel, "pack", packs, [place, weights, biases])
    first = lax.ppermute(sent, "section", [(0, 1), (1, 0)])

    windows, pulls, edges = windows_of(inflow, cotangent, place, slabs, width, span)
    first, windows, edges = lax.optimization_barrier((first, windows, edges))
    second = swapped(first, 1)

    tables = [((2, 9 * LANES, 3 * LANES), BF16)] * 2 + [((2, 8, LANES), F32)]
    own_fwd, own_bwd, own_row = call(table_kernel, "own_table", tables, [place, own])
    far_fwd, far_bwd, far_row = call(table_kernel, "far_table", tables, [place, first, second])

    dims = (micros, rows_y, depth, width, chunk_y, slabs, local_z * columns)
    padded = (rows_y + 2) * depth
    full = rows_y * depth
    piece = ((slabs, micros, local_y, width, LANES), F32)
    work = 2 * micros * full * 9 * LANES * 3 * LANES
    acts, kept, front = call(
        functools.partial(forward_kernel, dims),
        "forward",
        [((4, micros, padded, 2 * LANES), BF16), ((4, micros, full, LANES), F32), piece],
        [place, own_fwd, own_row, far_fwd, far_row, *windows, *edges],
        [pltpu.VMEM((1, micros, full, LANES), F32)],
        4 * work,
    )
    outward = spread([front[turn] for turn in range(slabs)])
    back, sums = call(
        functools.partial(backward_kernel, dims, scale),
        "backward",
        [piece, ((BLOCKS, chans, LANES), F32)],
        [place, own_bwd, far_bwd, acts, kept, *pulls, *edges],
        [
            pltpu.VMEM((2, micros, padded, 2 * LANES), BF16),
            pltpu.VMEM((4, micros, full, LANES), F32),
            pltpu.VMEM((1, micros, full, LANES), F32),
            pltpu.VMEM((3 * LANES + 8, 3 * LANES), F32),
        ],
        6 * work,
    )

    mine = summed_over_grid(sums.reshape(BLOCKS * chans, LANES))
    near = spread([mine] * slabs)
    near, back = lax.optimization_barrier((near, back))
    quarter = jnp.concatenate(near, axis=0)
    beside = swapped(quarter, 2)
    inward = spread([back[turn] for turn in range(slabs)])
    across = swapped(jnp.concatenate([quarter, beside], axis=0), 1)
    section_out = restored(outward, inflow.shape, place)
    section_grad = restored(inward, inflow.shape, place)
    chunk = mine.shape[0]
    weight_total, bias_total = call(
        functools.partial(unpack_kernel, chunk),
        "unpack",
        [((2, TAPS, chans, chans), F32), ((2, chans), F32)],
        [place, *near, beside, across],
        [pltpu.VMEM((4 * slabs * chunk, LANES), F32)],
    )
    return (section_out, section_grad, weight_total, bias_total)


def solution(mesh):
    grid = P(None, None, None, "gy", "gz")
    section_grid = P("section", None, None, None, "gy", "gz")
    return jax.shard_map(
        per_device,
        mesh=mesh,
        in_specs=(grid, P("section", None, None, None), P("section", None), grid),
        out_specs=(section_grid, section_grid, P("section", None, None, None), P("section", None)),
        check_vma=False,
    )
```

```python
import functools
import math

import jax
import jax.numpy as jnp
from jax import lax
from jax.experimental import pallas as pl
from jax.experimental.pallas import tpu as pltpu
from jax.sharding import PartitionSpec as P

HALO = 8
LANES = 128
TAPS = 27
BLOCKS = 28
BF16 = jnp.bfloat16
F32 = jnp.float32
SMEM = pl.BlockSpec(memory_space=pltpu.SMEM)
VMEM = pl.BlockSpec(memory_space=pltpu.VMEM)


def call(kernel, name, outs, args, scratch=(), flops=0, specs=None):
    arrays = [jax.ShapeDtypeStruct(shape, kind) for shape, kind in outs]
    sized = [item for item in [*arrays, *args[1:], *scratch] if hasattr(item.dtype, "itemsize")]
    size = sum(math.prod(item.shape) * item.dtype.itemsize for item in sized)
    return pl.pallas_call(
        kernel,
        out_shape=arrays,
        in_specs=[SMEM] + (specs or [VMEM] * (len(args) - 1)),
        out_specs=[VMEM] * len(arrays),
        scratch_shapes=list(scratch),
        compiler_params=pltpu.CompilerParams(
            vmem_limit_bytes=56 * 1024 * 1024 if specs else size + 6 * 1024 * 1024
        ),
        cost_estimate=pl.CostEstimate(flops=flops, bytes_accessed=size, transcendentals=0),
        name=name,
    )(*args)


def split_terms(values):
    high = values.astype(BF16)
    return high, (values - high.astype(F32)).astype(BF16)


def start_kernel(dims, place, weights, biases, inflow, cotangent, own, sent, rows, pair, inner, *refs):
    micros, chans, size_x, local_y, local_z = dims
    blocks, small, fields, sems = refs
    copies = [
        pltpu.make_async_copy(weights, blocks, sems.at[0]),
        pltpu.make_async_copy(biases, small, sems.at[1]),
        pltpu.make_async_copy(inflow, fields.at[0], sems.at[2]),
        pltpu.make_async_copy(cotangent, fields.at[1], sems.at[3]),
    ]
    for copy in copies:
        copy.start()
    step = size_x * local_y
    odd = place[4] % 2 == 1
    for field in range(2):
        copies[2 + field].wait()
        for micro in range(micros):
            for y in range(local_y):
                first = micro * chans * step + y
                parts = [
                    fields[field, pl.ds(first + x * local_y, chans, stride=step), :]
                    for x in range(size_x)
                ]
                turned_rows = jnp.concatenate(parts, axis=0).T
                rows[field, micro, y] = turned_rows
                low, high = turned_rows[:HALO], turned_rows[local_z - HALO :]
                pair[field, micro, y] = jnp.where(odd, low, high)
                inner[field, micro, y] = jnp.where(odd, high, low)
    copies[0].wait()
    copies[1].wait()
    half = sent.shape[0]
    for tap in range(TAPS):
        own[tap] = jnp.concatenate([blocks[0, tap], blocks[1, tap]], axis=1)
    own[TAPS] = jnp.zeros((chans, LANES), F32)
    own[TAPS, 0:1, :] = jnp.concatenate([small[0:1, :], small[1:2, :]], axis=1)
    start = place[2] // 2 * half

    def copy(index, carry):
        sent[index] = own[start + index]
        return carry

    lax.fori_loop(0, half, copy, 0)


def window_kernel(dims, place, rows, pair, inner, *refs):
    slabs, width, span, columns = dims
    outs, wide = refs[:-1], refs[-1]
    slab, column = place[1], place[4]
    odd = column % 2 == 1
    _, micros, local_y, local_z, _ = rows.shape
    for field in range(2):
        for micro in range(micros):
            for y in range(local_y):
                one, two = pair[field, micro, y], inner[field, micro, y]
                before = jnp.where(column > 0, jnp.where(odd, one, two), 0.0)
                after = jnp.where(column < columns - 1, jnp.where(odd, two, one), 0.0)
                wide[micro, y, :HALO] = before
                wide[micro, y, HALO : HALO + local_z] = rows[field, micro, y]
                wide[micro, y, HALO + local_z :] = after
                for turn in range(slabs):
                    start = (slab ^ turn) * width
                    if width % 8 == 0:
                        start = pl.multiple_of(start, 8)
                    outs[field * slabs + turn][micro, y] = wide[micro, y, pl.ds(start, span)]


def table_kernel(place, *refs):
    parts, (fwd, bwd, row) = refs[:-3], refs[-3:]
    swap = place[2]
    count = parts[0].shape[0]
    chans = parts[0].shape[1]

    def block_of(tap):
        if len(parts) == 1:
            return parts[0][tap]
        index = tap % count
        return jnp.where(swap // 2 == tap // count, parts[0][index], parts[1][index])

    for b in range(3):
        for c in range(3):
            taps = [block_of(9 * a + 3 * b + c) for a in range(3)]
            for layer in range(2):
                lanes = slice(layer * chans, (layer + 1) * chans)
                below, level, above = [tap[:, lanes] for tap in taps]
                top = jnp.concatenate([level, above], axis=1)
                low = jnp.concatenate([below, level], axis=1)
                block = jnp.concatenate([top, low], axis=0)
                for target, value, r, at in ((fwd, block.T, b, c), (bwd, block, 2 - b, 2 - c)):
                    hi, lo = split_terms(value)
                    at = slice(at * LANES, (at + 1) * LANES)
                    target[layer, 2 * r * LANES : (2 * r + 1) * LANES, at] = hi
                    target[layer, (2 * r + 1) * LANES : (2 * r + 2) * LANES, at] = hi
                    target[layer, (6 + r) * LANES : (7 + r) * LANES, at] = lo
    last = block_of(TAPS)[0:1, :]
    for layer in range(2):
        part = last[:, layer * chans : (layer + 1) * chans]
        row[layer] = jnp.broadcast_to(jnp.concatenate([part, part], axis=1), (8, LANES))


def cut_kernel(dims, place, *refs):
    micros, chans, size_x, local_y, local_z, slabs, width, span, edged, fields = dims
    sources, refs = refs[:fields], refs[fields:]
    outs, wide = refs[:-1], refs[-1]
    slab = place[1]
    step = size_x * local_y
    for field, source in enumerate(sources):
        windows = outs[field * slabs : (field + 1) * slabs]
        edges = outs[fields * slabs :]
        for micro in range(micros):
            for y in range(local_y):
                first = micro * chans * step + y
                parts = [
                    source[pl.ds(first + x * local_y, chans, stride=step), :] for x in range(size_x)
                ]
                wide[field, micro, y, HALO : HALO + local_z] = jnp.concatenate(parts, axis=0).T
                wide[field, micro, y, :HALO] = jnp.zeros((HALO, LANES), F32)
                wide[field, micro, y, HALO + local_z :] = jnp.zeros((HALO, LANES), F32)
                if edged:
                    for turn in range(slabs):
                        start = lax.rem(slab + turn, slabs) * width
                        if width % 8 == 0:
                            start = pl.multiple_of(start, 8)
                        windows[turn][micro, y] = wide[field, micro, y, pl.ds(start, span)]
                    low = wide[field, micro, y, local_z : local_z + HALO]
                    high = wide[field, micro, y, HALO : 2 * HALO]
                    for m in range(slabs):
                        edges[m][field, micro, y] = jnp.where(slab == m, low, high)
                else:
                    windows[0][micro, y] = wide[field, micro, y, HALO : HALO + local_z]


class Slab:
    def __init__(self, dims, place):
        self.micros, self.rows_y, self.depth, self.width, self.chunk_y, self.slabs, limit_z = dims
        self.section, self.slab, self.swap, origin = place[0], place[1], place[2], place[3]
        self.chunk = self.chunk_y * self.depth
        self.chunks = self.rows_y // self.chunk_y
        self.per_owner = self.rows_y // self.slabs
        zs = lax.broadcasted_iota(jnp.int32, (self.depth, LANES), 0)
        inside = (zs + origin >= 0) & (zs + origin < limit_z)
        self.in_grid = inside.astype(F32)[None]
        self.mine = ((zs >= HALO) & (zs < HALO + self.width)).astype(F32)[None]

    def over_chunks(self, body):
        if self.chunks == 1:
            body(0, 0)
        else:

            def step(part, carry):
                body(part, pl.multiple_of(part * self.chunk, 16))
                return carry

            lax.fori_loop(0, self.chunks, step, 0)

    def masked(self, values, mask):
        cut = values.reshape(-1, self.depth, LANES) * mask
        return cut.reshape(values.shape)

    def put_rows(self, target, lead, start, values):
        hi, lo = split_terms(values)
        at = pl.ds(start + self.depth, self.chunk)
        for micro in range(self.micros):
            rows = slice(micro * self.chunk, (micro + 1) * self.chunk)
            target[lead, micro, at, slice(0, LANES)] = hi[rows]
            target[lead, micro, at, slice(LANES, 2 * LANES)] = lo[rows]

    def pieces_of(self, source, lead, start):
        pieces = []
        for b in range(3):
            at = pl.ds(start + b * self.depth, self.chunk)
            parts = [source[lead, micro, at, :] for micro in range(self.micros)]
            pieces.append(jnp.concatenate(parts, axis=0))
        return pieces

    def conv(self, source, lead, start, table):
        pieces = self.pieces_of(source, lead, start)
        left = jnp.concatenate(pieces + [piece[:, :LANES] for piece in pieces], axis=1)
        out = jnp.dot(left, table[...], preferred_element_type=F32)
        before = pltpu.roll(out[:, :LANES], 1, 0)
        after = pltpu.roll(out[:, 2 * LANES :], out.shape[0] - 1, 0)
        return before + out[:, LANES : 2 * LANES] + after

    def by_owner(self, layer, own, other, body):
        mine = layer // 2 == self.section
        pl.when(mine)(lambda: body(own, layer % 2))
        pl.when(jnp.logical_not(mine))(lambda: body(other, layer % 2))

    def blank_edges(self, target):
        blank = jnp.zeros((self.depth, 2 * LANES), BF16)
        for lead in range(target.shape[0]):
            for micro in range(self.micros):
                for edge in (0, self.rows_y + 1):
                    target[lead, micro, edge * self.depth : (edge + 1) * self.depth, :] = blank

    def read(self, source, lead, start):
        at = pl.ds(start, self.chunk)
        return jnp.concatenate([source[lead, micro, at, :] for micro in range(self.micros)], axis=0)

    def write(self, target, lead, start, values):
        for micro in range(self.micros):
            rows = slice(micro * self.chunk, (micro + 1) * self.chunk)
            target[lead, micro, pl.ds(start, self.chunk), :] = values[rows]

    def emit(self, target, part, values):
        inner = values.reshape(self.micros, self.chunk_y, self.depth, LANES)
        for y in range(self.chunk_y):
            row = part * self.chunk_y + y
            to = (row // self.per_owner) ^ self.slab
            for micro in range(self.micros):
                value = inner[micro, y, HALO : HALO + self.width, :]
                target[to, micro, row % self.per_owner] = value

    def fill(self, field, windows):
        span = windows[0].shape[2]
        for micro in range(self.micros):
            for turn, window in enumerate(windows):
                owner = self.slab ^ turn
                for y in range(self.per_owner):
                    value = window[micro, y]
                    if span < self.depth:
                        extra = jnp.zeros((self.depth - span, LANES), F32)
                        value = jnp.concatenate([value, extra], axis=0)
                    start = pl.multiple_of((owner * self.per_owner + y) * self.depth, 16)
                    field[0, micro, pl.ds(start, self.depth), :] = value


def forward_kernel(dims, place, own, own_row, other, other_row, *refs):
    slab = Slab(dims, place)
    refs, (acts, kept, front, field) = refs[:-4], refs[-4:]
    slab.blank_edges(acts)
    slab.fill(field, refs)
    slab.over_chunks(
        lambda part, start: slab.put_rows(acts, 0, start, slab.read(field, 0, start))
    )

    def layer_step(layer, carry):
        def run(tables, half):
            table, row = tables

            def body(part, start):
                pre = slab.conv(acts, layer, start, table.at[half]) + row[half][0:1, :]
                grown = 1.0 + jnp.exp(-pre)
                sigma = 1.0 / grown
                slab.write(kept, layer, start, sigma * (1.0 + pre * (1.0 - sigma)))
                out = slab.masked(pre / grown, slab.in_grid)
                pl.when(layer < 3)(lambda: slab.put_rows(acts, layer + 1, start, out))
                pl.when(layer == 2 * slab.section + 1)(lambda: slab.emit(front, part, out))

            slab.over_chunks(body)

        slab.by_owner(layer, (own, own_row), (other, other_row), run)
        return carry

    lax.fori_loop(0, 4, layer_step, 0)


def backward_kernel(dims, scale, place, own, other, acts, kept, *refs):
    slab = Slab(dims, place)
    refs, (back, sums, rim, slopes, field, acc) = refs[:-6], refs[-6:]
    slab.blank_edges(rim)
    slab.fill(field, refs)

    def take_gradient(layer, start, gradient):
        slope = slab.masked(gradient * slab.read(kept, layer, start), slab.in_grid)
        slab.write(slopes, layer, start, slab.masked(slope, slab.mine))
        slab.put_rows(rim, layer % 2, start, slope)

    slab.over_chunks(lambda part, start: take_gradient(3, start, slab.read(field, 0, start)))

    def layer_step(index, carry):
        layer = 3 - index

        def run(table, half):
            def body(part, start):
                gradient = slab.conv(rim, layer % 2, start, table.at[half])
                pl.when(layer > 0)(lambda: take_gradient(layer - 1, start, gradient))
                pl.when(layer == 2 * slab.section)(lambda: slab.emit(back, part, gradient))

            slab.over_chunks(body)

        slab.by_owner(layer, own, other, run)
        return carry

    lax.fori_loop(0, jnp.where(slab.section == 0, 4, 2), layer_step, 0)

    quarter = BLOCKS // 4
    chans = LANES // 2

    def spot(tap):
        return (tap // quarter ^ slab.swap) * quarter + tap % quarter

    sums[spot(TAPS)] = jnp.zeros((chans, LANES), F32)
    for slot in range(2):
        layer = 2 * slab.section + slot
        acc[...] = jnp.zeros(acc.shape, F32)

        def gather(part, start):
            slope = slab.read(slopes, layer, start)
            moved = [pltpu.roll(slope, slope.shape[0] - 1, 0), slope, pltpu.roll(slope, 1, 0)]
            terms = [split_terms(value) for value in moved]
            left_hi = jnp.concatenate([hi for hi, lo in terms], axis=1)
            left_lo = jnp.concatenate([lo for hi, lo in terms], axis=1)
            pieces = slab.pieces_of(acts, layer, start)
            full = jnp.concatenate(pieces, axis=1)
            high = jnp.concatenate([piece[:, :LANES] for piece in pieces], axis=1)
            over_rows = (((0,), (0,)), ((), ()))
            one = lax.dot_general(left_hi, full, over_rows, preferred_element_type=F32)
            two = lax.dot_general(left_lo, high, over_rows, preferred_element_type=F32)
            for b in range(3):
                at = slice(b * LANES, (b + 1) * LANES)
                acc[0 : 3 * LANES, at] += (
                    one[:, 2 * b * LANES : (2 * b + 1) * LANES]
                    + one[:, (2 * b + 1) * LANES : (2 * b + 2) * LANES]
                    + two[:, at]
                )
            acc[3 * LANES : 3 * LANES + 1, 0:LANES] += jnp.sum(slope, axis=0, keepdims=True)

        slab.over_chunks(gather)
        lanes = slice(slot * chans, (slot + 1) * chans)
        for b in range(3):
            for c in range(3):
                block = acc[c * LANES : (c + 1) * LANES, b * LANES : (b + 1) * LANES] * scale
                tap = 3 * b + c
                sums[spot(tap), :, lanes] = block[chans:, :chans]
                sums[spot(9 + tap), :, lanes] = block[:chans, :chans] + block[chans:, chans:]
                sums[spot(18 + tap), :, lanes] = block[:chans, chans:]
        row = acc[3 * LANES : 3 * LANES + 1, 0:LANES] * scale
        sums[spot(TAPS), 0:1, lanes] = row[:, :chans] + row[:, chans:]


def unpack_kernel(chunk, place, *refs):
    slab, swap = place[1], place[2]
    near, (beside, across, weight, bias, whole) = refs[:-5], refs[-5:]
    slabs = len(near)
    quarter = slabs * chunk
    chans = weight.shape[-1]

    def put(relative, turn, values):
        at = (relative ^ swap) * quarter + (slab ^ turn) * chunk
        whole[pl.ds(pl.multiple_of(at, 8), chunk), :] = values

    for turn in range(slabs):
        first = turn * chunk
        put(0, turn, near[turn][...])
        put(1, turn, beside[first : first + chunk, :])
        for part in range(2):
            start = part * quarter + first
            put(2 + part, turn, across[start : start + chunk, :])
    for layer in range(2):
        lanes = slice(layer * chans, (layer + 1) * chans)
        for tap in range(BLOCKS):
            at = tap // 7 * quarter + tap % 7 * chans
            if tap < TAPS:
                weight[layer, tap] = whole[at : at + chans, lanes]
            else:
                bias[layer : layer + 1, :] = whole[at : at + 1, lanes]


def restore_kernel(dims, place, *refs):
    micros, chans, size_x, local_y, width = dims
    pieces, (target, whole) = refs[:-2], refs[-2:]
    slab = place[1]
    slabs = len(pieces)
    step = size_x * local_y
    for micro in range(micros):
        for y in range(local_y):
            for turn in range(slabs):
                start = (slab ^ turn) * width
                if width % 8 == 0:
                    start = pl.multiple_of(start, 8)
                whole[pl.ds(start, width), :] = pieces[turn][micro, y]
            block = whole[...].T
            for x in range(size_x):
                first = micro * chans * step + x * local_y + y
                part = block[x * chans : (x + 1) * chans]
                target[pl.ds(first, chans, stride=step), :] = part


def spread(blocks):
    slabs = len(blocks)
    if slabs <= 8:
        got = [blocks[0]]
        for turn in range(1, slabs):
            route = [(i, i ^ turn) for i in range(slabs)]
            got.append(lax.ppermute(blocks[turn], "gy", route))
        return got
    order = jnp.arange(slabs) ^ lax.axis_index("gy")
    got = lax.all_to_all(jnp.stack(blocks)[order], "gy", 0, 0)[order]
    return [got[turn] for turn in range(slabs)]


def swapped(block, bit):
    count = lax.axis_size("gz")
    return lax.ppermute(block, "gz", [(i, i ^ bit) for i in range(count)])


def summed_over_grid(block):
    slabs = lax.axis_size("gy")
    slab = lax.axis_index("gy")
    for bit in (1, 2):
        rows = block.shape[0] // 2
        block = block[:rows] + swapped(block[rows:], bit)
    chunk = -(-block.shape[0] // (8 * slabs)) * 8
    block = jnp.pad(block, ((0, slabs * chunk - block.shape[0]), (0, 0)))
    parts = block.reshape(slabs, chunk, LANES)
    sent = [
        lax.dynamic_index_in_dim(parts, slab ^ turn, 0, keepdims=False)
        for turn in range(slabs)
    ]
    return sum(spread(sent))


def restored(pieces, shape, place):
    micros, chans, size_x, local_y, local_z = shape
    width = pieces[0].shape[2]
    dims = (micros, chans, size_x, local_y, width)
    rows = micros * chans * size_x * local_y
    kernel = functools.partial(restore_kernel, dims)
    scratch = [pltpu.VMEM((local_z, LANES), F32)]
    (whole,) = call(kernel, "restore", [((rows, local_z), F32)], [place, *pieces], scratch)
    return whole.reshape(1, *shape)


def per_device(inflow, weights, biases, cotangent):
    micros, chans, size_x, local_y, local_z = inflow.shape
    slabs, columns = lax.axis_size("gy"), lax.axis_size("gz")
    rows_y = local_y * slabs
    width = local_z // slabs
    span = width + 2 * HALO
    depth = -(-span // 16) * 16
    chunk_y = max(n for n in range(1, rows_y + 1) if rows_y % n == 0 and n * depth <= 384)
    scale = 1.0 / math.sqrt(micros * size_x * rows_y * local_z * columns)
    slab, column = lax.axis_index("gy"), lax.axis_index("gz")
    swap = 2 * (column % 2) + column // 2 % 2
    origin = column * local_z + slab * width - HALO
    place = [lax.axis_index("section"), slab, swap, origin, column]
    place = jnp.stack(place).astype(jnp.int32)

    half = BLOCKS // 2
    rows = micros * chans * size_x * local_y
    ends = ((2, micros, local_y, HALO, LANES), F32)
    got = call(
        functools.partial(start_kernel, inflow.shape),
        "start",
        [
            ((BLOCKS, chans, LANES), F32),
            ((half, chans, LANES), F32),
            ((2, micros, local_y, local_z, LANES), F32),
            ends,
            ends,
        ],
        [place, weights, biases, inflow.reshape(rows, local_z), cotangent.reshape(rows, local_z)],
        [
            pltpu.VMEM(weights.shape, F32),
            pltpu.VMEM(biases.shape, F32),
            pltpu.VMEM((2, rows, local_z), F32),
            pltpu.SemaphoreType.DMA((4,)),
        ],
        specs=[pl.BlockSpec(memory_space=pl.ANY)] * 4,
    )
    own, sent, fields, pair, inner = got
    first = lax.ppermute(sent, "section", [(0, 1), (1, 0)])
    pair = swapped(pair, 1)
    route = [(i, i + 1) for i in range(1, columns - 1, 2)]
    inner = lax.ppermute(inner, "gz", route + [(after, before) for before, after in route])
    windows = call(
        functools.partial(window_kernel, (slabs, width, span, columns)),
        "windows",
        [((micros, local_y, span, LANES), F32)] * (2 * slabs),
        [place, fields, pair, inner],
        [pltpu.VMEM((micros, local_y, local_z + 2 * HALO, LANES), F32)],
    )
    flows, pulls = spread(windows[:slabs]), spread(windows[slabs:])
    first, flows = lax.optimization_barrier((first, flows))
    second = swapped(first, 1)

    tables = [((2, 9 * LANES, 3 * LANES), BF16)] * 2 + [((2, 8, LANES), F32)]
    own_fwd, own_bwd, own_row = call(table_kernel, "own_table", tables, [place, own])
    far_fwd, far_bwd, far_row = call(table_kernel, "far_table", tables, [place, first, second])

    dims = (micros, rows_y, depth, width, chunk_y, slabs, local_z * columns)
    padded = (rows_y + 2) * depth
    full = rows_y * depth
    piece = ((slabs, micros, local_y, width, LANES), F32)
    work = 2 * micros * full * 9 * LANES * 3 * LANES
    acts, kept, front = call(
        functools.partial(forward_kernel, dims),
        "forward",
        [((4, micros, padded, 2 * LANES), BF16), ((4, micros, full, LANES), F32), piece],
        [place, own_fwd, own_row, far_fwd, far_row, *flows],
        [pltpu.VMEM((1, micros, full, LANES), F32)],
        4 * work,
    )
    outward = spread([front[turn] for turn in range(slabs)])
    back, sums = call(
        functools.partial(backward_kernel, dims, scale),
        "backward",
        [piece, ((BLOCKS, chans, LANES), F32)],
        [place, own_bwd, far_bwd, acts, kept, *pulls],
        [
            pltpu.VMEM((2, micros, padded, 2 * LANES), BF16),
            pltpu.VMEM((4, micros, full, LANES), F32),
            pltpu.VMEM((1, micros, full, LANES), F32),
            pltpu.VMEM((3 * LANES + 8, 3 * LANES), F32),
        ],
        6 * work,
    )

    sums, outward = lax.optimization_barrier((sums, outward))
    mine = summed_over_grid(sums.reshape(BLOCKS * chans, LANES))
    near = spread([mine] * slabs)
    near, back = lax.optimization_barrier((near, back))
    quarter = jnp.concatenate(near, axis=0)
    beside = swapped(quarter, 2)
    inward = spread([back[turn] for turn in range(slabs)])
    beside, inward = lax.optimization_barrier((beside, inward))
    across = swapped(jnp.concatenate([quarter, beside], axis=0), 1)
    section_out = restored(outward, inflow.shape, place)
    section_grad = restored(inward, inflow.shape, place)
    chunk = mine.shape[0]
    weight_total, bias_total = call(
        functools.partial(unpack_kernel, chunk),
        "unpack",
        [((2, TAPS, chans, chans), F32), ((2, chans), F32)],
        [place, *near, beside, across],
        [pltpu.VMEM((4 * slabs * chunk, LANES), F32)],
    )
    return (section_out, section_grad, weight_total, bias_total)


def solution(mesh):
    grid = P(None, None, None, "gy", "gz")
    section_grid = P("section", None, None, None, "gy", "gz")
    return jax.shard_map(
        per_device,
        mesh=mesh,
        in_specs=(grid, P("section", None, None, None), P("section", None), grid),
        out_specs=(section_grid, section_grid, P("section", None, None, None), P("section", None)),
        check_vma=False,
    )
```

```python
import functools
import math

import jax
import jax.numpy as jnp
from jax import lax
from jax.experimental import pallas as pl
from jax.experimental.pallas import tpu as pltpu
from jax.sharding import PartitionSpec as P

HALO = 8
LANES = 128
TAPS = 27
BLOCKS = 28
BF16 = jnp.bfloat16
F32 = jnp.float32
VMEM = pl.BlockSpec(memory_space=pltpu.VMEM)


def call(kernel, name, outs, args, scratch=(), flops=0):
    arrays = [jax.ShapeDtypeStruct(shape, kind) for shape, kind in outs]
    size = sum(math.prod(item.shape) * item.dtype.itemsize for item in [*arrays, *args, *scratch])
    return pl.pallas_call(
        kernel,
        out_shape=arrays,
        in_specs=[VMEM] * len(args),
        out_specs=[VMEM] * len(arrays),
        scratch_shapes=list(scratch),
        compiler_params=pltpu.CompilerParams(vmem_limit_bytes=size + 6 * 1024 * 1024),
        cost_estimate=pl.CostEstimate(flops=flops, bytes_accessed=1024, transcendentals=0),
        name=name,
    )(*args)


def column_bits():
    column = lax.axis_index("gz")
    return 2 * (column % 2) + column // 2 % 2


def split_terms(values):
    high = values.astype(BF16)
    return high, (values - high.astype(F32)).astype(BF16)


def pack_kernel(weights, biases, own, sent):
    chans = weights.shape[2]
    half = sent.shape[0]
    for tap in range(TAPS):
        own[tap] = jnp.concatenate([weights[0, tap], weights[1, tap]], axis=1)
    own[TAPS] = jnp.zeros((chans, LANES), F32)
    own[TAPS, 0:1, :] = jnp.concatenate([biases[0:1, :], biases[1:2, :]], axis=1)
    start = lax.axis_index("gz") % 2 * half

    def copy(index, carry):
        sent[index] = own[start + index]
        return carry

    lax.fori_loop(0, half, copy, 0)


def turn_kernel(dims, inflow, cotangent, rows, pair, inner):
    micros, chans, size_x, local_y, local_z = dims
    step = size_x * local_y
    odd = lax.axis_index("gz") % 2 == 1
    for field, source in enumerate((inflow, cotangent)):
        for micro in range(micros):
            for y in range(local_y):
                first = micro * chans * step + y
                parts = [
                    source[pl.ds(first + x * local_y, chans, stride=step), :] for x in range(size_x)
                ]
                turned = jnp.concatenate(parts, axis=0).T
                rows[field, micro, y] = turned
                low, high = turned[:HALO], turned[local_z - HALO :]
                pair[field, micro, y] = jnp.where(odd, low, high)
                inner[field, micro, y] = jnp.where(odd, high, low)


def window_kernel(dims, rows, pair, inner, *refs):
    slabs, width, span, columns = dims
    outs, wide = refs[:-1], refs[-1]
    slab, column = lax.axis_index("gy"), lax.axis_index("gz")
    odd = column % 2 == 1
    _, micros, local_y, local_z, _ = rows.shape
    for field in range(2):
        for micro in range(micros):
            for y in range(local_y):
                one, two = pair[field, micro, y], inner[field, micro, y]
                before = jnp.where(column > 0, jnp.where(odd, one, two), 0.0)
                after = jnp.where(column < columns - 1, jnp.where(odd, two, one), 0.0)
                wide[micro, y, :HALO] = before
                wide[micro, y, HALO : HALO + local_z] = rows[field, micro, y]
                wide[micro, y, HALO + local_z :] = after
                for turn in range(slabs):
                    start = (slab ^ turn) * width
                    if width % 8 == 0:
                        start = pl.multiple_of(start, 8)
                    outs[field * slabs + turn][micro, y] = wide[micro, y, pl.ds(start, span)]


def table_kernel(*refs):
    parts, (fwd, bwd, row) = refs[:-3], refs[-3:]
    odd = lax.axis_index("gz") % 2
    count = parts[0].shape[0]
    chans = parts[0].shape[1]

    def block_of(tap):
        if len(parts) == 1:
            return parts[0][tap]
        index = tap % count
        return jnp.where(odd == tap // count, parts[0][index], parts[1][index])

    for b in range(3):
        for c in range(3):
            taps = [block_of(9 * a + 3 * b + c) for a in range(3)]
            for layer in range(2):
                lanes = slice(layer * chans, (layer + 1) * chans)
                below, level, above = [tap[:, lanes] for tap in taps]
                top = jnp.concatenate([level, above], axis=1)
                low = jnp.concatenate([below, level], axis=1)
                block = jnp.concatenate([top, low], axis=0)
                for target, value, r, at in ((fwd, block.T, b, c), (bwd, block, 2 - b, 2 - c)):
                    hi, lo = split_terms(value)
                    at = slice(at * LANES, (at + 1) * LANES)
                    target[layer, 2 * r * LANES : (2 * r + 1) * LANES, at] = hi
                    target[layer, (2 * r + 1) * LANES : (2 * r + 2) * LANES, at] = hi
                    target[layer, (6 + r) * LANES : (7 + r) * LANES, at] = lo
    last = block_of(TAPS)[0:1, :]
    for layer in range(2):
        part = last[:, layer * chans : (layer + 1) * chans]
        row[layer] = jnp.broadcast_to(jnp.concatenate([part, part], axis=1), (8, LANES))


def cut_kernel(dims, place, *refs):
    micros, chans, size_x, local_y, local_z, slabs, width, span, edged, fields = dims
    sources, refs = refs[:fields], refs[fields:]
    outs, wide = refs[:-1], refs[-1]
    slab = place[1]
    step = size_x * local_y
    for field, source in enumerate(sources):
        windows = outs[field * slabs : (field + 1) * slabs]
        edges = outs[fields * slabs :]
        for micro in range(micros):
            for y in range(local_y):
                first = micro * chans * step + y
                parts = [
                    source[pl.ds(first + x * local_y, chans, stride=step), :] for x in range(size_x)
                ]
                wide[field, micro, y, HALO : HALO + local_z] = jnp.concatenate(parts, axis=0).T
                wide[field, micro, y, :HALO] = jnp.zeros((HALO, LANES), F32)
                wide[field, micro, y, HALO + local_z :] = jnp.zeros((HALO, LANES), F32)
                if edged:
                    for turn in range(slabs):
                        start = lax.rem(slab + turn, slabs) * width
                        if width % 8 == 0:
                            start = pl.multiple_of(start, 8)
                        windows[turn][micro, y] = wide[field, micro, y, pl.ds(start, span)]
                    low = wide[field, micro, y, local_z : local_z + HALO]
                    high = wide[field, micro, y, HALO : 2 * HALO]
                    for m in range(slabs):
                        edges[m][field, micro, y] = jnp.where(slab == m, low, high)
                else:
                    windows[0][micro, y] = wide[field, micro, y, HALO : HALO + local_z]


class Slab:
    def __init__(self, dims):
        self.micros, self.rows_y, self.depth, self.width, self.chunk_y, self.slabs, limit_z = dims
        self.section, self.slab = lax.axis_index("section"), lax.axis_index("gy")
        origin = (lax.axis_index("gz") * self.slabs + self.slab) * self.width - HALO
        self.chunk = self.chunk_y * self.depth
        self.chunks = self.rows_y // self.chunk_y
        self.per_owner = self.rows_y // self.slabs
        zs = lax.broadcasted_iota(jnp.int32, (self.depth, LANES), 0)
        inside = (zs + origin >= 0) & (zs + origin < limit_z)
        self.in_grid = inside.astype(F32)[None]
        self.mine = ((zs >= HALO) & (zs < HALO + self.width)).astype(F32)[None]

    def over_chunks(self, body):
        if self.chunks == 1:
            body(0, 0)
        else:

            def step(part, carry):
                body(part, pl.multiple_of(part * self.chunk, 16))
                return carry

            lax.fori_loop(0, self.chunks, step, 0)

    def masked(self, values, mask):
        cut = values.reshape(-1, self.depth, LANES) * mask
        return cut.reshape(values.shape)

    def put_rows(self, target, lead, start, values):
        hi, lo = split_terms(values)
        at = pl.ds(start + self.depth, self.chunk)
        for micro in range(self.micros):
            rows = slice(micro * self.chunk, (micro + 1) * self.chunk)
            target[lead, micro, at, slice(0, LANES)] = hi[rows]
            target[lead, micro, at, slice(LANES, 2 * LANES)] = lo[rows]

    def pieces_of(self, source, lead, start):
        pieces = []
        for b in range(3):
            at = pl.ds(start + b * self.depth, self.chunk)
            parts = [source[lead, micro, at, :] for micro in range(self.micros)]
            pieces.append(jnp.concatenate(parts, axis=0))
        return pieces

    def conv(self, source, lead, start, table):
        pieces = self.pieces_of(source, lead, start)
        left = jnp.concatenate(pieces + [piece[:, :LANES] for piece in pieces], axis=1)
        out = jnp.dot(left, table[...], preferred_element_type=F32)
        before = pltpu.roll(out[:, :LANES], 1, 0)
        after = pltpu.roll(out[:, 2 * LANES :], out.shape[0] - 1, 0)
        return before + out[:, LANES : 2 * LANES] + after

    def by_owner(self, layer, own, other, body):
        mine = layer // 2 == self.section
        pl.when(mine)(lambda: body(own, layer % 2))
        pl.when(jnp.logical_not(mine))(lambda: body(other, layer % 2))

    def blank_edges(self, target):
        blank = jnp.zeros((self.depth, 2 * LANES), BF16)
        for lead in range(target.shape[0]):
            for micro in range(self.micros):
                for edge in (0, self.rows_y + 1):
                    target[lead, micro, edge * self.depth : (edge + 1) * self.depth, :] = blank

    def read(self, source, lead, start):
        at = pl.ds(start, self.chunk)
        return jnp.concatenate([source[lead, micro, at, :] for micro in range(self.micros)], axis=0)

    def write(self, target, lead, start, values):
        for micro in range(self.micros):
            rows = slice(micro * self.chunk, (micro + 1) * self.chunk)
            target[lead, micro, pl.ds(start, self.chunk), :] = values[rows]

    def emit(self, target, part, values):
        inner = values.reshape(self.micros, self.chunk_y, self.depth, LANES)
        for y in range(self.chunk_y):
            row = part * self.chunk_y + y
            to = (row // self.per_owner) ^ self.slab
            for micro in range(self.micros):
                value = inner[micro, y, HALO : HALO + self.width, :]
                target[to, micro, row % self.per_owner] = value

    def fill(self, field, windows):
        span = windows[0].shape[2]
        for micro in range(self.micros):
            for turn, window in enumerate(windows):
                owner = self.slab ^ turn
                for y in range(self.per_owner):
                    value = window[micro, y]
                    if span < self.depth:
                        extra = jnp.zeros((self.depth - span, LANES), F32)
                        value = jnp.concatenate([value, extra], axis=0)
                    start = pl.multiple_of((owner * self.per_owner + y) * self.depth, 16)
                    field[0, micro, pl.ds(start, self.depth), :] = value


def forward_kernel(dims, own, own_row, other, other_row, *refs):
    slab = Slab(dims)
    refs, (acts, kept, front, field) = refs[:-4], refs[-4:]
    slab.blank_edges(acts)
    slab.fill(field, refs)
    slab.over_chunks(
        lambda part, start: slab.put_rows(acts, 0, start, slab.read(field, 0, start))
    )

    def layer_step(layer, carry):
        def run(tables, half):
            table, row = tables

            def body(part, start):
                pre = slab.conv(acts, layer, start, table.at[half]) + row[half][0:1, :]
                sigma = 1.0 / (1.0 + jnp.exp(-pre))
                slab.write(kept, layer, start, sigma * (1.0 + pre * (1.0 - sigma)))
                out = slab.masked(pre * sigma, slab.in_grid)
                pl.when(layer < 3)(lambda: slab.put_rows(acts, layer + 1, start, out))
                pl.when(layer == 2 * slab.section + 1)(lambda: slab.emit(front, part, out))

            slab.over_chunks(body)

        slab.by_owner(layer, (own, own_row), (other, other_row), run)
        return carry

    lax.fori_loop(0, 4, layer_step, 0)


def backward_kernel(dims, scale, own, other, acts, kept, *refs):
    slab = Slab(dims)
    refs, (back, sums, rim, slopes, field, acc) = refs[:-6], refs[-6:]
    slab.blank_edges(rim)
    slab.fill(field, refs)

    def take_gradient(layer, start, gradient):
        slope = slab.masked(gradient * slab.read(kept, layer, start), slab.in_grid)
        slab.write(slopes, layer, start, slab.masked(slope, slab.mine))
        slab.put_rows(rim, layer % 2, start, slope)

    slab.over_chunks(lambda part, start: take_gradient(3, start, slab.read(field, 0, start)))

    def layer_step(index, carry):
        layer = 3 - index

        def run(table, half):
            def body(part, start):
                gradient = slab.conv(rim, layer % 2, start, table.at[half])
                pl.when(layer > 0)(lambda: take_gradient(layer - 1, start, gradient))
                pl.when(layer == 2 * slab.section)(lambda: slab.emit(back, part, gradient))

            slab.over_chunks(body)

        slab.by_owner(layer, own, other, run)
        return carry

    lax.fori_loop(0, jnp.where(slab.section == 0, 4, 2), layer_step, 0)

    quarter = BLOCKS // 4
    chans = LANES // 2
    swap = column_bits()

    def spot(tap):
        return (tap // quarter ^ swap) * quarter + tap % quarter

    sums[spot(TAPS)] = jnp.zeros((chans, LANES), F32)
    for slot in range(2):
        layer = 2 * slab.section + slot
        acc[...] = jnp.zeros(acc.shape, F32)

        def gather(part, start):
            slope = slab.read(slopes, layer, start)
            moved = [pltpu.roll(slope, slope.shape[0] - 1, 0), slope, pltpu.roll(slope, 1, 0)]
            terms = [split_terms(value) for value in moved]
            left_hi = jnp.concatenate([hi for hi, lo in terms], axis=1)
            left_lo = jnp.concatenate([lo for hi, lo in terms], axis=1)
            pieces = slab.pieces_of(acts, layer, start)
            full = jnp.concatenate(pieces, axis=1)
            high = jnp.concatenate([piece[:, :LANES] for piece in pieces], axis=1)
            over_rows = (((0,), (0,)), ((), ()))
            one = lax.dot_general(left_hi, full, over_rows, preferred_element_type=F32)
            two = lax.dot_general(left_lo, high, over_rows, preferred_element_type=F32)
            for b in range(3):
                at = slice(b * LANES, (b + 1) * LANES)
                acc[0 : 3 * LANES, at] += (
                    one[:, 2 * b * LANES : (2 * b + 1) * LANES]
                    + one[:, (2 * b + 1) * LANES : (2 * b + 2) * LANES]
                    + two[:, at]
                )
            acc[3 * LANES : 3 * LANES + 1, 0:LANES] += jnp.sum(slope, axis=0, keepdims=True)

        slab.over_chunks(gather)
        lanes = slice(slot * chans, (slot + 1) * chans)
        for b in range(3):
            for c in range(3):
                block = acc[c * LANES : (c + 1) * LANES, b * LANES : (b + 1) * LANES] * scale
                tap = 3 * b + c
                sums[spot(tap), :, lanes] = block[chans:, :chans]
                sums[spot(9 + tap), :, lanes] = block[:chans, :chans] + block[chans:, chans:]
                sums[spot(18 + tap), :, lanes] = block[:chans, chans:]
        row = acc[3 * LANES : 3 * LANES + 1, 0:LANES] * scale
        sums[spot(TAPS), 0:1, lanes] = row[:, :chans] + row[:, chans:]


def unpack_kernel(chunk, *refs):
    slab, swap = lax.axis_index("gy"), column_bits()
    near, (beside, across, weight, bias, whole) = refs[:-5], refs[-5:]
    slabs = len(near)
    quarter = slabs * chunk
    chans = weight.shape[-1]

    def put(relative, turn, values):
        at = (relative ^ swap) * quarter + (slab ^ turn) * chunk
        whole[pl.ds(pl.multiple_of(at, 8), chunk), :] = values

    for turn in range(slabs):
        first = turn * chunk
        put(0, turn, near[turn][...])
        put(1, turn, beside[first : first + chunk, :])
        for part in range(2):
            start = part * quarter + first
            put(2 + part, turn, across[start : start + chunk, :])
    for layer in range(2):
        lanes = slice(layer * chans, (layer + 1) * chans)
        for tap in range(BLOCKS):
            at = tap // 7 * quarter + tap % 7 * chans
            if tap < TAPS:
                weight[layer, tap] = whole[at : at + chans, lanes]
            else:
                bias[layer : layer + 1, :] = whole[at : at + 1, lanes]


def restore_kernel(dims, *refs):
    micros, chans, size_x, local_y, width = dims
    pieces, (target, whole) = refs[:-2], refs[-2:]
    slab = lax.axis_index("gy")
    slabs = len(pieces)
    step = size_x * local_y
    for micro in range(micros):
        for y in range(local_y):
            for turn in range(slabs):
                start = (slab ^ turn) * width
                if width % 8 == 0:
                    start = pl.multiple_of(start, 8)
                whole[pl.ds(start, width), :] = pieces[turn][micro, y]
            block = whole[...].T
            for x in range(size_x):
                first = micro * chans * step + x * local_y + y
                part = block[x * chans : (x + 1) * chans]
                target[pl.ds(first, chans, stride=step), :] = part


def spread(blocks):
    slabs = len(blocks)
    if slabs <= 8:
        got = [blocks[0]]
        for turn in range(1, slabs):
            route = [(i, i ^ turn) for i in range(slabs)]
            got.append(lax.ppermute(blocks[turn], "gy", route))
        return got
    order = jnp.arange(slabs) ^ lax.axis_index("gy")
    got = lax.all_to_all(jnp.stack(blocks)[order], "gy", 0, 0)[order]
    return [got[turn] for turn in range(slabs)]


def swapped(block, bit):
    count = lax.axis_size("gz")
    return lax.ppermute(block, "gz", [(i, i ^ bit) for i in range(count)])


def halved(block, bit):
    rows = block.shape[0] // 2
    return block[:rows] + swapped(block[rows:], bit)


def restored(pieces, shape):
    micros, chans, size_x, local_y, local_z = shape
    width = pieces[0].shape[2]
    dims = (micros, chans, size_x, local_y, width)
    rows = micros * chans * size_x * local_y
    kernel = functools.partial(restore_kernel, dims)
    scratch = [pltpu.VMEM((local_z, LANES), F32)]
    (whole,) = call(kernel, "restore", [((rows, local_z), F32)], [*pieces], scratch)
    return whole.reshape(1, *shape)


def per_device(inflow, weights, biases, cotangent):
    micros, chans, size_x, local_y, local_z = inflow.shape
    slabs, columns = lax.axis_size("gy"), lax.axis_size("gz")
    rows_y = local_y * slabs
    width = local_z // slabs
    span = width + 2 * HALO
    depth = -(-span // 16) * 16
    chunk_y = max(n for n in range(1, rows_y + 1) if rows_y % n == 0 and n * depth <= 384)
    scale = 1.0 / math.sqrt(micros * size_x * rows_y * local_z * columns)
    half = BLOCKS // 2
    rows = micros * chans * size_x * local_y
    ends = ((2, micros, local_y, HALO, LANES), F32)
    fields, pair, inner = call(
        functools.partial(turn_kernel, inflow.shape),
        "turn",
        [((2, micros, local_y, local_z, LANES), F32), ends, ends],
        [inflow.reshape(rows, local_z), cotangent.reshape(rows, local_z)],
    )
    pair = swapped(pair, 1)
    route = [(i, i + 1) for i in range(1, columns - 1, 2)]
    inner = lax.ppermute(inner, "gz", route + [(after, before) for before, after in route])
    packs = [((BLOCKS, chans, LANES), F32), ((half, chans, LANES), F32)]
    weights, fields = lax.optimization_barrier((weights, fields))
    own, sent = call(pack_kernel, "pack", packs, [weights, biases])
    first = lax.ppermute(sent, "section", [(0, 1), (1, 0)])
    windows = call(
        functools.partial(window_kernel, (slabs, width, span, columns)),
        "windows",
        [((micros, local_y, span, LANES), F32)] * (2 * slabs),
        [fields, pair, inner],
        [pltpu.VMEM((micros, local_y, local_z + 2 * HALO, LANES), F32)],
    )
    flows, pulls = spread(windows[:slabs]), spread(windows[slabs:])
    first, flows = lax.optimization_barrier((first, flows))
    second = swapped(first, 1)

    tables = [((2, 9 * LANES, 3 * LANES), BF16)] * 2 + [((2, 8, LANES), F32)]
    own_fwd, own_bwd, own_row = call(table_kernel, "own_table", tables, [own])
    far_fwd, far_bwd, far_row = call(table_kernel, "far_table", tables, [first, second])

    dims = (micros, rows_y, depth, width, chunk_y, slabs, local_z * columns)
    padded = (rows_y + 2) * depth
    full = rows_y * depth
    piece = ((slabs, micros, local_y, width, LANES), F32)
    work = 2 * micros * full * 9 * LANES * 3 * LANES
    acts, kept, front = call(
        functools.partial(forward_kernel, dims),
        "forward",
        [((4, micros, padded, 2 * LANES), BF16), ((4, micros, full, LANES), F32), piece],
        [own_fwd, own_row, far_fwd, far_row, *flows],
        [pltpu.VMEM((1, micros, full, LANES), F32)],
    )
    back, sums = call(
        functools.partial(backward_kernel, dims, scale),
        "backward",
        [piece, ((BLOCKS, chans, LANES), F32)],
        [own_bwd, far_bwd, acts, kept, *pulls],
        [
            pltpu.VMEM((2, micros, padded, 2 * LANES), BF16),
            pltpu.VMEM((4, micros, full, LANES), F32),
            pltpu.VMEM((1, micros, full, LANES), F32),
            pltpu.VMEM((3 * LANES + 8, 3 * LANES), F32),
        ],
        6 * work,
    )

    block = halved(sums.reshape(BLOCKS * chans, LANES), 1)
    block, front = lax.optimization_barrier((block, front))
    outward = spread([front[turn] for turn in range(slabs)])
    block = halved(block, 2)
    block, outward = lax.optimization_barrier((block, outward))
    chunk = -(-block.shape[0] // (8 * slabs)) * 8
    block = jnp.pad(block, ((0, slabs * chunk - block.shape[0]), (0, 0)))
    parts = block.reshape(slabs, chunk, LANES)
    slab = lax.axis_index("gy")
    sent = [
        lax.dynamic_index_in_dim(parts, slab ^ turn, 0, keepdims=False) for turn in range(slabs)
    ]
    near = spread([sum(spread(sent))] * slabs)
    near, back = lax.optimization_barrier((near, back))
    quarter = jnp.concatenate(near, axis=0)
    beside = swapped(quarter, 2)
    inward = spread([back[turn] for turn in range(slabs)])
    across = swapped(jnp.concatenate([quarter, beside], axis=0), 1)
    section_out = restored(outward, inflow.shape)
    weight_total, bias_total = call(
        functools.partial(unpack_kernel, chunk),
        "unpack",
        [((2, TAPS, chans, chans), F32), ((2, chans), F32)],
        [*near, beside, across],
        [pltpu.VMEM((4 * slabs * chunk, LANES), F32)],
    )
    section_grad = restored(inward, inflow.shape)
    return (section_out, section_grad, weight_total, bias_total)


def solution(mesh):
    grid = P(None, None, None, "gy", "gz")
    section_grid = P("section", None, None, None, "gy", "gz")
    return jax.shard_map(
        per_device,
        mesh=mesh,
        in_specs=(grid, P("section", None, None, None), P("section", None), grid),
        out_specs=(section_grid, section_grid, P("section", None, None, None), P("section", None)),
        check_vma=False,
    )
```

```python
import functools
import math

import jax
import jax.numpy as jnp
from jax import lax
from jax.experimental import pallas as pl
from jax.experimental.pallas import tpu as pltpu
from jax.sharding import PartitionSpec as P

HALO = 8
HALOS = (8, 4)
LANES = 128
TAPS = 27
BLOCKS = 28
BF16 = jnp.bfloat16
F32 = jnp.float32
VMEM = pl.BlockSpec(memory_space=pltpu.VMEM)


def call(kernel, name, outs, args, scratch=(), flops=0):
    arrays = [jax.ShapeDtypeStruct(shape, kind) for shape, kind in outs]
    size = sum(math.prod(item.shape) * item.dtype.itemsize for item in [*arrays, *args, *scratch])
    return pl.pallas_call(
        kernel,
        out_shape=arrays,
        in_specs=[VMEM] * len(args),
        out_specs=[VMEM] * len(arrays),
        scratch_shapes=list(scratch),
        compiler_params=pltpu.CompilerParams(vmem_limit_bytes=size + 6 * 1024 * 1024),
        cost_estimate=pl.CostEstimate(flops=flops, bytes_accessed=1024, transcendentals=0),
        name=name,
    )(*args)


def column_bits():
    column = lax.axis_index("gz")
    return 2 * (column % 2) + column // 2 % 2


def split_terms(values):
    high = values.astype(BF16)
    return high, (values - high.astype(F32)).astype(BF16)


def pack_kernel(weights, biases, own):
    chans = weights.shape[2]
    for tap in range(TAPS):
        own[tap] = jnp.concatenate([weights[0, tap], weights[1, tap]], axis=1)
    own[TAPS] = jnp.zeros((chans, LANES), F32)
    own[TAPS, 0:1, :] = jnp.concatenate([biases[0:1, :], biases[1:2, :]], axis=1)


def turn_kernel(dims, inflow, cotangent, rows, pair, inner):
    micros, chans, size_x, local_y, local_z = dims
    step = size_x * local_y
    odd = lax.axis_index("gz") % 2 == 1
    for field, source in enumerate((inflow, cotangent)):
        for micro in range(micros):
            for y in range(local_y):
                first = micro * chans * step + y
                parts = [
                    source[pl.ds(first + x * local_y, chans, stride=step), :] for x in range(size_x)
                ]
                turned = jnp.concatenate(parts, axis=0).T
                rows[field, micro, y] = turned
                low, high = turned[:HALO], turned[local_z - HALO :]
                pair[field, micro, y] = jnp.where(odd, low, high)
                inner[field, micro, y] = jnp.where(odd, high, low)


def window_kernel(dims, rows, pair, inner, *refs):
    slabs, width, columns = dims
    outs, wide = refs[:-1], refs[-1]
    slab, column = lax.axis_index("gy"), lax.axis_index("gz")
    odd = column % 2 == 1
    _, micros, local_y, local_z, _ = rows.shape
    for field, halo in enumerate(HALOS):
        at = slice(0, width + 2 * halo) if field == 0 else slice(width + 2 * HALO, None)
        for micro in range(micros):
            for y in range(local_y):
                one, two = pair[field, micro, y], inner[field, micro, y]
                before = jnp.where(column > 0, jnp.where(odd, one, two), 0.0)
                after = jnp.where(column < columns - 1, jnp.where(odd, two, one), 0.0)
                wide[field, micro, y, :HALO] = before
                wide[field, micro, y, HALO : HALO + local_z] = rows[field, micro, y]
                wide[field, micro, y, HALO + local_z :] = after
                for turn in range(slabs):
                    start = (slab ^ turn) * width + HALO - halo
                    if width % 8 == 0 and halo % 8 == 0:
                        start = pl.multiple_of(start, 8)
                    outs[turn][micro, y, at] = wide[field, micro, y, pl.ds(start, width + 2 * halo)]


def table_kernel(source, fwd, bwd, row):
    chans = source.shape[1]
    for b in range(3):
        for c in range(3):
            taps = [source[9 * a + 3 * b + c] for a in range(3)]
            for layer in range(2):
                lanes = slice(layer * chans, (layer + 1) * chans)
                below, level, above = [tap[:, lanes] for tap in taps]
                top = jnp.concatenate([level, above], axis=1)
                low = jnp.concatenate([below, level], axis=1)
                block = jnp.concatenate([top, low], axis=0)
                for target, value, r, at in ((fwd, block.T, b, c), (bwd, block, 2 - b, 2 - c)):
                    hi, lo = split_terms(value)
                    at = slice(at * LANES, (at + 1) * LANES)
                    target[layer, 2 * r * LANES : (2 * r + 1) * LANES, at] = hi
                    target[layer, (2 * r + 1) * LANES : (2 * r + 2) * LANES, at] = hi
                    target[layer, (6 + r) * LANES : (7 + r) * LANES, at] = lo
    last = source[TAPS, 0:1, :]
    for layer in range(2):
        part = last[:, layer * chans : (layer + 1) * chans]
        row[layer] = jnp.broadcast_to(jnp.concatenate([part, part], axis=1), (8, LANES))


def cut_kernel(dims, place, *refs):
    micros, chans, size_x, local_y, local_z, slabs, width, span, edged, fields = dims
    sources, refs = refs[:fields], refs[fields:]
    outs, wide = refs[:-1], refs[-1]
    slab = place[1]
    step = size_x * local_y
    for field, source in enumerate(sources):
        windows = outs[field * slabs : (field + 1) * slabs]
        edges = outs[fields * slabs :]
        for micro in range(micros):
            for y in range(local_y):
                first = micro * chans * step + y
                parts = [
                    source[pl.ds(first + x * local_y, chans, stride=step), :] for x in range(size_x)
                ]
                wide[field, micro, y, HALO : HALO + local_z] = jnp.concatenate(parts, axis=0).T
                wide[field, micro, y, :HALO] = jnp.zeros((HALO, LANES), F32)
                wide[field, micro, y, HALO + local_z :] = jnp.zeros((HALO, LANES), F32)
                if edged:
                    for turn in range(slabs):
                        start = lax.rem(slab + turn, slabs) * width
                        if width % 8 == 0:
                            start = pl.multiple_of(start, 8)
                        windows[turn][micro, y] = wide[field, micro, y, pl.ds(start, span)]
                    low = wide[field, micro, y, local_z : local_z + HALO]
                    high = wide[field, micro, y, HALO : 2 * HALO]
                    for m in range(slabs):
                        edges[m][field, micro, y] = jnp.where(slab == m, low, high)
                else:
                    windows[0][micro, y] = wide[field, micro, y, HALO : HALO + local_z]


class Slab:
    def __init__(self, dims):
        self.micros, self.rows_y, self.depth, self.width, self.chunk_y, self.slabs, limit_z = dims
        self.section, self.slab = lax.axis_index("section"), lax.axis_index("gy")
        origin = (lax.axis_index("gz") * self.slabs + self.slab) * self.width - HALO
        self.chunk = self.chunk_y * self.depth
        self.chunks = self.rows_y // self.chunk_y
        self.per_owner = self.rows_y // self.slabs
        zs = lax.broadcasted_iota(jnp.int32, (self.depth, LANES), 0)
        inside = (zs + origin >= 0) & (zs + origin < limit_z)
        self.in_grid = inside.astype(F32)[None]
        self.mine = ((zs >= HALO) & (zs < HALO + self.width)).astype(F32)[None]

    def over_chunks(self, body):
        if self.chunks == 1:
            body(0)
        else:

            def step(part, carry):
                body(pl.multiple_of(part * self.chunk, 16))
                return carry

            lax.fori_loop(0, self.chunks, step, 0)

    def masked(self, values, mask):
        return (values.reshape(-1, self.depth, LANES) * mask).reshape(values.shape)

    def put_rows(self, target, lead, micro, start, values):
        hi, lo = split_terms(values)
        at = pl.ds(start + self.depth, self.chunk)
        target[lead, micro, at, slice(0, LANES)] = hi
        target[lead, micro, at, slice(LANES, 2 * LANES)] = lo

    def pieces_of(self, source, lead, micro, start):
        return [
            source[lead, micro, pl.ds(start + b * self.depth, self.chunk), :] for b in range(3)
        ]

    def conv(self, source, lead, start, table):
        lefts = []
        for micro in range(self.micros):
            pieces = self.pieces_of(source, lead, micro, start)
            lefts.append(jnp.concatenate(pieces + [piece[:, :LANES] for piece in pieces], axis=1))
        results = []
        for left in lefts:
            out = jnp.dot(left, table[...], preferred_element_type=F32)
            before = pltpu.roll(out[:, :LANES], 1, 0)
            after = pltpu.roll(out[:, 2 * LANES :], out.shape[0] - 1, 0)
            results.append(before + out[:, LANES : 2 * LANES] + after)
        return results

    def by_owner(self, layer, own, other, body):
        mine = layer // 2 == self.section
        pl.when(mine)(lambda: body(own, layer % 2))
        pl.when(jnp.logical_not(mine))(lambda: body(other, layer % 2))

    def blank_edges(self, target):
        blank = jnp.zeros((self.depth, 2 * LANES), BF16)
        for lead in range(target.shape[0]):
            for micro in range(self.micros):
                for edge in (0, self.rows_y + 1):
                    target[lead, micro, edge * self.depth : (edge + 1) * self.depth, :] = blank

    def fill(self, field, windows, which):
        halo = HALOS[which]
        span = self.width + 2 * halo
        at = 0 if which == 0 else self.width + 2 * HALO
        extra = [HALO - halo, self.depth - span - (HALO - halo)]
        for micro in range(self.micros):
            for turn, window in enumerate(windows):
                owner = self.slab ^ turn
                for y in range(self.per_owner):
                    blanks = [jnp.zeros((rows, LANES), F32) for rows in extra]
                    parts = [blanks[0], window[micro, y, at : at + span], blanks[1]]
                    parts = [part for part in parts if part.shape[0]]
                    start = pl.multiple_of((owner * self.per_owner + y) * self.depth, 16)
                    value = jnp.concatenate(parts, axis=0) if len(parts) > 1 else parts[0]
                    field[micro, pl.ds(start, self.depth), :] = value

    def cut_out(self, targets, slot, source):
        for turn, target in enumerate(targets):
            owner = self.slab ^ turn
            for micro in range(self.micros):
                for y in range(self.per_owner):
                    start = (owner * self.per_owner + y) * self.depth + HALO
                    rows = pl.ds(pl.multiple_of(start, 8), self.width)
                    target[slot, micro, y] = source[micro, rows, :]


def forward_kernel(dims, own, own_row, other, other_row, *refs):
    slab = Slab(dims)
    windows, (acts, kept, front, field) = refs[:-4], refs[-4:]
    slab.blank_edges(acts)
    slab.fill(field, windows, 0)

    def take_in(start):
        for micro in range(slab.micros):
            slab.put_rows(acts, 0, micro, start, field[micro, pl.ds(start, slab.chunk), :])

    slab.over_chunks(take_in)

    def layer_step(layer, carry):
        def run(tables, half):
            table, row = tables

            def body(start):
                at = pl.ds(start, slab.chunk)
                sums = slab.conv(acts, layer, start, table.at[half])
                outs = []
                for micro, total in enumerate(sums):
                    pre = total + row[half][0:1, :]
                    sigma = 1.0 / (1.0 + jnp.exp(-pre))
                    kept[layer, micro, at, :] = sigma * (1.0 + pre * (1.0 - sigma))
                    out = slab.masked(pre * sigma, slab.in_grid)
                    slab.put_rows(acts, layer + 1, micro, start, out)
                    outs.append(out)

                @pl.when(layer == 2 * slab.section + 1)
                def _():
                    for micro, out in enumerate(outs):
                        front[micro, at, :] = out

            slab.over_chunks(body)

        slab.by_owner(layer, (own, own_row), (other, other_row), run)
        return carry

    lax.fori_loop(0, 4, layer_step, 0)


def backward_kernel(dims, scale, own, other, acts, kept, front, *refs):
    slab = Slab(dims)
    windows, refs = refs[: slab.slabs], refs[slab.slabs :]
    outs, (sums, rim, slopes, field, acc) = refs[: slab.slabs], refs[slab.slabs :]
    slab.blank_edges(rim)
    slab.cut_out(outs, 0, front)
    slab.fill(field, windows, 1)

    def take_gradient(layer, micro, start, gradient):
        at = pl.ds(start, slab.chunk)
        slope = slab.masked(gradient * kept[layer, micro, at, :], slab.in_grid)
        slopes[layer, micro, at, :] = slab.masked(slope, slab.mine)
        slab.put_rows(rim, layer % 2, micro, start, slope)

    def take_cotangent(start):
        for micro in range(slab.micros):
            take_gradient(3, micro, start, field[micro, pl.ds(start, slab.chunk), :])

    slab.over_chunks(take_cotangent)

    def layer_step(index, carry):
        layer = 3 - index

        def run(table, half):
            def body(start):
                gradients = slab.conv(rim, layer % 2, start, table.at[half])
                last = layer == 2 * slab.section

                @pl.when(last)
                def _():
                    for micro, gradient in enumerate(gradients):
                        field[micro, pl.ds(start, slab.chunk), :] = gradient

                @pl.when(jnp.logical_not(last))
                def _():
                    for micro, gradient in enumerate(gradients):
                        take_gradient(layer - 1, micro, start, gradient)

            slab.over_chunks(body)

        slab.by_owner(layer, own, other, run)
        return carry

    lax.fori_loop(0, jnp.where(slab.section == 0, 4, 2), layer_step, 0)
    slab.cut_out(outs, 1, field)

    quarter = BLOCKS // 4
    chans = LANES // 2
    swap = column_bits()

    def spot(tap):
        return (tap // quarter ^ swap) * quarter + tap % quarter

    def products(layer, start):
        at = pl.ds(start, slab.chunk)
        slope = jnp.concatenate([slopes[layer, micro, at, :] for micro in range(slab.micros)])
        moved = [pltpu.roll(slope, slope.shape[0] - 1, 0), slope, pltpu.roll(slope, 1, 0)]
        terms = [split_terms(value) for value in moved]
        left_hi = jnp.concatenate([hi for hi, lo in terms], axis=1)
        left_lo = jnp.concatenate([lo for hi, lo in terms], axis=1)
        pieces = [slab.pieces_of(acts, layer, micro, start) for micro in range(slab.micros)]
        pieces = [jnp.concatenate(parts, axis=0) for parts in zip(*pieces)]
        full = jnp.concatenate(pieces, axis=1)
        high = jnp.concatenate([piece[:, :LANES] for piece in pieces], axis=1)
        over_rows = (((0,), (0,)), ((), ()))
        one = lax.dot_general(left_hi, full, over_rows, preferred_element_type=F32)
        two = lax.dot_general(left_lo, high, over_rows, preferred_element_type=F32)
        total = []
        for b in range(3):
            hi = one[:, 2 * b * LANES : (2 * b + 1) * LANES]
            lo = one[:, (2 * b + 1) * LANES : (2 * b + 2) * LANES]
            total.append(hi + lo + two[:, b * LANES : (b + 1) * LANES])
        return total, jnp.sum(slope, axis=0, keepdims=True)

    sums[spot(TAPS)] = jnp.zeros((chans, LANES), F32)
    for slot in range(2):
        layer = 2 * slab.section + slot
        if slab.chunks == 1:
            total, row = products(layer, 0)
        else:
            acc[...] = jnp.zeros(acc.shape, F32)

            def gather(start):
                total, row = products(layer, start)
                for b in range(3):
                    acc[0 : 3 * LANES, b * LANES : (b + 1) * LANES] += total[b]
                acc[3 * LANES : 3 * LANES + 1, 0:LANES] += row

            slab.over_chunks(gather)
            total = [acc[0 : 3 * LANES, b * LANES : (b + 1) * LANES] for b in range(3)]
            row = acc[3 * LANES : 3 * LANES + 1, 0:LANES]
        lanes = slice(slot * chans, (slot + 1) * chans)
        for b in range(3):
            for c in range(3):
                block = total[b][c * LANES : (c + 1) * LANES] * scale
                tap = 3 * b + c
                sums[spot(tap), :, lanes] = block[chans:, :chans]
                sums[spot(9 + tap), :, lanes] = block[:chans, :chans] + block[chans:, chans:]
                sums[spot(18 + tap), :, lanes] = block[:chans, chans:]
        row = row * scale
        sums[spot(TAPS), 0:1, lanes] = row[:, :chans] + row[:, chans:]


def unpack_kernel(kept, theirs, beside, across, weight, bias, whole):
    half = kept.shape[0]
    chans = weight.shape[-1]
    odd, swap = lax.axis_index("gy") % 2, column_bits()
    parts = [(kept, 0), (theirs, 0), (beside, 0), (beside, half)]
    parts += [(across, half * i) for i in range(4)]
    for index, (source, first) in enumerate(parts):
        at = ((index // 2 ^ swap) * 2 + (index % 2 ^ odd)) * half
        whole[pl.ds(pl.multiple_of(at, 8), half), :] = source[first : first + half, :]
    for layer in range(2):
        lanes = slice(layer * chans, (layer + 1) * chans)
        for tap in range(TAPS):
            weight[layer, tap] = whole[tap * chans : (tap + 1) * chans, lanes]
        bias[layer : layer + 1, :] = whole[TAPS * chans : TAPS * chans + 1, lanes]


def restore_kernel(dims, *refs):
    micros, chans, size_x, local_y, width = dims
    pieces, (*targets, whole) = refs[:-3], refs[-3:]
    slab = lax.axis_index("gy")
    step = size_x * local_y
    for slot, target in enumerate(targets):
        for micro in range(micros):
            for y in range(local_y):
                for turn, piece in enumerate(pieces):
                    start = (slab ^ turn) * width
                    if width % 8 == 0:
                        start = pl.multiple_of(start, 8)
                    whole[slot, micro, y, pl.ds(start, width), :] = piece[slot, micro, y]
                block = whole[slot, micro, y].T
                for x in range(size_x):
                    first = micro * chans * step + x * local_y + y
                    part = block[x * chans : (x + 1) * chans]
                    target[pl.ds(first, chans, stride=step), :] = part


def spread(blocks):
    slabs = len(blocks)
    if slabs <= 8:
        got = [blocks[0]]
        for turn in range(1, slabs):
            route = [(i, i ^ turn) for i in range(slabs)]
            got.append(lax.ppermute(blocks[turn], "gy", route))
        return got
    order = jnp.arange(slabs) ^ lax.axis_index("gy")
    got = lax.all_to_all(jnp.stack(blocks)[order], "gy", 0, 0)[order]
    return [got[turn] for turn in range(slabs)]


def swapped(block, bit, axis="gz"):
    return lax.ppermute(block, axis, [(i, i ^ bit) for i in range(lax.axis_size(axis))])


def halved(block, bit):
    rows = block.shape[0] // 2
    return block[:rows] + swapped(block[rows:], bit)


def per_device(inflow, weights, biases, cotangent):
    micros, chans, size_x, local_y, local_z = inflow.shape
    slabs, columns = lax.axis_size("gy"), lax.axis_size("gz")
    rows_y = local_y * slabs
    width = local_z // slabs
    span = width + 2 * HALO
    depth = -(-span // 16) * 16
    chunk_y = max(n for n in range(1, rows_y + 1) if rows_y % n == 0 and n * depth <= 384)
    scale = 1.0 / math.sqrt(micros * size_x * rows_y * local_z * columns)
    rows = micros * chans * size_x * local_y
    ends = ((2, micros, local_y, HALO, LANES), F32)
    (own,) = call(pack_kernel, "pack", [((BLOCKS, chans, LANES), F32)], [weights, biases])
    fields, pair, inner = call(
        functools.partial(turn_kernel, inflow.shape),
        "turn",
        [((2, micros, local_y, local_z, LANES), F32), ends, ends],
        [inflow.reshape(rows, local_z), cotangent.reshape(rows, local_z)],
    )
    far = lax.ppermute(own, "section", [(0, 1), (1, 0)])
    pair = swapped(pair, 1)
    route = [(i, i + 1) for i in range(1, columns - 1, 2)]
    inner = lax.ppermute(inner, "gz", route + [(after, before) for before, after in route])
    reach = sum(width + 2 * halo for halo in HALOS)
    windows = call(
        functools.partial(window_kernel, (slabs, width, columns)),
        "windows",
        [((micros, local_y, reach, LANES), F32)] * slabs,
        [fields, pair, inner],
        [pltpu.VMEM((2, micros, local_y, local_z + 2 * HALO, LANES), F32)],
    )
    windows = spread(windows)
    far, windows = lax.optimization_barrier((far, windows))

    tables = [((2, 9 * LANES, 3 * LANES), BF16)] * 2 + [((2, 8, LANES), F32)]
    own_fwd, own_bwd, own_row = call(table_kernel, "own_table", tables, [own])
    far_fwd, far_bwd, far_row = call(table_kernel, "far_table", tables, [far])

    dims = (micros, rows_y, depth, width, chunk_y, slabs, local_z * columns)
    padded = (rows_y + 2) * depth
    full = rows_y * depth
    acts, kept, front = call(
        functools.partial(forward_kernel, dims),
        "forward",
        [
            ((5, micros, padded, 2 * LANES), BF16),
            ((4, micros, full, LANES), F32),
            ((micros, full, LANES), F32),
        ],
        [own_fwd, own_row, far_fwd, far_row, *windows],
        [pltpu.VMEM((micros, full, LANES), F32)],
    )
    *outs, sums = call(
        functools.partial(backward_kernel, dims, scale),
        "backward",
        [((2, micros, local_y, width, LANES), F32)] * slabs + [((BLOCKS, chans, LANES), F32)],
        [own_bwd, far_bwd, acts, kept, front, *windows],
        [
            pltpu.VMEM((2, micros, padded, 2 * LANES), BF16),
            pltpu.VMEM((4, micros, full, LANES), F32),
            pltpu.VMEM((micros, full, LANES), F32),
            pltpu.VMEM((3 * LANES + 8, 3 * LANES), F32),
        ],
    )

    block = halved(sums.reshape(BLOCKS * chans, LANES), 1)
    block, outs = lax.optimization_barrier((block, outs))
    outs = spread(outs)
    block = halved(block, 2)
    block, outs = lax.optimization_barrier((block, outs))
    half = block.shape[0] // 2
    odd = lax.axis_index("gy") % 2 == 1
    kept_half = jnp.where(odd, block[half:], block[:half])
    kept_half = kept_half + swapped(jnp.where(odd, block[:half], block[half:]), 1, "gy")
    bit = 2
    while bit < slabs:
        kept_half = kept_half + swapped(kept_half, bit, "gy")
        bit *= 2
    theirs = swapped(kept_half, 1, "gy")
    quarter = jnp.concatenate([kept_half, theirs], axis=0)
    beside = swapped(quarter, 2)
    across = swapped(jnp.concatenate([quarter, beside], axis=0), 1)
    section_out, section_grad = call(
        functools.partial(restore_kernel, (micros, chans, size_x, local_y, width)),
        "restore",
        [((rows, local_z), F32)] * 2,
        outs,
        [pltpu.VMEM((2, micros, local_y, local_z, LANES), F32)],
    )
    weight_total, bias_total = call(
        unpack_kernel,
        "unpack",
        [((2, TAPS, chans, chans), F32), ((2, chans), F32)],
        [kept_half, theirs, beside, across],
        [pltpu.VMEM((BLOCKS * chans, LANES), F32)],
    )
    shape = (1, *inflow.shape)
    return (section_out.reshape(shape), section_grad.reshape(shape), weight_total, bias_total)


def solution(mesh):
    grid = P(None, None, None, "gy", "gz")
    section_grid = P("section", None, None, None, "gy", "gz")
    return jax.shard_map(
        per_device,
        mesh=mesh,
        in_specs=(grid, P("section", None, None, None), P("section", None), grid),
        out_specs=(section_grid, section_grid, P("section", None, None, None), P("section", None)),
        check_vma=False,
    )
```

```python
import functools
import math

import jax
import jax.numpy as jnp
from jax import lax
from jax.experimental import pallas as pl
from jax.experimental.pallas import tpu as pltpu
from jax.sharding import PartitionSpec as P

HALO = 8
HALOS = (8, 4)
LANES = 128
TAPS = 27
BLOCKS = 28
BF16 = jnp.bfloat16
F32 = jnp.float32
VMEM = pl.BlockSpec(memory_space=pltpu.VMEM)


def call(kernel, name, outs, args, scratch=(), flops=0):
    arrays = [jax.ShapeDtypeStruct(shape, kind) for shape, kind in outs]
    size = sum(math.prod(item.shape) * item.dtype.itemsize for item in [*arrays, *args, *scratch])
    return pl.pallas_call(
        kernel,
        out_shape=arrays,
        in_specs=[VMEM] * len(args),
        out_specs=[VMEM] * len(arrays),
        scratch_shapes=list(scratch),
        compiler_params=pltpu.CompilerParams(vmem_limit_bytes=size + 6 * 1024 * 1024),
        cost_estimate=pl.CostEstimate(flops=flops, bytes_accessed=1024, transcendentals=0),
        name=name,
    )(*args)


def column_bits():
    column = lax.axis_index("gz")
    return 2 * (column % 2) + column // 2 % 2


def split_terms(values):
    high = values.astype(BF16)
    return high, (values - high.astype(F32)).astype(BF16)


def pack_kernel(weights, biases, own, sent):
    chans = weights.shape[2]
    for tap in range(TAPS):
        own[tap] = jnp.concatenate([weights[0, tap], weights[1, tap]], axis=1)
    own[TAPS] = jnp.zeros((chans, LANES), F32)
    own[TAPS, 0:1, :] = jnp.concatenate([biases[0:1, :], biases[1:2, :]], axis=1)
    half = sent.shape[0]
    start = lax.axis_index("gz") % 2 * half
    for index in range(half):
        sent[index] = own[start + index]


def turn_kernel(dims, inflow, cotangent, rows, pair, inner):
    micros, chans, size_x, local_y, local_z = dims
    step = size_x * local_y
    odd = lax.axis_index("gz") % 2 == 1
    for field, source in enumerate((inflow, cotangent)):
        for micro in range(micros):
            for y in range(local_y):
                first = micro * chans * step + y
                parts = [
                    source[pl.ds(first + x * local_y, chans, stride=step), :] for x in range(size_x)
                ]
                turned = jnp.concatenate(parts, axis=0).T
                rows[field, micro, y] = turned
                low, high = turned[:HALO], turned[local_z - HALO :]
                pair[field, micro, y] = jnp.where(odd, low, high)
                inner[field, micro, y] = jnp.where(odd, high, low)


def window_kernel(dims, rows, pair, inner, *refs):
    slabs, width, columns = dims
    outs, wide = refs[:-1], refs[-1]
    slab, column = lax.axis_index("gy"), lax.axis_index("gz")
    odd = column % 2 == 1
    _, micros, local_y, local_z, _ = rows.shape
    for field, halo in enumerate(HALOS):
        at = slice(0, width + 2 * halo) if field == 0 else slice(width + 2 * HALO, None)
        for micro in range(micros):
            for y in range(local_y):
                one, two = pair[field, micro, y], inner[field, micro, y]
                before = jnp.where(column > 0, jnp.where(odd, one, two), 0.0)
                after = jnp.where(column < columns - 1, jnp.where(odd, two, one), 0.0)
                wide[field, micro, y, :HALO] = before
                wide[field, micro, y, HALO : HALO + local_z] = rows[field, micro, y]
                wide[field, micro, y, HALO + local_z :] = after
                for turn in range(slabs):
                    start = (slab ^ turn) * width + HALO - halo
                    if width % 8 == 0 and halo % 8 == 0:
                        start = pl.multiple_of(start, 8)
                    outs[turn][micro, y, at] = wide[field, micro, y, pl.ds(start, width + 2 * halo)]


def table_kernel(*refs):
    parts, (fwd, bwd, row) = refs[:-3], refs[-3:]
    odd = lax.axis_index("gz") % 2
    count, chans, _ = parts[0].shape

    def block_of(tap):
        if len(parts) == 1:
            return parts[0][tap]
        index = tap % count
        return jnp.where(odd == tap // count, parts[0][index], parts[1][index])

    for b in range(3):
        for c in range(3):
            taps = [block_of(9 * a + 3 * b + c) for a in range(3)]
            for layer in range(2):
                lanes = slice(layer * chans, (layer + 1) * chans)
                below, level, above = [tap[:, lanes] for tap in taps]
                top = jnp.concatenate([level, above], axis=1)
                low = jnp.concatenate([below, level], axis=1)
                block = jnp.concatenate([top, low], axis=0)
                for target, value, r, at in ((fwd, block.T, b, c), (bwd, block, 2 - b, 2 - c)):
                    hi, lo = split_terms(value)
                    at = slice(at * LANES, (at + 1) * LANES)
                    target[layer, 2 * r * LANES : (2 * r + 1) * LANES, at] = hi
                    target[layer, (2 * r + 1) * LANES : (2 * r + 2) * LANES, at] = hi
                    target[layer, (6 + r) * LANES : (7 + r) * LANES, at] = lo
    last = block_of(TAPS)[0:1, :]
    for layer in range(2):
        part = last[:, layer * chans : (layer + 1) * chans]
        row[layer] = jnp.broadcast_to(jnp.concatenate([part, part], axis=1), (8, LANES))


def cut_kernel(dims, place, *refs):
    micros, chans, size_x, local_y, local_z, slabs, width, span, edged, fields = dims
    sources, refs = refs[:fields], refs[fields:]
    outs, wide = refs[:-1], refs[-1]
    slab = place[1]
    step = size_x * local_y
    for field, source in enumerate(sources):
        windows = outs[field * slabs : (field + 1) * slabs]
        edges = outs[fields * slabs :]
        for micro in range(micros):
            for y in range(local_y):
                first = micro * chans * step + y
                parts = [
                    source[pl.ds(first + x * local_y, chans, stride=step), :] for x in range(size_x)
                ]
                wide[field, micro, y, HALO : HALO + local_z] = jnp.concatenate(parts, axis=0).T
                wide[field, micro, y, :HALO] = jnp.zeros((HALO, LANES), F32)
                wide[field, micro, y, HALO + local_z :] = jnp.zeros((HALO, LANES), F32)
                if edged:
                    for turn in range(slabs):
                        start = lax.rem(slab + turn, slabs) * width
                        if width % 8 == 0:
                            start = pl.multiple_of(start, 8)
                        windows[turn][micro, y] = wide[field, micro, y, pl.ds(start, span)]
                    low = wide[field, micro, y, local_z : local_z + HALO]
                    high = wide[field, micro, y, HALO : 2 * HALO]
                    for m in range(slabs):
                        edges[m][field, micro, y] = jnp.where(slab == m, low, high)
                else:
                    windows[0][micro, y] = wide[field, micro, y, HALO : HALO + local_z]


class Slab:
    def __init__(self, dims):
        self.micros, self.rows_y, self.depth, self.width, self.chunk_y, self.slabs, limit_z = dims
        self.section, self.slab = lax.axis_index("section"), lax.axis_index("gy")
        origin = (lax.axis_index("gz") * self.slabs + self.slab) * self.width - HALO
        self.chunk = self.chunk_y * self.depth
        self.chunks = self.rows_y // self.chunk_y
        self.per_owner = self.rows_y // self.slabs
        zs = lax.broadcasted_iota(jnp.int32, (self.depth, LANES), 0)
        inside = (zs + origin >= 0) & (zs + origin < limit_z)
        self.in_grid = inside.astype(F32)[None]
        self.mine = ((zs >= HALO) & (zs < HALO + self.width)).astype(F32)[None]

    def over_chunks(self, body):
        if self.chunks == 1:
            body(0)
        else:

            def step(part, carry):
                body(pl.multiple_of(part * self.chunk, 16))
                return carry

            lax.fori_loop(0, self.chunks, step, 0)

    def masked(self, values, mask):
        return (values.reshape(-1, self.depth, LANES) * mask).reshape(values.shape)

    def put_rows(self, target, lead, micro, start, values):
        hi, lo = split_terms(values)
        at = pl.ds(start + self.depth, self.chunk)
        target[lead, micro, at, slice(0, LANES)] = hi
        target[lead, micro, at, slice(LANES, 2 * LANES)] = lo

    def pieces_of(self, source, lead, micro, start):
        return [
            source[lead, micro, pl.ds(start + b * self.depth, self.chunk), :] for b in range(3)
        ]

    def conv(self, source, lead, start, table):
        lefts = []
        for micro in range(self.micros):
            pieces = self.pieces_of(source, lead, micro, start)
            lefts.append(jnp.concatenate(pieces + [piece[:, :LANES] for piece in pieces], axis=1))
        results = []
        for left in lefts:
            out = jnp.dot(left, table[...], preferred_element_type=F32)
            before = pltpu.roll(out[:, :LANES], 1, 0)
            after = pltpu.roll(out[:, 2 * LANES :], out.shape[0] - 1, 0)
            results.append(before + out[:, LANES : 2 * LANES] + after)
        return results

    def by_owner(self, layer, own, other, body):
        mine = layer // 2 == self.section
        pl.when(mine)(lambda: body(own, layer % 2))
        pl.when(jnp.logical_not(mine))(lambda: body(other, layer % 2))

    def blank_edges(self, target):
        blank = jnp.zeros((self.depth, 2 * LANES), BF16)
        for lead in range(target.shape[0]):
            for micro in range(self.micros):
                for edge in (0, self.rows_y + 1):
                    target[lead, micro, edge * self.depth : (edge + 1) * self.depth, :] = blank

    def fill(self, field, windows, which):
        halo = HALOS[which]
        span = self.width + 2 * halo
        at = 0 if which == 0 else self.width + 2 * HALO
        extra = [HALO - halo, self.depth - span - (HALO - halo)]
        for micro in range(self.micros):
            for turn, window in enumerate(windows):
                owner = self.slab ^ turn
                for y in range(self.per_owner):
                    blanks = [jnp.zeros((rows, LANES), F32) for rows in extra]
                    parts = [blanks[0], window[micro, y, at : at + span], blanks[1]]
                    parts = [part for part in parts if part.shape[0]]
                    start = pl.multiple_of((owner * self.per_owner + y) * self.depth, 16)
                    value = jnp.concatenate(parts, axis=0) if len(parts) > 1 else parts[0]
                    field[micro, pl.ds(start, self.depth), :] = value

    def cut_out(self, targets, slot, source):
        for turn, target in enumerate(targets):
            owner = self.slab ^ turn
            for micro in range(self.micros):
                for y in range(self.per_owner):
                    start = (owner * self.per_owner + y) * self.depth + HALO
                    rows = pl.ds(pl.multiple_of(start, 8), self.width)
                    target[slot, micro, y] = source[micro, rows, :]


def forward_kernel(dims, own, own_row, other, other_row, *refs):
    slab = Slab(dims)
    windows, (acts, kept, front, field) = refs[:-4], refs[-4:]
    slab.blank_edges(acts)
    slab.fill(field, windows, 0)

    def take_in(start):
        for micro in range(slab.micros):
            slab.put_rows(acts, 0, micro, start, field[micro, pl.ds(start, slab.chunk), :])

    slab.over_chunks(take_in)

    def layer_step(layer, carry):
        def run(tables, half):
            table, row = tables

            def body(start):
                at = pl.ds(start, slab.chunk)
                sums = slab.conv(acts, layer, start, table.at[half])
                outs = []
                for micro, total in enumerate(sums):
                    pre = total + row[half][0:1, :]
                    sigma = 1.0 / (1.0 + jnp.exp(-pre))
                    kept[layer, micro, at, :] = sigma * (1.0 + pre * (1.0 - sigma))
                    out = slab.masked(pre * sigma, slab.in_grid)
                    slab.put_rows(acts, layer + 1, micro, start, out)
                    outs.append(out)

                @pl.when(layer == 2 * slab.section + 1)
                def _():
                    for micro, out in enumerate(outs):
                        front[micro, at, :] = out

            slab.over_chunks(body)

        slab.by_owner(layer, (own, own_row), (other, other_row), run)
        return carry

    lax.fori_loop(0, 4, layer_step, 0)


def backward_kernel(dims, scale, own, other, acts, kept, front, *refs):
    slab = Slab(dims)
    windows, refs = refs[: slab.slabs], refs[slab.slabs :]
    outs, (sums, rim, slopes, field, acc) = refs[: slab.slabs], refs[slab.slabs :]
    slab.blank_edges(rim)
    slab.cut_out(outs, 0, front)
    slab.fill(field, windows, 1)

    def take_gradient(layer, micro, start, gradient):
        at = pl.ds(start, slab.chunk)
        slope = slab.masked(gradient * kept[layer, micro, at, :], slab.in_grid)
        slopes[layer, micro, at, :] = slab.masked(slope, slab.mine)
        slab.put_rows(rim, layer % 2, micro, start, slope)

    def take_cotangent(start):
        for micro in range(slab.micros):
            take_gradient(3, micro, start, field[micro, pl.ds(start, slab.chunk), :])

    slab.over_chunks(take_cotangent)

    def layer_step(index, carry):
        layer = 3 - index

        def run(table, half):
            def body(start):
                gradients = slab.conv(rim, layer % 2, start, table.at[half])
                last = layer == 2 * slab.section

                @pl.when(last)
                def _():
                    for micro, gradient in enumerate(gradients):
                        field[micro, pl.ds(start, slab.chunk), :] = gradient

                @pl.when(jnp.logical_not(last))
                def _():
                    for micro, gradient in enumerate(gradients):
                        take_gradient(layer - 1, micro, start, gradient)

            slab.over_chunks(body)

        slab.by_owner(layer, own, other, run)
        return carry

    lax.fori_loop(0, jnp.where(slab.section == 0, 4, 2), layer_step, 0)
    slab.cut_out(outs, 1, field)

    quarter = BLOCKS // 4
    chans = LANES // 2
    swap = column_bits()

    def spot(tap):
        return (tap // quarter ^ swap) * quarter + tap % quarter

    def products(layer, start):
        at = pl.ds(start, slab.chunk)
        slope = jnp.concatenate([slopes[layer, micro, at, :] for micro in range(slab.micros)])
        moved = [pltpu.roll(slope, slope.shape[0] - 1, 0), slope, pltpu.roll(slope, 1, 0)]
        terms = [split_terms(value) for value in moved]
        left_hi = jnp.concatenate([hi for hi, lo in terms], axis=1)
        left_lo = jnp.concatenate([lo for hi, lo in terms], axis=1)
        pieces = [slab.pieces_of(acts, layer, micro, start) for micro in range(slab.micros)]
        pieces = [jnp.concatenate(parts, axis=0) for parts in zip(*pieces)]
        full = jnp.concatenate(pieces, axis=1)
        high = jnp.concatenate([piece[:, :LANES] for piece in pieces], axis=1)
        over_rows = (((0,), (0,)), ((), ()))
        one = lax.dot_general(left_hi, full, over_rows, preferred_element_type=F32)
        two = lax.dot_general(left_lo, high, over_rows, preferred_element_type=F32)
        total = []
        for b in range(3):
            hi = one[:, 2 * b * LANES : (2 * b + 1) * LANES]
            lo = one[:, (2 * b + 1) * LANES : (2 * b + 2) * LANES]
            total.append(hi + lo + two[:, b * LANES : (b + 1) * LANES])
        return total, jnp.sum(slope, axis=0, keepdims=True)

    sums[spot(TAPS)] = jnp.zeros((chans, LANES), F32)
    for slot in range(2):
        layer = 2 * slab.section + slot
        if slab.chunks == 1:
            total, row = products(layer, 0)
        else:
            acc[...] = jnp.zeros(acc.shape, F32)

            def gather(start):
                total, row = products(layer, start)
                for b in range(3):
                    acc[0 : 3 * LANES, b * LANES : (b + 1) * LANES] += total[b]
                acc[3 * LANES : 3 * LANES + 1, 0:LANES] += row

            slab.over_chunks(gather)
            total = [acc[0 : 3 * LANES, b * LANES : (b + 1) * LANES] for b in range(3)]
            row = acc[3 * LANES : 3 * LANES + 1, 0:LANES]
        lanes = slice(slot * chans, (slot + 1) * chans)
        for b in range(3):
            for c in range(3):
                block = total[b][c * LANES : (c + 1) * LANES] * scale
                tap = 3 * b + c
                sums[spot(tap), :, lanes] = block[chans:, :chans]
                sums[spot(9 + tap), :, lanes] = block[:chans, :chans] + block[chans:, chans:]
                sums[spot(18 + tap), :, lanes] = block[:chans, chans:]
        row = row * scale
        sums[spot(TAPS), 0:1, lanes] = row[:, :chans] + row[:, chans:]


def unpack_kernel(near, core, weight, bias, whole):
    part = near.shape[0] // 4
    chans = weight.shape[-1]
    odd, swap = lax.axis_index("gy") % 2, column_bits()
    for index in range(8):
        source = near if index < 4 else core
        first = index % 4 * part
        at = ((index // 2 ^ swap) * 2 + (index % 2 ^ odd)) * part
        whole[pl.ds(pl.multiple_of(at, 8), part), :] = source[first : first + part, :]
    for layer in range(2):
        lanes = slice(layer * chans, (layer + 1) * chans)
        for tap in range(TAPS):
            weight[layer, tap] = whole[tap * chans : (tap + 1) * chans, lanes]
        bias[layer : layer + 1, :] = whole[TAPS * chans : TAPS * chans + 1, lanes]


def restore_kernel(dims, *refs):
    micros, chans, size_x, local_y, width = dims
    pieces, (*targets, whole) = refs[:-3], refs[-3:]
    slab = lax.axis_index("gy")
    step = size_x * local_y
    for slot, target in enumerate(targets):
        for micro in range(micros):
            for y in range(local_y):
                for turn, piece in enumerate(pieces):
                    start = (slab ^ turn) * width
                    if width % 8 == 0:
                        start = pl.multiple_of(start, 8)
                    whole[slot, micro, y, pl.ds(start, width), :] = piece[slot, micro, y]
                block = whole[slot, micro, y].T
                for x in range(size_x):
                    first = micro * chans * step + x * local_y + y
                    part = block[x * chans : (x + 1) * chans]
                    target[pl.ds(first, chans, stride=step), :] = part


def spread(blocks):
    slabs = len(blocks)
    if slabs <= 8:
        got = [blocks[0]]
        for turn in range(1, slabs):
            route = [(i, i ^ turn) for i in range(slabs)]
            got.append(lax.ppermute(blocks[turn], "gy", route))
        return got
    order = jnp.arange(slabs) ^ lax.axis_index("gy")
    got = lax.all_to_all(jnp.stack(blocks)[order], "gy", 0, 0)[order]
    return [got[turn] for turn in range(slabs)]


def swapped(block, bit, axis="gz"):
    return lax.ppermute(block, axis, [(i, i ^ bit) for i in range(lax.axis_size(axis))])


def around(above, beside, across):
    slabs, columns = lax.axis_size("gy"), lax.axis_size("gz")
    route = [
        (i * columns + g, (i ^ 1) * columns + (g ^ 2)) for i in range(slabs) for g in range(columns)
    ]
    beside = swapped(beside, 2)
    across = lax.ppermute(across, ("gy", "gz"), route)
    return [swapped(above, 1, "gy"), beside, across]


def per_device(inflow, weights, biases, cotangent):
    micros, chans, size_x, local_y, local_z = inflow.shape
    slabs, columns = lax.axis_size("gy"), lax.axis_size("gz")
    rows_y = local_y * slabs
    width = local_z // slabs
    span = width + 2 * HALO
    depth = -(-span // 16) * 16
    chunk_y = max(n for n in range(1, rows_y + 1) if rows_y % n == 0 and n * depth <= 384)
    scale = 1.0 / math.sqrt(micros * size_x * rows_y * local_z * columns)
    rows = micros * chans * size_x * local_y
    ends = ((2, micros, local_y, HALO, LANES), F32)
    packs = [((BLOCKS, chans, LANES), F32), ((BLOCKS // 2, chans, LANES), F32)]
    own, sent = call(pack_kernel, "pack", packs, [weights, biases])
    fields, pair, inner = call(
        functools.partial(turn_kernel, inflow.shape),
        "turn",
        [((2, micros, local_y, local_z, LANES), F32), ends, ends],
        [inflow.reshape(rows, local_z), cotangent.reshape(rows, local_z)],
    )
    near_half = lax.ppermute(sent, "section", [(0, 1), (1, 0)])
    pair = swapped(pair, 1)
    route = [(i, i + 1) for i in range(1, columns - 1, 2)]
    inner = lax.ppermute(inner, "gz", route + [(after, before) for before, after in route])
    reach = sum(width + 2 * halo for halo in HALOS)
    windows = call(
        functools.partial(window_kernel, (slabs, width, columns)),
        "windows",
        [((micros, local_y, reach, LANES), F32)] * slabs,
        [fields, pair, inner],
        [pltpu.VMEM((2, micros, local_y, local_z + 2 * HALO, LANES), F32)],
    )
    windows = spread(windows)
    near_half, windows = lax.optimization_barrier((near_half, windows))
    far_half = swapped(near_half, 1)

    tables = [((2, 9 * LANES, 3 * LANES), BF16)] * 2 + [((2, 8, LANES), F32)]
    own_fwd, own_bwd, own_row = call(table_kernel, "own_table", tables, [own])
    far_fwd, far_bwd, far_row = call(table_kernel, "far_table", tables, [near_half, far_half])

    dims = (micros, rows_y, depth, width, chunk_y, slabs, local_z * columns)
    padded = (rows_y + 2) * depth
    full = rows_y * depth
    acts, kept, front = call(
        functools.partial(forward_kernel, dims),
        "forward",
        [
            ((5, micros, padded, 2 * LANES), BF16),
            ((4, micros, full, LANES), F32),
            ((micros, full, LANES), F32),
        ],
        [own_fwd, own_row, far_fwd, far_row, *windows],
        [pltpu.VMEM((micros, full, LANES), F32)],
    )
    *outs, sums = call(
        functools.partial(backward_kernel, dims, scale),
        "backward",
        [((2, micros, local_y, width, LANES), F32)] * slabs + [((BLOCKS, chans, LANES), F32)],
        [own_bwd, far_bwd, acts, kept, front, *windows],
        [
            pltpu.VMEM((2, micros, padded, 2 * LANES), BF16),
            pltpu.VMEM((4, micros, full, LANES), F32),
            pltpu.VMEM((micros, full, LANES), F32),
            pltpu.VMEM((3 * LANES + 8, 3 * LANES), F32),
        ],
    )

    block = sums.reshape(BLOCKS * chans, LANES)
    half = block.shape[0] // 2
    block = block[:half] + swapped(block[half:], 1)
    block, outs = lax.optimization_barrier((block, outs))
    outs = spread(outs)
    part = half // 4
    odd = lax.axis_index("gy") % 2 == 1
    lows, highs = [block[i * part : (i + 1) * part] for i in (0, 2)], [
        block[i * part : (i + 1) * part] for i in (1, 3)
    ]
    mine, beside = [jnp.where(odd, high, low) for low, high in zip(lows, highs)]
    above, across = [jnp.where(odd, low, high) for low, high in zip(lows, highs)]
    kept = mine + sum(around(above, beside, across))
    kept, outs = lax.optimization_barrier((kept, outs))
    bit = 2
    while bit < slabs:
        kept = kept + swapped(kept, bit, "gy")
        bit *= 2
    near = jnp.concatenate([kept, *around(kept, kept, kept)], axis=0)
    core = swapped(near, 1)
    section_out, section_grad = call(
        functools.partial(restore_kernel, (micros, chans, size_x, local_y, width)),
        "restore",
        [((rows, local_z), F32)] * 2,
        outs,
        [pltpu.VMEM((2, micros, local_y, local_z, LANES), F32)],
    )
    weight_total, bias_total = call(
        unpack_kernel,
        "unpack",
        [((2, TAPS, chans, chans), F32), ((2, chans), F32)],
        [near, core],
        [pltpu.VMEM((BLOCKS * chans, LANES), F32)],
    )
    shape = (1, *inflow.shape)
    return (section_out.reshape(shape), section_grad.reshape(shape), weight_total, bias_total)


def solution(mesh):
    grid = P(None, None, None, "gy", "gz")
    section_grid = P("section", None, None, None, "gy", "gz")
    return jax.shard_map(
        per_device,
        mesh=mesh,
        in_specs=(grid, P("section", None, None, None), P("section", None), grid),
        out_specs=(section_grid, section_grid, P("section", None, None, None), P("section", None)),
        check_vma=False,
    )
```

```python
import functools
import math

import jax
import jax.numpy as jnp
from jax import lax
from jax.experimental import pallas as pl
from jax.experimental.pallas import tpu as pltpu
from jax.sharding import PartitionSpec as P

HALO = 8
HALOS = (8, 4)
LANES = 128
TAPS = 27
BLOCKS = 28
BF16 = jnp.bfloat16
F32 = jnp.float32
VMEM = pl.BlockSpec(memory_space=pltpu.VMEM)


def call(kernel, name, outs, args, scratch=(), flops=0):
    arrays = [jax.ShapeDtypeStruct(shape, kind) for shape, kind in outs]
    size = sum(math.prod(item.shape) * item.dtype.itemsize for item in [*arrays, *args, *scratch])
    return pl.pallas_call(
        kernel,
        out_shape=arrays,
        in_specs=[VMEM] * len(args),
        out_specs=[VMEM] * len(arrays),
        scratch_shapes=list(scratch),
        compiler_params=pltpu.CompilerParams(vmem_limit_bytes=size + 6 * 1024 * 1024),
        cost_estimate=pl.CostEstimate(flops=flops, bytes_accessed=1024, transcendentals=0),
        name=name,
    )(*args)


def column_bits():
    column = lax.axis_index("gz")
    return 2 * (column % 2) + column // 2 % 2


def split_terms(values):
    high = values.astype(BF16)
    return high, (values - high.astype(F32)).astype(BF16)


def pack_kernel(weights, biases, own, sent):
    chans = weights.shape[2]
    for tap in range(TAPS):
        own[tap] = jnp.concatenate([weights[0, tap], weights[1, tap]], axis=1)
    own[TAPS] = jnp.zeros((chans, LANES), F32)
    own[TAPS, 0:1, :] = jnp.concatenate([biases[0:1, :], biases[1:2, :]], axis=1)
    half = sent.shape[0]
    start = lax.axis_index("gz") % 2 * half
    for index in range(half):
        sent[index] = own[start + index]


def turned_rows(dims, source, micro, y):
    _, chans, size_x, local_y, _ = dims
    step = size_x * local_y
    first = micro * chans * step + y
    parts = [source[pl.ds(first + x * local_y, chans, stride=step), :] for x in range(size_x)]
    return jnp.concatenate(parts, axis=0).T


def turn_kernel(dims, inflow, cotangent, rows, pair, inner):
    micros, _, _, local_y, local_z = dims
    odd = lax.axis_index("gz") % 2 == 1
    for field, source in enumerate((inflow, cotangent)):
        for micro in range(micros):
            for y in range(local_y):
                turned = turned_rows(dims, source, micro, y)
                rows[field, micro, y] = turned
                low, high = turned[:HALO], turned[local_z - HALO :]
                pair[field, micro, y] = jnp.where(odd, low, high)
                inner[field, micro, y] = jnp.where(odd, high, low)


def cut_kernel(dims, slabs, width, inflow, cotangent, *refs):
    micros, _, _, local_y, local_z = dims
    outs, wide = refs[:-1], refs[-1]
    slab = lax.axis_index("gy")
    for field, (source, halo) in enumerate(zip((inflow, cotangent), HALOS)):
        at = slice(0, width + 2 * halo) if field == 0 else slice(width + 2 * HALO, None)
        for micro in range(micros):
            for y in range(local_y):
                wide[field, micro, y, :HALO] = jnp.zeros((HALO, LANES), F32)
                wide[field, micro, y, HALO + local_z :] = jnp.zeros((HALO, LANES), F32)
                turned = turned_rows(dims, source, micro, y)
                wide[field, micro, y, HALO : HALO + local_z] = turned
                for turn in range(slabs):
                    start = (slab ^ turn) * width + HALO - halo
                    if width % 8 == 0 and halo % 8 == 0:
                        start = pl.multiple_of(start, 8)
                    outs[turn][micro, y, at] = wide[field, micro, y, pl.ds(start, width + 2 * halo)]


def edge_kernel(width, *refs):
    windows, edge = refs[:-1], refs[-1]
    slab = lax.axis_index("gy")
    micros, local_y = windows[0].shape[:2]
    for field, halo in enumerate(HALOS):
        base = halo if field == 0 else width + 2 * HALO + halo
        for turn, window in enumerate(windows):
            owner = slab ^ turn
            for micro in range(micros):
                for y in range(local_y):
                    low = window[micro, y, base : base + HALO]
                    high = window[micro, y, base + width - HALO : base + width]
                    edge[field, micro, owner * local_y + y] = jnp.where(slab == 0, low, high)


def window_kernel(dims, rows, pair, inner, *refs):
    slabs, width, columns = dims
    outs, wide = refs[:-1], refs[-1]
    slab, column = lax.axis_index("gy"), lax.axis_index("gz")
    odd = column % 2 == 1
    _, micros, local_y, local_z, _ = rows.shape
    for field, halo in enumerate(HALOS):
        at = slice(0, width + 2 * halo) if field == 0 else slice(width + 2 * HALO, None)
        for micro in range(micros):
            for y in range(local_y):
                one, two = pair[field, micro, y], inner[field, micro, y]
                before = jnp.where(column > 0, jnp.where(odd, one, two), 0.0)
                after = jnp.where(column < columns - 1, jnp.where(odd, two, one), 0.0)
                wide[field, micro, y, :HALO] = before
                wide[field, micro, y, HALO : HALO + local_z] = rows[field, micro, y]
                wide[field, micro, y, HALO + local_z :] = after
                for turn in range(slabs):
                    start = (slab ^ turn) * width + HALO - halo
                    if width % 8 == 0 and halo % 8 == 0:
                        start = pl.multiple_of(start, 8)
                    outs[turn][micro, y, at] = wide[field, micro, y, pl.ds(start, width + 2 * halo)]


def table_kernel(*refs):
    parts, (fwd, bwd, row) = refs[:-3], refs[-3:]
    odd = lax.axis_index("gz") % 2
    count, chans, _ = parts[0].shape

    def block_of(tap):
        if len(parts) == 1:
            return parts[0][tap]
        index = tap % count
        return jnp.where(odd == tap // count, parts[0][index], parts[1][index])

    for b in range(3):
        for c in range(3):
            taps = [block_of(9 * a + 3 * b + c) for a in range(3)]
            for layer in range(2):
                lanes = slice(layer * chans, (layer + 1) * chans)
                below, level, above = [tap[:, lanes] for tap in taps]
                top = jnp.concatenate([level, above], axis=1)
                low = jnp.concatenate([below, level], axis=1)
                block = jnp.concatenate([top, low], axis=0)
                for target, value, r, at in ((fwd, block.T, b, c), (bwd, block, 2 - b, 2 - c)):
                    hi, lo = split_terms(value)
                    at = slice(at * LANES, (at + 1) * LANES)
                    target[layer, 2 * r * LANES : (2 * r + 1) * LANES, at] = hi
                    target[layer, (2 * r + 1) * LANES : (2 * r + 2) * LANES, at] = hi
                    target[layer, (6 + r) * LANES : (7 + r) * LANES, at] = lo
    last = block_of(TAPS)[0:1, :]
    for layer in range(2):
        part = last[:, layer * chans : (layer + 1) * chans]
        row[layer] = jnp.broadcast_to(jnp.concatenate([part, part], axis=1), (8, LANES))


class Slab:
    def __init__(self, dims):
        self.micros, self.rows_y, self.depth, self.width, self.chunk_y, self.slabs, limit_z = dims
        self.section, self.slab = lax.axis_index("section"), lax.axis_index("gy")
        origin = (lax.axis_index("gz") * self.slabs + self.slab) * self.width - HALO
        self.chunk = self.chunk_y * self.depth
        self.chunks = self.rows_y // self.chunk_y
        self.per_owner = self.rows_y // self.slabs
        zs = lax.broadcasted_iota(jnp.int32, (self.depth, LANES), 0)
        inside = (zs + origin >= 0) & (zs + origin < limit_z)
        self.in_grid = inside.astype(F32)[None]
        self.mine = ((zs >= HALO) & (zs < HALO + self.width)).astype(F32)[None]

    def over_chunks(self, body):
        if self.chunks == 1:
            body(0)
        else:

            def step(part, carry):
                body(pl.multiple_of(part * self.chunk, 16))
                return carry

            lax.fori_loop(0, self.chunks, step, 0)

    def masked(self, values, mask):
        return (values.reshape(-1, self.depth, LANES) * mask).reshape(values.shape)

    def put_rows(self, target, lead, micro, start, values):
        hi, lo = split_terms(values)
        at = pl.ds(start + self.depth, self.chunk)
        target[lead, micro, at, slice(0, LANES)] = hi
        target[lead, micro, at, slice(LANES, 2 * LANES)] = lo

    def pieces_of(self, source, lead, micro, start):
        return [
            source[lead, micro, pl.ds(start + b * self.depth, self.chunk), :] for b in range(3)
        ]

    def conv(self, source, lead, start, table):
        lefts = []
        for micro in range(self.micros):
            pieces = self.pieces_of(source, lead, micro, start)
            lefts.append(jnp.concatenate(pieces + [piece[:, :LANES] for piece in pieces], axis=1))
        results = []
        for left in lefts:
            out = jnp.dot(left, table[...], preferred_element_type=F32)
            before = pltpu.roll(out[:, :LANES], 1, 0)
            after = pltpu.roll(out[:, 2 * LANES :], out.shape[0] - 1, 0)
            results.append(before + out[:, LANES : 2 * LANES] + after)
        return results

    def by_owner(self, layer, own, other, body):
        mine = layer // 2 == self.section
        pl.when(mine)(lambda: body(own, layer % 2))
        pl.when(jnp.logical_not(mine))(lambda: body(other, layer % 2))

    def blank_edges(self, target):
        blank = jnp.zeros((self.depth, 2 * LANES), BF16)
        for lead in range(target.shape[0]):
            for micro in range(self.micros):
                for edge in (0, self.rows_y + 1):
                    target[lead, micro, edge * self.depth : (edge + 1) * self.depth, :] = blank

    def fill(self, field, windows, which, edge):
        halo = HALOS[which]
        span = self.width + 2 * halo
        at = 0 if which == 0 else self.width + 2 * HALO
        extra = [HALO - halo, self.depth - span - (HALO - halo)]
        for micro in range(self.micros):
            for turn, window in enumerate(windows):
                owner = self.slab ^ turn
                for y in range(self.per_owner):
                    blanks = [jnp.zeros((rows, LANES), F32) for rows in extra]
                    parts = [blanks[0], window[micro, y, at : at + span], blanks[1]]
                    parts = [part for part in parts if part.shape[0]]
                    start = pl.multiple_of((owner * self.per_owner + y) * self.depth, 16)
                    value = jnp.concatenate(parts, axis=0) if len(parts) > 1 else parts[0]
                    field[micro, pl.ds(start, self.depth), :] = value
        if edge is None:
            return
        for side, rows, at in (
            (0, slice(HALO - halo, HALO), HALO - halo),
            (self.slabs - 1, slice(0, halo), HALO + self.width),
        ):

            @pl.when(self.slab == side)
            def _():
                for micro in range(self.micros):
                    for y in range(self.rows_y):
                        start = y * self.depth + at
                        field[micro, start : start + halo, :] = edge[which, micro, y, rows]

    def cut_out(self, targets, source):
        for turn, target in enumerate(targets):
            owner = self.slab ^ turn
            for micro in range(self.micros):
                for y in range(self.per_owner):
                    start = (owner * self.per_owner + y) * self.depth + HALO
                    rows = pl.ds(pl.multiple_of(start, 8), self.width)
                    target[micro, y] = source[micro, rows, :]


def forward_kernel(dims, edged, own, own_row, other, other_row, *refs):
    slab = Slab(dims)
    windows, (*edge, acts, kept) = refs[: slab.slabs], refs[slab.slabs : slab.slabs + edged + 2]
    outs, (whole, field) = refs[slab.slabs + edged + 2 : -2], refs[-2:]
    slab.blank_edges(acts)
    slab.fill(field, windows, 0, edge[0] if edged else None)

    def take_in(start):
        for micro in range(slab.micros):
            slab.put_rows(acts, 0, micro, start, field[micro, pl.ds(start, slab.chunk), :])

    slab.over_chunks(take_in)

    def layer_step(layer, carry):
        def run(tables, half):
            table, row = tables

            def body(start):
                at = pl.ds(start, slab.chunk)
                sums = slab.conv(acts, layer, start, table.at[half])
                values = []
                for micro, total in enumerate(sums):
                    pre = total + row[half][0:1, :]
                    sigma = 1.0 / (1.0 + jnp.exp(-pre))
                    kept[layer, micro, at, :] = sigma * (1.0 + pre * (1.0 - sigma))
                    out = slab.masked(pre * sigma, slab.in_grid)
                    slab.put_rows(acts, layer + 1, micro, start, out)
                    values.append(out)

                @pl.when(layer == 2 * slab.section + 1)
                def _():
                    for micro, value in enumerate(values):
                        whole[micro, at, :] = value

            slab.over_chunks(body)

        slab.by_owner(layer, (own, own_row), (other, other_row), run)
        return carry

    lax.fori_loop(0, 4, layer_step, 0)
    slab.cut_out(outs, whole)


def backward_kernel(dims, edged, scale, own, other, acts, kept, *refs):
    slab = Slab(dims)
    windows, refs = refs[: slab.slabs], refs[slab.slabs :]
    edge, refs = refs[:edged], refs[edged:]
    outs, (sums, rim, slopes, field, acc) = refs[: slab.slabs], refs[slab.slabs :]
    slab.blank_edges(rim)
    slab.fill(field, windows, 1, edge[0] if edged else None)

    def take_gradient(layer, micro, start, gradient):
        at = pl.ds(start, slab.chunk)
        slope = slab.masked(gradient * kept[layer, micro, at, :], slab.in_grid)
        slopes[layer, micro, at, :] = slab.masked(slope, slab.mine)
        slab.put_rows(rim, layer % 2, micro, start, slope)

    def take_cotangent(start):
        for micro in range(slab.micros):
            take_gradient(3, micro, start, field[micro, pl.ds(start, slab.chunk), :])

    slab.over_chunks(take_cotangent)

    def layer_step(index, carry):
        layer = 3 - index

        def run(table, half):
            def body(start):
                gradients = slab.conv(rim, layer % 2, start, table.at[half])
                last = layer == 2 * slab.section

                @pl.when(last)
                def _():
                    for micro, gradient in enumerate(gradients):
                        field[micro, pl.ds(start, slab.chunk), :] = gradient

                @pl.when(jnp.logical_not(last))
                def _():
                    for micro, gradient in enumerate(gradients):
                        take_gradient(layer - 1, micro, start, gradient)

            slab.over_chunks(body)

        slab.by_owner(layer, own, other, run)
        return carry

    lax.fori_loop(0, jnp.where(slab.section == 0, 4, 2), layer_step, 0)
    slab.cut_out(outs, field)

    quarter = BLOCKS // 4
    chans = LANES // 2
    swap = column_bits()

    def spot(tap):
        return (tap // quarter ^ swap) * quarter + tap % quarter

    def products(layer, start):
        at = pl.ds(start, slab.chunk)
        slope = jnp.concatenate([slopes[layer, micro, at, :] for micro in range(slab.micros)])
        moved = [pltpu.roll(slope, slope.shape[0] - 1, 0), slope, pltpu.roll(slope, 1, 0)]
        terms = [split_terms(value) for value in moved]
        left_hi = jnp.concatenate([hi for hi, lo in terms], axis=1)
        left_lo = jnp.concatenate([lo for hi, lo in terms], axis=1)
        pieces = [slab.pieces_of(acts, layer, micro, start) for micro in range(slab.micros)]
        pieces = [jnp.concatenate(parts, axis=0) for parts in zip(*pieces)]
        full = jnp.concatenate(pieces, axis=1)
        high = jnp.concatenate([piece[:, :LANES] for piece in pieces], axis=1)
        over_rows = (((0,), (0,)), ((), ()))
        one = lax.dot_general(left_hi, full, over_rows, preferred_element_type=F32)
        two = lax.dot_general(left_lo, high, over_rows, preferred_element_type=F32)
        total = []
        for b in range(3):
            hi = one[:, 2 * b * LANES : (2 * b + 1) * LANES]
            lo = one[:, (2 * b + 1) * LANES : (2 * b + 2) * LANES]
            total.append(hi + lo + two[:, b * LANES : (b + 1) * LANES])
        return total, jnp.sum(slope, axis=0, keepdims=True)

    sums[spot(TAPS)] = jnp.zeros((chans, LANES), F32)
    for slot in range(2):
        layer = 2 * slab.section + slot
        if slab.chunks == 1:
            total, row = products(layer, 0)
        else:
            acc[...] = jnp.zeros(acc.shape, F32)

            def gather(start):
                total, row = products(layer, start)
                for b in range(3):
                    acc[0 : 3 * LANES, b * LANES : (b + 1) * LANES] += total[b]
                acc[3 * LANES : 3 * LANES + 1, 0:LANES] += row

            slab.over_chunks(gather)
            total = [acc[0 : 3 * LANES, b * LANES : (b + 1) * LANES] for b in range(3)]
            row = acc[3 * LANES : 3 * LANES + 1, 0:LANES]
        lanes = slice(slot * chans, (slot + 1) * chans)
        for b in range(3):
            for c in range(3):
                block = total[b][c * LANES : (c + 1) * LANES] * scale
                tap = 3 * b + c
                sums[spot(tap), :, lanes] = block[chans:, :chans]
                sums[spot(9 + tap), :, lanes] = block[:chans, :chans] + block[chans:, chans:]
                sums[spot(18 + tap), :, lanes] = block[:chans, chans:]
        row = row * scale
        sums[spot(TAPS), 0:1, lanes] = row[:, :chans] + row[:, chans:]


def unpack_kernel(near, core, weight, bias, whole):
    part = near.shape[0] // 4
    chans = weight.shape[-1]
    odd, swap = lax.axis_index("gy") % 2, column_bits()
    for index in range(8):
        source = near if index < 4 else core
        first = index % 4 * part
        at = ((index // 2 ^ swap) * 2 + (index % 2 ^ odd)) * part
        whole[pl.ds(pl.multiple_of(at, 8), part), :] = source[first : first + part, :]
    for layer in range(2):
        lanes = slice(layer * chans, (layer + 1) * chans)
        for tap in range(TAPS):
            weight[layer, tap] = whole[tap * chans : (tap + 1) * chans, lanes]
        bias[layer : layer + 1, :] = whole[TAPS * chans : TAPS * chans + 1, lanes]


def restore_kernel(dims, *refs):
    micros, chans, size_x, local_y, width = dims
    pieces, (*targets, whole) = refs[:-3], refs[-3:]
    slab = lax.axis_index("gy")
    step = size_x * local_y
    slabs = len(pieces) // 2
    for slot, target in enumerate(targets):
        for micro in range(micros):
            for y in range(local_y):
                for turn in range(slabs):
                    start = (slab ^ turn) * width
                    if width % 8 == 0:
                        start = pl.multiple_of(start, 8)
                    rows = pl.ds(start, width)
                    whole[slot, micro, y, rows, :] = pieces[slot * slabs + turn][micro, y]
                block = whole[slot, micro, y].T
                for x in range(size_x):
                    first = micro * chans * step + x * local_y + y
                    part = block[x * chans : (x + 1) * chans]
                    target[pl.ds(first, chans, stride=step), :] = part


def spread(blocks):
    slabs = len(blocks)
    if slabs <= 8:
        got = [blocks[0]]
        for turn in range(1, slabs):
            route = [(i, i ^ turn) for i in range(slabs)]
            got.append(lax.ppermute(blocks[turn], "gy", route))
        return got
    order = jnp.arange(slabs) ^ lax.axis_index("gy")
    got = lax.all_to_all(jnp.stack(blocks)[order], "gy", 0, 0)[order]
    return [got[turn] for turn in range(slabs)]


def swapped(block, bit, axis="gz"):
    return lax.ppermute(block, axis, [(i, i ^ bit) for i in range(lax.axis_size(axis))])


def around(above, beside, across):
    slabs, columns = lax.axis_size("gy"), lax.axis_size("gz")
    route = [
        (i * columns + g, (i ^ 1) * columns + (g ^ 2)) for i in range(slabs) for g in range(columns)
    ]
    beside = swapped(beside, 2)
    across = lax.ppermute(across, ("gy", "gz"), route)
    return [swapped(above, 1, "gy"), beside, across]


def per_device(inflow, weights, biases, cotangent):
    micros, chans, size_x, local_y, local_z = inflow.shape
    slabs, columns = lax.axis_size("gy"), lax.axis_size("gz")
    rows_y = local_y * slabs
    width = local_z // slabs
    span = width + 2 * HALO
    depth = -(-span // 16) * 16
    chunk_y = max(n for n in range(1, rows_y + 1) if rows_y % n == 0 and n * depth <= 384)
    scale = 1.0 / math.sqrt(micros * size_x * rows_y * local_z * columns)
    rows = micros * chans * size_x * local_y
    blocks = [inflow.reshape(rows, local_z), cotangent.reshape(rows, local_z)]
    packs = [((BLOCKS, chans, LANES), F32), ((BLOCKS // 2, chans, LANES), F32)]
    own, sent = call(pack_kernel, "pack", packs, [weights, biases])
    near_half = lax.ppermute(sent, "section", [(0, 1), (1, 0)])
    reach = sum(width + 2 * halo for halo in HALOS)
    cuts = [((micros, local_y, reach, LANES), F32)] * slabs
    wide = pltpu.VMEM((2, micros, local_y, local_z + 2 * HALO, LANES), F32)
    edged = width >= HALO and slabs > 1
    if edged:
        kernel = functools.partial(cut_kernel, inflow.shape, slabs, width)
        windows = call(kernel, "cut", cuts, blocks, [wide])
    else:
        ends = ((2, micros, local_y, HALO, LANES), F32)
        kernel = functools.partial(turn_kernel, inflow.shape)
        whole = ((2, micros, local_y, local_z, LANES), F32)
        fields, pair, inner = call(kernel, "turn", [whole, ends, ends], blocks)
        pair = swapped(pair, 1)
        route = [(i, i + 1) for i in range(1, columns - 1, 2)]
        inner = lax.ppermute(inner, "gz", route + [(after, before) for before, after in route])
        kernel = functools.partial(window_kernel, (slabs, width, columns))
        windows = call(kernel, "windows", cuts, [fields, pair, inner], [wide])
    windows = spread(windows)

    tables = [((2, 9 * LANES, 3 * LANES), BF16)] * 2 + [((2, 8, LANES), F32)]
    own_fwd, own_bwd, own_row = call(table_kernel, "own_table", tables, [own])
    near_half, windows, own_row = lax.optimization_barrier((near_half, windows, own_row))
    edges = []
    if edged:
        edge = ((2, micros, rows_y, HALO, LANES), F32)
        edges = call(functools.partial(edge_kernel, width), "edge", [edge], windows)
        last = (slabs - 1) * columns
        route = [(g, last + g - 1) for g in range(1, columns)]
        route += [(after, before) for before, after in route]
        edges = [lax.ppermute(edges[0], ("gy", "gz"), route)]
    far_half = swapped(near_half, 1)
    far_fwd, far_bwd, far_row = call(table_kernel, "far_table", tables, [near_half, far_half])

    dims = (micros, rows_y, depth, width, chunk_y, slabs, local_z * columns)
    padded = (rows_y + 2) * depth
    full = rows_y * depth
    piece = ((micros, local_y, width, LANES), F32)
    acts, kept, *fronts = call(
        functools.partial(forward_kernel, dims, edged),
        "forward",
        [((5, micros, padded, 2 * LANES), BF16), ((4, micros, full, LANES), F32)] + [piece] * slabs,
        [own_fwd, own_row, far_fwd, far_row, *windows, *edges],
        [pltpu.VMEM((micros, full, LANES), F32)] * 2,
    )
    if slabs == 4:
        passed = swapped(jnp.stack(fronts[2:]), 2, "gy")
    *backs, sums = call(
        functools.partial(backward_kernel, dims, edged, scale),
        "backward",
        [piece] * slabs + [((BLOCKS, chans, LANES), F32)],
        [own_bwd, far_bwd, acts, kept, *windows, *edges],
        [
            pltpu.VMEM((2, micros, padded, 2 * LANES), BF16),
            pltpu.VMEM((4, micros, full, LANES), F32),
            pltpu.VMEM((micros, full, LANES), F32),
            pltpu.VMEM((3 * LANES + 8, 3 * LANES), F32),
        ],
        12 * micros * full * 9 * LANES * 3 * LANES,
    )
    if slabs == 4:
        sums, passed = lax.optimization_barrier((sums, passed))

    block = sums.reshape(BLOCKS * chans, LANES)
    half = block.shape[0] // 2
    block = block[:half] + swapped(block[half:], 1)
    block, fronts, backs = lax.optimization_barrier((block, fronts, backs))
    if slabs == 4:
        near = swapped(jnp.stack([fronts[1], passed[1], backs[1]]), 1, "gy")
        outs = [near, swapped(backs[2], 2, "gy"), swapped(backs[3], 3, "gy")]
    else:
        outs = spread([jnp.stack(pair) for pair in zip(fronts, backs)])
    part = half // 4
    odd = lax.axis_index("gy") % 2 == 1
    lows, highs = [block[i * part : (i + 1) * part] for i in (0, 2)], [
        block[i * part : (i + 1) * part] for i in (1, 3)
    ]
    mine, beside = [jnp.where(odd, high, low) for low, high in zip(lows, highs)]
    above, across = [jnp.where(odd, low, high) for low, high in zip(lows, highs)]
    kept = mine + sum(around(above, beside, across))
    kept, outs = lax.optimization_barrier((kept, outs))
    bit = 2
    while bit < slabs:
        kept = kept + swapped(kept, bit, "gy")
        bit *= 2
    if slabs == 4:
        outs = [fronts[0], outs[0][0], passed[0], outs[0][1], backs[0], outs[0][2], *outs[1:]]
    else:
        outs = [out[slot] for slot in range(2) for out in outs]
    near = jnp.concatenate([kept, *around(kept, kept, kept)], axis=0)
    core = swapped(near, 1)
    section_out, section_grad = call(
        functools.partial(restore_kernel, (micros, chans, size_x, local_y, width)),
        "restore",
        [((rows, local_z), F32)] * 2,
        outs,
        [pltpu.VMEM((2, micros, local_y, local_z, LANES), F32)],
    )
    weight_total, bias_total = call(
        unpack_kernel,
        "unpack",
        [((2, TAPS, chans, chans), F32), ((2, chans), F32)],
        [near, core],
        [pltpu.VMEM((BLOCKS * chans, LANES), F32)],
    )
    shape = (1, *inflow.shape)
    return (section_out.reshape(shape), section_grad.reshape(shape), weight_total, bias_total)


def solution(mesh):
    grid = P(None, None, None, "gy", "gz")
    section_grid = P("section", None, None, None, "gy", "gz")
    return jax.shard_map(
        per_device,
        mesh=mesh,
        in_specs=(grid, P("section", None, None, None), P("section", None), grid),
        out_specs=(section_grid, section_grid, P("section", None, None, None), P("section", None)),
        check_vma=False,
    )
```

```python
import functools
import math

import jax
import jax.numpy as jnp
from jax import lax
from jax.experimental import pallas as pl
from jax.experimental.pallas import tpu as pltpu
from jax.sharding import PartitionSpec as P

HALO = 8
HALOS = (8, 4)
LANES = 128
TAPS = 27
BLOCKS = 28
BF16 = jnp.bfloat16
F32 = jnp.float32
VMEM = pl.BlockSpec(memory_space=pltpu.VMEM)


def call(kernel, name, outs, args, scratch=(), flops=0):
    arrays = [jax.ShapeDtypeStruct(shape, kind) for shape, kind in outs]
    size = sum(math.prod(item.shape) * item.dtype.itemsize for item in [*arrays, *args, *scratch])
    return pl.pallas_call(
        kernel,
        out_shape=arrays,
        in_specs=[VMEM] * len(args),
        out_specs=[VMEM] * len(arrays),
        scratch_shapes=list(scratch),
        compiler_params=pltpu.CompilerParams(vmem_limit_bytes=size + 6 * 1024 * 1024),
        cost_estimate=pl.CostEstimate(flops=flops, bytes_accessed=1024, transcendentals=0),
        name=name,
    )(*args)


def column_bits():
    column = lax.axis_index("gz")
    return 2 * (column % 2) + column // 2 % 2


def split_terms(values):
    high = values.astype(BF16)
    return high, (values - high.astype(F32)).astype(BF16)


def pack_kernel(weights, biases, own, sent):
    chans = weights.shape[2]
    for tap in range(TAPS):
        own[tap] = jnp.concatenate([weights[0, tap], weights[1, tap]], axis=1)
    own[TAPS] = jnp.zeros((chans, LANES), F32)
    own[TAPS, 0:1, :] = jnp.concatenate([biases[0:1, :], biases[1:2, :]], axis=1)
    half = sent.shape[0]
    start = lax.axis_index("gz") % 2 * half
    for index in range(half):
        sent[index] = own[start + index]


def turned_rows(dims, source, micro, y):
    _, chans, size_x, local_y, _ = dims
    step = size_x * local_y
    first = micro * chans * step + y
    parts = [source[pl.ds(first + x * local_y, chans, stride=step), :] for x in range(size_x)]
    return jnp.concatenate(parts, axis=0).T


def turn_kernel(dims, inflow, cotangent, rows, pair, inner):
    micros, _, _, local_y, local_z = dims
    odd = lax.axis_index("gz") % 2 == 1
    for field, source in enumerate((inflow, cotangent)):
        for micro in range(micros):
            for y in range(local_y):
                turned = turned_rows(dims, source, micro, y)
                rows[field, micro, y] = turned
                low, high = turned[:HALO], turned[local_z - HALO :]
                pair[field, micro, y] = jnp.where(odd, low, high)
                inner[field, micro, y] = jnp.where(odd, high, low)


def window_kernel(dims, rows, pair, inner, *refs):
    slabs, width, columns = dims
    outs, wide = refs[:-1], refs[-1]
    slab, column = lax.axis_index("gy"), lax.axis_index("gz")
    odd = column % 2 == 1
    _, micros, local_y, local_z, _ = rows.shape
    for field, halo in enumerate(HALOS):
        at = slice(0, width + 2 * halo) if field == 0 else slice(width + 2 * HALO, None)
        for micro in range(micros):
            for y in range(local_y):
                one, two = pair[field, micro, y], inner[field, micro, y]
                before = jnp.where(column > 0, jnp.where(odd, one, two), 0.0)
                after = jnp.where(column < columns - 1, jnp.where(odd, two, one), 0.0)
                wide[field, micro, y, :HALO] = before
                wide[field, micro, y, HALO : HALO + local_z] = rows[field, micro, y]
                wide[field, micro, y, HALO + local_z :] = after
                for turn in range(slabs):
                    start = (slab ^ turn) * width + HALO - halo
                    if width % 8 == 0 and halo % 8 == 0:
                        start = pl.multiple_of(start, 8)
                    outs[turn][micro, y, at] = wide[field, micro, y, pl.ds(start, width + 2 * halo)]


def table_kernel(*refs):
    parts, (fwd, bwd, row) = refs[:-3], refs[-3:]
    odd = lax.axis_index("gz") % 2
    count, chans, _ = parts[0].shape

    def block_of(tap):
        if len(parts) == 1:
            return parts[0][tap]
        index = tap % count
        return jnp.where(odd == tap // count, parts[0][index], parts[1][index])

    for b in range(3):
        for c in range(3):
            taps = [block_of(9 * a + 3 * b + c) for a in range(3)]
            for layer in range(2):
                lanes = slice(layer * chans, (layer + 1) * chans)
                below, level, above = [tap[:, lanes] for tap in taps]
                top = jnp.concatenate([level, above], axis=1)
                low = jnp.concatenate([below, level], axis=1)
                block = jnp.concatenate([top, low], axis=0)
                for target, value, r, at in ((fwd, block.T, b, c), (bwd, block, 2 - b, 2 - c)):
                    hi, lo = split_terms(value)
                    at = slice(at * LANES, (at + 1) * LANES)
                    target[layer, 2 * r * LANES : (2 * r + 1) * LANES, at] = hi
                    target[layer, (2 * r + 1) * LANES : (2 * r + 2) * LANES, at] = hi
                    target[layer, (6 + r) * LANES : (7 + r) * LANES, at] = lo
    last = block_of(TAPS)[0:1, :]
    for layer in range(2):
        part = last[:, layer * chans : (layer + 1) * chans]
        row[layer] = jnp.broadcast_to(jnp.concatenate([part, part], axis=1), (8, LANES))


class Slab:
    def __init__(self, dims):
        self.micros, self.rows_y, self.depth, self.width, self.chunk_y, self.slabs, limit_z = dims
        self.section, self.slab = lax.axis_index("section"), lax.axis_index("gy")
        origin = (lax.axis_index("gz") * self.slabs + self.slab) * self.width - HALO
        self.chunk = self.chunk_y * self.depth
        self.chunks = self.rows_y // self.chunk_y
        self.per_owner = self.rows_y // self.slabs
        zs = lax.broadcasted_iota(jnp.int32, (self.depth, LANES), 0)
        inside = (zs + origin >= 0) & (zs + origin < limit_z)
        self.in_grid = inside.astype(F32)[None]
        self.mine = ((zs >= HALO) & (zs < HALO + self.width)).astype(F32)[None]

    def over_chunks(self, body):
        if self.chunks == 1:
            body(0)
        else:

            def step(part, carry):
                body(pl.multiple_of(part * self.chunk, 16))
                return carry

            lax.fori_loop(0, self.chunks, step, 0)

    def masked(self, values, mask):
        return (values.reshape(-1, self.depth, LANES) * mask).reshape(values.shape)

    def put_rows(self, target, lead, micro, start, values):
        hi, lo = split_terms(values)
        at = pl.ds(start + self.depth, self.chunk)
        target[lead, micro, at, slice(0, LANES)] = hi
        target[lead, micro, at, slice(LANES, 2 * LANES)] = lo

    def pieces_of(self, source, lead, micro, start):
        return [
            source[lead, micro, pl.ds(start + b * self.depth, self.chunk), :] for b in range(3)
        ]

    def conv(self, source, lead, start, table):
        lefts = []
        for micro in range(self.micros):
            pieces = self.pieces_of(source, lead, micro, start)
            lefts.append(jnp.concatenate(pieces + [piece[:, :LANES] for piece in pieces], axis=1))
        results = []
        for left in lefts:
            out = jnp.dot(left, table[...], preferred_element_type=F32)
            before = pltpu.roll(out[:, :LANES], 1, 0)
            after = pltpu.roll(out[:, 2 * LANES :], out.shape[0] - 1, 0)
            results.append(before + out[:, LANES : 2 * LANES] + after)
        return results

    def by_owner(self, layer, own, other, body):
        mine = layer // 2 == self.section
        pl.when(mine)(lambda: body(own, layer % 2))
        pl.when(jnp.logical_not(mine))(lambda: body(other, layer % 2))

    def blank_edges(self, target):
        blank = jnp.zeros((self.depth, 2 * LANES), BF16)
        for lead in range(target.shape[0]):
            for micro in range(self.micros):
                for edge in (0, self.rows_y + 1):
                    target[lead, micro, edge * self.depth : (edge + 1) * self.depth, :] = blank

    def fill(self, field, windows, which):
        halo = HALOS[which]
        span = self.width + 2 * halo
        at = 0 if which == 0 else self.width + 2 * HALO
        extra = [HALO - halo, self.depth - span - (HALO - halo)]
        for micro in range(self.micros):
            for turn, window in enumerate(windows):
                owner = self.slab ^ turn
                for y in range(self.per_owner):
                    blanks = [jnp.zeros((rows, LANES), F32) for rows in extra]
                    parts = [blanks[0], window[micro, y, at : at + span], blanks[1]]
                    parts = [part for part in parts if part.shape[0]]
                    start = pl.multiple_of((owner * self.per_owner + y) * self.depth, 16)
                    value = jnp.concatenate(parts, axis=0) if len(parts) > 1 else parts[0]
                    field[micro, pl.ds(start, self.depth), :] = value

    def cut_out(self, targets, source):
        for turn, target in enumerate(targets):
            owner = self.slab ^ turn
            for micro in range(self.micros):
                for y in range(self.per_owner):
                    start = (owner * self.per_owner + y) * self.depth + HALO
                    rows = pl.ds(pl.multiple_of(start, 8), self.width)
                    target[micro, y] = source[micro, rows, :]


def forward_kernel(dims, own, own_row, other, other_row, *refs):
    slab = Slab(dims)
    windows, (acts, kept) = refs[: slab.slabs], refs[slab.slabs : slab.slabs + 2]
    outs, (whole, field) = refs[slab.slabs + 2 : -2], refs[-2:]
    slab.blank_edges(acts)
    slab.fill(field, windows, 0)

    def take_in(start):
        for micro in range(slab.micros):
            slab.put_rows(acts, 0, micro, start, field[micro, pl.ds(start, slab.chunk), :])

    slab.over_chunks(take_in)

    def layer_step(layer, carry):
        def run(tables, half):
            table, row = tables

            def body(start):
                at = pl.ds(start, slab.chunk)
                sums = slab.conv(acts, layer, start, table.at[half])
                values = []
                for micro, total in enumerate(sums):
                    pre = total + row[half][0:1, :]
                    sigma = 1.0 / (1.0 + jnp.exp(-pre))
                    kept[layer, micro, at, :] = sigma * (1.0 + pre * (1.0 - sigma))
                    out = slab.masked(pre * sigma, slab.in_grid)
                    slab.put_rows(acts, layer + 1, micro, start, out)
                    values.append(out)

                @pl.when(layer == 2 * slab.section + 1)
                def _():
                    for micro, value in enumerate(values):
                        whole[micro, at, :] = value

            slab.over_chunks(body)

        slab.by_owner(layer, (own, own_row), (other, other_row), run)
        return carry

    lax.fori_loop(0, 4, layer_step, 0)
    slab.cut_out(outs, whole)


def backward_kernel(dims, scale, own, other, acts, kept, *refs):
    slab = Slab(dims)
    windows, refs = refs[: slab.slabs], refs[slab.slabs :]
    outs, (sums, rim, slopes, field, acc) = refs[: slab.slabs], refs[slab.slabs :]
    slab.blank_edges(rim)
    slab.fill(field, windows, 1)

    def take_gradient(layer, micro, start, gradient):
        at = pl.ds(start, slab.chunk)
        slope = slab.masked(gradient * kept[layer, micro, at, :], slab.in_grid)
        slopes[layer, micro, at, :] = slab.masked(slope, slab.mine)
        slab.put_rows(rim, layer % 2, micro, start, slope)

    def take_cotangent(start):
        for micro in range(slab.micros):
            take_gradient(3, micro, start, field[micro, pl.ds(start, slab.chunk), :])

    slab.over_chunks(take_cotangent)

    def layer_step(index, carry):
        layer = 3 - index

        def run(table, half):
            def body(start):
                gradients = slab.conv(rim, layer % 2, start, table.at[half])
                last = layer == 2 * slab.section

                @pl.when(last)
                def _():
                    for micro, gradient in enumerate(gradients):
                        field[micro, pl.ds(start, slab.chunk), :] = gradient

                @pl.when(jnp.logical_not(last))
                def _():
                    for micro, gradient in enumerate(gradients):
                        take_gradient(layer - 1, micro, start, gradient)

            slab.over_chunks(body)

        slab.by_owner(layer, own, other, run)
        return carry

    lax.fori_loop(0, jnp.where(slab.section == 0, 4, 2), layer_step, 0)
    slab.cut_out(outs, field)

    quarter = BLOCKS // 4
    chans = LANES // 2
    swap = column_bits()

    def spot(tap):
        return (tap // quarter ^ swap) * quarter + tap % quarter

    def products(layer, start):
        at = pl.ds(start, slab.chunk)
        slope = jnp.concatenate([slopes[layer, micro, at, :] for micro in range(slab.micros)])
        moved = [pltpu.roll(slope, slope.shape[0] - 1, 0), slope, pltpu.roll(slope, 1, 0)]
        terms = [split_terms(value) for value in moved]
        left_hi = jnp.concatenate([hi for hi, lo in terms], axis=1)
        left_lo = jnp.concatenate([lo for hi, lo in terms], axis=1)
        pieces = [slab.pieces_of(acts, layer, micro, start) for micro in range(slab.micros)]
        pieces = [jnp.concatenate(parts, axis=0) for parts in zip(*pieces)]
        full = jnp.concatenate(pieces, axis=1)
        high = jnp.concatenate([piece[:, :LANES] for piece in pieces], axis=1)
        over_rows = (((0,), (0,)), ((), ()))
        one = lax.dot_general(left_hi, full, over_rows, preferred_element_type=F32)
        two = lax.dot_general(left_lo, high, over_rows, preferred_element_type=F32)
        total = []
        for b in range(3):
            hi = one[:, 2 * b * LANES : (2 * b + 1) * LANES]
            lo = one[:, (2 * b + 1) * LANES : (2 * b + 2) * LANES]
            total.append(hi + lo + two[:, b * LANES : (b + 1) * LANES])
        return total, jnp.sum(slope, axis=0, keepdims=True)

    sums[spot(TAPS)] = jnp.zeros((chans, LANES), F32)
    for slot in range(2):
        layer = 2 * slab.section + slot
        if slab.chunks == 1:
            total, row = products(layer, 0)
        else:
            acc[...] = jnp.zeros(acc.shape, F32)

            def gather(start):
                total, row = products(layer, start)
                for b in range(3):
                    acc[0 : 3 * LANES, b * LANES : (b + 1) * LANES] += total[b]
                acc[3 * LANES : 3 * LANES + 1, 0:LANES] += row

            slab.over_chunks(gather)
            total = [acc[0 : 3 * LANES, b * LANES : (b + 1) * LANES] for b in range(3)]
            row = acc[3 * LANES : 3 * LANES + 1, 0:LANES]
        lanes = slice(slot * chans, (slot + 1) * chans)
        for b in range(3):
            for c in range(3):
                block = total[b][c * LANES : (c + 1) * LANES] * scale
                tap = 3 * b + c
                sums[spot(tap), :, lanes] = block[chans:, :chans]
                sums[spot(9 + tap), :, lanes] = block[:chans, :chans] + block[chans:, chans:]
                sums[spot(18 + tap), :, lanes] = block[:chans, chans:]
        row = row * scale
        sums[spot(TAPS), 0:1, lanes] = row[:, :chans] + row[:, chans:]


def unpack_kernel(near, core, weight, bias, whole):
    part = near.shape[0] // 4
    chans = weight.shape[-1]
    odd, swap = lax.axis_index("gy") % 2, column_bits()
    for index in range(8):
        source = near if index < 4 else core
        first = index % 4 * part
        at = ((index // 2 ^ swap) * 2 + (index % 2 ^ odd)) * part
        whole[pl.ds(pl.multiple_of(at, 8), part), :] = source[first : first + part, :]
    for layer in range(2):
        lanes = slice(layer * chans, (layer + 1) * chans)
        for tap in range(TAPS):
            weight[layer, tap] = whole[tap * chans : (tap + 1) * chans, lanes]
        bias[layer : layer + 1, :] = whole[TAPS * chans : TAPS * chans + 1, lanes]


def restore_kernel(dims, *refs):
    micros, chans, size_x, local_y, width = dims
    pieces, (*targets, whole) = refs[:-3], refs[-3:]
    slab = lax.axis_index("gy")
    step = size_x * local_y
    slabs = len(pieces) // 2
    for slot, target in enumerate(targets):
        for micro in range(micros):
            for y in range(local_y):
                for turn in range(slabs):
                    start = (slab ^ turn) * width
                    if width % 8 == 0:
                        start = pl.multiple_of(start, 8)
                    rows = pl.ds(start, width)
                    whole[slot, micro, y, rows, :] = pieces[slot * slabs + turn][micro, y]
                block = whole[slot, micro, y].T
                for x in range(size_x):
                    first = micro * chans * step + x * local_y + y
                    part = block[x * chans : (x + 1) * chans]
                    target[pl.ds(first, chans, stride=step), :] = part


def spread(blocks):
    slabs = len(blocks)
    if slabs <= 8:
        got = [blocks[0]]
        for turn in range(1, slabs):
            route = [(i, i ^ turn) for i in range(slabs)]
            got.append(lax.ppermute(blocks[turn], "gy", route))
        return got
    order = jnp.arange(slabs) ^ lax.axis_index("gy")
    got = lax.all_to_all(jnp.stack(blocks)[order], "gy", 0, 0)[order]
    return [got[turn] for turn in range(slabs)]


def swapped(block, bit, axis="gz"):
    return lax.ppermute(block, axis, [(i, i ^ bit) for i in range(lax.axis_size(axis))])


def around(above, beside, across):
    slabs, columns = lax.axis_size("gy"), lax.axis_size("gz")
    route = [
        (i * columns + g, (i ^ 1) * columns + (g ^ 2)) for i in range(slabs) for g in range(columns)
    ]
    beside = swapped(beside, 2)
    across = lax.ppermute(across, ("gy", "gz"), route)
    return [swapped(above, 1, "gy"), beside, across]


def per_device(inflow, weights, biases, cotangent):
    micros, chans, size_x, local_y, local_z = inflow.shape
    slabs, columns = lax.axis_size("gy"), lax.axis_size("gz")
    rows_y = local_y * slabs
    width = local_z // slabs
    span = width + 2 * HALO
    depth = -(-span // 16) * 16
    chunk_y = max(n for n in range(1, rows_y + 1) if rows_y % n == 0 and n * depth <= 384)
    scale = 1.0 / math.sqrt(micros * size_x * rows_y * local_z * columns)
    rows = micros * chans * size_x * local_y
    blocks = [inflow.reshape(rows, local_z), cotangent.reshape(rows, local_z)]
    ends = ((2, micros, local_y, HALO, LANES), F32)
    fields, pair, inner = call(
        functools.partial(turn_kernel, inflow.shape),
        "turn",
        [((2, micros, local_y, local_z, LANES), F32), ends, ends],
        blocks,
    )
    packs = [((BLOCKS, chans, LANES), F32), ((BLOCKS // 2, chans, LANES), F32)]
    own, sent = call(pack_kernel, "pack", packs, [weights, biases])
    pair = swapped(pair, 1)
    route = [(i, i + 1) for i in range(1, columns - 1, 2)]
    inner = lax.ppermute(inner, "gz", route + [(after, before) for before, after in route])
    windows = call(
        functools.partial(window_kernel, (slabs, width, columns)),
        "windows",
        [((micros, local_y, sum(width + 2 * halo for halo in HALOS), LANES), F32)] * slabs,
        [fields, pair, inner],
        [pltpu.VMEM((2, micros, local_y, local_z + 2 * HALO, LANES), F32)],
    )
    sent, windows = lax.optimization_barrier((sent, windows))
    near_half = lax.ppermute(sent, "section", [(0, 1), (1, 0)])
    windows = spread(windows)

    tables = [((2, 9 * LANES, 3 * LANES), BF16)] * 2 + [((2, 8, LANES), F32)]
    own_fwd, own_bwd, own_row = call(table_kernel, "own_table", tables, [own])
    near_half, windows, own_row = lax.optimization_barrier((near_half, windows, own_row))
    far_half = swapped(near_half, 1)
    far_fwd, far_bwd, far_row = call(table_kernel, "far_table", tables, [near_half, far_half])

    dims = (micros, rows_y, depth, width, chunk_y, slabs, local_z * columns)
    padded = (rows_y + 2) * depth
    full = rows_y * depth
    piece = ((micros, local_y, width, LANES), F32)
    acts, kept, *fronts = call(
        functools.partial(forward_kernel, dims),
        "forward",
        [((5, micros, padded, 2 * LANES), BF16), ((4, micros, full, LANES), F32)] + [piece] * slabs,
        [own_fwd, own_row, far_fwd, far_row, *windows],
        [pltpu.VMEM((micros, full, LANES), F32)] * 2,
    )
    if slabs == 4:
        passed = swapped(jnp.stack(fronts[2:]), 2, "gy")
    *backs, sums = call(
        functools.partial(backward_kernel, dims, scale),
        "backward",
        [piece] * slabs + [((BLOCKS, chans, LANES), F32)],
        [own_bwd, far_bwd, acts, kept, *windows],
        [
            pltpu.VMEM((2, micros, padded, 2 * LANES), BF16),
            pltpu.VMEM((4, micros, full, LANES), F32),
            pltpu.VMEM((micros, full, LANES), F32),
            pltpu.VMEM((3 * LANES + 8, 3 * LANES), F32),
        ],
        12 * micros * full * 9 * LANES * 3 * LANES,
    )
    if slabs == 4:
        sums, passed = lax.optimization_barrier((sums, passed))

    block = sums.reshape(BLOCKS * chans, LANES)
    half = block.shape[0] // 2
    block = block[:half] + swapped(block[half:], 1)
    block, fronts, backs = lax.optimization_barrier((block, fronts, backs))
    if slabs == 4:
        near = swapped(jnp.stack([fronts[1], passed[1], backs[1]]), 1, "gy")
        outs = [near, swapped(backs[2], 2, "gy"), swapped(backs[3], 3, "gy")]
    else:
        outs = spread([jnp.stack(pair) for pair in zip(fronts, backs)])
    part = half // 4
    block = block[: 2 * part] + swapped(block[2 * part :], 2)
    block, outs = lax.optimization_barrier((block, outs))
    odd = lax.axis_index("gy") % 2 == 1
    kept = jnp.where(odd, block[part:], block[:part])
    kept = kept + swapped(jnp.where(odd, block[:part], block[part:]), 1, "gy")
    bit = 2
    while bit < slabs:
        kept = kept + swapped(kept, bit, "gy")
        bit *= 2
    if slabs == 4:
        outs = [fronts[0], outs[0][0], passed[0], outs[0][1], backs[0], outs[0][2], *outs[1:]]
    else:
        outs = [out[slot] for slot in range(2) for out in outs]
    near = jnp.concatenate([kept, *around(kept, kept, kept)], axis=0)
    core = swapped(near, 1)
    section_out, section_grad = call(
        functools.partial(restore_kernel, (micros, chans, size_x, local_y, width)),
        "restore",
        [((rows, local_z), F32)] * 2,
        outs,
        [pltpu.VMEM((2, micros, local_y, local_z, LANES), F32)],
    )
    weight_total, bias_total = call(
        unpack_kernel,
        "unpack",
        [((2, TAPS, chans, chans), F32), ((2, chans), F32)],
        [near, core],
        [pltpu.VMEM((BLOCKS * chans, LANES), F32)],
    )
    shape = (1, *inflow.shape)
    return (section_out.reshape(shape), section_grad.reshape(shape), weight_total, bias_total)


def solution(mesh):
    grid = P(None, None, None, "gy", "gz")
    section_grid = P("section", None, None, None, "gy", "gz")
    return jax.shard_map(
        per_device,
        mesh=mesh,
        in_specs=(grid, P("section", None, None, None), P("section", None), grid),
        out_specs=(section_grid, section_grid, P("section", None, None, None), P("section", None)),
        check_vma=False,
    )
```

```python
import functools
import math

import jax
import jax.numpy as jnp
from jax import lax
from jax.experimental import pallas as pl
from jax.experimental.pallas import tpu as pltpu
from jax.sharding import PartitionSpec as P

HALO = 8
HALOS = (8, 4)
LANES = 128
TAPS = 27
BLOCKS = 28
BF16 = jnp.bfloat16
F32 = jnp.float32
VMEM = pl.BlockSpec(memory_space=pltpu.VMEM)


def call(kernel, name, outs, args, scratch=(), flops=0):
    arrays = [jax.ShapeDtypeStruct(shape, kind) for shape, kind in outs]
    size = sum(math.prod(item.shape) * item.dtype.itemsize for item in [*arrays, *args, *scratch])
    return pl.pallas_call(
        kernel,
        out_shape=arrays,
        in_specs=[VMEM] * len(args),
        out_specs=[VMEM] * len(arrays),
        scratch_shapes=list(scratch),
        compiler_params=pltpu.CompilerParams(vmem_limit_bytes=size + 6 * 1024 * 1024),
        cost_estimate=pl.CostEstimate(flops=flops, bytes_accessed=1024, transcendentals=0),
        name=name,
    )(*args)


def column_bits():
    column = lax.axis_index("gz")
    return 2 * (column % 2) + column // 2 % 2


def split_terms(values):
    high = values.astype(BF16)
    return high, (values - high.astype(F32)).astype(BF16)


def pack_kernel(weights, biases, own, sent):
    chans = weights.shape[2]
    for tap in range(TAPS):
        own[tap] = jnp.concatenate([weights[0, tap], weights[1, tap]], axis=1)
    own[TAPS] = jnp.zeros((chans, LANES), F32)
    own[TAPS, 0:1, :] = jnp.concatenate([biases[0:1, :], biases[1:2, :]], axis=1)
    half = sent.shape[0]
    start = lax.axis_index("gz") % 2 * half
    for index in range(half):
        sent[index] = own[start + index]


def turned_rows(dims, source, micro, y):
    _, chans, size_x, local_y, _ = dims
    step = size_x * local_y
    first = micro * chans * step + y
    parts = [source[pl.ds(first + x * local_y, chans, stride=step), :] for x in range(size_x)]
    return jnp.concatenate(parts, axis=0).T


def turn_kernel(dims, inflow, cotangent, rows, pair, inner):
    micros, _, _, local_y, local_z = dims
    odd = lax.axis_index("gz") % 2 == 1
    for field, source in enumerate((inflow, cotangent)):
        for micro in range(micros):
            for y in range(local_y):
                turned = turned_rows(dims, source, micro, y)
                rows[field, micro, y] = turned
                low, high = turned[:HALO], turned[local_z - HALO :]
                pair[field, micro, y] = jnp.where(odd, low, high)
                inner[field, micro, y] = jnp.where(odd, high, low)


def window_kernel(dims, rows, pair, inner, *refs):
    slabs, width, columns = dims
    outs, wide = refs[:-1], refs[-1]
    slab, column = lax.axis_index("gy"), lax.axis_index("gz")
    section = lax.axis_index("section")
    odd = column % 2 == 1
    _, micros, local_y, local_z, _ = rows.shape
    for field, halo in enumerate(HALOS):
        at = slice(0, width + 2 * halo) if field == 0 else slice(width + 2 * HALO, None)
        for y in range(local_y):
            for micro in range(micros):
                one, two = pair[field, micro, y], inner[field, micro, y]
                before = jnp.where(column > 0, jnp.where(odd, one, two), 0.0)
                after = jnp.where(column < columns - 1, jnp.where(odd, two, one), 0.0)
                wide[field, micro, y, :HALO] = before
                wide[field, micro, y, HALO : HALO + local_z] = rows[field, micro, y]
                wide[field, micro, y, HALO + local_z :] = after
            for turn, out in enumerate(outs):
                start = (slab ^ turn % slabs) * width + HALO - halo
                if width % 8 == 0 and halo % 8 == 0:
                    start = pl.multiple_of(start, 8)
                micro = section if turn < slabs else 1 - section
                out[y, at] = wide[field, micro, y, pl.ds(start, width + 2 * halo)]


def table_kernel(*refs):
    parts, (fwd, bwd, row) = refs[:-3], refs[-3:]
    odd = lax.axis_index("gz") % 2
    count, chans, _ = parts[0].shape

    def block_of(tap):
        if len(parts) == 1:
            return parts[0][tap]
        index = tap % count
        return jnp.where(odd == tap // count, parts[0][index], parts[1][index])

    for b in range(3):
        for c in range(3):
            taps = [block_of(9 * a + 3 * b + c) for a in range(3)]
            for layer in range(2):
                lanes = slice(layer * chans, (layer + 1) * chans)
                below, level, above = [tap[:, lanes] for tap in taps]
                top = jnp.concatenate([level, above], axis=1)
                low = jnp.concatenate([below, level], axis=1)
                block = jnp.concatenate([top, low], axis=0)
                for target, value, r, at in ((fwd, block.T, b, c), (bwd, block, 2 - b, 2 - c)):
                    hi, lo = split_terms(value)
                    at = slice(at * LANES, (at + 1) * LANES)
                    target[layer, 2 * r * LANES : (2 * r + 1) * LANES, at] = hi
                    target[layer, (2 * r + 1) * LANES : (2 * r + 2) * LANES, at] = hi
                    target[layer, (6 + r) * LANES : (7 + r) * LANES, at] = lo
    last = block_of(TAPS)[0:1, :]
    for layer in range(2):
        part = last[:, layer * chans : (layer + 1) * chans]
        row[layer] = jnp.broadcast_to(jnp.concatenate([part, part], axis=1), (8, LANES))


class Slab:
    def __init__(self, dims):
        self.micros, self.rows_y, self.depth, self.width, self.chunk_y, self.slabs, limit_z = dims
        self.section, self.slab = lax.axis_index("section"), lax.axis_index("gy")
        origin = (lax.axis_index("gz") * self.slabs + self.slab) * self.width - HALO
        self.chunk = self.chunk_y * self.depth
        self.chunks = self.rows_y // self.chunk_y
        self.per_owner = self.rows_y // self.slabs
        zs = lax.broadcasted_iota(jnp.int32, (self.depth, LANES), 0)
        inside = (zs + origin >= 0) & (zs + origin < limit_z)
        self.in_grid = inside.astype(F32)[None]
        self.mine = ((zs >= HALO) & (zs < HALO + self.width)).astype(F32)[None]

    def over_chunks(self, body):
        if self.chunks == 1:
            body(0)
        else:

            def step(part, carry):
                body(pl.multiple_of(part * self.chunk, 16))
                return carry

            lax.fori_loop(0, self.chunks, step, 0)

    def masked(self, values, mask):
        return (values.reshape(-1, self.depth, LANES) * mask).reshape(values.shape)

    def put_rows(self, target, lead, micro, start, values):
        hi, lo = split_terms(values)
        at = pl.ds(start + self.depth, self.chunk)
        target[lead, micro, at, slice(0, LANES)] = hi
        target[lead, micro, at, slice(LANES, 2 * LANES)] = lo

    def pieces_of(self, source, lead, micro, start):
        return [
            source[lead, micro, pl.ds(start + b * self.depth, self.chunk), :] for b in range(3)
        ]

    def conv(self, source, lead, start, table):
        lefts = []
        for micro in range(self.micros):
            pieces = self.pieces_of(source, lead, micro, start)
            lefts.append(jnp.concatenate(pieces + [piece[:, :LANES] for piece in pieces], axis=1))
        results = []
        for left in lefts:
            out = jnp.dot(left, table[...], preferred_element_type=F32)
            before = pltpu.roll(out[:, :LANES], 1, 0)
            after = pltpu.roll(out[:, 2 * LANES :], out.shape[0] - 1, 0)
            results.append(before + out[:, LANES : 2 * LANES] + after)
        return results

    def by_owner(self, layer, own, other, body):
        mine = layer // 2 == self.section
        pl.when(mine)(lambda: body(own, layer % 2))
        pl.when(jnp.logical_not(mine))(lambda: body(other, layer % 2))

    def blank_edges(self, target):
        blank = jnp.zeros((self.depth, 2 * LANES), BF16)
        for lead in range(target.shape[0]):
            for micro in range(self.micros):
                for edge in (0, self.rows_y + 1):
                    target[lead, micro, edge * self.depth : (edge + 1) * self.depth, :] = blank

    def fill(self, field, windows, which):
        halo = HALOS[which]
        span = self.width + 2 * halo
        at = 0 if which == 0 else self.width + 2 * HALO
        extra = [HALO - halo, self.depth - span - (HALO - halo)]
        for index, window in enumerate(windows):
            owner = self.slab ^ index % self.slabs
            micro = self.section if index < self.slabs else 1 - self.section
            for y in range(self.per_owner):
                blanks = [jnp.zeros((rows, LANES), F32) for rows in extra]
                parts = [blanks[0], window[y, at : at + span], blanks[1]]
                parts = [part for part in parts if part.shape[0]]
                start = pl.multiple_of((owner * self.per_owner + y) * self.depth, 16)
                value = jnp.concatenate(parts, axis=0) if len(parts) > 1 else parts[0]
                field[micro, pl.ds(start, self.depth), :] = value

    def cut_out(self, targets, source):
        for turn, target in enumerate(targets):
            owner = self.slab ^ turn
            for micro in range(self.micros):
                for y in range(self.per_owner):
                    start = (owner * self.per_owner + y) * self.depth + HALO
                    rows = pl.ds(pl.multiple_of(start, 8), self.width)
                    target[micro, y] = source[micro, rows, :]


def forward_kernel(dims, own, own_row, other, other_row, *refs):
    slab = Slab(dims)
    windows, (acts, kept, *outs), (whole, field) = (
        refs[: 2 * slab.slabs],
        refs[2 * slab.slabs : -2],
        refs[-2:],
    )
    slab.blank_edges(acts)
    slab.fill(field, windows, 0)

    def take_in(start):
        for micro in range(slab.micros):
            slab.put_rows(acts, 0, micro, start, field[micro, pl.ds(start, slab.chunk), :])

    slab.over_chunks(take_in)

    def layer_step(layer, carry):
        def run(tables, half):
            table, row = tables

            def body(start):
                at = pl.ds(start, slab.chunk)
                sums = slab.conv(acts, layer, start, table.at[half])
                values = []
                for micro, total in enumerate(sums):
                    pre = total + row[half][0:1, :]
                    sigma = 1.0 / (1.0 + jnp.exp(-pre))
                    kept[layer, micro, at, :] = sigma * (1.0 + pre * (1.0 - sigma))
                    out = slab.masked(pre * sigma, slab.in_grid)
                    slab.put_rows(acts, layer + 1, micro, start, out)
                    values.append(out)

                @pl.when(layer == 2 * slab.section + 1)
                def _():
                    for micro, value in enumerate(values):
                        whole[micro, at, :] = value

            slab.over_chunks(body)

        slab.by_owner(layer, (own, own_row), (other, other_row), run)
        return carry

    lax.fori_loop(0, 4, layer_step, 0)
    slab.cut_out(outs, whole)


def backward_kernel(dims, scale, own, other, acts, kept, *refs):
    slab = Slab(dims)
    windows, refs = refs[: 2 * slab.slabs], refs[2 * slab.slabs :]
    outs, (sums, rim, slopes, field, acc) = refs[: slab.slabs], refs[slab.slabs :]
    slab.blank_edges(rim)
    slab.fill(field, windows, 1)

    def take_gradient(layer, micro, start, gradient):
        at = pl.ds(start, slab.chunk)
        slope = slab.masked(gradient * kept[layer, micro, at, :], slab.in_grid)
        slopes[layer, micro, at, :] = slab.masked(slope, slab.mine)
        slab.put_rows(rim, layer % 2, micro, start, slope)

    def take_cotangent(start):
        for micro in range(slab.micros):
            take_gradient(3, micro, start, field[micro, pl.ds(start, slab.chunk), :])

    slab.over_chunks(take_cotangent)

    def layer_step(index, carry):
        layer = 3 - index

        def run(table, half):
            def body(start):
                gradients = slab.conv(rim, layer % 2, start, table.at[half])
                last = layer == 2 * slab.section

                @pl.when(last)
                def _():
                    for micro, gradient in enumerate(gradients):
                        field[micro, pl.ds(start, slab.chunk), :] = gradient

                @pl.when(jnp.logical_not(last))
                def _():
                    for micro, gradient in enumerate(gradients):
                        take_gradient(layer - 1, micro, start, gradient)

            slab.over_chunks(body)

        slab.by_owner(layer, own, other, run)
        return carry

    lax.fori_loop(0, jnp.where(slab.section == 0, 4, 2), layer_step, 0)
    slab.cut_out(outs, field)

    quarter = BLOCKS // 4
    chans = LANES // 2
    swap = column_bits()

    def spot(tap):
        return (tap // quarter ^ swap) * quarter + tap % quarter

    def products(layer, start):
        at = pl.ds(start, slab.chunk)
        slope = jnp.concatenate([slopes[layer, micro, at, :] for micro in range(slab.micros)])
        moved = [pltpu.roll(slope, slope.shape[0] - 1, 0), slope, pltpu.roll(slope, 1, 0)]
        terms = [split_terms(value) for value in moved]
        left_hi = jnp.concatenate([hi for hi, lo in terms], axis=1)
        left_lo = jnp.concatenate([lo for hi, lo in terms], axis=1)
        pieces = [slab.pieces_of(acts, layer, micro, start) for micro in range(slab.micros)]
        pieces = [jnp.concatenate(parts, axis=0) for parts in zip(*pieces)]
        full = jnp.concatenate(pieces, axis=1)
        high = jnp.concatenate([piece[:, :LANES] for piece in pieces], axis=1)
        over_rows = (((0,), (0,)), ((), ()))
        one = lax.dot_general(left_hi, full, over_rows, preferred_element_type=F32)
        two = lax.dot_general(left_lo, high, over_rows, preferred_element_type=F32)
        total = []
        for b in range(3):
            hi = one[:, 2 * b * LANES : (2 * b + 1) * LANES]
            lo = one[:, (2 * b + 1) * LANES : (2 * b + 2) * LANES]
            total.append(hi + lo + two[:, b * LANES : (b + 1) * LANES])
        return total, jnp.sum(slope, axis=0, keepdims=True)

    sums[spot(TAPS)] = jnp.zeros((chans, LANES), F32)
    for slot in range(2):
        layer = 2 * slab.section + slot
        if slab.chunks == 1:
            total, row = products(layer, 0)
        else:
            acc[...] = jnp.zeros(acc.shape, F32)

            def gather(start):
                total, row = products(layer, start)
                for b in range(3):
                    acc[0 : 3 * LANES, b * LANES : (b + 1) * LANES] += total[b]
                acc[3 * LANES : 3 * LANES + 1, 0:LANES] += row

            slab.over_chunks(gather)
            total = [acc[0 : 3 * LANES, b * LANES : (b + 1) * LANES] for b in range(3)]
            row = acc[3 * LANES : 3 * LANES + 1, 0:LANES]
        lanes = slice(slot * chans, (slot + 1) * chans)
        for b in range(3):
            for c in range(3):
                block = total[b][c * LANES : (c + 1) * LANES] * scale
                tap = 3 * b + c
                sums[spot(tap), :, lanes] = block[chans:, :chans]
                sums[spot(9 + tap), :, lanes] = block[:chans, :chans] + block[chans:, chans:]
                sums[spot(18 + tap), :, lanes] = block[:chans, chans:]
        row = row * scale
        sums[spot(TAPS), 0:1, lanes] = row[:, :chans] + row[:, chans:]


def unpack_kernel(near, core, weight, bias, whole):
    part = near.shape[0] // 4
    chans = weight.shape[-1]
    odd, swap = lax.axis_index("gy") % 2, column_bits()
    for index in range(8):
        source = near if index < 4 else core
        first = index % 4 * part
        at = ((index // 2 ^ swap) * 2 + (index % 2 ^ odd)) * part
        whole[pl.ds(pl.multiple_of(at, 8), part), :] = source[first : first + part, :]
    for layer in range(2):
        lanes = slice(layer * chans, (layer + 1) * chans)
        for tap in range(TAPS):
            weight[layer, tap] = whole[tap * chans : (tap + 1) * chans, lanes]
        bias[layer : layer + 1, :] = whole[TAPS * chans : TAPS * chans + 1, lanes]


def restore_kernel(dims, *refs):
    micros, chans, size_x, local_y, width = dims
    pieces, (*targets, whole) = refs[:-3], refs[-3:]
    slab = lax.axis_index("gy")
    step = size_x * local_y
    slabs = len(pieces) // 2
    for slot, target in enumerate(targets):
        for micro in range(micros):
            for y in range(local_y):
                for turn in range(slabs):
                    start = (slab ^ turn) * width
                    if width % 8 == 0:
                        start = pl.multiple_of(start, 8)
                    rows = pl.ds(start, width)
                    whole[slot, micro, y, rows, :] = pieces[slot * slabs + turn][micro, y]
                block = whole[slot, micro, y].T
                for x in range(size_x):
                    first = micro * chans * step + x * local_y + y
                    part = block[x * chans : (x + 1) * chans]
                    target[pl.ds(first, chans, stride=step), :] = part


def spread(blocks):
    slabs = len(blocks)
    if slabs <= 8:
        got = [blocks[0]]
        for turn in range(1, slabs):
            route = [(i, i ^ turn) for i in range(slabs)]
            got.append(lax.ppermute(blocks[turn], "gy", route))
        return got
    order = jnp.arange(slabs) ^ lax.axis_index("gy")
    got = lax.all_to_all(jnp.stack(blocks)[order], "gy", 0, 0)[order]
    return [got[turn] for turn in range(slabs)]


def swapped(block, bit, axis="gz"):
    return lax.ppermute(block, axis, [(i, i ^ bit) for i in range(lax.axis_size(axis))])


def crossed(block):
    return lax.ppermute(block, "section", [(0, 1), (1, 0)])


def around(above, beside, across):
    slabs, columns = lax.axis_size("gy"), lax.axis_size("gz")
    route = [
        (i * columns + g, (i ^ 1) * columns + (g ^ 2)) for i in range(slabs) for g in range(columns)
    ]
    beside = swapped(beside, 2)
    across = lax.ppermute(across, ("gy", "gz"), route)
    return [swapped(above, 1, "gy"), beside, across]


def per_device(inflow, weights, biases, cotangent):
    micros, chans, size_x, local_y, local_z = inflow.shape
    assert micros == lax.axis_size("section") == 2
    slabs, columns = lax.axis_size("gy"), lax.axis_size("gz")
    rows_y = local_y * slabs
    width = local_z // slabs
    span = width + 2 * HALO
    depth = -(-span // 16) * 16
    chunk_y = max(n for n in range(1, rows_y + 1) if rows_y % n == 0 and n * depth <= 384)
    scale = 1.0 / math.sqrt(micros * size_x * rows_y * local_z * columns)
    rows = micros * chans * size_x * local_y
    blocks = [inflow.reshape(rows, local_z), cotangent.reshape(rows, local_z)]
    ends = ((2, micros, local_y, HALO, LANES), F32)
    fields, pair, inner = call(
        functools.partial(turn_kernel, inflow.shape),
        "turn",
        [((2, micros, local_y, local_z, LANES), F32), ends, ends],
        blocks,
    )
    packs = [((BLOCKS, chans, LANES), F32), ((BLOCKS // 2, chans, LANES), F32)]
    own, sent = call(pack_kernel, "pack", packs, [weights, biases])
    pair = swapped(pair, 1)
    route = [(i, i + 1) for i in range(1, columns - 1, 2)]
    inner = lax.ppermute(inner, "gz", route + [(after, before) for before, after in route])
    windows = call(
        functools.partial(window_kernel, (slabs, width, columns)),
        "windows",
        [((local_y, sum(width + 2 * halo for halo in HALOS), LANES), F32)] * (slabs + 1),
        [fields, pair, inner],
        [pltpu.VMEM((2, micros, local_y, local_z + 2 * HALO, LANES), F32)],
    )
    sent, windows = lax.optimization_barrier((sent, windows))
    near_half = crossed(sent)
    *mine, home = windows
    mine = spread(mine)

    tables = [((2, 9 * LANES, 3 * LANES), BF16)] * 2 + [((2, 8, LANES), F32)]
    own_fwd, own_bwd, own_row = call(table_kernel, "own_table", tables, [own])
    if slabs <= 8:
        theirs = [home] + [crossed(window) for window in mine[1:]]
    else:
        theirs = list(crossed(jnp.stack(mine)))
    windows = mine + theirs
    near_half, mine, own_row = lax.optimization_barrier((near_half, mine, own_row))
    far_half = swapped(near_half, 1)
    far_fwd, far_bwd, far_row = call(table_kernel, "far_table", tables, [near_half, far_half])

    dims = (micros, rows_y, depth, width, chunk_y, slabs, local_z * columns)
    padded = (rows_y + 2) * depth
    full = rows_y * depth
    piece = ((micros, local_y, width, LANES), F32)
    acts, kept, *fronts = call(
        functools.partial(forward_kernel, dims),
        "forward",
        [((5, micros, padded, 2 * LANES), BF16), ((4, micros, full, LANES), F32)] + [piece] * slabs,
        [own_fwd, own_row, far_fwd, far_row, *windows],
        [pltpu.VMEM((micros, full, LANES), F32)] * 2,
    )
    if slabs == 4:
        passed = swapped(jnp.stack(fronts[2:]), 2, "gy")
    *backs, sums = call(
        functools.partial(backward_kernel, dims, scale),
        "backward",
        [piece] * slabs + [((BLOCKS, chans, LANES), F32)],
        [own_bwd, far_bwd, acts, kept, *windows],
        [
            pltpu.VMEM((2, micros, padded, 2 * LANES), BF16),
            pltpu.VMEM((4, micros, full, LANES), F32),
            pltpu.VMEM((micros, full, LANES), F32),
            pltpu.VMEM((3 * LANES + 8, 3 * LANES), F32),
        ],
        12 * micros * full * 9 * LANES * 3 * LANES,
    )
    if slabs == 4:
        sums, passed = lax.optimization_barrier((sums, passed))

    block = sums.reshape(BLOCKS * chans, LANES)
    half = block.shape[0] // 2
    block = block[:half] + swapped(block[half:], 1)
    block, fronts, backs = lax.optimization_barrier((block, fronts, backs))
    if slabs == 4:
        near = swapped(jnp.stack([fronts[1], passed[1], backs[1]]), 1, "gy")
        outs = [near, swapped(backs[2], 2, "gy"), swapped(backs[3], 3, "gy")]
    else:
        outs = spread([jnp.stack(pair) for pair in zip(fronts, backs)])
    part = half // 4
    block = block[: 2 * part] + swapped(block[2 * part :], 2)
    block, outs = lax.optimization_barrier((block, outs))
    odd = lax.axis_index("gy") % 2 == 1
    kept = jnp.where(odd, block[part:], block[:part])
    kept = kept + swapped(jnp.where(odd, block[:part], block[part:]), 1, "gy")
    bit = 2
    while bit < slabs:
        kept = kept + swapped(kept, bit, "gy")
        bit *= 2
    if slabs == 4:
        outs = [fronts[0], outs[0][0], passed[0], outs[0][1], backs[0], outs[0][2], *outs[1:]]
    else:
        outs = [out[slot] for slot in range(2) for out in outs]
    near = jnp.concatenate([kept, *around(kept, kept, kept)], axis=0)
    core = swapped(near, 1)
    section_out, section_grad = call(
        functools.partial(restore_kernel, (micros, chans, size_x, local_y, width)),
        "restore",
        [((rows, local_z), F32)] * 2,
        outs,
        [pltpu.VMEM((2, micros, local_y, local_z, LANES), F32)],
    )
    weight_total, bias_total = call(
        unpack_kernel,
        "unpack",
        [((2, TAPS, chans, chans), F32), ((2, chans), F32)],
        [near, core],
        [pltpu.VMEM((BLOCKS * chans, LANES), F32)],
    )
    shape = (1, *inflow.shape)
    return (section_out.reshape(shape), section_grad.reshape(shape), weight_total, bias_total)


def solution(mesh):
    grid = P(None, None, None, "gy", "gz")
    section_grid = P("section", None, None, None, "gy", "gz")
    return jax.shard_map(
        per_device,
        mesh=mesh,
        in_specs=(grid, P("section", None, None, None), P("section", None), grid),
        out_specs=(section_grid, section_grid, P("section", None, None, None), P("section", None)),
        check_vma=False,
    )
```

```python
import functools
import math

import jax
import jax.numpy as jnp
from jax import lax
from jax.experimental import pallas as pl
from jax.experimental.pallas import tpu as pltpu
from jax.sharding import PartitionSpec as P

HALO = 8
HALOS = (8, 4)
LANES = 128
TAPS = 27
BLOCKS = 28
BF16 = jnp.bfloat16
F32 = jnp.float32
VMEM = pl.BlockSpec(memory_space=pltpu.VMEM)


def call(kernel, name, outs, args, scratch=(), flops=0):
    arrays = [jax.ShapeDtypeStruct(shape, kind) for shape, kind in outs]
    size = sum(math.prod(item.shape) * item.dtype.itemsize for item in [*arrays, *args, *scratch])
    return pl.pallas_call(
        kernel,
        out_shape=arrays,
        in_specs=[VMEM] * len(args),
        out_specs=[VMEM] * len(arrays),
        scratch_shapes=list(scratch),
        compiler_params=pltpu.CompilerParams(vmem_limit_bytes=size + 6 * 1024 * 1024),
        cost_estimate=pl.CostEstimate(flops=flops, bytes_accessed=1024, transcendentals=0),
        name=name,
    )(*args)


def column_bits():
    column = lax.axis_index("gz")
    return 2 * (column % 2) + column // 2 % 2


def split_terms(values):
    high = values.astype(BF16)
    return high, (values - high.astype(F32)).astype(BF16)


def pack_kernel(weights, biases, own, sent):
    chans = weights.shape[2]
    for tap in range(TAPS):
        own[tap] = jnp.concatenate([weights[0, tap], weights[1, tap]], axis=1)
    own[TAPS] = jnp.zeros((chans, LANES), F32)
    own[TAPS, 0:1, :] = jnp.concatenate([biases[0:1, :], biases[1:2, :]], axis=1)
    half = sent.shape[0]
    start = lax.axis_index("gz") % 2 * half
    for index in range(half):
        sent[index] = own[start + index]


def turned_rows(dims, source, micro, y):
    _, chans, size_x, local_y, _ = dims
    step = size_x * local_y
    first = micro * chans * step + y
    parts = [source[pl.ds(first + x * local_y, chans, stride=step), :] for x in range(size_x)]
    return jnp.concatenate(parts, axis=0).T


def turn_kernel(dims, inflow, cotangent, rows, pair, inner):
    micros, _, _, local_y, local_z = dims
    odd = lax.axis_index("gz") % 2 == 1
    for field, source in enumerate((inflow, cotangent)):
        for micro in range(micros):
            for y in range(local_y):
                turned = turned_rows(dims, source, micro, y)
                rows[field, micro, y] = turned
                low, high = turned[:HALO], turned[local_z - HALO :]
                pair[field, micro, y] = jnp.where(odd, low, high)
                inner[field, micro, y] = jnp.where(odd, high, low)


def window_kernel(dims, rows, pair, inner, *refs):
    slabs, width, columns = dims
    outs, wide = refs[:-1], refs[-1]
    slab, column = lax.axis_index("gy"), lax.axis_index("gz")
    section = lax.axis_index("section")
    odd = column % 2 == 1
    _, micros, local_y, local_z, _ = rows.shape
    for field, halo in enumerate(HALOS):
        at = slice(0, width + 2 * halo) if field == 0 else slice(width + 2 * HALO, None)
        for y in range(local_y):
            for micro in range(micros):
                one, two = pair[field, micro, y], inner[field, micro, y]
                before = jnp.where(column > 0, jnp.where(odd, one, two), 0.0)
                after = jnp.where(column < columns - 1, jnp.where(odd, two, one), 0.0)
                wide[field, micro, y, :HALO] = before
                wide[field, micro, y, HALO : HALO + local_z] = rows[field, micro, y]
                wide[field, micro, y, HALO + local_z :] = after
            for turn, out in enumerate(outs):
                start = (slab ^ turn % slabs) * width + HALO - halo
                if width % 8 == 0 and halo % 8 == 0:
                    start = pl.multiple_of(start, 8)
                micro = section if turn < slabs else 1 - section
                out[y, at] = wide[field, micro, y, pl.ds(start, width + 2 * halo)]


def table_kernel(*refs):
    parts, (fwd, bwd, row) = refs[:-3], refs[-3:]
    odd = lax.axis_index("gz") % 2
    count, chans, _ = parts[0].shape

    def block_of(tap):
        if len(parts) == 1:
            return parts[0][tap]
        index = tap % count
        return jnp.where(odd == tap // count, parts[0][index], parts[1][index])

    for b in range(3):
        for c in range(3):
            taps = [block_of(9 * a + 3 * b + c) for a in range(3)]
            for layer in range(2):
                own_lanes = slice(layer * chans, (layer + 1) * chans)
                below, level, above = [tap[:, own_lanes] for tap in taps]
                top = jnp.concatenate([level, above], axis=1)
                low = jnp.concatenate([below, level], axis=1)
                block = jnp.concatenate([top, low], axis=0)
                for target, value, r, at in ((fwd, block.T, b, c), (bwd, block, 2 - b, 2 - c)):
                    hi, lo = split_terms(value)
                    if at == 1:
                        for row_at in (9 + 2 * r, 10 + 2 * r):
                            rows = slice(row_at * LANES, (row_at + 1) * LANES)
                            target[layer, rows, 0:LANES] = hi
                            target[layer, rows, LANES : 2 * LANES] = lo
                    else:
                        lanes = slice(at // 2 * LANES, (at // 2 + 1) * LANES)
                        for row_at, term in ((2 * r, hi), (2 * r + 1, hi), (6 + r, lo)):
                            rows = slice(row_at * LANES, (row_at + 1) * LANES)
                            target[layer, rows, lanes] = term
    last = block_of(TAPS)[0:1, :]
    for layer in range(2):
        part = last[:, layer * chans : (layer + 1) * chans]
        row[layer] = jnp.broadcast_to(jnp.concatenate([part, part], axis=1), (8, LANES))


class Slab:
    def __init__(self, dims):
        self.micros, self.rows_y, self.depth, self.width, self.chunk_y, self.slabs, limit_z = dims
        self.section, self.slab = lax.axis_index("section"), lax.axis_index("gy")
        origin = (lax.axis_index("gz") * self.slabs + self.slab) * self.width - HALO
        self.chunk = self.chunk_y * self.depth
        self.chunks = self.rows_y // self.chunk_y
        self.per_owner = self.rows_y // self.slabs
        zs = lax.broadcasted_iota(jnp.int32, (self.depth, LANES), 0)
        inside = (zs + origin >= 0) & (zs + origin < limit_z)
        self.in_grid = inside.astype(F32)[None]
        self.mine = ((zs >= HALO) & (zs < HALO + self.width)).astype(F32)[None]

    def over_chunks(self, body):
        if self.chunks == 1:
            body(0)
        else:

            def step(part, carry):
                body(pl.multiple_of(part * self.chunk, 16))
                return carry

            lax.fori_loop(0, self.chunks, step, 0)

    def masked(self, values, mask):
        return (values.reshape(-1, self.depth, LANES) * mask).reshape(values.shape)

    def put_rows(self, target, lead, micro, start, values):
        hi, lo = split_terms(values)
        at = pl.ds(start + self.depth, self.chunk)
        target[lead, micro, at, slice(0, LANES)] = hi
        target[lead, micro, at, slice(LANES, 2 * LANES)] = lo

    def pieces_of(self, source, lead, micro, start):
        return [
            source[lead, micro, pl.ds(start + b * self.depth, self.chunk), :] for b in range(3)
        ]

    def conv(self, source, lead, start, table):
        lefts = []
        for micro in range(self.micros):
            pieces = self.pieces_of(source, lead, micro, start)
            lefts.append(jnp.concatenate(pieces + [piece[:, :LANES] for piece in pieces], axis=1))
        results = []
        for left in lefts:
            outer = jnp.dot(left, table[0 : 9 * LANES, :], preferred_element_type=F32)
            middle = jnp.dot(
                left[:, 0 : 6 * LANES],
                table[9 * LANES : 15 * LANES, :],
                preferred_element_type=F32,
            )
            before = pltpu.roll(outer[:, :LANES], 1, 0)
            after = pltpu.roll(outer[:, LANES:], outer.shape[0] - 1, 0)
            results.append(before + (middle[:, :LANES] + middle[:, LANES:]) + after)
        return results

    def by_owner(self, layer, own, other, body):
        mine = layer // 2 == self.section
        pl.when(mine)(lambda: body(own, layer % 2))
        pl.when(jnp.logical_not(mine))(lambda: body(other, layer % 2))

    def blank_edges(self, target):
        blank = jnp.zeros((self.depth, 2 * LANES), BF16)
        for lead in range(target.shape[0]):
            for micro in range(self.micros):
                for edge in (0, self.rows_y + 1):
                    target[lead, micro, edge * self.depth : (edge + 1) * self.depth, :] = blank

    def fill(self, field, windows, which):
        halo = HALOS[which]
        span = self.width + 2 * halo
        at = 0 if which == 0 else self.width + 2 * HALO
        extra = [HALO - halo, self.depth - span - (HALO - halo)]
        for index, window in enumerate(windows):
            owner = self.slab ^ index % self.slabs
            micro = self.section if index < self.slabs else 1 - self.section
            for y in range(self.per_owner):
                blanks = [jnp.zeros((rows, LANES), F32) for rows in extra]
                parts = [blanks[0], window[y, at : at + span], blanks[1]]
                parts = [part for part in parts if part.shape[0]]
                start = pl.multiple_of((owner * self.per_owner + y) * self.depth, 16)
                value = jnp.concatenate(parts, axis=0) if len(parts) > 1 else parts[0]
                field[micro, pl.ds(start, self.depth), :] = value

    def cut_out(self, targets, source):
        for turn, target in enumerate(targets):
            owner = self.slab ^ turn
            for micro in range(self.micros):
                for y in range(self.per_owner):
                    start = (owner * self.per_owner + y) * self.depth + HALO
                    rows = pl.ds(pl.multiple_of(start, 8), self.width)
                    target[micro, y] = source[micro, rows, :]


def forward_kernel(dims, own, own_row, other, other_row, *refs):
    slab = Slab(dims)
    windows, (acts, kept, *outs), (whole, field) = (
        refs[: 2 * slab.slabs],
        refs[2 * slab.slabs : -2],
        refs[-2:],
    )
    slab.blank_edges(acts)
    slab.fill(field, windows, 0)

    def take_in(start):
        for micro in range(slab.micros):
            slab.put_rows(acts, 0, micro, start, field[micro, pl.ds(start, slab.chunk), :])

    slab.over_chunks(take_in)

    def layer_step(layer, carry):
        def run(tables, half):
            table, row = tables

            def body(start):
                at = pl.ds(start, slab.chunk)
                sums = slab.conv(acts, layer, start, table.at[half])
                values = []
                for micro, total in enumerate(sums):
                    pre = total + row[half][0:1, :]
                    sigma = 1.0 / (1.0 + jnp.exp(-pre))
                    kept[layer, micro, at, :] = sigma * (1.0 + pre * (1.0 - sigma))
                    out = slab.masked(pre * sigma, slab.in_grid)
                    slab.put_rows(acts, layer + 1, micro, start, out)
                    values.append(out)

                @pl.when(layer == 2 * slab.section + 1)
                def _():
                    for micro, value in enumerate(values):
                        whole[micro, at, :] = value

            slab.over_chunks(body)

        slab.by_owner(layer, (own, own_row), (other, other_row), run)
        return carry

    lax.fori_loop(0, 4, layer_step, 0)
    slab.cut_out(outs, whole)


def backward_kernel(dims, scale, own, other, acts, kept, *refs):
    slab = Slab(dims)
    windows, refs = refs[: 2 * slab.slabs], refs[2 * slab.slabs :]
    outs, (sums, rim, slopes, field, acc) = refs[: slab.slabs], refs[slab.slabs :]
    slab.blank_edges(rim)
    slab.fill(field, windows, 1)

    def take_gradient(layer, micro, start, gradient):
        at = pl.ds(start, slab.chunk)
        slope = slab.masked(gradient * kept[layer, micro, at, :], slab.in_grid)
        slopes[layer, micro, at, :] = slab.masked(slope, slab.mine)
        slab.put_rows(rim, layer % 2, micro, start, slope)

    def take_cotangent(start):
        for micro in range(slab.micros):
            take_gradient(3, micro, start, field[micro, pl.ds(start, slab.chunk), :])

    slab.over_chunks(take_cotangent)

    def layer_step(index, carry):
        layer = 3 - index

        def run(table, half):
            def body(start):
                gradients = slab.conv(rim, layer % 2, start, table.at[half])
                last = layer == 2 * slab.section

                @pl.when(last)
                def _():
                    for micro, gradient in enumerate(gradients):
                        field[micro, pl.ds(start, slab.chunk), :] = gradient

                @pl.when(jnp.logical_not(last))
                def _():
                    for micro, gradient in enumerate(gradients):
                        take_gradient(layer - 1, micro, start, gradient)

            slab.over_chunks(body)

        slab.by_owner(layer, own, other, run)
        return carry

    lax.fori_loop(0, jnp.where(slab.section == 0, 4, 2), layer_step, 0)
    slab.cut_out(outs, field)

    quarter = BLOCKS // 4
    chans = LANES // 2
    swap = column_bits()

    def spot(tap):
        return (tap // quarter ^ swap) * quarter + tap % quarter

    def products(layer, start):
        at = pl.ds(start, slab.chunk)
        slope = jnp.concatenate([slopes[layer, micro, at, :] for micro in range(slab.micros)])
        moved = [pltpu.roll(slope, slope.shape[0] - 1, 0), slope, pltpu.roll(slope, 1, 0)]
        terms = [split_terms(value) for value in moved]
        left_hi = jnp.concatenate([hi for hi, lo in terms], axis=1)
        left_lo = jnp.concatenate([lo for hi, lo in terms], axis=1)
        pieces = [slab.pieces_of(acts, layer, micro, start) for micro in range(slab.micros)]
        pieces = [jnp.concatenate(parts, axis=0) for parts in zip(*pieces)]
        full = jnp.concatenate(pieces, axis=1)
        high = jnp.concatenate([piece[:, :LANES] for piece in pieces], axis=1)
        over_rows = (((0,), (0,)), ((), ()))
        one = lax.dot_general(left_hi, full, over_rows, preferred_element_type=F32)
        two = lax.dot_general(left_lo, high, over_rows, preferred_element_type=F32)
        total = []
        for b in range(3):
            hi = one[:, 2 * b * LANES : (2 * b + 1) * LANES]
            lo = one[:, (2 * b + 1) * LANES : (2 * b + 2) * LANES]
            total.append(hi + lo + two[:, b * LANES : (b + 1) * LANES])
        return total, jnp.sum(slope, axis=0, keepdims=True)

    sums[spot(TAPS)] = jnp.zeros((chans, LANES), F32)
    for slot in range(2):
        layer = 2 * slab.section + slot
        if slab.chunks == 1:
            total, row = products(layer, 0)
        else:
            acc[...] = jnp.zeros(acc.shape, F32)

            def gather(start):
                total, row = products(layer, start)
                for b in range(3):
                    acc[0 : 3 * LANES, b * LANES : (b + 1) * LANES] += total[b]
                acc[3 * LANES : 3 * LANES + 1, 0:LANES] += row

            slab.over_chunks(gather)
            total = [acc[0 : 3 * LANES, b * LANES : (b + 1) * LANES] for b in range(3)]
            row = acc[3 * LANES : 3 * LANES + 1, 0:LANES]
        lanes = slice(slot * chans, (slot + 1) * chans)
        for b in range(3):
            for c in range(3):
                block = total[b][c * LANES : (c + 1) * LANES] * scale
                tap = 3 * b + c
                sums[spot(tap), :, lanes] = block[chans:, :chans]
                sums[spot(9 + tap), :, lanes] = block[:chans, :chans] + block[chans:, chans:]
                sums[spot(18 + tap), :, lanes] = block[:chans, chans:]
        row = row * scale
        sums[spot(TAPS), 0:1, lanes] = row[:, :chans] + row[:, chans:]


def unpack_kernel(near, core, weight, bias, whole):
    part = near.shape[0] // 4
    chans = weight.shape[-1]
    odd, swap = lax.axis_index("gy") % 2, column_bits()
    for index in range(8):
        source = near if index < 4 else core
        first = index % 4 * part
        at = ((index // 2 ^ swap) * 2 + (index % 2 ^ odd)) * part
        whole[pl.ds(pl.multiple_of(at, 8), part), :] = source[first : first + part, :]
    for layer in range(2):
        lanes = slice(layer * chans, (layer + 1) * chans)
        for tap in range(TAPS):
            weight[layer, tap] = whole[tap * chans : (tap + 1) * chans, lanes]
        bias[layer : layer + 1, :] = whole[TAPS * chans : TAPS * chans + 1, lanes]


def restore_kernel(dims, *refs):
    micros, chans, size_x, local_y, width = dims
    pieces, (*targets, whole) = refs[:-3], refs[-3:]
    slab = lax.axis_index("gy")
    step = size_x * local_y
    slabs = len(pieces) // 2
    for slot, target in enumerate(targets):
        for micro in range(micros):
            for y in range(local_y):
                for turn in range(slabs):
                    start = (slab ^ turn) * width
                    if width % 8 == 0:
                        start = pl.multiple_of(start, 8)
                    rows = pl.ds(start, width)
                    whole[slot, micro, y, rows, :] = pieces[slot * slabs + turn][micro, y]
                block = whole[slot, micro, y].T
                for x in range(size_x):
                    first = micro * chans * step + x * local_y + y
                    part = block[x * chans : (x + 1) * chans]
                    target[pl.ds(first, chans, stride=step), :] = part


def spread(blocks):
    slabs = len(blocks)
    if slabs <= 8:
        got = [blocks[0]]
        for turn in range(1, slabs):
            route = [(i, i ^ turn) for i in range(slabs)]
            got.append(lax.ppermute(blocks[turn], "gy", route))
        return got
    order = jnp.arange(slabs) ^ lax.axis_index("gy")
    got = lax.all_to_all(jnp.stack(blocks)[order], "gy", 0, 0)[order]
    return [got[turn] for turn in range(slabs)]


def swapped(block, bit, axis="gz"):
    return lax.ppermute(block, axis, [(i, i ^ bit) for i in range(lax.axis_size(axis))])


def crossed(block):
    return lax.ppermute(block, "section", [(0, 1), (1, 0)])


def around(above, beside, across):
    slabs, columns = lax.axis_size("gy"), lax.axis_size("gz")
    route = [
        (i * columns + g, (i ^ 1) * columns + (g ^ 2)) for i in range(slabs) for g in range(columns)
    ]
    beside = swapped(beside, 2)
    across = lax.ppermute(across, ("gy", "gz"), route)
    return [swapped(above, 1, "gy"), beside, across]


def per_device(inflow, weights, biases, cotangent):
    micros, chans, size_x, local_y, local_z = inflow.shape
    assert micros == lax.axis_size("section") == 2
    slabs, columns = lax.axis_size("gy"), lax.axis_size("gz")
    rows_y = local_y * slabs
    width = local_z // slabs
    span = width + 2 * HALO
    depth = -(-span // 16) * 16
    chunk_y = max(n for n in range(1, rows_y + 1) if rows_y % n == 0 and n * depth <= 384)
    scale = 1.0 / math.sqrt(micros * size_x * rows_y * local_z * columns)
    rows = micros * chans * size_x * local_y
    blocks = [inflow.reshape(rows, local_z), cotangent.reshape(rows, local_z)]
    ends = ((2, micros, local_y, HALO, LANES), F32)
    fields, pair, inner = call(
        functools.partial(turn_kernel, inflow.shape),
        "turn",
        [((2, micros, local_y, local_z, LANES), F32), ends, ends],
        blocks,
    )
    packs = [((BLOCKS, chans, LANES), F32), ((BLOCKS // 2, chans, LANES), F32)]
    own, sent = call(pack_kernel, "pack", packs, [weights, biases])
    pair = swapped(pair, 1)
    route = [(i, i + 1) for i in range(1, columns - 1, 2)]
    inner = lax.ppermute(inner, "gz", route + [(after, before) for before, after in route])
    windows = call(
        functools.partial(window_kernel, (slabs, width, columns)),
        "windows",
        [((local_y, sum(width + 2 * halo for halo in HALOS), LANES), F32)] * (slabs + 1),
        [fields, pair, inner],
        [pltpu.VMEM((2, micros, local_y, local_z + 2 * HALO, LANES), F32)],
    )
    sent, windows = lax.optimization_barrier((sent, windows))
    near_half = crossed(sent)
    *mine, home = windows
    mine = spread(mine)

    tables = [((2, 15 * LANES, 2 * LANES), BF16)] * 2 + [((2, 8, LANES), F32)]
    own_fwd, own_bwd, own_row = call(table_kernel, "own_table", tables, [own])
    if slabs <= 8:
        theirs = [home] + [crossed(window) for window in mine[1:]]
    else:
        theirs = list(crossed(jnp.stack(mine)))
    windows = mine + theirs
    gate = [*theirs[1:3], *mine[3:]]
    near_half, own_row, *_ = lax.optimization_barrier((near_half, own_row, *gate))
    far_half = swapped(near_half, 1)
    far_fwd, far_bwd, far_row = call(table_kernel, "far_table", tables, [near_half, far_half])

    dims = (micros, rows_y, depth, width, chunk_y, slabs, local_z * columns)
    padded = (rows_y + 2) * depth
    full = rows_y * depth
    piece = ((micros, local_y, width, LANES), F32)
    acts, kept, *fronts = call(
        functools.partial(forward_kernel, dims),
        "forward",
        [((5, micros, padded, 2 * LANES), BF16), ((4, micros, full, LANES), F32)] + [piece] * slabs,
        [own_fwd, own_row, far_fwd, far_row, *windows],
        [pltpu.VMEM((micros, full, LANES), F32)] * 2,
    )
    if slabs == 4:
        passed = swapped(jnp.stack(fronts[2:]), 2, "gy")
    *backs, sums = call(
        functools.partial(backward_kernel, dims, scale),
        "backward",
        [piece] * slabs + [((BLOCKS, chans, LANES), F32)],
        [own_bwd, far_bwd, acts, kept, *windows],
        [
            pltpu.VMEM((2, micros, padded, 2 * LANES), BF16),
            pltpu.VMEM((4, micros, full, LANES), F32),
            pltpu.VMEM((micros, full, LANES), F32),
            pltpu.VMEM((3 * LANES + 8, 3 * LANES), F32),
        ],
        12 * micros * full * 9 * LANES * 3 * LANES,
    )
    if slabs == 4:
        sums, passed = lax.optimization_barrier((sums, passed))

    block = sums.reshape(BLOCKS * chans, LANES)
    half = block.shape[0] // 2
    block = block[:half] + swapped(block[half:], 1)
    block, fronts, backs = lax.optimization_barrier((block, fronts, backs))
    if slabs == 4:
        near = swapped(jnp.stack([fronts[1], passed[1], backs[1]]), 1, "gy")
        outs = [near, swapped(backs[2], 2, "gy"), swapped(backs[3], 3, "gy")]
    else:
        outs = spread([jnp.stack(pair) for pair in zip(fronts, backs)])
    part = half // 4
    block = block[: 2 * part] + swapped(block[2 * part :], 2)
    block, outs = lax.optimization_barrier((block, outs))
    odd = lax.axis_index("gy") % 2 == 1
    kept = jnp.where(odd, block[part:], block[:part])
    kept = kept + swapped(jnp.where(odd, block[:part], block[part:]), 1, "gy")
    bit = 2
    while bit < slabs:
        kept = kept + swapped(kept, bit, "gy")
        bit *= 2
    if slabs == 4:
        outs = [fronts[0], outs[0][0], passed[0], outs[0][1], backs[0], outs[0][2], *outs[1:]]
    else:
        outs = [out[slot] for slot in range(2) for out in outs]
    near = jnp.concatenate([kept, *around(kept, kept, kept)], axis=0)
    core = swapped(near, 1)
    section_out, section_grad = call(
        functools.partial(restore_kernel, (micros, chans, size_x, local_y, width)),
        "restore",
        [((rows, local_z), F32)] * 2,
        outs,
        [pltpu.VMEM((2, micros, local_y, local_z, LANES), F32)],
    )
    weight_total, bias_total = call(
        unpack_kernel,
        "unpack",
        [((2, TAPS, chans, chans), F32), ((2, chans), F32)],
        [near, core],
        [pltpu.VMEM((BLOCKS * chans, LANES), F32)],
    )
    shape = (1, *inflow.shape)
    return (section_out.reshape(shape), section_grad.reshape(shape), weight_total, bias_total)


def solution(mesh):
    grid = P(None, None, None, "gy", "gz")
    section_grid = P("section", None, None, None, "gy", "gz")
    return jax.shard_map(
        per_device,
        mesh=mesh,
        in_specs=(grid, P("section", None, None, None), P("section", None), grid),
        out_specs=(section_grid, section_grid, P("section", None, None, None), P("section", None)),
        check_vma=False,
    )
```

```python
import functools
import math

import jax
import jax.numpy as jnp
from jax import lax
from jax.experimental import pallas as pl
from jax.experimental.pallas import tpu as pltpu
from jax.sharding import PartitionSpec as P

HALO = 8
HALOS = (8, 4)
LANES = 128
TAPS = 27
BLOCKS = 28
BF16 = jnp.bfloat16
F32 = jnp.float32
VMEM = pl.BlockSpec(memory_space=pltpu.VMEM)


def call(kernel, name, outs, args, scratch=(), flops=0):
    arrays = [jax.ShapeDtypeStruct(shape, kind) for shape, kind in outs]
    size = sum(math.prod(item.shape) * item.dtype.itemsize for item in [*arrays, *args, *scratch])
    return pl.pallas_call(
        kernel,
        out_shape=arrays,
        in_specs=[VMEM] * len(args),
        out_specs=[VMEM] * len(arrays),
        scratch_shapes=list(scratch),
        compiler_params=pltpu.CompilerParams(vmem_limit_bytes=size + 6 * 1024 * 1024),
        cost_estimate=pl.CostEstimate(flops=flops, bytes_accessed=1024, transcendentals=0),
        name=name,
    )(*args)


def column_bits():
    column = lax.axis_index("gz")
    return 2 * (column % 2) + column // 2 % 2


def split_terms(values):
    high = values.astype(BF16)
    return high, (values - high.astype(F32)).astype(BF16)


def pack_kernel(weights, biases, own, sent):
    chans = weights.shape[2]
    for tap in range(TAPS):
        own[tap] = jnp.concatenate([weights[0, tap], weights[1, tap]], axis=1)
    own[TAPS] = jnp.zeros((chans, LANES), F32)
    own[TAPS, 0:1, :] = jnp.concatenate([biases[0:1, :], biases[1:2, :]], axis=1)
    half = sent.shape[0]
    start = lax.axis_index("gz") % 2 * half
    for index in range(half):
        sent[index] = own[start + index]


def turned_rows(dims, source, micro, y):
    _, chans, size_x, local_y, _ = dims
    step = size_x * local_y
    first = micro * chans * step + y
    parts = [source[pl.ds(first + x * local_y, chans, stride=step), :] for x in range(size_x)]
    return jnp.concatenate(parts, axis=0).T


def turn_kernel(dims, inflow, cotangent, rows, pair, inner):
    micros, _, _, local_y, local_z = dims
    odd = lax.axis_index("gz") % 2 == 1
    for field, source in enumerate((inflow, cotangent)):
        for micro in range(micros):
            for y in range(local_y):
                turned = turned_rows(dims, source, micro, y)
                rows[field, micro, y] = turned
                low, high = turned[:HALO], turned[local_z - HALO :]
                pair[field, micro, y] = jnp.where(odd, low, high)
                inner[field, micro, y] = jnp.where(odd, high, low)


def window_kernel(dims, rows, pair, inner, *refs):
    slabs, width, columns = dims
    outs, wide = refs[:-1], refs[-1]
    slab, column = lax.axis_index("gy"), lax.axis_index("gz")
    section = lax.axis_index("section")
    odd = column % 2 == 1
    _, micros, local_y, local_z, _ = rows.shape
    for field, halo in enumerate(HALOS):
        at = slice(0, width + 2 * halo) if field == 0 else slice(width + 2 * HALO, None)
        for y in range(local_y):
            for micro in range(micros):
                one, two = pair[field, micro, y], inner[field, micro, y]
                before = jnp.where(column > 0, jnp.where(odd, one, two), 0.0)
                after = jnp.where(column < columns - 1, jnp.where(odd, two, one), 0.0)
                wide[field, micro, y, :HALO] = before
                wide[field, micro, y, HALO : HALO + local_z] = rows[field, micro, y]
                wide[field, micro, y, HALO + local_z :] = after
            for turn, out in enumerate(outs):
                start = (slab ^ turn % slabs) * width + HALO - halo
                if width % 8 == 0 and halo % 8 == 0:
                    start = pl.multiple_of(start, 8)
                micro = section if turn < slabs else 1 - section
                out[y, at] = wide[field, micro, y, pl.ds(start, width + 2 * halo)]


def table_kernel(*refs):
    parts, (fwd, bwd, row) = refs[:-3], refs[-3:]
    odd = lax.axis_index("gz") % 2
    count, chans, _ = parts[0].shape

    def block_of(tap):
        if len(parts) == 1:
            return parts[0][tap]
        index = tap % count
        return jnp.where(odd == tap // count, parts[0][index], parts[1][index])

    for b in range(3):
        for c in range(3):
            taps = [block_of(9 * a + 3 * b + c) for a in range(3)]
            for layer in range(2):
                own_lanes = slice(layer * chans, (layer + 1) * chans)
                below, level, above = [tap[:, own_lanes] for tap in taps]
                top = jnp.concatenate([level, above], axis=1)
                low = jnp.concatenate([below, level], axis=1)
                block = jnp.concatenate([top, low], axis=0)
                for target, value, r, at in ((fwd, block.T, b, c), (bwd, block, 2 - b, 2 - c)):
                    hi, lo = split_terms(value)
                    if at == 1:
                        for row_at in (9 + 2 * r, 10 + 2 * r):
                            rows = slice(row_at * LANES, (row_at + 1) * LANES)
                            target[layer, rows, 0:LANES] = hi
                            target[layer, rows, LANES : 2 * LANES] = lo
                    else:
                        lanes = slice(at // 2 * LANES, (at // 2 + 1) * LANES)
                        for row_at, term in ((2 * r, hi), (2 * r + 1, hi), (6 + r, lo)):
                            rows = slice(row_at * LANES, (row_at + 1) * LANES)
                            target[layer, rows, lanes] = term
    last = block_of(TAPS)[0:1, :]
    for layer in range(2):
        part = last[:, layer * chans : (layer + 1) * chans]
        row[layer] = jnp.broadcast_to(jnp.concatenate([part, part], axis=1), (8, LANES))


class Slab:
    def __init__(self, dims):
        self.micros, self.rows_y, self.depth, self.width, self.chunk_y, self.slabs, limit_z = dims
        self.section, self.slab = lax.axis_index("section"), lax.axis_index("gy")
        origin = (lax.axis_index("gz") * self.slabs + self.slab) * self.width - HALO
        self.chunk = self.chunk_y * self.depth
        self.chunks = self.rows_y // self.chunk_y
        self.per_owner = self.rows_y // self.slabs
        zs = lax.broadcasted_iota(jnp.int32, (self.depth, LANES), 0)
        inside = (zs + origin >= 0) & (zs + origin < limit_z)
        self.in_grid = inside.astype(F32)[None]
        self.mine = ((zs >= HALO) & (zs < HALO + self.width)).astype(F32)[None]

    def over_chunks(self, body):
        if self.chunks == 1:
            body(0)
        else:

            def step(part, carry):
                body(pl.multiple_of(part * self.chunk, 16))
                return carry

            lax.fori_loop(0, self.chunks, step, 0)

    def masked(self, values, mask):
        return (values.reshape(-1, self.depth, LANES) * mask).reshape(values.shape)

    def put_rows(self, target, lead, micro, start, values):
        hi, lo = split_terms(values)
        at = pl.ds(start + self.depth, self.chunk)
        target[lead, micro, at, slice(0, LANES)] = hi
        target[lead, micro, at, slice(LANES, 2 * LANES)] = lo

    def pieces_of(self, source, lead, micro, start):
        return [
            source[lead, micro, pl.ds(start + b * self.depth, self.chunk), :] for b in range(3)
        ]

    def conv(self, source, lead, start, table):
        lefts = []
        for micro in range(self.micros):
            pieces = self.pieces_of(source, lead, micro, start)
            lefts.append(jnp.concatenate(pieces + [piece[:, :LANES] for piece in pieces], axis=1))
        results = []
        for left in lefts:
            outer = jnp.dot(left, table[0 : 9 * LANES, :], preferred_element_type=F32)
            middle = jnp.dot(
                left[:, 0 : 6 * LANES],
                table[9 * LANES : 15 * LANES, :],
                preferred_element_type=F32,
            )
            before = pltpu.roll(outer[:, :LANES], 1, 0)
            after = pltpu.roll(outer[:, LANES:], outer.shape[0] - 1, 0)
            results.append(before + (middle[:, :LANES] + middle[:, LANES:]) + after)
        return results

    def by_owner(self, layer, own, other, body):
        mine = layer // 2 == self.section
        pl.when(mine)(lambda: body(own, layer % 2))
        pl.when(jnp.logical_not(mine))(lambda: body(other, layer % 2))

    def blank_edges(self, target):
        blank = jnp.zeros((self.depth, 2 * LANES), BF16)
        for lead in range(target.shape[0]):
            for micro in range(self.micros):
                for edge in (0, self.rows_y + 1):
                    target[lead, micro, edge * self.depth : (edge + 1) * self.depth, :] = blank

    def fill(self, field, windows, which):
        halo = HALOS[which]
        span = self.width + 2 * halo
        at = 0 if which == 0 else self.width + 2 * HALO
        extra = [HALO - halo, self.depth - span - (HALO - halo)]
        for index, window in enumerate(windows):
            owner = self.slab ^ index % self.slabs
            micro = self.section if index < self.slabs else 1 - self.section
            for y in range(self.per_owner):
                blanks = [jnp.zeros((rows, LANES), F32) for rows in extra]
                parts = [blanks[0], window[y, at : at + span], blanks[1]]
                parts = [part for part in parts if part.shape[0]]
                start = pl.multiple_of((owner * self.per_owner + y) * self.depth, 16)
                value = jnp.concatenate(parts, axis=0) if len(parts) > 1 else parts[0]
                field[micro, pl.ds(start, self.depth), :] = value

    def cut_out(self, targets, source):
        for turn, target in enumerate(targets):
            owner = self.slab ^ turn
            for micro in range(self.micros):
                for y in range(self.per_owner):
                    start = (owner * self.per_owner + y) * self.depth + HALO
                    rows = pl.ds(pl.multiple_of(start, 8), self.width)
                    target[micro, y] = source[micro, rows, :]


def forward_kernel(dims, own, own_row, other, other_row, *refs):
    slab = Slab(dims)
    windows, (acts, kept, *outs), (whole, field) = (
        refs[: 2 * slab.slabs],
        refs[2 * slab.slabs : -2],
        refs[-2:],
    )
    slab.blank_edges(acts)
    slab.fill(field, windows, 0)

    def take_in(start):
        for micro in range(slab.micros):
            slab.put_rows(acts, 0, micro, start, field[micro, pl.ds(start, slab.chunk), :])

    slab.over_chunks(take_in)

    def layer_step(layer, carry):
        def run(tables, half):
            table, row = tables

            def body(start):
                at = pl.ds(start, slab.chunk)
                sums = slab.conv(acts, layer, start, table.at[half])
                values = []
                for micro, total in enumerate(sums):
                    pre = total + row[half][0:1, :]
                    sigma = 1.0 / (1.0 + jnp.exp(-pre))
                    kept[layer, micro, at, :] = sigma * (1.0 + pre * (1.0 - sigma))
                    out = slab.masked(pre * sigma, slab.in_grid)
                    slab.put_rows(acts, layer + 1, micro, start, out)
                    values.append(out)

                @pl.when(layer == 2 * slab.section + 1)
                def _():
                    for micro, value in enumerate(values):
                        whole[micro, at, :] = value

            slab.over_chunks(body)

        slab.by_owner(layer, (own, own_row), (other, other_row), run)
        return carry

    lax.fori_loop(0, 4, layer_step, 0)
    slab.cut_out(outs, whole)


def backward_kernel(dims, scale, own, other, acts, kept, *refs):
    slab = Slab(dims)
    windows, refs = refs[: 2 * slab.slabs], refs[2 * slab.slabs :]
    outs, (sums, rim, slopes, field, acc) = refs[: slab.slabs], refs[slab.slabs :]
    slab.blank_edges(rim)
    slab.fill(field, windows, 1)

    def take_gradient(layer, micro, start, gradient):
        at = pl.ds(start, slab.chunk)
        slope = slab.masked(gradient * kept[layer, micro, at, :], slab.in_grid)
        slopes[layer, micro, at, :] = slab.masked(slope, slab.mine)
        slab.put_rows(rim, layer % 2, micro, start, slope)

    def take_cotangent(start):
        for micro in range(slab.micros):
            take_gradient(3, micro, start, field[micro, pl.ds(start, slab.chunk), :])

    slab.over_chunks(take_cotangent)

    def layer_step(index, carry):
        layer = 3 - index

        def run(table, half):
            def body(start):
                gradients = slab.conv(rim, layer % 2, start, table.at[half])
                last = layer == 2 * slab.section

                @pl.when(last)
                def _():
                    for micro, gradient in enumerate(gradients):
                        field[micro, pl.ds(start, slab.chunk), :] = gradient

                @pl.when(jnp.logical_not(last))
                def _():
                    for micro, gradient in enumerate(gradients):
                        take_gradient(layer - 1, micro, start, gradient)

            slab.over_chunks(body)

        slab.by_owner(layer, own, other, run)
        return carry

    lax.fori_loop(0, jnp.where(slab.section == 0, 4, 2), layer_step, 0)
    slab.cut_out(outs, field)

    quarter = BLOCKS // 4
    chans = LANES // 2
    swap = column_bits()

    def spot(tap):
        return (tap // quarter ^ swap) * quarter + tap % quarter

    def products(layer, start):
        at = pl.ds(start, slab.chunk)
        slope = jnp.concatenate([slopes[layer, micro, at, :] for micro in range(slab.micros)])
        moved = [pltpu.roll(slope, slope.shape[0] - 1, 0), slope, pltpu.roll(slope, 1, 0)]
        terms = [split_terms(value) for value in moved]
        left_hi = jnp.concatenate([hi for hi, lo in terms], axis=1)
        left_lo = jnp.concatenate([lo for hi, lo in terms], axis=1)
        pieces = [slab.pieces_of(acts, layer, micro, start) for micro in range(slab.micros)]
        pieces = [jnp.concatenate(parts, axis=0) for parts in zip(*pieces)]
        full = jnp.concatenate(pieces, axis=1)
        high = jnp.concatenate([piece[:, :LANES] for piece in pieces], axis=1)
        over_rows = (((0,), (0,)), ((), ()))
        one = lax.dot_general(left_hi, full, over_rows, preferred_element_type=F32)
        two = lax.dot_general(left_lo, high, over_rows, preferred_element_type=F32)
        total = []
        for b in range(3):
            hi = one[:, 2 * b * LANES : (2 * b + 1) * LANES]
            lo = one[:, (2 * b + 1) * LANES : (2 * b + 2) * LANES]
            total.append(hi + lo + two[:, b * LANES : (b + 1) * LANES])
        return total, jnp.sum(slope, axis=0, keepdims=True)

    sums[spot(TAPS)] = jnp.zeros((chans, LANES), F32)
    for slot in range(2):
        layer = 2 * slab.section + slot
        if slab.chunks == 1:
            total, row = products(layer, 0)
        else:
            acc[...] = jnp.zeros(acc.shape, F32)

            def gather(start):
                total, row = products(layer, start)
                for b in range(3):
                    acc[0 : 3 * LANES, b * LANES : (b + 1) * LANES] += total[b]
                acc[3 * LANES : 3 * LANES + 1, 0:LANES] += row

            slab.over_chunks(gather)
            total = [acc[0 : 3 * LANES, b * LANES : (b + 1) * LANES] for b in range(3)]
            row = acc[3 * LANES : 3 * LANES + 1, 0:LANES]
        lanes = slice(slot * chans, (slot + 1) * chans)
        for b in range(3):
            for c in range(3):
                block = total[b][c * LANES : (c + 1) * LANES] * scale
                tap = 3 * b + c
                sums[spot(tap), :, lanes] = block[chans:, :chans]
                sums[spot(9 + tap), :, lanes] = block[:chans, :chans] + block[chans:, chans:]
                sums[spot(18 + tap), :, lanes] = block[:chans, chans:]
        row = row * scale
        sums[spot(TAPS), 0:1, lanes] = row[:, :chans] + row[:, chans:]


def unpack_kernel(near, core, weight, bias, whole):
    part = near.shape[0] // 4
    chans = weight.shape[-1]
    odd, swap = lax.axis_index("gy") % 2, column_bits()
    for index in range(8):
        source = near if index < 4 else core
        first = index % 4 * part
        at = ((index // 2 ^ swap) * 2 + (index % 2 ^ odd)) * part
        whole[pl.ds(pl.multiple_of(at, 8), part), :] = source[first : first + part, :]
    for layer in range(2):
        lanes = slice(layer * chans, (layer + 1) * chans)
        for tap in range(TAPS):
            weight[layer, tap] = whole[tap * chans : (tap + 1) * chans, lanes]
        bias[layer : layer + 1, :] = whole[TAPS * chans : TAPS * chans + 1, lanes]


def restore_kernel(dims, *refs):
    micros, chans, size_x, local_y, width = dims
    pieces, (*targets, whole) = refs[:-3], refs[-3:]
    slab = lax.axis_index("gy")
    step = size_x * local_y
    slabs = len(pieces) // 2
    for slot, target in enumerate(targets):
        for micro in range(micros):
            for y in range(local_y):
                for turn in range(slabs):
                    start = (slab ^ turn) * width
                    if width % 8 == 0:
                        start = pl.multiple_of(start, 8)
                    rows = pl.ds(start, width)
                    whole[slot, micro, y, rows, :] = pieces[slot * slabs + turn][micro, y]
                block = whole[slot, micro, y].T
                for x in range(size_x):
                    first = micro * chans * step + x * local_y + y
                    part = block[x * chans : (x + 1) * chans]
                    target[pl.ds(first, chans, stride=step), :] = part


def spread(blocks):
    slabs = len(blocks)
    if slabs <= 8:
        got = [blocks[0]]
        for turn in range(1, slabs):
            route = [(i, i ^ turn) for i in range(slabs)]
            got.append(lax.ppermute(blocks[turn], "gy", route))
        return got
    order = jnp.arange(slabs) ^ lax.axis_index("gy")
    got = lax.all_to_all(jnp.stack(blocks)[order], "gy", 0, 0)[order]
    return [got[turn] for turn in range(slabs)]


def swapped(block, bit, axis="gz"):
    return lax.ppermute(block, axis, [(i, i ^ bit) for i in range(lax.axis_size(axis))])


def crossed(block):
    return lax.ppermute(block, "section", [(0, 1), (1, 0)])


def around(above, beside, across):
    slabs, columns = lax.axis_size("gy"), lax.axis_size("gz")
    route = [
        (i * columns + g, (i ^ 1) * columns + (g ^ 2)) for i in range(slabs) for g in range(columns)
    ]
    beside = swapped(beside, 2)
    across = lax.ppermute(across, ("gy", "gz"), route)
    return [swapped(above, 1, "gy"), beside, across]


def per_device(inflow, weights, biases, cotangent):
    micros, chans, size_x, local_y, local_z = inflow.shape
    assert micros == lax.axis_size("section") == 2
    slabs, columns = lax.axis_size("gy"), lax.axis_size("gz")
    rows_y = local_y * slabs
    width = local_z // slabs
    span = width + 2 * HALO
    depth = -(-span // 16) * 16
    chunk_y = max(n for n in range(1, rows_y + 1) if rows_y % n == 0 and n * depth <= 384)
    scale = 1.0 / math.sqrt(micros * size_x * rows_y * local_z * columns)
    rows = micros * chans * size_x * local_y
    blocks = [inflow.reshape(rows, local_z), cotangent.reshape(rows, local_z)]
    ends = ((2, micros, local_y, HALO, LANES), F32)
    fields, pair, inner = call(
        functools.partial(turn_kernel, inflow.shape),
        "turn",
        [((2, micros, local_y, local_z, LANES), F32), ends, ends],
        blocks,
    )
    packs = [((BLOCKS, chans, LANES), F32), ((BLOCKS // 2, chans, LANES), F32)]
    own, sent = call(pack_kernel, "pack", packs, [weights, biases])
    pair = swapped(pair, 1)
    route = [(i, i + 1) for i in range(1, columns - 1, 2)]
    inner = lax.ppermute(inner, "gz", route + [(after, before) for before, after in route])
    windows = call(
        functools.partial(window_kernel, (slabs, width, columns)),
        "windows",
        [((local_y, sum(width + 2 * halo for halo in HALOS), LANES), F32)] * (slabs + 1),
        [fields, pair, inner],
        [pltpu.VMEM((2, micros, local_y, local_z + 2 * HALO, LANES), F32)],
    )
    sent, windows = lax.optimization_barrier((sent, windows))
    near_half = crossed(sent)
    *mine, home = windows
    mine = spread(mine)

    tables = [((2, 15 * LANES, 2 * LANES), BF16)] * 2 + [((2, 8, LANES), F32)]
    own_fwd, own_bwd, own_row = call(table_kernel, "own_table", tables, [own])
    if slabs <= 8:
        theirs = [home] + [crossed(window) for window in mine[1:]]
    else:
        theirs = list(crossed(jnp.stack(mine)))
    windows = mine + theirs
    gate = [theirs[1], *mine[2:]]
    near_half, own_row, *_ = lax.optimization_barrier((near_half, own_row, *gate))
    far_half = swapped(near_half, 1)
    far_fwd, far_bwd, far_row = call(table_kernel, "far_table", tables, [near_half, far_half])

    dims = (micros, rows_y, depth, width, chunk_y, slabs, local_z * columns)
    padded = (rows_y + 2) * depth
    full = rows_y * depth
    piece = ((micros, local_y, width, LANES), F32)
    acts, kept, *fronts = call(
        functools.partial(forward_kernel, dims),
        "forward",
        [((5, micros, padded, 2 * LANES), BF16), ((4, micros, full, LANES), F32)] + [piece] * slabs,
        [own_fwd, own_row, far_fwd, far_row, *windows],
        [pltpu.VMEM((micros, full, LANES), F32)] * 2,
    )
    if slabs == 4:
        passed = swapped(fronts[3], 2, "gy")
    *backs, sums = call(
        functools.partial(backward_kernel, dims, scale),
        "backward",
        [piece] * slabs + [((BLOCKS, chans, LANES), F32)],
        [own_bwd, far_bwd, acts, kept, *windows],
        [
            pltpu.VMEM((2, micros, padded, 2 * LANES), BF16),
            pltpu.VMEM((4, micros, full, LANES), F32),
            pltpu.VMEM((micros, full, LANES), F32),
            pltpu.VMEM((3 * LANES + 8, 3 * LANES), F32),
        ],
        12 * micros * full * 9 * LANES * 3 * LANES,
    )
    if slabs == 4:
        sums, passed = lax.optimization_barrier((sums, passed))

    block = sums.reshape(BLOCKS * chans, LANES)
    half = block.shape[0] // 2
    block = block[:half] + swapped(block[half:], 1)
    block, fronts, backs = lax.optimization_barrier((block, fronts, backs))
    if slabs == 4:
        outs = [
            swapped(jnp.stack([fronts[1], passed, backs[1]]), 1, "gy"),
            swapped(backs[3], 3, "gy"),
        ]
    else:
        outs = spread([jnp.stack(pair) for pair in zip(fronts, backs)])
    part = half // 4
    block = block[: 2 * part] + swapped(block[2 * part :], 2)
    block, outs = lax.optimization_barrier((block, outs))
    odd = lax.axis_index("gy") % 2 == 1
    kept = jnp.where(odd, block[part:], block[:part])
    kept = kept + swapped(jnp.where(odd, block[:part], block[part:]), 1, "gy")
    bit = 2
    while bit < slabs:
        kept = kept + swapped(kept, bit, "gy")
        bit *= 2
    if slabs == 4:
        kept, far = lax.optimization_barrier((kept, [fronts[2], backs[2]]))
        far = swapped(jnp.stack(far), 2, "gy")
    near = jnp.concatenate([kept, *around(kept, kept, kept)], axis=0)
    if slabs == 4:
        near, far = lax.optimization_barrier((near, far))
        (first, relayed, back), last = outs
        outs = [fronts[0], first, far[0], relayed, backs[0], back, far[1], last]
    else:
        outs = [out[slot] for slot in range(2) for out in outs]
    core = swapped(near, 1)
    section_out, section_grad = call(
        functools.partial(restore_kernel, (micros, chans, size_x, local_y, width)),
        "restore",
        [((rows, local_z), F32)] * 2,
        outs,
        [pltpu.VMEM((2, micros, local_y, local_z, LANES), F32)],
    )
    weight_total, bias_total = call(
        unpack_kernel,
        "unpack",
        [((2, TAPS, chans, chans), F32), ((2, chans), F32)],
        [near, core],
        [pltpu.VMEM((BLOCKS * chans, LANES), F32)],
    )
    shape = (1, *inflow.shape)
    return (section_out.reshape(shape), section_grad.reshape(shape), weight_total, bias_total)


def solution(mesh):
    grid = P(None, None, None, "gy", "gz")
    section_grid = P("section", None, None, None, "gy", "gz")
    return jax.shard_map(
        per_device,
        mesh=mesh,
        in_specs=(grid, P("section", None, None, None), P("section", None), grid),
        out_specs=(section_grid, section_grid, P("section", None, None, None), P("section", None)),
        check_vma=False,
    )
```

```python
import functools
import math

import jax
import jax.numpy as jnp
from jax import lax
from jax.experimental import pallas as pl
from jax.experimental.pallas import tpu as pltpu
from jax.sharding import PartitionSpec as P

HALO = 8
HALOS = (8, 4)
LANES = 128
TAPS = 27
BLOCKS = 28
BF16 = jnp.bfloat16
F32 = jnp.float32
VMEM = pl.BlockSpec(memory_space=pltpu.VMEM)


def call(kernel, name, outs, args, scratch=(), flops=0):
    arrays = [jax.ShapeDtypeStruct(shape, kind) for shape, kind in outs]
    size = sum(math.prod(item.shape) * item.dtype.itemsize for item in [*arrays, *args, *scratch])
    return pl.pallas_call(
        kernel,
        out_shape=arrays,
        in_specs=[VMEM] * len(args),
        out_specs=[VMEM] * len(arrays),
        scratch_shapes=list(scratch),
        compiler_params=pltpu.CompilerParams(vmem_limit_bytes=size + 6 * 1024 * 1024),
        cost_estimate=pl.CostEstimate(flops=flops, bytes_accessed=1024, transcendentals=0),
        name=name,
    )(*args)


def column_bits():
    column = lax.axis_index("gz")
    return 2 * (column % 2) + column // 2 % 2


def split_terms(values):
    high = values.astype(BF16)
    return high, (values - high.astype(F32)).astype(BF16)


def pack_kernel(weights, biases, own, sent):
    chans = weights.shape[2]
    for tap in range(TAPS):
        own[tap] = jnp.concatenate([weights[0, tap], weights[1, tap]], axis=1)
    own[TAPS] = jnp.zeros((chans, LANES), F32)
    own[TAPS, 0:1, :] = jnp.concatenate([biases[0:1, :], biases[1:2, :]], axis=1)
    half = sent.shape[0]
    start = lax.axis_index("gz") % 2 * half
    for index in range(half):
        sent[index] = own[start + index]


def turned_rows(dims, source, micro, y):
    _, chans, size_x, local_y, _ = dims
    step = size_x * local_y
    first = micro * chans * step + y
    parts = [source[pl.ds(first + x * local_y, chans, stride=step), :] for x in range(size_x)]
    return jnp.concatenate(parts, axis=0).T


def turn_kernel(dims, inflow, cotangent, rows, pair, inner):
    micros, _, _, local_y, local_z = dims
    odd = lax.axis_index("gz") % 2 == 1
    for field, source in enumerate((inflow, cotangent)):
        for micro in range(micros):
            for y in range(local_y):
                turned = turned_rows(dims, source, micro, y)
                rows[field, micro, y] = turned
                low, high = turned[:HALO], turned[local_z - HALO :]
                pair[field, micro, y] = jnp.where(odd, low, high)
                inner[field, micro, y] = jnp.where(odd, high, low)


def window_kernel(dims, rows, pair, inner, *refs):
    slabs, width, columns = dims
    outs, wide = refs[:-1], refs[-1]
    slab, column = lax.axis_index("gy"), lax.axis_index("gz")
    section = lax.axis_index("section")
    odd = column % 2 == 1
    _, micros, local_y, local_z, _ = rows.shape
    for field, halo in enumerate(HALOS):
        at = slice(0, width + 2 * halo) if field == 0 else slice(width + 2 * HALO, None)
        for y in range(local_y):
            for micro in range(micros):
                one, two = pair[field, micro, y], inner[field, micro, y]
                before = jnp.where(column > 0, jnp.where(odd, one, two), 0.0)
                after = jnp.where(column < columns - 1, jnp.where(odd, two, one), 0.0)
                wide[field, micro, y, :HALO] = before
                wide[field, micro, y, HALO : HALO + local_z] = rows[field, micro, y]
                wide[field, micro, y, HALO + local_z :] = after
            for turn, out in enumerate(outs):
                start = (slab ^ turn % slabs) * width + HALO - halo
                if width % 8 == 0 and halo % 8 == 0:
                    start = pl.multiple_of(start, 8)
                micro = section if turn < slabs else 1 - section
                out[y, at] = wide[field, micro, y, pl.ds(start, width + 2 * halo)]


def table_kernel(*refs):
    parts, (fwd, bwd, row) = refs[:-3], refs[-3:]
    odd = lax.axis_index("gz") % 2
    count, chans, _ = parts[0].shape

    def block_of(tap):
        if len(parts) == 1:
            return parts[0][tap]
        index = tap % count
        return jnp.where(odd == tap // count, parts[0][index], parts[1][index])

    for b in range(3):
        for c in range(3):
            taps = [block_of(9 * a + 3 * b + c) for a in range(3)]
            for layer in range(2):
                own_lanes = slice(layer * chans, (layer + 1) * chans)
                below, level, above = [tap[:, own_lanes] for tap in taps]
                top = jnp.concatenate([level, above], axis=1)
                low = jnp.concatenate([below, level], axis=1)
                block = jnp.concatenate([top, low], axis=0)
                for target, value, r, at in ((fwd, block.T, b, c), (bwd, block, 2 - b, 2 - c)):
                    hi, lo = split_terms(value)
                    if at == 1:
                        for row_at in (9 + 2 * r, 10 + 2 * r):
                            rows = slice(row_at * LANES, (row_at + 1) * LANES)
                            target[layer, rows, 0:LANES] = hi
                            target[layer, rows, LANES : 2 * LANES] = lo
                    else:
                        lanes = slice(at // 2 * LANES, (at // 2 + 1) * LANES)
                        for row_at, term in ((2 * r, hi), (2 * r + 1, hi), (6 + r, lo)):
                            rows = slice(row_at * LANES, (row_at + 1) * LANES)
                            target[layer, rows, lanes] = term
    last = block_of(TAPS)[0:1, :]
    for layer in range(2):
        part = last[:, layer * chans : (layer + 1) * chans]
        row[layer] = jnp.broadcast_to(jnp.concatenate([part, part], axis=1), (8, LANES))


class Slab:
    def __init__(self, dims):
        self.micros, self.rows_y, self.depth, self.width, self.chunk_y, self.slabs, limit_z = dims
        self.section, self.slab = lax.axis_index("section"), lax.axis_index("gy")
        origin = (lax.axis_index("gz") * self.slabs + self.slab) * self.width - HALO
        self.chunk = self.chunk_y * self.depth
        self.chunks = self.rows_y // self.chunk_y
        self.per_owner = self.rows_y // self.slabs
        zs = lax.broadcasted_iota(jnp.int32, (self.depth, LANES), 0)
        inside = (zs + origin >= 0) & (zs + origin < limit_z)
        self.in_grid = inside.astype(F32)[None]
        self.mine = ((zs >= HALO) & (zs < HALO + self.width)).astype(F32)[None]

    def over_chunks(self, body):
        if self.chunks == 1:
            body(0)
        else:

            def step(part, carry):
                body(pl.multiple_of(part * self.chunk, 16))
                return carry

            lax.fori_loop(0, self.chunks, step, 0)

    def masked(self, values, mask):
        return (values.reshape(-1, self.depth, LANES) * mask).reshape(values.shape)

    def put_rows(self, target, lead, micro, start, values):
        hi, lo = split_terms(values)
        at = pl.ds(start + self.depth, self.chunk)
        target[lead, micro, at, slice(0, LANES)] = hi
        target[lead, micro, at, slice(LANES, 2 * LANES)] = lo

    def pieces_of(self, source, lead, micro, start):
        return [
            source[lead, micro, pl.ds(start + b * self.depth, self.chunk), :] for b in range(3)
        ]

    def conv(self, source, lead, start, table):
        lefts = []
        for micro in range(self.micros):
            pieces = self.pieces_of(source, lead, micro, start)
            lefts.append(jnp.concatenate(pieces + [piece[:, :LANES] for piece in pieces], axis=1))
        results = []
        for left in lefts:
            outer = jnp.dot(left, table[0 : 9 * LANES, :], preferred_element_type=F32)
            middle = jnp.dot(
                left[:, 0 : 6 * LANES],
                table[9 * LANES : 15 * LANES, :],
                preferred_element_type=F32,
            )
            before = pltpu.roll(outer[:, :LANES], 1, 0)
            after = pltpu.roll(outer[:, LANES:], outer.shape[0] - 1, 0)
            results.append(before + (middle[:, :LANES] + middle[:, LANES:]) + after)
        return results

    def by_owner(self, layer, own, other, body):
        mine = layer // 2 == self.section
        pl.when(mine)(lambda: body(own, layer % 2))
        pl.when(jnp.logical_not(mine))(lambda: body(other, layer % 2))

    def blank_edges(self, target):
        blank = jnp.zeros((self.depth, 2 * LANES), BF16)
        for lead in range(target.shape[0]):
            for micro in range(self.micros):
                for edge in (0, self.rows_y + 1):
                    target[lead, micro, edge * self.depth : (edge + 1) * self.depth, :] = blank

    def fill(self, field, windows, which):
        halo = HALOS[which]
        span = self.width + 2 * halo
        at = 0 if which == 0 else self.width + 2 * HALO
        extra = [HALO - halo, self.depth - span - (HALO - halo)]
        for index, window in enumerate(windows):
            owner = self.slab ^ index % self.slabs
            micro = self.section if index < self.slabs else 1 - self.section
            for y in range(self.per_owner):
                blanks = [jnp.zeros((rows, LANES), F32) for rows in extra]
                parts = [blanks[0], window[y, at : at + span], blanks[1]]
                parts = [part for part in parts if part.shape[0]]
                start = pl.multiple_of((owner * self.per_owner + y) * self.depth, 16)
                value = jnp.concatenate(parts, axis=0) if len(parts) > 1 else parts[0]
                field[micro, pl.ds(start, self.depth), :] = value

    def cut_out(self, targets, source):
        for turn, target in enumerate(targets):
            owner = self.slab ^ turn
            for micro in range(self.micros):
                for y in range(self.per_owner):
                    start = (owner * self.per_owner + y) * self.depth + HALO
                    rows = pl.ds(pl.multiple_of(start, 8), self.width)
                    target[micro, y] = source[micro, rows, :]


def forward_kernel(dims, own, own_row, other, other_row, *refs):
    slab = Slab(dims)
    windows, (acts, kept, *outs), (whole, field) = (
        refs[: 2 * slab.slabs],
        refs[2 * slab.slabs : -2],
        refs[-2:],
    )
    slab.blank_edges(acts)
    slab.fill(field, windows, 0)

    def take_in(start):
        for micro in range(slab.micros):
            slab.put_rows(acts, 0, micro, start, field[micro, pl.ds(start, slab.chunk), :])

    slab.over_chunks(take_in)

    def layer_step(layer, carry):
        def run(tables, half):
            table, row = tables

            def body(start):
                at = pl.ds(start, slab.chunk)
                sums = slab.conv(acts, layer, start, table.at[half])
                values = []
                for micro, total in enumerate(sums):
                    pre = total + row[half][0:1, :]
                    sigma = 1.0 / (1.0 + jnp.exp(-pre))
                    kept[layer, micro, at, :] = sigma * (1.0 + pre * (1.0 - sigma))
                    out = slab.masked(pre * sigma, slab.in_grid)
                    slab.put_rows(acts, layer + 1, micro, start, out)
                    values.append(out)

                @pl.when(layer == 2 * slab.section + 1)
                def _():
                    for micro, value in enumerate(values):
                        whole[micro, at, :] = value

            slab.over_chunks(body)

        slab.by_owner(layer, (own, own_row), (other, other_row), run)
        return carry

    lax.fori_loop(0, 4, layer_step, 0)
    slab.cut_out(outs, whole)


def backward_kernel(dims, scale, own, other, acts, kept, *refs):
    slab = Slab(dims)
    windows, refs = refs[: 2 * slab.slabs], refs[2 * slab.slabs :]
    outs, (sums, rim, slopes, field, acc) = refs[: slab.slabs], refs[slab.slabs :]
    slab.blank_edges(rim)
    slab.fill(field, windows, 1)

    def take_gradient(layer, micro, start, gradient):
        at = pl.ds(start, slab.chunk)
        slope = slab.masked(gradient * kept[layer, micro, at, :], slab.in_grid)
        slopes[layer, micro, at, :] = slab.masked(slope, slab.mine)
        slab.put_rows(rim, layer % 2, micro, start, slope)

    def take_cotangent(start):
        for micro in range(slab.micros):
            take_gradient(3, micro, start, field[micro, pl.ds(start, slab.chunk), :])

    slab.over_chunks(take_cotangent)

    def layer_step(index, carry):
        layer = 3 - index

        def run(table, half):
            def body(start):
                gradients = slab.conv(rim, layer % 2, start, table.at[half])
                last = layer == 2 * slab.section

                @pl.when(last)
                def _():
                    for micro, gradient in enumerate(gradients):
                        field[micro, pl.ds(start, slab.chunk), :] = gradient

                @pl.when(jnp.logical_not(last))
                def _():
                    for micro, gradient in enumerate(gradients):
                        take_gradient(layer - 1, micro, start, gradient)

            slab.over_chunks(body)

        slab.by_owner(layer, own, other, run)
        return carry

    lax.fori_loop(0, jnp.where(slab.section == 0, 4, 2), layer_step, 0)
    slab.cut_out(outs, field)

    quarter = BLOCKS // 4
    chans = LANES // 2
    swap = column_bits()

    def spot(tap):
        return (tap // quarter ^ swap) * quarter + tap % quarter

    def products(layer, start):
        at = pl.ds(start, slab.chunk)
        slope = jnp.concatenate([slopes[layer, micro, at, :] for micro in range(slab.micros)])
        moved = [pltpu.roll(slope, slope.shape[0] - 1, 0), slope, pltpu.roll(slope, 1, 0)]
        terms = [split_terms(value) for value in moved]
        left_hi = jnp.concatenate([hi for hi, lo in terms], axis=1)
        left_lo = jnp.concatenate([lo for hi, lo in terms], axis=1)
        pieces = [slab.pieces_of(acts, layer, micro, start) for micro in range(slab.micros)]
        pieces = [jnp.concatenate(parts, axis=0) for parts in zip(*pieces)]
        full = jnp.concatenate(pieces, axis=1)
        high = jnp.concatenate([piece[:, :LANES] for piece in pieces], axis=1)
        over_rows = (((0,), (0,)), ((), ()))
        one = lax.dot_general(left_hi, full, over_rows, preferred_element_type=F32)
        two = lax.dot_general(left_lo, high, over_rows, preferred_element_type=F32)
        total = []
        for b in range(3):
            hi = one[:, 2 * b * LANES : (2 * b + 1) * LANES]
            lo = one[:, (2 * b + 1) * LANES : (2 * b + 2) * LANES]
            total.append(hi + lo + two[:, b * LANES : (b + 1) * LANES])
        return total, jnp.sum(slope, axis=0, keepdims=True)

    sums[spot(TAPS)] = jnp.zeros((chans, LANES), F32)
    for slot in range(2):
        layer = 2 * slab.section + slot
        if slab.chunks == 1:
            total, row = products(layer, 0)
        else:
            acc[...] = jnp.zeros(acc.shape, F32)

            def gather(start):
                total, row = products(layer, start)
                for b in range(3):
                    acc[0 : 3 * LANES, b * LANES : (b + 1) * LANES] += total[b]
                acc[3 * LANES : 3 * LANES + 1, 0:LANES] += row

            slab.over_chunks(gather)
            total = [acc[0 : 3 * LANES, b * LANES : (b + 1) * LANES] for b in range(3)]
            row = acc[3 * LANES : 3 * LANES + 1, 0:LANES]
        lanes = slice(slot * chans, (slot + 1) * chans)
        for b in range(3):
            for c in range(3):
                block = total[b][c * LANES : (c + 1) * LANES] * scale
                tap = 3 * b + c
                sums[spot(tap), :, lanes] = block[chans:, :chans]
                sums[spot(9 + tap), :, lanes] = block[:chans, :chans] + block[chans:, chans:]
                sums[spot(18 + tap), :, lanes] = block[:chans, chans:]
        row = row * scale
        sums[spot(TAPS), 0:1, lanes] = row[:, :chans] + row[:, chans:]


def unpack_kernel(*refs):
    sources, (weight, bias, whole) = refs[:-3], refs[-3:]
    part = sources[0].shape[0] // 4
    chans = weight.shape[-1]
    odd, swap = lax.axis_index("gy") % 2, column_bits()
    for number, source in enumerate(sources):
        for index in range(4):
            quarter = number // 2 * 2 + index // 2
            at = (((quarter ^ swap) * 2 + (index % 2 ^ odd)) * 2 + number % 2) * part
            rows = source[index * part : (index + 1) * part, :]
            whole[pl.ds(pl.multiple_of(at, 8), part), :] = rows
    for layer in range(2):
        lanes = slice(layer * chans, (layer + 1) * chans)
        for tap in range(TAPS):
            weight[layer, tap] = whole[tap * chans : (tap + 1) * chans, lanes]
        bias[layer : layer + 1, :] = whole[TAPS * chans : TAPS * chans + 1, lanes]


def restore_kernel(dims, *refs):
    micros, chans, size_x, local_y, width = dims
    pieces, (*targets, whole) = refs[:-3], refs[-3:]
    slab = lax.axis_index("gy")
    step = size_x * local_y
    slabs = len(pieces) // 2
    for slot, target in enumerate(targets):
        for micro in range(micros):
            for y in range(local_y):
                for turn in range(slabs):
                    start = (slab ^ turn) * width
                    if width % 8 == 0:
                        start = pl.multiple_of(start, 8)
                    rows = pl.ds(start, width)
                    whole[slot, micro, y, rows, :] = pieces[slot * slabs + turn][micro, y]
                block = whole[slot, micro, y].T
                for x in range(size_x):
                    first = micro * chans * step + x * local_y + y
                    part = block[x * chans : (x + 1) * chans]
                    target[pl.ds(first, chans, stride=step), :] = part


def spread(blocks):
    slabs = len(blocks)
    if slabs <= 8:
        got = [blocks[0]]
        for turn in range(1, slabs):
            route = [(i, i ^ turn) for i in range(slabs)]
            got.append(lax.ppermute(blocks[turn], "gy", route))
        return got
    order = jnp.arange(slabs) ^ lax.axis_index("gy")
    got = lax.all_to_all(jnp.stack(blocks)[order], "gy", 0, 0)[order]
    return [got[turn] for turn in range(slabs)]


def swapped(block, bit, axis="gz"):
    return lax.ppermute(block, axis, [(i, i ^ bit) for i in range(lax.axis_size(axis))])


def crossed(block):
    return lax.ppermute(block, "section", [(0, 1), (1, 0)])


def around(above, beside, across):
    slabs, columns = lax.axis_size("gy"), lax.axis_size("gz")
    route = [
        (i * columns + g, (i ^ 1) * columns + (g ^ 2)) for i in range(slabs) for g in range(columns)
    ]
    beside = swapped(beside, 2)
    across = lax.ppermute(across, ("gy", "gz"), route)
    return [swapped(above, 1, "gy"), beside, across]


def per_device(inflow, weights, biases, cotangent):
    micros, chans, size_x, local_y, local_z = inflow.shape
    assert micros == lax.axis_size("section") == 2
    slabs, columns = lax.axis_size("gy"), lax.axis_size("gz")
    rows_y = local_y * slabs
    width = local_z // slabs
    span = width + 2 * HALO
    depth = -(-span // 16) * 16
    chunk_y = max(n for n in range(1, rows_y + 1) if rows_y % n == 0 and n * depth <= 384)
    scale = 1.0 / math.sqrt(micros * size_x * rows_y * local_z * columns)
    rows = micros * chans * size_x * local_y
    blocks = [inflow.reshape(rows, local_z), cotangent.reshape(rows, local_z)]
    ends = ((2, micros, local_y, HALO, LANES), F32)
    fields, pair, inner = call(
        functools.partial(turn_kernel, inflow.shape),
        "turn",
        [((2, micros, local_y, local_z, LANES), F32), ends, ends],
        blocks,
    )
    packs = [((BLOCKS, chans, LANES), F32), ((BLOCKS // 2, chans, LANES), F32)]
    own, sent = call(pack_kernel, "pack", packs, [weights, biases])
    pair = swapped(pair, 1)
    route = [(i, i + 1) for i in range(1, columns - 1, 2)]
    inner = lax.ppermute(inner, "gz", route + [(after, before) for before, after in route])
    windows = call(
        functools.partial(window_kernel, (slabs, width, columns)),
        "windows",
        [((local_y, sum(width + 2 * halo for halo in HALOS), LANES), F32)] * (slabs + 1),
        [fields, pair, inner],
        [pltpu.VMEM((2, micros, local_y, local_z + 2 * HALO, LANES), F32)],
    )
    sent, windows = lax.optimization_barrier((sent, windows))
    near_half = crossed(sent)
    *mine, home = windows
    mine = spread(mine)

    tables = [((2, 15 * LANES, 2 * LANES), BF16)] * 2 + [((2, 8, LANES), F32)]
    own_fwd, own_bwd, own_row = call(table_kernel, "own_table", tables, [own])
    if slabs <= 8:
        theirs = [home] + [crossed(window) for window in mine[1:]]
    else:
        theirs = list(crossed(jnp.stack(mine)))
    windows = mine + theirs
    gate = [theirs[1], *mine[2:]]
    near_half, own_row, *_ = lax.optimization_barrier((near_half, own_row, *gate))
    far_half = swapped(near_half, 1)
    far_fwd, far_bwd, far_row = call(table_kernel, "far_table", tables, [near_half, far_half])

    dims = (micros, rows_y, depth, width, chunk_y, slabs, local_z * columns)
    padded = (rows_y + 2) * depth
    full = rows_y * depth
    piece = ((micros, local_y, width, LANES), F32)
    acts, kept, *fronts = call(
        functools.partial(forward_kernel, dims),
        "forward",
        [((5, micros, padded, 2 * LANES), BF16), ((4, micros, full, LANES), F32)] + [piece] * slabs,
        [own_fwd, own_row, far_fwd, far_row, *windows],
        [pltpu.VMEM((micros, full, LANES), F32)] * 2,
    )
    if slabs == 4:
        passed = swapped(jnp.stack(fronts[2:]), 2, "gy")
    *backs, sums = call(
        functools.partial(backward_kernel, dims, scale),
        "backward",
        [piece] * slabs + [((BLOCKS, chans, LANES), F32)],
        [own_bwd, far_bwd, acts, kept, *windows],
        [
            pltpu.VMEM((2, micros, padded, 2 * LANES), BF16),
            pltpu.VMEM((4, micros, full, LANES), F32),
            pltpu.VMEM((micros, full, LANES), F32),
            pltpu.VMEM((3 * LANES + 8, 3 * LANES), F32),
        ],
        12 * micros * full * 9 * LANES * 3 * LANES,
    )
    if slabs == 4:
        sums, passed = lax.optimization_barrier((sums, passed))

    part = BLOCKS * chans // 16
    blocks = sums.reshape(8, 2, part, LANES)
    odd = lax.axis_index("gy") % 2 == 1
    streams = []
    for stream in range(2):
        block = blocks[:, stream].reshape(8 * part, LANES)
        streams.append(block[: 4 * part] + swapped(block[4 * part :], 1))
    streams[0], fronts, backs = lax.optimization_barrier((streams[0], fronts, backs))
    if slabs == 4:
        near = swapped(jnp.stack([fronts[1], passed[1], backs[1]]), 1, "gy")
        outs = [near, swapped(backs[2], 2, "gy"), swapped(backs[3], 3, "gy")]
    else:
        outs = spread([jnp.stack(pair) for pair in zip(fronts, backs)])
    streams = [block[: 2 * part] + swapped(block[2 * part :], 2) for block in streams]
    streams[1], outs = lax.optimization_barrier((streams[1], outs))
    sums = []
    for block in streams:
        kept = jnp.where(odd, block[part:], block[:part])
        kept = kept + swapped(jnp.where(odd, block[:part], block[part:]), 1, "gy")
        bit = 2
        while bit < slabs:
            kept = kept + swapped(kept, bit, "gy")
            bit *= 2
        sums.append(jnp.concatenate([kept, *around(kept, kept, kept)], axis=0))
    sums += [swapped(block, 1) for block in sums]
    if slabs == 4:
        outs = [fronts[0], outs[0][0], passed[0], outs[0][1], backs[0], outs[0][2], *outs[1:]]
    else:
        outs = [out[slot] for slot in range(2) for out in outs]
    section_out, section_grad = call(
        functools.partial(restore_kernel, (micros, chans, size_x, local_y, width)),
        "restore",
        [((rows, local_z), F32)] * 2,
        outs,
        [pltpu.VMEM((2, micros, local_y, local_z, LANES), F32)],
    )
    weight_total, bias_total = call(
        unpack_kernel,
        "unpack",
        [((2, TAPS, chans, chans), F32), ((2, chans), F32)],
        sums,
        [pltpu.VMEM((BLOCKS * chans, LANES), F32)],
    )
    shape = (1, *inflow.shape)
    return (section_out.reshape(shape), section_grad.reshape(shape), weight_total, bias_total)


def solution(mesh):
    grid = P(None, None, None, "gy", "gz")
    section_grid = P("section", None, None, None, "gy", "gz")
    return jax.shard_map(
        per_device,
        mesh=mesh,
        in_specs=(grid, P("section", None, None, None), P("section", None), grid),
        out_specs=(section_grid, section_grid, P("section", None, None, None), P("section", None)),
        check_vma=False,
    )
```

```python
import functools
import math

import jax
import jax.numpy as jnp
from jax import lax
from jax.experimental import pallas as pl
from jax.experimental.pallas import tpu as pltpu
from jax.sharding import PartitionSpec as P

HALO = 8
HALOS = (8, 4)
LANES = 128
TAPS = 27
BLOCKS = 28
BF16 = jnp.bfloat16
F32 = jnp.float32
VMEM = pl.BlockSpec(memory_space=pltpu.VMEM)


def call(kernel, name, outs, args, scratch=(), flops=0):
    arrays = [jax.ShapeDtypeStruct(shape, kind) for shape, kind in outs]
    size = sum(math.prod(item.shape) * item.dtype.itemsize for item in [*arrays, *args, *scratch])
    return pl.pallas_call(
        kernel,
        out_shape=arrays,
        in_specs=[VMEM] * len(args),
        out_specs=[VMEM] * len(arrays),
        scratch_shapes=list(scratch),
        compiler_params=pltpu.CompilerParams(vmem_limit_bytes=size + 6 * 1024 * 1024),
        cost_estimate=pl.CostEstimate(flops=flops, bytes_accessed=1024, transcendentals=0),
        name=name,
    )(*args)


def column_bits():
    column = lax.axis_index("gz")
    return 2 * (column % 2) + column // 2 % 2


def split_terms(values):
    high = values.astype(BF16)
    return high, (values - high.astype(F32)).astype(BF16)


def pack_kernel(weights, biases, own, sent):
    chans = weights.shape[2]
    for tap in range(TAPS):
        own[tap] = jnp.concatenate([weights[0, tap], weights[1, tap]], axis=1)
    own[TAPS] = jnp.zeros((chans, LANES), F32)
    own[TAPS, 0:1, :] = jnp.concatenate([biases[0:1, :], biases[1:2, :]], axis=1)
    half = sent.shape[0]
    start = lax.axis_index("gz") % 2 * half
    for index in range(half):
        sent[index] = own[start + index]


def turned_rows(dims, source, micro, y):
    _, chans, size_x, local_y, _ = dims
    step = size_x * local_y
    first = micro * chans * step + y
    parts = [source[pl.ds(first + x * local_y, chans, stride=step), :] for x in range(size_x)]
    return jnp.concatenate(parts, axis=0).T


def turn_kernel(dims, inflow, cotangent, rows, pair, inner):
    micros, _, _, local_y, local_z = dims
    odd = lax.axis_index("gz") % 2 == 1
    for field, source in enumerate((inflow, cotangent)):
        for micro in range(micros):
            for y in range(local_y):
                turned = turned_rows(dims, source, micro, y)
                rows[field, micro, y] = turned
                low, high = turned[:HALO], turned[local_z - HALO :]
                pair[field, micro, y] = jnp.where(odd, low, high)
                inner[field, micro, y] = jnp.where(odd, high, low)


def window_kernel(dims, rows, pair, inner, *refs):
    slabs, width, columns = dims
    outs, wide = refs[:-1], refs[-1]
    slab, column = lax.axis_index("gy"), lax.axis_index("gz")
    section = lax.axis_index("section")
    odd = column % 2 == 1
    _, micros, local_y, local_z, _ = rows.shape
    for field, halo in enumerate(HALOS):
        at = slice(0, width + 2 * halo) if field == 0 else slice(width + 2 * HALO, None)
        for y in range(local_y):
            for micro in range(micros):
                one, two = pair[field, micro, y], inner[field, micro, y]
                before = jnp.where(column > 0, jnp.where(odd, one, two), 0.0)
                after = jnp.where(column < columns - 1, jnp.where(odd, two, one), 0.0)
                wide[field, micro, y, :HALO] = before
                wide[field, micro, y, HALO : HALO + local_z] = rows[field, micro, y]
                wide[field, micro, y, HALO + local_z :] = after
            for turn, out in enumerate(outs):
                start = (slab ^ turn % slabs) * width + HALO - halo
                if width % 8 == 0 and halo % 8 == 0:
                    start = pl.multiple_of(start, 8)
                micro = section if turn < slabs else 1 - section
                out[y, at] = wide[field, micro, y, pl.ds(start, width + 2 * halo)]


def table_kernel(*refs):
    parts, (fwd, bwd, row) = refs[:-3], refs[-3:]
    odd = lax.axis_index("gz") % 2
    count, chans, _ = parts[0].shape

    def block_of(tap):
        if len(parts) == 1:
            return parts[0][tap]
        index = tap % count
        return jnp.where(odd == tap // count, parts[0][index], parts[1][index])

    for b in range(3):
        for c in range(3):
            taps = [block_of(9 * a + 3 * b + c) for a in range(3)]
            for layer in range(2):
                own_lanes = slice(layer * chans, (layer + 1) * chans)
                below, level, above = [tap[:, own_lanes] for tap in taps]
                top = jnp.concatenate([level, above], axis=1)
                low = jnp.concatenate([below, level], axis=1)
                block = jnp.concatenate([top, low], axis=0)
                for target, value, r, at in ((fwd, block.T, b, c), (bwd, block, 2 - b, 2 - c)):
                    hi, lo = split_terms(value)
                    if at == 1:
                        for row_at in (9 + 2 * r, 10 + 2 * r):
                            rows = slice(row_at * LANES, (row_at + 1) * LANES)
                            target[layer, rows, 0:LANES] = hi
                            target[layer, rows, LANES : 2 * LANES] = lo
                    else:
                        lanes = slice(at // 2 * LANES, (at // 2 + 1) * LANES)
                        for row_at, term in ((2 * r, hi), (2 * r + 1, hi), (6 + r, lo)):
                            rows = slice(row_at * LANES, (row_at + 1) * LANES)
                            target[layer, rows, lanes] = term
    last = block_of(TAPS)[0:1, :]
    for layer in range(2):
        part = last[:, layer * chans : (layer + 1) * chans]
        row[layer] = jnp.broadcast_to(jnp.concatenate([part, part], axis=1), (8, LANES))


class Slab:
    def __init__(self, dims):
        self.micros, self.rows_y, self.depth, self.width, self.chunk_y, self.slabs, limit_z = dims
        self.section, self.slab = lax.axis_index("section"), lax.axis_index("gy")
        origin = (lax.axis_index("gz") * self.slabs + self.slab) * self.width - HALO
        self.chunk = self.chunk_y * self.depth
        self.chunks = self.rows_y // self.chunk_y
        self.per_owner = self.rows_y // self.slabs
        zs = lax.broadcasted_iota(jnp.int32, (self.depth, LANES), 0)
        inside = (zs + origin >= 0) & (zs + origin < limit_z)
        self.in_grid = inside.astype(F32)[None]
        self.mine = ((zs >= HALO) & (zs < HALO + self.width)).astype(F32)[None]

    def over_chunks(self, body):
        if self.chunks == 1:
            body(0)
        else:

            def step(part, carry):
                body(pl.multiple_of(part * self.chunk, 16))
                return carry

            lax.fori_loop(0, self.chunks, step, 0)

    def masked(self, values, mask):
        return (values.reshape(-1, self.depth, LANES) * mask).reshape(values.shape)

    def put_rows(self, target, lead, micro, start, values):
        hi, lo = split_terms(values)
        at = pl.ds(start + self.depth, self.chunk)
        target[lead, micro, at, slice(0, LANES)] = hi
        target[lead, micro, at, slice(LANES, 2 * LANES)] = lo

    def pieces_of(self, source, lead, micro, start):
        return [
            source[lead, micro, pl.ds(start + b * self.depth, self.chunk), :] for b in range(3)
        ]

    def conv(self, source, lead, start, table):
        lefts = []
        for micro in range(self.micros):
            pieces = self.pieces_of(source, lead, micro, start)
            lefts.append(jnp.concatenate(pieces + [piece[:, :LANES] for piece in pieces], axis=1))
        results = []
        for left in lefts:
            outer = jnp.dot(left, table[0 : 9 * LANES, :], preferred_element_type=F32)
            middle = jnp.dot(
                left[:, 0 : 6 * LANES],
                table[9 * LANES : 15 * LANES, :],
                preferred_element_type=F32,
            )
            before = pltpu.roll(outer[:, :LANES], 1, 0)
            after = pltpu.roll(outer[:, LANES:], outer.shape[0] - 1, 0)
            results.append(before + (middle[:, :LANES] + middle[:, LANES:]) + after)
        return results

    def by_owner(self, layer, own, other, body):
        mine = layer // 2 == self.section
        pl.when(mine)(lambda: body(own, layer % 2))
        pl.when(jnp.logical_not(mine))(lambda: body(other, layer % 2))

    def blank_edges(self, target):
        blank = jnp.zeros((self.depth, 2 * LANES), BF16)
        for lead in range(target.shape[0]):
            for micro in range(self.micros):
                for edge in (0, self.rows_y + 1):
                    target[lead, micro, edge * self.depth : (edge + 1) * self.depth, :] = blank

    def fill(self, field, windows, which):
        halo = HALOS[which]
        span = self.width + 2 * halo
        at = 0 if which == 0 else self.width + 2 * HALO
        extra = [HALO - halo, self.depth - span - (HALO - halo)]
        for index, window in enumerate(windows):
            owner = self.slab ^ index % self.slabs
            micro = self.section if index < self.slabs else 1 - self.section
            for y in range(self.per_owner):
                blanks = [jnp.zeros((rows, LANES), F32) for rows in extra]
                parts = [blanks[0], window[y, at : at + span], blanks[1]]
                parts = [part for part in parts if part.shape[0]]
                start = pl.multiple_of((owner * self.per_owner + y) * self.depth, 16)
                value = jnp.concatenate(parts, axis=0) if len(parts) > 1 else parts[0]
                field[micro, pl.ds(start, self.depth), :] = value

    def cut_out(self, targets, source):
        for turn, target in enumerate(targets):
            owner = self.slab ^ turn
            for micro in range(self.micros):
                for y in range(self.per_owner):
                    start = (owner * self.per_owner + y) * self.depth + HALO
                    rows = pl.ds(pl.multiple_of(start, 8), self.width)
                    target[micro, y] = source[micro, rows, :]


def forward_kernel(dims, own, own_row, other, other_row, *refs):
    slab = Slab(dims)
    windows, (acts, kept, *outs), (whole, field) = (
        refs[: 2 * slab.slabs],
        refs[2 * slab.slabs : -2],
        refs[-2:],
    )
    slab.blank_edges(acts)
    slab.fill(field, windows, 0)

    def take_in(start):
        for micro in range(slab.micros):
            slab.put_rows(acts, 0, micro, start, field[micro, pl.ds(start, slab.chunk), :])

    slab.over_chunks(take_in)

    def layer_step(layer, carry):
        def run(tables, half):
            table, row = tables

            def body(start):
                at = pl.ds(start, slab.chunk)
                sums = slab.conv(acts, layer, start, table.at[half])
                values = []
                for micro, total in enumerate(sums):
                    pre = total + row[half][0:1, :]
                    sigma = 1.0 / (1.0 + jnp.exp(-pre))
                    kept[layer, micro, at, :] = sigma * (1.0 + pre * (1.0 - sigma))
                    out = slab.masked(pre * sigma, slab.in_grid)
                    slab.put_rows(acts, layer + 1, micro, start, out)
                    values.append(out)

                @pl.when(layer == 2 * slab.section + 1)
                def _():
                    for micro, value in enumerate(values):
                        whole[micro, at, :] = value

            slab.over_chunks(body)

        slab.by_owner(layer, (own, own_row), (other, other_row), run)
        return carry

    lax.fori_loop(0, 4, layer_step, 0)
    slab.cut_out(outs, whole)


def backward_kernel(dims, scale, own, other, acts, kept, *refs):
    slab = Slab(dims)
    windows, refs = refs[: 2 * slab.slabs], refs[2 * slab.slabs :]
    outs, (sums, rim, slopes, field, acc) = refs[: slab.slabs], refs[slab.slabs :]
    slab.blank_edges(rim)
    slab.fill(field, windows, 1)

    def take_gradient(layer, micro, start, gradient):
        at = pl.ds(start, slab.chunk)
        slope = slab.masked(gradient * kept[layer, micro, at, :], slab.in_grid)
        slopes[layer, micro, at, :] = slab.masked(slope, slab.mine)
        slab.put_rows(rim, layer % 2, micro, start, slope)

    def take_cotangent(start):
        for micro in range(slab.micros):
            take_gradient(3, micro, start, field[micro, pl.ds(start, slab.chunk), :])

    slab.over_chunks(take_cotangent)

    def layer_step(index, carry):
        layer = 3 - index

        def run(table, half):
            def body(start):
                gradients = slab.conv(rim, layer % 2, start, table.at[half])
                last = layer == 2 * slab.section

                @pl.when(last)
                def _():
                    for micro, gradient in enumerate(gradients):
                        field[micro, pl.ds(start, slab.chunk), :] = gradient

                @pl.when(jnp.logical_not(last))
                def _():
                    for micro, gradient in enumerate(gradients):
                        take_gradient(layer - 1, micro, start, gradient)

            slab.over_chunks(body)

        slab.by_owner(layer, own, other, run)
        return carry

    lax.fori_loop(0, jnp.where(slab.section == 0, 4, 2), layer_step, 0)
    slab.cut_out(outs, field)

    quarter = BLOCKS // 4
    chans = LANES // 2
    swap = column_bits()

    def spot(tap):
        return (tap // quarter ^ swap) * quarter + tap % quarter

    def products(layer, start):
        at = pl.ds(start, slab.chunk)
        slope = jnp.concatenate([slopes[layer, micro, at, :] for micro in range(slab.micros)])
        moved = [pltpu.roll(slope, slope.shape[0] - 1, 0), slope, pltpu.roll(slope, 1, 0)]
        terms = [split_terms(value) for value in moved]
        left_hi = jnp.concatenate([hi for hi, lo in terms], axis=1)
        left_lo = jnp.concatenate([lo for hi, lo in terms], axis=1)
        pieces = [slab.pieces_of(acts, layer, micro, start) for micro in range(slab.micros)]
        pieces = [jnp.concatenate(parts, axis=0) for parts in zip(*pieces)]
        full = jnp.concatenate(pieces, axis=1)
        high = jnp.concatenate([piece[:, :LANES] for piece in pieces], axis=1)
        over_rows = (((0,), (0,)), ((), ()))
        one = lax.dot_general(left_hi, full, over_rows, preferred_element_type=F32)
        two = lax.dot_general(left_lo, high, over_rows, preferred_element_type=F32)
        total = []
        for b in range(3):
            hi = one[:, 2 * b * LANES : (2 * b + 1) * LANES]
            lo = one[:, (2 * b + 1) * LANES : (2 * b + 2) * LANES]
            total.append(hi + lo + two[:, b * LANES : (b + 1) * LANES])
        return total, jnp.sum(slope, axis=0, keepdims=True)

    sums[spot(TAPS)] = jnp.zeros((chans, LANES), F32)
    for slot in range(2):
        layer = 2 * slab.section + slot
        if slab.chunks == 1:
            total, row = products(layer, 0)
        else:
            acc[...] = jnp.zeros(acc.shape, F32)

            def gather(start):
                total, row = products(layer, start)
                for b in range(3):
                    acc[0 : 3 * LANES, b * LANES : (b + 1) * LANES] += total[b]
                acc[3 * LANES : 3 * LANES + 1, 0:LANES] += row

            slab.over_chunks(gather)
            total = [acc[0 : 3 * LANES, b * LANES : (b + 1) * LANES] for b in range(3)]
            row = acc[3 * LANES : 3 * LANES + 1, 0:LANES]
        lanes = slice(slot * chans, (slot + 1) * chans)
        for b in range(3):
            for c in range(3):
                block = total[b][c * LANES : (c + 1) * LANES] * scale
                tap = 3 * b + c
                sums[spot(tap), :, lanes] = block[chans:, :chans]
                sums[spot(9 + tap), :, lanes] = block[:chans, :chans] + block[chans:, chans:]
                sums[spot(18 + tap), :, lanes] = block[:chans, chans:]
        row = row * scale
        sums[spot(TAPS), 0:1, lanes] = row[:, :chans] + row[:, chans:]


def unpack_kernel(*refs):
    sources, (weight, bias, whole) = refs[:-3], refs[-3:]
    part = sources[0].shape[0] // 4
    chans = weight.shape[-1]
    odd, swap = lax.axis_index("gy") % 2, column_bits()
    for number, source in enumerate(sources):
        for index in range(4):
            quarter = number // 2 * 2 + index // 2
            at = (((quarter ^ swap) * 2 + (index % 2 ^ odd)) * 2 + number % 2) * part
            rows = source[index * part : (index + 1) * part, :]
            whole[pl.ds(pl.multiple_of(at, 8), part), :] = rows
    for layer in range(2):
        lanes = slice(layer * chans, (layer + 1) * chans)
        for tap in range(TAPS):
            weight[layer, tap] = whole[tap * chans : (tap + 1) * chans, lanes]
        bias[layer : layer + 1, :] = whole[TAPS * chans : TAPS * chans + 1, lanes]


def restore_kernel(dims, *refs):
    micros, chans, size_x, local_y, width = dims
    pieces, (*targets, whole) = refs[:-3], refs[-3:]
    slab = lax.axis_index("gy")
    step = size_x * local_y
    slabs = len(pieces) // 2
    for slot, target in enumerate(targets):
        for micro in range(micros):
            for y in range(local_y):
                for turn in range(slabs):
                    start = (slab ^ turn) * width
                    if width % 8 == 0:
                        start = pl.multiple_of(start, 8)
                    rows = pl.ds(start, width)
                    whole[slot, micro, y, rows, :] = pieces[slot * slabs + turn][micro, y]
                block = whole[slot, micro, y].T
                for x in range(size_x):
                    first = micro * chans * step + x * local_y + y
                    part = block[x * chans : (x + 1) * chans]
                    target[pl.ds(first, chans, stride=step), :] = part


def spread(blocks):
    slabs = len(blocks)
    if slabs <= 8:
        got = [blocks[0]]
        for turn in range(1, slabs):
            route = [(i, i ^ turn) for i in range(slabs)]
            got.append(lax.ppermute(blocks[turn], "gy", route))
        return got
    order = jnp.arange(slabs) ^ lax.axis_index("gy")
    got = lax.all_to_all(jnp.stack(blocks)[order], "gy", 0, 0)[order]
    return [got[turn] for turn in range(slabs)]


def swapped(block, bit, axis="gz"):
    return lax.ppermute(block, axis, [(i, i ^ bit) for i in range(lax.axis_size(axis))])


def crossed(block):
    return lax.ppermute(block, "section", [(0, 1), (1, 0)])


def around(above, beside, across):
    slabs, columns = lax.axis_size("gy"), lax.axis_size("gz")
    route = [
        (i * columns + g, (i ^ 1) * columns + (g ^ 2)) for i in range(slabs) for g in range(columns)
    ]
    beside = swapped(beside, 2)
    across = lax.ppermute(across, ("gy", "gz"), route)
    return [swapped(above, 1, "gy"), beside, across]


def per_device(inflow, weights, biases, cotangent):
    micros, chans, size_x, local_y, local_z = inflow.shape
    assert micros == lax.axis_size("section") == 2
    slabs, columns = lax.axis_size("gy"), lax.axis_size("gz")
    rows_y = local_y * slabs
    width = local_z // slabs
    span = width + 2 * HALO
    depth = -(-span // 16) * 16
    chunk_y = max(n for n in range(1, rows_y + 1) if rows_y % n == 0 and n * depth <= 384)
    scale = 1.0 / math.sqrt(micros * size_x * rows_y * local_z * columns)
    rows = micros * chans * size_x * local_y
    blocks = [inflow.reshape(rows, local_z), cotangent.reshape(rows, local_z)]
    ends = ((2, micros, local_y, HALO, LANES), F32)
    fields, pair, inner = call(
        functools.partial(turn_kernel, inflow.shape),
        "turn",
        [((2, micros, local_y, local_z, LANES), F32), ends, ends],
        blocks,
    )
    packs = [((BLOCKS, chans, LANES), F32), ((BLOCKS // 2, chans, LANES), F32)]
    own, sent = call(pack_kernel, "pack", packs, [weights, biases])
    pair = swapped(pair, 1)
    route = [(i, i + 1) for i in range(1, columns - 1, 2)]
    inner = lax.ppermute(inner, "gz", route + [(after, before) for before, after in route])
    windows = call(
        functools.partial(window_kernel, (slabs, width, columns)),
        "windows",
        [((local_y, sum(width + 2 * halo for halo in HALOS), LANES), F32)] * (slabs + 1),
        [fields, pair, inner],
        [pltpu.VMEM((2, micros, local_y, local_z + 2 * HALO, LANES), F32)],
    )
    sent, windows = lax.optimization_barrier((sent, windows))
    near_half = crossed(sent)
    *mine, home = windows
    mine = spread(mine)

    tables = [((2, 15 * LANES, 2 * LANES), BF16)] * 2 + [((2, 8, LANES), F32)]
    own_fwd, own_bwd, own_row = call(table_kernel, "own_table", tables, [own])
    if slabs <= 8:
        theirs = [home] + [crossed(window) for window in mine[1:]]
    else:
        theirs = list(crossed(jnp.stack(mine)))
    windows = mine + theirs
    gate = [theirs[1], *mine[2:]]
    near_half, own_row, *_ = lax.optimization_barrier((near_half, own_row, *gate))
    far_half = swapped(near_half, 1)
    far_fwd, far_bwd, far_row = call(table_kernel, "far_table", tables, [near_half, far_half])

    dims = (micros, rows_y, depth, width, chunk_y, slabs, local_z * columns)
    padded = (rows_y + 2) * depth
    full = rows_y * depth
    piece = ((micros, local_y, width, LANES), F32)
    acts, kept, *fronts = call(
        functools.partial(forward_kernel, dims),
        "forward",
        [((5, micros, padded, 2 * LANES), BF16), ((4, micros, full, LANES), F32)] + [piece] * slabs,
        [own_fwd, own_row, far_fwd, far_row, *windows],
        [pltpu.VMEM((micros, full, LANES), F32)] * 2,
    )
    if slabs == 4:
        passed = swapped(fronts[3], 2, "gy")
    *backs, sums = call(
        functools.partial(backward_kernel, dims, scale),
        "backward",
        [piece] * slabs + [((BLOCKS, chans, LANES), F32)],
        [own_bwd, far_bwd, acts, kept, *windows],
        [
            pltpu.VMEM((2, micros, padded, 2 * LANES), BF16),
            pltpu.VMEM((4, micros, full, LANES), F32),
            pltpu.VMEM((micros, full, LANES), F32),
            pltpu.VMEM((3 * LANES + 8, 3 * LANES), F32),
        ],
        12 * micros * full * 9 * LANES * 3 * LANES,
    )
    if slabs == 4:
        sums, passed = lax.optimization_barrier((sums, passed))

    part = BLOCKS * chans // 16
    blocks = sums.reshape(8, 2, part, LANES)
    odd = lax.axis_index("gy") % 2 == 1
    streams = []
    for stream in range(2):
        block = blocks[:, stream].reshape(8 * part, LANES)
        streams.append(block[: 4 * part] + swapped(block[4 * part :], 1))
    streams[0], fronts, backs = lax.optimization_barrier((streams[0], fronts, backs))
    if slabs == 4:
        near = swapped(jnp.stack([fronts[1], passed, backs[1]]), 1, "gy")
        far = swapped(jnp.stack([fronts[2], backs[2]]), 2, "gy")
        outs = [near, far, swapped(backs[3], 3, "gy")]
    else:
        outs = spread([jnp.stack(pair) for pair in zip(fronts, backs)])
    streams = [block[: 2 * part] + swapped(block[2 * part :], 2) for block in streams]
    streams[1], outs = lax.optimization_barrier((streams[1], outs))
    sums = []
    for block in streams:
        kept = jnp.where(odd, block[part:], block[:part])
        kept = kept + swapped(jnp.where(odd, block[:part], block[part:]), 1, "gy")
        bit = 2
        while bit < slabs:
            kept = kept + swapped(kept, bit, "gy")
            bit *= 2
        sums.append(jnp.concatenate([kept, *around(kept, kept, kept)], axis=0))
    sums += [swapped(block, 1) for block in sums]
    if slabs == 4:
        near, far, last = outs
        outs = [fronts[0], near[0], far[0], near[1], backs[0], near[2], far[1], last]
    else:
        outs = [out[slot] for slot in range(2) for out in outs]
    section_out, section_grad = call(
        functools.partial(restore_kernel, (micros, chans, size_x, local_y, width)),
        "restore",
        [((rows, local_z), F32)] * 2,
        outs,
        [pltpu.VMEM((2, micros, local_y, local_z, LANES), F32)],
    )
    weight_total, bias_total = call(
        unpack_kernel,
        "unpack",
        [((2, TAPS, chans, chans), F32), ((2, chans), F32)],
        sums,
        [pltpu.VMEM((BLOCKS * chans, LANES), F32)],
    )
    shape = (1, *inflow.shape)
    return (section_out.reshape(shape), section_grad.reshape(shape), weight_total, bias_total)


def solution(mesh):
    grid = P(None, None, None, "gy", "gz")
    section_grid = P("section", None, None, None, "gy", "gz")
    return jax.shard_map(
        per_device,
        mesh=mesh,
        in_specs=(grid, P("section", None, None, None), P("section", None), grid),
        out_specs=(section_grid, section_grid, P("section", None, None, None), P("section", None)),
        check_vma=False,
    )
```

```python
import functools
import math

import jax
import jax.numpy as jnp
from jax import lax
from jax.experimental import pallas as pl
from jax.experimental.pallas import tpu as pltpu
from jax.sharding import PartitionSpec as P

HALO = 8
HALOS = (8, 4)
LANES = 128
TAPS = 27
BLOCKS = 28
BF16 = jnp.bfloat16
F32 = jnp.float32
VMEM = pl.BlockSpec(memory_space=pltpu.VMEM)


def call(kernel, name, outs, args, scratch=(), flops=0):
    arrays = [jax.ShapeDtypeStruct(shape, kind) for shape, kind in outs]
    size = sum(math.prod(item.shape) * item.dtype.itemsize for item in [*arrays, *args, *scratch])
    return pl.pallas_call(
        kernel,
        out_shape=arrays,
        in_specs=[VMEM] * len(args),
        out_specs=[VMEM] * len(arrays),
        scratch_shapes=list(scratch),
        compiler_params=pltpu.CompilerParams(vmem_limit_bytes=size + 6 * 1024 * 1024),
        cost_estimate=pl.CostEstimate(flops=flops, bytes_accessed=1024, transcendentals=0),
        name=name,
    )(*args)


def column_bits():
    column = lax.axis_index("gz")
    return 2 * (column % 2) + column // 2 % 2


def split_terms(values):
    high = values.astype(BF16)
    return high, (values - high.astype(F32)).astype(BF16)


def pack_kernel(weights, biases, own, sent):
    chans = weights.shape[2]
    for tap in range(TAPS):
        own[tap] = jnp.concatenate([weights[0, tap], weights[1, tap]], axis=1)
    own[TAPS] = jnp.zeros((chans, LANES), F32)
    own[TAPS, 0:1, :] = jnp.concatenate([biases[0:1, :], biases[1:2, :]], axis=1)
    half = sent.shape[0]
    start = lax.axis_index("gz") % 2 * half
    for index in range(half):
        sent[index] = own[start + index]


def turned_rows(dims, source, micro, y):
    _, chans, size_x, local_y, _ = dims
    step = size_x * local_y
    first = micro * chans * step + y
    parts = [source[pl.ds(first + x * local_y, chans, stride=step), :] for x in range(size_x)]
    return jnp.concatenate(parts, axis=0).T


def turn_kernel(dims, inflow, cotangent, rows, pair, inner):
    micros, _, _, local_y, local_z = dims
    odd = lax.axis_index("gz") % 2 == 1
    for field, source in enumerate((inflow, cotangent)):
        for micro in range(micros):
            for y in range(local_y):
                turned = turned_rows(dims, source, micro, y)
                rows[field, micro, y] = turned
                low, high = turned[:HALO], turned[local_z - HALO :]
                pair[field, micro, y] = jnp.where(odd, low, high)
                inner[field, micro, y] = jnp.where(odd, high, low)


def window_kernel(dims, rows, pair, inner, *refs):
    slabs, width, columns = dims
    outs, wide = refs[:-1], refs[-1]
    slab, column = lax.axis_index("gy"), lax.axis_index("gz")
    section = lax.axis_index("section")
    odd = column % 2 == 1
    _, micros, local_y, local_z, _ = rows.shape
    for field, halo in enumerate(HALOS):
        at = slice(0, width + 2 * halo) if field == 0 else slice(width + 2 * HALO, None)
        for y in range(local_y):
            for micro in range(micros):
                one, two = pair[field, micro, y], inner[field, micro, y]
                before = jnp.where(column > 0, jnp.where(odd, one, two), 0.0)
                after = jnp.where(column < columns - 1, jnp.where(odd, two, one), 0.0)
                wide[field, micro, y, :HALO] = before
                wide[field, micro, y, HALO : HALO + local_z] = rows[field, micro, y]
                wide[field, micro, y, HALO + local_z :] = after
            for turn, out in enumerate(outs):
                start = (slab ^ turn % slabs) * width + HALO - halo
                if width % 8 == 0 and halo % 8 == 0:
                    start = pl.multiple_of(start, 8)
                micro = section if turn < slabs else 1 - section
                out[y, at] = wide[field, micro, y, pl.ds(start, width + 2 * halo)]


def table_kernel(*refs):
    parts, (fwd, bwd, row) = refs[:-3], refs[-3:]
    odd = lax.axis_index("gz") % 2
    count, chans, _ = parts[0].shape

    def block_of(tap):
        if len(parts) == 1:
            return parts[0][tap]
        index = tap % count
        return jnp.where(odd == tap // count, parts[0][index], parts[1][index])

    for b in range(3):
        for c in range(3):
            taps = [block_of(9 * a + 3 * b + c) for a in range(3)]
            for layer in range(2):
                own_lanes = slice(layer * chans, (layer + 1) * chans)
                below, level, above = [tap[:, own_lanes] for tap in taps]
                top = jnp.concatenate([level, above], axis=1)
                low = jnp.concatenate([below, level], axis=1)
                block = jnp.concatenate([top, low], axis=0)
                for target, value, r, at in ((fwd, block.T, b, c), (bwd, block, 2 - b, 2 - c)):
                    hi, lo = split_terms(value)
                    if at == 1:
                        for row_at in (9 + 2 * r, 10 + 2 * r):
                            rows = slice(row_at * LANES, (row_at + 1) * LANES)
                            target[layer, rows, 0:LANES] = hi
                            target[layer, rows, LANES : 2 * LANES] = lo
                    else:
                        lanes = slice(at // 2 * LANES, (at // 2 + 1) * LANES)
                        for row_at, term in ((2 * r, hi), (2 * r + 1, hi), (6 + r, lo)):
                            rows = slice(row_at * LANES, (row_at + 1) * LANES)
                            target[layer, rows, lanes] = term
    last = block_of(TAPS)[0:1, :]
    for layer in range(2):
        part = last[:, layer * chans : (layer + 1) * chans]
        row[layer] = jnp.broadcast_to(jnp.concatenate([part, part], axis=1), (8, LANES))


class Slab:
    def __init__(self, dims):
        self.micros, self.rows_y, self.depth, self.width, self.chunk_y, self.slabs, limit_z = dims
        self.section, self.slab = lax.axis_index("section"), lax.axis_index("gy")
        origin = (lax.axis_index("gz") * self.slabs + self.slab) * self.width - HALO
        self.chunk = self.chunk_y * self.depth
        self.chunks = self.rows_y // self.chunk_y
        self.per_owner = self.rows_y // self.slabs
        zs = lax.broadcasted_iota(jnp.int32, (self.depth, LANES), 0)
        inside = (zs + origin >= 0) & (zs + origin < limit_z)
        self.in_grid = inside.astype(F32)[None]
        self.mine = ((zs >= HALO) & (zs < HALO + self.width)).astype(F32)[None]

    def over_chunks(self, body):
        if self.chunks == 1:
            body(0)
        else:

            def step(part, carry):
                body(pl.multiple_of(part * self.chunk, 16))
                return carry

            lax.fori_loop(0, self.chunks, step, 0)

    def masked(self, values, mask):
        return (values.reshape(-1, self.depth, LANES) * mask).reshape(values.shape)

    def put_rows(self, target, lead, micro, start, values):
        hi, lo = split_terms(values)
        at = pl.ds(start + self.depth, self.chunk)
        target[lead, micro, at, slice(0, LANES)] = hi
        target[lead, micro, at, slice(LANES, 2 * LANES)] = lo

    def pieces_of(self, source, lead, micro, start):
        return [
            source[lead, micro, pl.ds(start + b * self.depth, self.chunk), :] for b in range(3)
        ]

    def conv(self, source, lead, start, table):
        lefts = []
        for micro in range(self.micros):
            pieces = self.pieces_of(source, lead, micro, start)
            lefts.append(jnp.concatenate(pieces + [piece[:, :LANES] for piece in pieces], axis=1))
        results = []
        for left in lefts:
            outer = jnp.dot(left, table[0 : 9 * LANES, :], preferred_element_type=F32)
            middle = jnp.dot(
                left[:, 0 : 6 * LANES],
                table[9 * LANES : 15 * LANES, :],
                preferred_element_type=F32,
            )
            before = pltpu.roll(outer[:, :LANES], 1, 0)
            after = pltpu.roll(outer[:, LANES:], outer.shape[0] - 1, 0)
            results.append(before + (middle[:, :LANES] + middle[:, LANES:]) + after)
        return results

    def by_owner(self, layer, own, other, body):
        mine = layer // 2 == self.section
        pl.when(mine)(lambda: body(own, layer % 2))
        pl.when(jnp.logical_not(mine))(lambda: body(other, layer % 2))

    def blank_edges(self, target):
        blank = jnp.zeros((self.depth, 2 * LANES), BF16)
        for lead in range(target.shape[0]):
            for micro in range(self.micros):
                for edge in (0, self.rows_y + 1):
                    target[lead, micro, edge * self.depth : (edge + 1) * self.depth, :] = blank

    def fill(self, field, windows, home, theirs, which):
        halo = HALOS[which]
        span = self.width + 2 * halo
        at = 0 if which == 0 else self.width + 2 * HALO
        extra = [HALO - halo, self.depth - span - (HALO - halo)]
        pieces = [(self.section, turn, window, at) for turn, window in enumerate(windows)]
        pieces.append((1 - self.section, 0, home, at))
        pieces += [(1 - self.section, turn + 1, window, 0) for turn, window in enumerate(theirs)]
        for micro, turn, window, first in pieces:
            owner = self.slab ^ turn
            for y in range(self.per_owner):
                blanks = [jnp.zeros((rows, LANES), F32) for rows in extra]
                parts = [blanks[0], window[y, first : first + span], blanks[1]]
                parts = [part for part in parts if part.shape[0]]
                start = pl.multiple_of((owner * self.per_owner + y) * self.depth, 16)
                value = jnp.concatenate(parts, axis=0) if len(parts) > 1 else parts[0]
                field[micro, pl.ds(start, self.depth), :] = value

    def cut_out(self, targets, source):
        for turn, target in enumerate(targets):
            owner = self.slab ^ turn
            for micro in range(self.micros):
                for y in range(self.per_owner):
                    start = (owner * self.per_owner + y) * self.depth + HALO
                    rows = pl.ds(pl.multiple_of(start, 8), self.width)
                    target[micro, y] = source[micro, rows, :]


def forward_kernel(dims, own, own_row, other, other_row, *refs):
    slab = Slab(dims)
    count = slab.slabs
    windows, home, theirs = refs[:count], refs[count], refs[count + 1 : 2 * count]
    (acts, kept, *outs), (whole, field) = refs[2 * count : -2], refs[-2:]
    slab.blank_edges(acts)
    slab.fill(field, windows, home, theirs, 0)

    def take_in(start):
        for micro in range(slab.micros):
            slab.put_rows(acts, 0, micro, start, field[micro, pl.ds(start, slab.chunk), :])

    slab.over_chunks(take_in)

    def layer_step(layer, carry):
        def run(tables, half):
            table, row = tables

            def body(start):
                at = pl.ds(start, slab.chunk)
                sums = slab.conv(acts, layer, start, table.at[half])
                values = []
                for micro, total in enumerate(sums):
                    pre = total + row[half][0:1, :]
                    sigma = 1.0 / (1.0 + jnp.exp(-pre))
                    kept[layer, micro, at, :] = sigma * (1.0 + pre * (1.0 - sigma))
                    out = slab.masked(pre * sigma, slab.in_grid)
                    slab.put_rows(acts, layer + 1, micro, start, out)
                    values.append(out)

                @pl.when(layer == 2 * slab.section + 1)
                def _():
                    for micro, value in enumerate(values):
                        whole[micro, at, :] = value

            slab.over_chunks(body)

        slab.by_owner(layer, (own, own_row), (other, other_row), run)
        return carry

    lax.fori_loop(0, 4, layer_step, 0)
    slab.cut_out(outs, whole)


def backward_kernel(dims, scale, own, other, acts, kept, *refs):
    slab = Slab(dims)
    (*windows, home, other_cells), refs = refs[: slab.slabs + 2], refs[slab.slabs + 2 :]
    theirs = [other_cells.at[turn] for turn in range(slab.slabs - 1)]
    outs, (sums, rim, slopes, field, acc) = refs[: slab.slabs], refs[slab.slabs :]
    slab.blank_edges(rim)
    slab.fill(field, windows, home, theirs, 1)

    def take_gradient(layer, micro, start, gradient):
        at = pl.ds(start, slab.chunk)
        slope = slab.masked(gradient * kept[layer, micro, at, :], slab.in_grid)
        slopes[layer, micro, at, :] = slab.masked(slope, slab.mine)
        slab.put_rows(rim, layer % 2, micro, start, slope)

    def take_cotangent(start):
        for micro in range(slab.micros):
            take_gradient(3, micro, start, field[micro, pl.ds(start, slab.chunk), :])

    slab.over_chunks(take_cotangent)

    def layer_step(index, carry):
        layer = 3 - index

        def run(table, half):
            def body(start):
                gradients = slab.conv(rim, layer % 2, start, table.at[half])
                last = layer == 2 * slab.section

                @pl.when(last)
                def _():
                    for micro, gradient in enumerate(gradients):
                        field[micro, pl.ds(start, slab.chunk), :] = gradient

                @pl.when(jnp.logical_not(last))
                def _():
                    for micro, gradient in enumerate(gradients):
                        take_gradient(layer - 1, micro, start, gradient)

            slab.over_chunks(body)

        slab.by_owner(layer, own, other, run)
        return carry

    lax.fori_loop(0, jnp.where(slab.section == 0, 4, 2), layer_step, 0)
    slab.cut_out(outs, field)

    quarter = BLOCKS // 4
    chans = LANES // 2
    swap = column_bits()

    def spot(tap):
        return (tap // quarter ^ swap) * quarter + tap % quarter

    def products(layer, start):
        at = pl.ds(start, slab.chunk)
        slope = jnp.concatenate([slopes[layer, micro, at, :] for micro in range(slab.micros)])
        moved = [pltpu.roll(slope, slope.shape[0] - 1, 0), slope, pltpu.roll(slope, 1, 0)]
        terms = [split_terms(value) for value in moved]
        left_hi = jnp.concatenate([hi for hi, lo in terms], axis=1)
        left_lo = jnp.concatenate([lo for hi, lo in terms], axis=1)
        pieces = [slab.pieces_of(acts, layer, micro, start) for micro in range(slab.micros)]
        pieces = [jnp.concatenate(parts, axis=0) for parts in zip(*pieces)]
        full = jnp.concatenate(pieces, axis=1)
        high = jnp.concatenate([piece[:, :LANES] for piece in pieces], axis=1)
        over_rows = (((0,), (0,)), ((), ()))
        one = lax.dot_general(left_hi, full, over_rows, preferred_element_type=F32)
        two = lax.dot_general(left_lo, high, over_rows, preferred_element_type=F32)
        total = []
        for b in range(3):
            hi = one[:, 2 * b * LANES : (2 * b + 1) * LANES]
            lo = one[:, (2 * b + 1) * LANES : (2 * b + 2) * LANES]
            total.append(hi + lo + two[:, b * LANES : (b + 1) * LANES])
        return total, jnp.sum(slope, axis=0, keepdims=True)

    sums[spot(TAPS)] = jnp.zeros((chans, LANES), F32)
    for slot in range(2):
        layer = 2 * slab.section + slot
        if slab.chunks == 1:
            total, row = products(layer, 0)
        else:
            acc[...] = jnp.zeros(acc.shape, F32)

            def gather(start):
                total, row = products(layer, start)
                for b in range(3):
                    acc[0 : 3 * LANES, b * LANES : (b + 1) * LANES] += total[b]
                acc[3 * LANES : 3 * LANES + 1, 0:LANES] += row

            slab.over_chunks(gather)
            total = [acc[0 : 3 * LANES, b * LANES : (b + 1) * LANES] for b in range(3)]
            row = acc[3 * LANES : 3 * LANES + 1, 0:LANES]
        lanes = slice(slot * chans, (slot + 1) * chans)
        for b in range(3):
            for c in range(3):
                block = total[b][c * LANES : (c + 1) * LANES] * scale
                tap = 3 * b + c
                sums[spot(tap), :, lanes] = block[chans:, :chans]
                sums[spot(9 + tap), :, lanes] = block[:chans, :chans] + block[chans:, chans:]
                sums[spot(18 + tap), :, lanes] = block[:chans, chans:]
        row = row * scale
        sums[spot(TAPS), 0:1, lanes] = row[:, :chans] + row[:, chans:]


def unpack_kernel(*refs):
    sources, (weight, bias, whole) = refs[:-3], refs[-3:]
    part = sources[0].shape[0] // 4
    chans = weight.shape[-1]
    odd, swap = lax.axis_index("gy") % 2, column_bits()
    for number, source in enumerate(sources):
        for index in range(4):
            quarter = number // 2 * 2 + index // 2
            at = (((quarter ^ swap) * 2 + (index % 2 ^ odd)) * 2 + number % 2) * part
            rows = source[index * part : (index + 1) * part, :]
            whole[pl.ds(pl.multiple_of(at, 8), part), :] = rows
    for layer in range(2):
        lanes = slice(layer * chans, (layer + 1) * chans)
        for tap in range(TAPS):
            weight[layer, tap] = whole[tap * chans : (tap + 1) * chans, lanes]
        bias[layer : layer + 1, :] = whole[TAPS * chans : TAPS * chans + 1, lanes]


def restore_kernel(dims, *refs):
    micros, chans, size_x, local_y, width = dims
    pieces, (*targets, whole) = refs[:-3], refs[-3:]
    slab = lax.axis_index("gy")
    step = size_x * local_y
    slabs = len(pieces) // 2
    for slot, target in enumerate(targets):
        for micro in range(micros):
            for y in range(local_y):
                for turn in range(slabs):
                    start = (slab ^ turn) * width
                    if width % 8 == 0:
                        start = pl.multiple_of(start, 8)
                    rows = pl.ds(start, width)
                    whole[slot, micro, y, rows, :] = pieces[slot * slabs + turn][micro, y]
                block = whole[slot, micro, y].T
                for x in range(size_x):
                    first = micro * chans * step + x * local_y + y
                    part = block[x * chans : (x + 1) * chans]
                    target[pl.ds(first, chans, stride=step), :] = part


def spread(blocks):
    slabs = len(blocks)
    if slabs <= 8:
        got = [blocks[0]]
        for turn in range(1, slabs):
            route = [(i, i ^ turn) for i in range(slabs)]
            got.append(lax.ppermute(blocks[turn], "gy", route))
        return got
    order = jnp.arange(slabs) ^ lax.axis_index("gy")
    got = lax.all_to_all(jnp.stack(blocks)[order], "gy", 0, 0)[order]
    return [got[turn] for turn in range(slabs)]


def swapped(block, bit, axis="gz"):
    return lax.ppermute(block, axis, [(i, i ^ bit) for i in range(lax.axis_size(axis))])


def crossed(block):
    return lax.ppermute(block, "section", [(0, 1), (1, 0)])


def around(above, beside, across):
    slabs, columns = lax.axis_size("gy"), lax.axis_size("gz")
    route = [
        (i * columns + g, (i ^ 1) * columns + (g ^ 2)) for i in range(slabs) for g in range(columns)
    ]
    beside = swapped(beside, 2)
    across = lax.ppermute(across, ("gy", "gz"), route)
    return [swapped(above, 1, "gy"), beside, across]


def per_device(inflow, weights, biases, cotangent):
    micros, chans, size_x, local_y, local_z = inflow.shape
    assert micros == lax.axis_size("section") == 2
    slabs, columns = lax.axis_size("gy"), lax.axis_size("gz")
    rows_y = local_y * slabs
    width = local_z // slabs
    span = width + 2 * HALO
    depth = -(-span // 16) * 16
    chunk_y = max(n for n in range(1, rows_y + 1) if rows_y % n == 0 and n * depth <= 384)
    scale = 1.0 / math.sqrt(micros * size_x * rows_y * local_z * columns)
    rows = micros * chans * size_x * local_y
    blocks = [inflow.reshape(rows, local_z), cotangent.reshape(rows, local_z)]
    ends = ((2, micros, local_y, HALO, LANES), F32)
    fields, pair, inner = call(
        functools.partial(turn_kernel, inflow.shape),
        "turn",
        [((2, micros, local_y, local_z, LANES), F32), ends, ends],
        blocks,
    )
    packs = [((BLOCKS, chans, LANES), F32), ((BLOCKS // 2, chans, LANES), F32)]
    own, sent = call(pack_kernel, "pack", packs, [weights, biases])
    pair = swapped(pair, 1)
    route = [(i, i + 1) for i in range(1, columns - 1, 2)]
    inner = lax.ppermute(inner, "gz", route + [(after, before) for before, after in route])
    windows = call(
        functools.partial(window_kernel, (slabs, width, columns)),
        "windows",
        [((local_y, sum(width + 2 * halo for halo in HALOS), LANES), F32)] * (slabs + 1),
        [fields, pair, inner],
        [pltpu.VMEM((2, micros, local_y, local_z + 2 * HALO, LANES), F32)],
    )
    sent, windows = lax.optimization_barrier((sent, windows))
    near_half = crossed(sent)
    *mine, home = windows
    mine = spread(mine)

    tables = [((2, 15 * LANES, 2 * LANES), BF16)] * 2 + [((2, 8, LANES), F32)]
    own_fwd, own_bwd, own_row = call(table_kernel, "own_table", tables, [own])
    ahead = [window[:, : width + 2 * HALOS[0]] for window in mine[1:]]
    if slabs <= 8:
        ahead = [crossed(window) for window in ahead]
    else:
        ahead = list(crossed(jnp.stack(ahead)))
    after = crossed(jnp.stack([window[:, width + 2 * HALOS[0] :] for window in mine[1:]]))
    gate = [ahead[0], *mine[2:]]
    near_half, own_row, *_ = lax.optimization_barrier((near_half, own_row, *gate))
    far_half = swapped(near_half, 1)
    far_fwd, far_bwd, far_row = call(table_kernel, "far_table", tables, [near_half, far_half])

    dims = (micros, rows_y, depth, width, chunk_y, slabs, local_z * columns)
    padded = (rows_y + 2) * depth
    full = rows_y * depth
    piece = ((micros, local_y, width, LANES), F32)
    acts, kept, *fronts = call(
        functools.partial(forward_kernel, dims),
        "forward",
        [((5, micros, padded, 2 * LANES), BF16), ((4, micros, full, LANES), F32)] + [piece] * slabs,
        [own_fwd, own_row, far_fwd, far_row, *mine, home, *ahead],
        [pltpu.VMEM((micros, full, LANES), F32)] * 2,
    )
    if slabs == 4:
        passed = swapped(jnp.stack(fronts[2:]), 2, "gy")
    *backs, sums = call(
        functools.partial(backward_kernel, dims, scale),
        "backward",
        [piece] * slabs + [((BLOCKS, chans, LANES), F32)],
        [own_bwd, far_bwd, acts, kept, *mine, home, after],
        [
            pltpu.VMEM((2, micros, padded, 2 * LANES), BF16),
            pltpu.VMEM((4, micros, full, LANES), F32),
            pltpu.VMEM((micros, full, LANES), F32),
            pltpu.VMEM((3 * LANES + 8, 3 * LANES), F32),
        ],
        12 * micros * full * 9 * LANES * 3 * LANES,
    )
    if slabs == 4:
        sums, passed = lax.optimization_barrier((sums, passed))

    part = BLOCKS * chans // 16
    blocks = sums.reshape(8, 2, part, LANES)
    odd = lax.axis_index("gy") % 2 == 1
    streams = []
    for stream in range(2):
        block = blocks[:, stream].reshape(8 * part, LANES)
        streams.append(block[: 4 * part] + swapped(block[4 * part :], 1))
    streams[0], fronts, backs = lax.optimization_barrier((streams[0], fronts, backs))
    if slabs == 4:
        near = swapped(jnp.stack([fronts[1], passed[1], backs[1]]), 1, "gy")
        outs = [near, swapped(backs[2], 2, "gy"), swapped(backs[3], 3, "gy")]
    else:
        outs = spread([jnp.stack(pair) for pair in zip(fronts, backs)])
    streams = [block[: 2 * part] + swapped(block[2 * part :], 2) for block in streams]
    streams[1], outs = lax.optimization_barrier((streams[1], outs))
    sums = []
    for block in streams:
        kept = jnp.where(odd, block[part:], block[:part])
        kept = kept + swapped(jnp.where(odd, block[:part], block[part:]), 1, "gy")
        bit = 2
        while bit < slabs:
            kept = kept + swapped(kept, bit, "gy")
            bit *= 2
        sums.append(jnp.concatenate([kept, *around(kept, kept, kept)], axis=0))
    sums += [swapped(block, 1) for block in sums]
    if slabs == 4:
        outs = [fronts[0], outs[0][0], passed[0], outs[0][1], backs[0], outs[0][2], *outs[1:]]
    else:
        outs = [out[slot] for slot in range(2) for out in outs]
    section_out, section_grad = call(
        functools.partial(restore_kernel, (micros, chans, size_x, local_y, width)),
        "restore",
        [((rows, local_z), F32)] * 2,
        outs,
        [pltpu.VMEM((2, micros, local_y, local_z, LANES), F32)],
    )
    weight_total, bias_total = call(
        unpack_kernel,
        "unpack",
        [((2, TAPS, chans, chans), F32), ((2, chans), F32)],
        sums,
        [pltpu.VMEM((BLOCKS * chans, LANES), F32)],
    )
    shape = (1, *inflow.shape)
    return (section_out.reshape(shape), section_grad.reshape(shape), weight_total, bias_total)


def solution(mesh):
    grid = P(None, None, None, "gy", "gz")
    section_grid = P("section", None, None, None, "gy", "gz")
    return jax.shard_map(
        per_device,
        mesh=mesh,
        in_specs=(grid, P("section", None, None, None), P("section", None), grid),
        out_specs=(section_grid, section_grid, P("section", None, None, None), P("section", None)),
        check_vma=False,
    )
```

```python
import functools
import math

import jax
import jax.numpy as jnp
from jax import lax
from jax.experimental import pallas as pl
from jax.experimental.pallas import tpu as pltpu
from jax.sharding import PartitionSpec as P

HALO = 8
HALOS = (8, 4)
LANES = 128
TAPS = 27
BLOCKS = 28
BF16 = jnp.bfloat16
F32 = jnp.float32
VMEM = pl.BlockSpec(memory_space=pltpu.VMEM)


def call(kernel, name, outs, args, scratch=(), flops=0):
    arrays = [jax.ShapeDtypeStruct(shape, kind) for shape, kind in outs]
    size = sum(math.prod(item.shape) * item.dtype.itemsize for item in [*arrays, *args, *scratch])
    return pl.pallas_call(
        kernel,
        out_shape=arrays,
        in_specs=[VMEM] * len(args),
        out_specs=[VMEM] * len(arrays),
        scratch_shapes=list(scratch),
        compiler_params=pltpu.CompilerParams(vmem_limit_bytes=size + 6 * 1024 * 1024),
        cost_estimate=pl.CostEstimate(flops=flops, bytes_accessed=1024, transcendentals=0),
        name=name,
    )(*args)


def column_bits():
    column = lax.axis_index("gz")
    return 2 * (column % 2) + column // 2 % 2


def split_terms(values):
    high = values.astype(BF16)
    return high, (values - high.astype(F32)).astype(BF16)


def pack_kernel(weights, biases, own, sent):
    chans = weights.shape[2]
    for tap in range(TAPS):
        own[tap] = jnp.concatenate([weights[0, tap], weights[1, tap]], axis=1)
    own[TAPS] = jnp.zeros((chans, LANES), F32)
    own[TAPS, 0:1, :] = jnp.concatenate([biases[0:1, :], biases[1:2, :]], axis=1)
    half = sent.shape[0]
    start = lax.axis_index("gz") % 2 * half
    for index in range(half):
        sent[index] = own[start + index]


def window_kernel(dims, rows, pair, inner, *refs):
    slabs, width, columns = dims
    outs, wide = refs[:-1], refs[-1]
    slab, column = lax.axis_index("gy"), lax.axis_index("gz")
    section = lax.axis_index("section")
    odd = column % 2 == 1
    _, micros, local_y, local_z, _ = rows.shape
    for field, halo in enumerate(HALOS):
        at = slice(0, width + 2 * halo) if field == 0 else slice(width + 2 * HALO, None)
        for y in range(local_y):
            for micro in range(micros):
                one, two = pair[field, micro, y], inner[field, micro, y]
                before = jnp.where(column > 0, jnp.where(odd, one, two), 0.0)
                after = jnp.where(column < columns - 1, jnp.where(odd, two, one), 0.0)
                wide[field, micro, y, :HALO] = before
                wide[field, micro, y, HALO : HALO + local_z] = rows[field, micro, y]
                wide[field, micro, y, HALO + local_z :] = after
            for turn, out in enumerate(outs):
                start = (slab ^ turn % slabs) * width + HALO - halo
                if width % 8 == 0 and halo % 8 == 0:
                    start = pl.multiple_of(start, 8)
                micro = section if turn < slabs else 1 - section
                out[y, at] = wide[field, micro, y, pl.ds(start, width + 2 * halo)]


def table_kernel(*refs):
    parts, (fwd, bwd, row) = refs[:-3], refs[-3:]
    odd = lax.axis_index("gz") % 2
    count, chans, _ = parts[0].shape

    def block_of(tap):
        if len(parts) == 1:
            return parts[0][tap]
        index = tap % count
        return jnp.where(odd == tap // count, parts[0][index], parts[1][index])

    for b in range(3):
        for c in range(3):
            taps = [block_of(9 * a + 3 * b + c) for a in range(3)]
            for layer in range(2):
                own_lanes = slice(layer * chans, (layer + 1) * chans)
                below, level, above = [tap[:, own_lanes] for tap in taps]
                top = jnp.concatenate([level, above], axis=1)
                low = jnp.concatenate([below, level], axis=1)
                block = jnp.concatenate([top, low], axis=0)
                for target, value, r, at in ((fwd, block.T, b, c), (bwd, block, 2 - b, 2 - c)):
                    hi, lo = split_terms(value)
                    if at == 1:
                        for row_at in (9 + 2 * r, 10 + 2 * r):
                            rows = slice(row_at * LANES, (row_at + 1) * LANES)
                            target[layer, rows, 0:LANES] = hi
                            target[layer, rows, LANES : 2 * LANES] = lo
                    else:
                        lanes = slice(at // 2 * LANES, (at // 2 + 1) * LANES)
                        for row_at, term in ((2 * r, hi), (2 * r + 1, hi), (6 + r, lo)):
                            rows = slice(row_at * LANES, (row_at + 1) * LANES)
                            target[layer, rows, lanes] = term
    last = block_of(TAPS)[0:1, :]
    for layer in range(2):
        part = last[:, layer * chans : (layer + 1) * chans]
        row[layer] = jnp.broadcast_to(jnp.concatenate([part, part], axis=1), (8, LANES))


class Slab:
    def __init__(self, dims):
        self.micros, self.rows_y, self.depth, self.width, self.chunk_y, self.slabs, limit_z = dims
        self.section, self.slab = lax.axis_index("section"), lax.axis_index("gy")
        origin = (lax.axis_index("gz") * self.slabs + self.slab) * self.width - HALO
        self.chunk = self.chunk_y * self.depth
        self.chunks = self.rows_y // self.chunk_y
        self.per_owner = self.rows_y // self.slabs
        zs = lax.broadcasted_iota(jnp.int32, (self.depth, LANES), 0)
        inside = (zs + origin >= 0) & (zs + origin < limit_z)
        self.in_grid = inside.astype(F32)[None]
        self.mine = ((zs >= HALO) & (zs < HALO + self.width)).astype(F32)[None]

    def over_chunks(self, body):
        if self.chunks == 1:
            body(0)
        else:

            def step(part, carry):
                body(pl.multiple_of(part * self.chunk, 16))
                return carry

            lax.fori_loop(0, self.chunks, step, 0)

    def masked(self, values, mask):
        return (values.reshape(-1, self.depth, LANES) * mask).reshape(values.shape)

    def put_rows(self, target, lead, micro, start, values):
        hi, lo = split_terms(values)
        at = pl.ds(start + self.depth, self.chunk)
        target[lead, micro, at, slice(0, LANES)] = hi
        target[lead, micro, at, slice(LANES, 2 * LANES)] = lo

    def pieces_of(self, source, lead, micro, start):
        return [
            source[lead, micro, pl.ds(start + b * self.depth, self.chunk), :] for b in range(3)
        ]

    def conv(self, source, lead, start, table):
        lefts = []
        for micro in range(self.micros):
            pieces = self.pieces_of(source, lead, micro, start)
            lefts.append(jnp.concatenate(pieces + [piece[:, :LANES] for piece in pieces], axis=1))
        results = []
        for left in lefts:
            outer = jnp.dot(left, table[0 : 9 * LANES, :], preferred_element_type=F32)
            middle = jnp.dot(
                left[:, 0 : 6 * LANES],
                table[9 * LANES : 15 * LANES, :],
                preferred_element_type=F32,
            )
            before = pltpu.roll(outer[:, :LANES], 1, 0)
            after = pltpu.roll(outer[:, LANES:], outer.shape[0] - 1, 0)
            results.append(before + (middle[:, :LANES] + middle[:, LANES:]) + after)
        return results

    def by_owner(self, layer, own, other, body):
        mine = layer // 2 == self.section
        pl.when(mine)(lambda: body(own, layer % 2))
        pl.when(jnp.logical_not(mine))(lambda: body(other, layer % 2))

    def blank_edges(self, target):
        blank = jnp.zeros((self.depth, 2 * LANES), BF16)
        for lead in range(target.shape[0]):
            for micro in range(self.micros):
                for edge in (0, self.rows_y + 1):
                    target[lead, micro, edge * self.depth : (edge + 1) * self.depth, :] = blank

    def fill(self, field, windows, home, theirs, which):
        halo = HALOS[which]
        span = self.width + 2 * halo
        at = 0 if which == 0 else self.width + 2 * HALO
        extra = [HALO - halo, self.depth - span - (HALO - halo)]
        pieces = [(self.section, turn, window, at) for turn, window in enumerate(windows)]
        pieces.append((1 - self.section, 0, home, at))
        pieces += [(1 - self.section, turn + 1, window, 0) for turn, window in enumerate(theirs)]
        for micro, turn, window, first in pieces:
            owner = self.slab ^ turn
            for y in range(self.per_owner):
                blanks = [jnp.zeros((rows, LANES), F32) for rows in extra]
                parts = [blanks[0], window[y, first : first + span], blanks[1]]
                parts = [part for part in parts if part.shape[0]]
                start = pl.multiple_of((owner * self.per_owner + y) * self.depth, 16)
                value = jnp.concatenate(parts, axis=0) if len(parts) > 1 else parts[0]
                field[micro, pl.ds(start, self.depth), :] = value

    def cut_out(self, targets, source):
        for turn, target in enumerate(targets):
            owner = self.slab ^ turn
            for micro in range(self.micros):
                for y in range(self.per_owner):
                    start = (owner * self.per_owner + y) * self.depth + HALO
                    rows = pl.ds(pl.multiple_of(start, 8), self.width)
                    target[micro, y] = source[micro, rows, :]


def forward_kernel(dims, own, own_row, other, other_row, *refs):
    slab = Slab(dims)
    count = slab.slabs
    windows, home, theirs = refs[:count], refs[count], refs[count + 1 : 2 * count]
    (acts, kept, *outs), (whole, field) = refs[2 * count : -2], refs[-2:]
    slab.blank_edges(acts)
    slab.fill(field, windows, home, theirs, 0)

    def take_in(start):
        for micro in range(slab.micros):
            slab.put_rows(acts, 0, micro, start, field[micro, pl.ds(start, slab.chunk), :])

    slab.over_chunks(take_in)

    def layer_step(layer, carry):
        def run(tables, half):
            table, row = tables

            def body(start):
                at = pl.ds(start, slab.chunk)
                sums = slab.conv(acts, layer, start, table.at[half])
                values = []
                for micro, total in enumerate(sums):
                    pre = total + row[half][0:1, :]
                    sigma = 1.0 / (1.0 + jnp.exp(-pre))
                    kept[layer, micro, at, :] = sigma * (1.0 + pre * (1.0 - sigma))
                    out = slab.masked(pre * sigma, slab.in_grid)
                    slab.put_rows(acts, layer + 1, micro, start, out)
                    values.append(out)

                @pl.when(layer == 2 * slab.section + 1)
                def _():
                    for micro, value in enumerate(values):
                        whole[micro, at, :] = value

            slab.over_chunks(body)

        slab.by_owner(layer, (own, own_row), (other, other_row), run)
        return carry

    lax.fori_loop(0, 4, layer_step, 0)
    slab.cut_out(outs, whole)


def backward_kernel(dims, scale, own, other, acts, kept, *refs):
    slab = Slab(dims)
    (*windows, home, other_cells), refs = refs[: slab.slabs + 2], refs[slab.slabs + 2 :]
    theirs = [other_cells.at[turn] for turn in range(slab.slabs - 1)]
    outs, (sums, rim, slopes, field, acc) = refs[: slab.slabs], refs[slab.slabs :]
    slab.blank_edges(rim)
    slab.fill(field, windows, home, theirs, 1)

    def take_gradient(layer, micro, start, gradient):
        at = pl.ds(start, slab.chunk)
        slope = slab.masked(gradient * kept[layer, micro, at, :], slab.in_grid)
        slopes[layer, micro, at, :] = slab.masked(slope, slab.mine)
        slab.put_rows(rim, layer % 2, micro, start, slope)

    def take_cotangent(start):
        for micro in range(slab.micros):
            take_gradient(3, micro, start, field[micro, pl.ds(start, slab.chunk), :])

    slab.over_chunks(take_cotangent)

    def layer_step(index, carry):
        layer = 3 - index

        def run(table, half):
            def body(start):
                gradients = slab.conv(rim, layer % 2, start, table.at[half])
                last = layer == 2 * slab.section

                @pl.when(last)
                def _():
                    for micro, gradient in enumerate(gradients):
                        field[micro, pl.ds(start, slab.chunk), :] = gradient

                @pl.when(jnp.logical_not(last))
                def _():
                    for micro, gradient in enumerate(gradients):
                        take_gradient(layer - 1, micro, start, gradient)

            slab.over_chunks(body)

        slab.by_owner(layer, own, other, run)
        return carry

    lax.fori_loop(0, jnp.where(slab.section == 0, 4, 2), layer_step, 0)
    slab.cut_out(outs, field)

    quarter = BLOCKS // 4
    chans = LANES // 2
    swap = column_bits()

    def spot(tap):
        return (tap // quarter ^ swap) * quarter + tap % quarter

    def products(layer, start):
        at = pl.ds(start, slab.chunk)
        slope = jnp.concatenate([slopes[layer, micro, at, :] for micro in range(slab.micros)])
        moved = [pltpu.roll(slope, slope.shape[0] - 1, 0), slope, pltpu.roll(slope, 1, 0)]
        terms = [split_terms(value) for value in moved]
        left_hi = jnp.concatenate([hi for hi, lo in terms], axis=1)
        left_lo = jnp.concatenate([lo for hi, lo in terms], axis=1)
        pieces = [slab.pieces_of(acts, layer, micro, start) for micro in range(slab.micros)]
        pieces = [jnp.concatenate(parts, axis=0) for parts in zip(*pieces)]
        full = jnp.concatenate(pieces, axis=1)
        high = jnp.concatenate([piece[:, :LANES] for piece in pieces], axis=1)
        over_rows = (((0,), (0,)), ((), ()))
        one = lax.dot_general(left_hi, full, over_rows, preferred_element_type=F32)
        two = lax.dot_general(left_lo, high, over_rows, preferred_element_type=F32)
        total = []
        for b in range(3):
            hi = one[:, 2 * b * LANES : (2 * b + 1) * LANES]
            lo = one[:, (2 * b + 1) * LANES : (2 * b + 2) * LANES]
            total.append(hi + lo + two[:, b * LANES : (b + 1) * LANES])
        return total, jnp.sum(slope, axis=0, keepdims=True)

    sums[spot(TAPS)] = jnp.zeros((chans, LANES), F32)
    for slot in range(2):
        layer = 2 * slab.section + slot
        if slab.chunks == 1:
            total, row = products(layer, 0)
        else:
            acc[...] = jnp.zeros(acc.shape, F32)

            def gather(start):
                total, row = products(layer, start)
                for b in range(3):
                    acc[0 : 3 * LANES, b * LANES : (b + 1) * LANES] += total[b]
                acc[3 * LANES : 3 * LANES + 1, 0:LANES] += row

            slab.over_chunks(gather)
            total = [acc[0 : 3 * LANES, b * LANES : (b + 1) * LANES] for b in range(3)]
            row = acc[3 * LANES : 3 * LANES + 1, 0:LANES]
        lanes = slice(slot * chans, (slot + 1) * chans)
        for b in range(3):
            for c in range(3):
                block = total[b][c * LANES : (c + 1) * LANES] * scale
                tap = 3 * b + c
                sums[spot(tap), :, lanes] = block[chans:, :chans]
                sums[spot(9 + tap), :, lanes] = block[:chans, :chans] + block[chans:, chans:]
                sums[spot(18 + tap), :, lanes] = block[:chans, chans:]
        row = row * scale
        sums[spot(TAPS), 0:1, lanes] = row[:, :chans] + row[:, chans:]


def unpack_kernel(*refs):
    sources, (weight, bias, whole) = refs[:-3], refs[-3:]
    part = sources[0].shape[0] // 4
    chans = weight.shape[-1]
    odd, swap = lax.axis_index("gy") % 2, column_bits()
    for number, source in enumerate(sources):
        for index in range(4):
            quarter = number // 2 * 2 + index // 2
            at = (((quarter ^ swap) * 2 + (index % 2 ^ odd)) * 2 + number % 2) * part
            rows = source[index * part : (index + 1) * part, :]
            whole[pl.ds(pl.multiple_of(at, 8), part), :] = rows
    for layer in range(2):
        lanes = slice(layer * chans, (layer + 1) * chans)
        for tap in range(TAPS):
            weight[layer, tap] = whole[tap * chans : (tap + 1) * chans, lanes]
        bias[layer : layer + 1, :] = whole[TAPS * chans : TAPS * chans + 1, lanes]


def restore_kernel(dims, *refs):
    micros, chans, size_x, local_y, width = dims
    pieces, (*targets, whole) = refs[:-3], refs[-3:]
    slab = lax.axis_index("gy")
    step = size_x * local_y
    slabs = len(pieces) // 2
    for slot, target in enumerate(targets):
        for micro in range(micros):
            for y in range(local_y):
                for turn in range(slabs):
                    start = (slab ^ turn) * width
                    if width % 8 == 0:
                        start = pl.multiple_of(start, 8)
                    rows = pl.ds(start, width)
                    whole[slot, micro, y, rows, :] = pieces[slot * slabs + turn][micro, y]
                block = whole[slot, micro, y].T
                for x in range(size_x):
                    first = micro * chans * step + x * local_y + y
                    part = block[x * chans : (x + 1) * chans]
                    target[pl.ds(first, chans, stride=step), :] = part


def spread(blocks):
    slabs = len(blocks)
    if slabs <= 8:
        got = [blocks[0]]
        for turn in range(1, slabs):
            route = [(i, i ^ turn) for i in range(slabs)]
            got.append(lax.ppermute(blocks[turn], "gy", route))
        return got
    order = jnp.arange(slabs) ^ lax.axis_index("gy")
    got = lax.all_to_all(jnp.stack(blocks)[order], "gy", 0, 0)[order]
    return [got[turn] for turn in range(slabs)]


def swapped(block, bit, axis="gz"):
    return lax.ppermute(block, axis, [(i, i ^ bit) for i in range(lax.axis_size(axis))])


def crossed(block):
    return lax.ppermute(block, "section", [(0, 1), (1, 0)])


def around(above, beside, across):
    slabs, columns = lax.axis_size("gy"), lax.axis_size("gz")
    route = [
        (i * columns + g, (i ^ 1) * columns + (g ^ 2)) for i in range(slabs) for g in range(columns)
    ]
    beside = swapped(beside, 2)
    across = lax.ppermute(across, ("gy", "gz"), route)
    return [swapped(above, 1, "gy"), beside, across]


def per_device(inflow, weights, biases, cotangent):
    micros, chans, size_x, local_y, local_z = inflow.shape
    assert micros == lax.axis_size("section") == 2
    slabs, columns = lax.axis_size("gy"), lax.axis_size("gz")
    rows_y = local_y * slabs
    width = local_z // slabs
    span = width + 2 * HALO
    depth = -(-span // 16) * 16
    chunk_y = max(n for n in range(1, rows_y + 1) if rows_y % n == 0 and n * depth <= 384)
    scale = 1.0 / math.sqrt(micros * size_x * rows_y * local_z * columns)
    rows = micros * chans * size_x * local_y
    fields = jnp.stack([inflow, cotangent]).transpose(0, 1, 4, 5, 3, 2)
    fields = fields.reshape(2, micros, local_y, local_z, size_x * chans)
    low, high = fields[:, :, :, :HALO], fields[:, :, :, local_z - HALO :]
    odd = lax.axis_index("gz") % 2 == 1
    pair = jnp.where(odd, low, high)
    inner = jnp.where(odd, high, low)
    packs = [((BLOCKS, chans, LANES), F32), ((BLOCKS // 2, chans, LANES), F32)]
    own, sent = call(pack_kernel, "pack", packs, [weights, biases])
    pair = swapped(pair, 1)
    route = [(i, i + 1) for i in range(1, columns - 1, 2)]
    inner = lax.ppermute(inner, "gz", route + [(after, before) for before, after in route])
    windows = call(
        functools.partial(window_kernel, (slabs, width, columns)),
        "windows",
        [((local_y, sum(width + 2 * halo for halo in HALOS), LANES), F32)] * (slabs + 1),
        [fields, pair, inner],
        [pltpu.VMEM((2, micros, local_y, local_z + 2 * HALO, LANES), F32)],
    )
    sent, windows = lax.optimization_barrier((sent, windows))
    near_half = crossed(sent)
    *mine, home = windows
    mine = spread(mine)

    tables = [((2, 15 * LANES, 2 * LANES), BF16)] * 2 + [((2, 8, LANES), F32)]
    own_fwd, own_bwd, own_row = call(table_kernel, "own_table", tables, [own])
    ahead = [window[:, : width + 2 * HALOS[0]] for window in mine[1:]]
    if slabs <= 8:
        ahead = [crossed(window) for window in ahead]
    else:
        ahead = list(crossed(jnp.stack(ahead)))
    after = crossed(jnp.stack([window[:, width + 2 * HALOS[0] :] for window in mine[1:]]))
    gate = [ahead[0], *mine[2:]]
    near_half, own_row, *_ = lax.optimization_barrier((near_half, own_row, *gate))
    far_half = swapped(near_half, 1)
    far_fwd, far_bwd, far_row = call(table_kernel, "far_table", tables, [near_half, far_half])

    dims = (micros, rows_y, depth, width, chunk_y, slabs, local_z * columns)
    padded = (rows_y + 2) * depth
    full = rows_y * depth
    piece = ((micros, local_y, width, LANES), F32)
    acts, kept, *fronts = call(
        functools.partial(forward_kernel, dims),
        "forward",
        [((5, micros, padded, 2 * LANES), BF16), ((4, micros, full, LANES), F32)] + [piece] * slabs,
        [own_fwd, own_row, far_fwd, far_row, *mine, home, *ahead],
        [pltpu.VMEM((micros, full, LANES), F32)] * 2,
    )
    if slabs == 4:
        passed = swapped(jnp.stack(fronts[2:]), 2, "gy")
    *backs, sums = call(
        functools.partial(backward_kernel, dims, scale),
        "backward",
        [piece] * slabs + [((BLOCKS, chans, LANES), F32)],
        [own_bwd, far_bwd, acts, kept, *mine, home, after],
        [
            pltpu.VMEM((2, micros, padded, 2 * LANES), BF16),
            pltpu.VMEM((4, micros, full, LANES), F32),
            pltpu.VMEM((micros, full, LANES), F32),
            pltpu.VMEM((3 * LANES + 8, 3 * LANES), F32),
        ],
        12 * micros * full * 9 * LANES * 3 * LANES,
    )
    if slabs == 4:
        sums, passed = lax.optimization_barrier((sums, passed))

    part = BLOCKS * chans // 16
    blocks = sums.reshape(8, 2, part, LANES)
    odd = lax.axis_index("gy") % 2 == 1
    streams = []
    for stream in range(2):
        block = blocks[:, stream].reshape(8 * part, LANES)
        streams.append(block[: 4 * part] + swapped(block[4 * part :], 1))
    streams[0], fronts, backs = lax.optimization_barrier((streams[0], fronts, backs))
    if slabs == 4:
        near = swapped(jnp.stack([fronts[1], passed[1], backs[1]]), 1, "gy")
        outs = [near, swapped(backs[2], 2, "gy"), swapped(backs[3], 3, "gy")]
    else:
        outs = spread([jnp.stack(pair) for pair in zip(fronts, backs)])
    streams = [block[: 2 * part] + swapped(block[2 * part :], 2) for block in streams]
    streams[1], outs = lax.optimization_barrier((streams[1], outs))
    sums = []
    for block in streams:
        kept = jnp.where(odd, block[part:], block[:part])
        kept = kept + swapped(jnp.where(odd, block[:part], block[part:]), 1, "gy")
        bit = 2
        while bit < slabs:
            kept = kept + swapped(kept, bit, "gy")
            bit *= 2
        sums.append(jnp.concatenate([kept, *around(kept, kept, kept)], axis=0))
    sums += [swapped(block, 1) for block in sums]
    if slabs == 4:
        outs = [fronts[0], outs[0][0], passed[0], outs[0][1], backs[0], outs[0][2], *outs[1:]]
    else:
        outs = [out[slot] for slot in range(2) for out in outs]
    section_out, section_grad = call(
        functools.partial(restore_kernel, (micros, chans, size_x, local_y, width)),
        "restore",
        [((rows, local_z), F32)] * 2,
        outs,
        [pltpu.VMEM((2, micros, local_y, local_z, LANES), F32)],
    )
    weight_total, bias_total = call(
        unpack_kernel,
        "unpack",
        [((2, TAPS, chans, chans), F32), ((2, chans), F32)],
        sums,
        [pltpu.VMEM((BLOCKS * chans, LANES), F32)],
    )
    shape = (1, *inflow.shape)
    return (section_out.reshape(shape), section_grad.reshape(shape), weight_total, bias_total)


def solution(mesh):
    grid = P(None, None, None, "gy", "gz")
    section_grid = P("section", None, None, None, "gy", "gz")
    return jax.shard_map(
        per_device,
        mesh=mesh,
        in_specs=(grid, P("section", None, None, None), P("section", None), grid),
        out_specs=(section_grid, section_grid, P("section", None, None, None), P("section", None)),
        check_vma=False,
    )
```

```python
import functools
import math

import jax
import jax.numpy as jnp
from jax import lax
from jax.experimental import pallas as pl
from jax.experimental.pallas import tpu as pltpu
from jax.sharding import PartitionSpec as P

HALO = 8
HALOS = (8, 4)
LANES = 128
TAPS = 27
BLOCKS = 28
BF16 = jnp.bfloat16
F32 = jnp.float32
VMEM = pl.BlockSpec(memory_space=pltpu.VMEM)


def call(kernel, name, outs, args, scratch=(), flops=0):
    arrays = [jax.ShapeDtypeStruct(shape, kind) for shape, kind in outs]
    size = sum(math.prod(item.shape) * item.dtype.itemsize for item in [*arrays, *args, *scratch])
    return pl.pallas_call(
        kernel,
        out_shape=arrays,
        in_specs=[VMEM] * len(args),
        out_specs=[VMEM] * len(arrays),
        scratch_shapes=list(scratch),
        compiler_params=pltpu.CompilerParams(vmem_limit_bytes=size + 6 * 1024 * 1024),
        cost_estimate=pl.CostEstimate(flops=flops, bytes_accessed=1024, transcendentals=0),
        name=name,
    )(*args)


def column_bits():
    column = lax.axis_index("gz")
    return 2 * (column % 2) + column // 2 % 2


def split_terms(values):
    high = values.astype(BF16)
    return high, (values - high.astype(F32)).astype(BF16)


def pack_kernel(weights, biases, own, sent):
    chans = weights.shape[2]
    for tap in range(TAPS):
        own[tap] = jnp.concatenate([weights[0, tap], weights[1, tap]], axis=1)
    own[TAPS] = jnp.zeros((chans, LANES), F32)
    own[TAPS, 0:1, :] = jnp.concatenate([biases[0:1, :], biases[1:2, :]], axis=1)
    half = sent.shape[0]
    start = lax.axis_index("gz") % 2 * half
    for index in range(half):
        sent[index] = own[start + index]


def window_kernel(dims, rows, pair, inner, *refs):
    slabs, width, columns = dims
    outs, wide = refs[:-1], refs[-1]
    slab, column = lax.axis_index("gy"), lax.axis_index("gz")
    section = lax.axis_index("section")
    odd = column % 2 == 1
    _, micros, local_y, local_z, _ = rows.shape
    for field, halo in enumerate(HALOS):
        at = slice(0, width + 2 * halo) if field == 0 else slice(width + 2 * HALO, None)
        for y in range(local_y):
            for micro in range(micros):
                one, two = pair[field, micro, y], inner[field, micro, y]
                before = jnp.where(column > 0, jnp.where(odd, one, two), 0.0)
                after = jnp.where(column < columns - 1, jnp.where(odd, two, one), 0.0)
                wide[field, micro, y, :HALO] = before
                wide[field, micro, y, HALO : HALO + local_z] = rows[field, micro, y]
                wide[field, micro, y, HALO + local_z :] = after
            for turn, out in enumerate(outs):
                start = (slab ^ turn % slabs) * width + HALO - halo
                if width % 8 == 0 and halo % 8 == 0:
                    start = pl.multiple_of(start, 8)
                micro = section if turn < slabs else 1 - section
                out[y, at] = wide[field, micro, y, pl.ds(start, width + 2 * halo)]


def table_kernel(*refs):
    parts, (fwd, bwd, row) = refs[:-3], refs[-3:]
    odd = lax.axis_index("gz") % 2
    count, chans, _ = parts[0].shape

    def block_of(tap):
        if len(parts) == 1:
            return parts[0][tap]
        index = tap % count
        return jnp.where(odd == tap // count, parts[0][index], parts[1][index])

    for b in range(3):
        for c in range(3):
            taps = [block_of(9 * a + 3 * b + c) for a in range(3)]
            for layer in range(2):
                own_lanes = slice(layer * chans, (layer + 1) * chans)
                below, level, above = [tap[:, own_lanes] for tap in taps]
                top = jnp.concatenate([level, above], axis=1)
                low = jnp.concatenate([below, level], axis=1)
                block = jnp.concatenate([top, low], axis=0)
                for target, value, r, at in ((fwd, block.T, b, c), (bwd, block, 2 - b, 2 - c)):
                    hi, lo = split_terms(value)
                    if at == 1:
                        for row_at in (9 + 2 * r, 10 + 2 * r):
                            rows = slice(row_at * LANES, (row_at + 1) * LANES)
                            target[layer, rows, 0:LANES] = hi
                            target[layer, rows, LANES : 2 * LANES] = lo
                    else:
                        lanes = slice(at // 2 * LANES, (at // 2 + 1) * LANES)
                        for row_at, term in ((2 * r, hi), (2 * r + 1, hi), (6 + r, lo)):
                            rows = slice(row_at * LANES, (row_at + 1) * LANES)
                            target[layer, rows, lanes] = term
    last = block_of(TAPS)[0:1, :]
    for layer in range(2):
        part = last[:, layer * chans : (layer + 1) * chans]
        row[layer] = jnp.broadcast_to(jnp.concatenate([part, part], axis=1), (8, LANES))


class Slab:
    def __init__(self, dims):
        self.micros, self.rows_y, self.depth, self.width, self.chunk_y, self.slabs, limit_z = dims
        self.section, self.slab = lax.axis_index("section"), lax.axis_index("gy")
        origin = (lax.axis_index("gz") * self.slabs + self.slab) * self.width - HALO
        self.chunk = self.chunk_y * self.depth
        self.chunks = self.rows_y // self.chunk_y
        self.per_owner = self.rows_y // self.slabs
        zs = lax.broadcasted_iota(jnp.int32, (self.depth, LANES), 0)
        inside = (zs + origin >= 0) & (zs + origin < limit_z)
        self.in_grid = inside.astype(F32)[None]
        self.mine = ((zs >= HALO) & (zs < HALO + self.width)).astype(F32)[None]

    def over_chunks(self, body):
        if self.chunks == 1:
            body(0)
        else:

            def step(part, carry):
                body(pl.multiple_of(part * self.chunk, 16))
                return carry

            lax.fori_loop(0, self.chunks, step, 0)

    def masked(self, values, mask):
        return (values.reshape(-1, self.depth, LANES) * mask).reshape(values.shape)

    def put_rows(self, target, lead, micro, start, values):
        hi, lo = split_terms(values)
        at = pl.ds(start + self.depth, self.chunk)
        target[lead, micro, at, slice(0, LANES)] = hi
        target[lead, micro, at, slice(LANES, 2 * LANES)] = lo

    def pieces_of(self, source, lead, micro, start):
        return [
            source[lead, micro, pl.ds(start + b * self.depth, self.chunk), :] for b in range(3)
        ]

    def conv(self, source, lead, start, table):
        lefts = []
        for micro in range(self.micros):
            pieces = self.pieces_of(source, lead, micro, start)
            lefts.append(jnp.concatenate(pieces + [piece[:, :LANES] for piece in pieces], axis=1))
        results = []
        for left in lefts:
            outer = jnp.dot(left, table[0 : 9 * LANES, :], preferred_element_type=F32)
            middle = jnp.dot(
                left[:, 0 : 6 * LANES],
                table[9 * LANES : 15 * LANES, :],
                preferred_element_type=F32,
            )
            before = pltpu.roll(outer[:, :LANES], 1, 0)
            after = pltpu.roll(outer[:, LANES:], outer.shape[0] - 1, 0)
            results.append(before + (middle[:, :LANES] + middle[:, LANES:]) + after)
        return results

    def by_owner(self, layer, own, other, body):
        mine = layer // 2 == self.section
        pl.when(mine)(lambda: body(own, layer % 2))
        pl.when(jnp.logical_not(mine))(lambda: body(other, layer % 2))

    def blank_edges(self, target):
        blank = jnp.zeros((self.depth, 2 * LANES), BF16)
        for lead in range(target.shape[0]):
            for micro in range(self.micros):
                for edge in (0, self.rows_y + 1):
                    target[lead, micro, edge * self.depth : (edge + 1) * self.depth, :] = blank

    def fill(self, field, windows, home, theirs, which):
        halo = HALOS[which]
        span = self.width + 2 * halo
        at = 0 if which == 0 else self.width + 2 * HALO
        extra = [HALO - halo, self.depth - span - (HALO - halo)]
        pieces = [(self.section, turn, window, at) for turn, window in enumerate(windows)]
        pieces.append((1 - self.section, 0, home, at))
        pieces += [(1 - self.section, turn + 1, window, 0) for turn, window in enumerate(theirs)]
        for micro, turn, window, first in pieces:
            owner = self.slab ^ turn
            for y in range(self.per_owner):
                blanks = [jnp.zeros((rows, LANES), F32) for rows in extra]
                parts = [blanks[0], window[y, first : first + span], blanks[1]]
                parts = [part for part in parts if part.shape[0]]
                start = pl.multiple_of((owner * self.per_owner + y) * self.depth, 16)
                value = jnp.concatenate(parts, axis=0) if len(parts) > 1 else parts[0]
                field[micro, pl.ds(start, self.depth), :] = value

    def cut_out(self, targets, source):
        for turn, target in enumerate(targets):
            owner = self.slab ^ turn
            for micro in range(self.micros):
                for y in range(self.per_owner):
                    start = (owner * self.per_owner + y) * self.depth + HALO
                    rows = pl.ds(pl.multiple_of(start, 8), self.width)
                    target[micro, y] = source[micro, rows, :]


def forward_kernel(dims, own, own_row, other, other_row, *refs):
    slab = Slab(dims)
    count = slab.slabs
    windows, home, theirs = refs[:count], refs[count], refs[count + 1 : 2 * count]
    (acts, kept, *outs), (whole, field) = refs[2 * count : -2], refs[-2:]
    slab.blank_edges(acts)
    slab.fill(field, windows, home, theirs, 0)

    def take_in(start):
        for micro in range(slab.micros):
            slab.put_rows(acts, 0, micro, start, field[micro, pl.ds(start, slab.chunk), :])

    slab.over_chunks(take_in)

    def layer_step(layer, carry):
        def run(tables, half):
            table, row = tables

            def body(start):
                at = pl.ds(start, slab.chunk)
                sums = slab.conv(acts, layer, start, table.at[half])
                values = []
                for micro, total in enumerate(sums):
                    pre = total + row[half][0:1, :]
                    sigma = 1.0 / (1.0 + jnp.exp(-pre))
                    kept[layer, micro, at, :] = sigma * (1.0 + pre * (1.0 - sigma))
                    out = slab.masked(pre * sigma, slab.in_grid)
                    slab.put_rows(acts, layer + 1, micro, start, out)
                    values.append(out)

                @pl.when(layer == 2 * slab.section + 1)
                def _():
                    for micro, value in enumerate(values):
                        whole[micro, at, :] = value

            slab.over_chunks(body)

        slab.by_owner(layer, (own, own_row), (other, other_row), run)
        return carry

    lax.fori_loop(0, 4, layer_step, 0)
    slab.cut_out(outs, whole)


def backward_kernel(dims, scale, own, other, acts, kept, *refs):
    slab = Slab(dims)
    (*windows, home, other_cells), refs = refs[: slab.slabs + 2], refs[slab.slabs + 2 :]
    theirs = [other_cells.at[turn] for turn in range(slab.slabs - 1)]
    outs, (sums, rim, slopes, field, acc) = refs[: slab.slabs], refs[slab.slabs :]
    slab.blank_edges(rim)
    slab.fill(field, windows, home, theirs, 1)

    def take_gradient(layer, micro, start, gradient):
        at = pl.ds(start, slab.chunk)
        slope = slab.masked(gradient * kept[layer, micro, at, :], slab.in_grid)
        slopes[layer, micro, at, :] = slab.masked(slope, slab.mine)
        slab.put_rows(rim, layer % 2, micro, start, slope)

    def take_cotangent(start):
        for micro in range(slab.micros):
            take_gradient(3, micro, start, field[micro, pl.ds(start, slab.chunk), :])

    slab.over_chunks(take_cotangent)

    def layer_step(index, carry):
        layer = 3 - index

        def run(table, half):
            def body(start):
                gradients = slab.conv(rim, layer % 2, start, table.at[half])
                last = layer == 2 * slab.section

                @pl.when(last)
                def _():
                    for micro, gradient in enumerate(gradients):
                        field[micro, pl.ds(start, slab.chunk), :] = gradient

                @pl.when(jnp.logical_not(last))
                def _():
                    for micro, gradient in enumerate(gradients):
                        take_gradient(layer - 1, micro, start, gradient)

            slab.over_chunks(body)

        slab.by_owner(layer, own, other, run)
        return carry

    lax.fori_loop(0, jnp.where(slab.section == 0, 4, 2), layer_step, 0)
    slab.cut_out(outs, field)

    quarter = BLOCKS // 4
    chans = LANES // 2
    swap = column_bits()

    def spot(tap):
        return (tap // quarter ^ swap) * quarter + tap % quarter

    def products(layer, start):
        at = pl.ds(start, slab.chunk)
        slope = jnp.concatenate([slopes[layer, micro, at, :] for micro in range(slab.micros)])
        moved = [pltpu.roll(slope, slope.shape[0] - 1, 0), slope, pltpu.roll(slope, 1, 0)]
        terms = [split_terms(value) for value in moved]
        left_hi = jnp.concatenate([hi for hi, lo in terms], axis=1)
        left_lo = jnp.concatenate([lo for hi, lo in terms], axis=1)
        pieces = [slab.pieces_of(acts, layer, micro, start) for micro in range(slab.micros)]
        pieces = [jnp.concatenate(parts, axis=0) for parts in zip(*pieces)]
        full = jnp.concatenate(pieces, axis=1)
        high = jnp.concatenate([piece[:, :LANES] for piece in pieces], axis=1)
        over_rows = (((0,), (0,)), ((), ()))
        one = lax.dot_general(left_hi, full, over_rows, preferred_element_type=F32)
        two = lax.dot_general(left_lo, high, over_rows, preferred_element_type=F32)
        total = []
        for b in range(3):
            hi = one[:, 2 * b * LANES : (2 * b + 1) * LANES]
            lo = one[:, (2 * b + 1) * LANES : (2 * b + 2) * LANES]
            total.append(hi + lo + two[:, b * LANES : (b + 1) * LANES])
        return total, jnp.sum(slope, axis=0, keepdims=True)

    sums[spot(TAPS)] = jnp.zeros((chans, LANES), F32)
    for slot in range(2):
        layer = 2 * slab.section + slot
        if slab.chunks == 1:
            total, row = products(layer, 0)
        else:
            acc[...] = jnp.zeros(acc.shape, F32)

            def gather(start):
                total, row = products(layer, start)
                for b in range(3):
                    acc[0 : 3 * LANES, b * LANES : (b + 1) * LANES] += total[b]
                acc[3 * LANES : 3 * LANES + 1, 0:LANES] += row

            slab.over_chunks(gather)
            total = [acc[0 : 3 * LANES, b * LANES : (b + 1) * LANES] for b in range(3)]
            row = acc[3 * LANES : 3 * LANES + 1, 0:LANES]
        lanes = slice(slot * chans, (slot + 1) * chans)
        for b in range(3):
            for c in range(3):
                block = total[b][c * LANES : (c + 1) * LANES] * scale
                tap = 3 * b + c
                sums[spot(tap), :, lanes] = block[chans:, :chans]
                sums[spot(9 + tap), :, lanes] = block[:chans, :chans] + block[chans:, chans:]
                sums[spot(18 + tap), :, lanes] = block[:chans, chans:]
        row = row * scale
        sums[spot(TAPS), 0:1, lanes] = row[:, :chans] + row[:, chans:]


def unpack_kernel(*refs):
    sources, (weight, bias, whole) = refs[:-3], refs[-3:]
    part = sources[0].shape[0] // 4
    chans = weight.shape[-1]
    odd, swap = lax.axis_index("gy") % 2, column_bits()
    for number, source in enumerate(sources):
        for index in range(4):
            quarter = number // 2 * 2 + index // 2
            at = (((quarter ^ swap) * 2 + (index % 2 ^ odd)) * 2 + number % 2) * part
            rows = source[index * part : (index + 1) * part, :]
            whole[pl.ds(pl.multiple_of(at, 8), part), :] = rows
    for layer in range(2):
        lanes = slice(layer * chans, (layer + 1) * chans)
        for tap in range(TAPS):
            weight[layer, tap] = whole[tap * chans : (tap + 1) * chans, lanes]
        bias[layer : layer + 1, :] = whole[TAPS * chans : TAPS * chans + 1, lanes]


def restore_kernel(dims, *refs):
    micros, chans, size_x, local_y, width = dims
    pieces, (*targets, whole) = refs[:-3], refs[-3:]
    slab = lax.axis_index("gy")
    step = size_x * local_y
    slabs = len(pieces) // 2
    for slot, target in enumerate(targets):
        for micro in range(micros):
            for y in range(local_y):
                for turn in range(slabs):
                    start = (slab ^ turn) * width
                    if width % 8 == 0:
                        start = pl.multiple_of(start, 8)
                    rows = pl.ds(start, width)
                    whole[slot, micro, y, rows, :] = pieces[slot * slabs + turn][micro, y]
                block = whole[slot, micro, y].T
                for x in range(size_x):
                    first = micro * chans * step + x * local_y + y
                    part = block[x * chans : (x + 1) * chans]
                    target[pl.ds(first, chans, stride=step), :] = part


def spread(blocks):
    slabs = len(blocks)
    if slabs <= 8:
        got = [blocks[0]]
        for turn in range(1, slabs):
            route = [(i, i ^ turn) for i in range(slabs)]
            got.append(lax.ppermute(blocks[turn], "gy", route))
        return got
    order = jnp.arange(slabs) ^ lax.axis_index("gy")
    got = lax.all_to_all(jnp.stack(blocks)[order], "gy", 0, 0)[order]
    return [got[turn] for turn in range(slabs)]


def swapped(block, bit, axis="gz"):
    return lax.ppermute(block, axis, [(i, i ^ bit) for i in range(lax.axis_size(axis))])


def crossed(block):
    return lax.ppermute(block, "section", [(0, 1), (1, 0)])


def around(above, beside, across):
    slabs, columns = lax.axis_size("gy"), lax.axis_size("gz")
    route = [
        (i * columns + g, (i ^ 1) * columns + (g ^ 2)) for i in range(slabs) for g in range(columns)
    ]
    beside = swapped(beside, 2)
    across = lax.ppermute(across, ("gy", "gz"), route)
    return [swapped(above, 1, "gy"), beside, across]


def per_device(inflow, weights, biases, cotangent):
    micros, chans, size_x, local_y, local_z = inflow.shape
    assert micros == lax.axis_size("section") == 2
    slabs, columns = lax.axis_size("gy"), lax.axis_size("gz")
    rows_y = local_y * slabs
    width = local_z // slabs
    span = width + 2 * HALO
    depth = -(-span // 16) * 16
    chunk_y = max(n for n in range(1, rows_y + 1) if rows_y % n == 0 and n * depth <= 384)
    scale = 1.0 / math.sqrt(micros * size_x * rows_y * local_z * columns)
    rows = micros * chans * size_x * local_y
    fields = jnp.stack([inflow, cotangent]).transpose(0, 1, 4, 5, 3, 2)
    fields = fields.reshape(2, micros, local_y, local_z, size_x * chans)
    low, high = fields[:, :, :, :HALO], fields[:, :, :, local_z - HALO :]
    odd = lax.axis_index("gz") % 2 == 1
    pair = jnp.where(odd, low, high)
    inner = jnp.where(odd, high, low)
    packs = [((BLOCKS, chans, LANES), F32), ((BLOCKS // 2, chans, LANES), F32)]
    own, sent = call(pack_kernel, "pack", packs, [weights, biases])
    pair = swapped(pair, 1)
    route = [(i, i + 1) for i in range(1, columns - 1, 2)]
    inner = lax.ppermute(inner, "gz", route + [(after, before) for before, after in route])
    windows = call(
        functools.partial(window_kernel, (slabs, width, columns)),
        "windows",
        [((local_y, sum(width + 2 * halo for halo in HALOS), LANES), F32)] * (slabs + 1),
        [fields, pair, inner],
        [pltpu.VMEM((2, micros, local_y, local_z + 2 * HALO, LANES), F32)],
    )
    sent, windows = lax.optimization_barrier((sent, windows))
    near_half = crossed(sent)
    *mine, home = windows
    mine = spread(mine)

    tables = [((2, 15 * LANES, 2 * LANES), BF16)] * 2 + [((2, 8, LANES), F32)]
    own_fwd, own_bwd, own_row = call(table_kernel, "own_table", tables, [own])
    ahead = [window[:, : width + 2 * HALOS[0]] for window in mine[1:]]
    if slabs <= 8:
        ahead = [crossed(window) for window in ahead]
    else:
        ahead = list(crossed(jnp.stack(ahead)))
    after = crossed(jnp.stack([window[:, width + 2 * HALOS[0] :] for window in mine[1:]]))
    gate = [ahead[0], *mine[2:]]
    near_half, own_row, *_ = lax.optimization_barrier((near_half, own_row, *gate))
    far_half = swapped(near_half, 1)
    far_fwd, far_bwd, far_row = call(table_kernel, "far_table", tables, [near_half, far_half])

    dims = (micros, rows_y, depth, width, chunk_y, slabs, local_z * columns)
    padded = (rows_y + 2) * depth
    full = rows_y * depth
    piece = ((micros, local_y, width, LANES), F32)
    acts, kept, *fronts = call(
        functools.partial(forward_kernel, dims),
        "forward",
        [((5, micros, padded, 2 * LANES), BF16), ((4, micros, full, LANES), F32)] + [piece] * slabs,
        [own_fwd, own_row, far_fwd, far_row, *mine, home, *ahead],
        [pltpu.VMEM((micros, full, LANES), F32)] * 2,
    )
    if slabs == 4:
        passed = swapped(jnp.stack(fronts[2:]), 2, "gy")
    *backs, sums = call(
        functools.partial(backward_kernel, dims, scale),
        "backward",
        [piece] * slabs + [((BLOCKS, chans, LANES), F32)],
        [own_bwd, far_bwd, acts, kept, *mine, home, after],
        [
            pltpu.VMEM((2, micros, padded, 2 * LANES), BF16),
            pltpu.VMEM((4, micros, full, LANES), F32),
            pltpu.VMEM((micros, full, LANES), F32),
            pltpu.VMEM((3 * LANES + 8, 3 * LANES), F32),
        ],
        12 * micros * full * 9 * LANES * 3 * LANES,
    )
    if slabs == 4:
        sums, passed = lax.optimization_barrier((sums, passed))

    part = BLOCKS * chans // 16
    blocks = sums.reshape(8, 2, part, LANES)
    odd = lax.axis_index("gy") % 2 == 1
    streams = []
    for stream in range(2):
        block = blocks[:, stream].reshape(8 * part, LANES)
        streams.append(block[: 4 * part] + swapped(block[4 * part :], 1))
    streams[0], fronts, backs = lax.optimization_barrier((streams[0], fronts, backs))
    if slabs == 4:
        near = swapped(jnp.stack([fronts[1], passed[1], backs[1]]), 1, "gy")
        outs = [near, swapped(backs[2], 2, "gy"), swapped(backs[3], 3, "gy")]
    else:
        outs = spread([jnp.stack(pair) for pair in zip(fronts, backs)])
    streams = [block[: 2 * part] + swapped(block[2 * part :], 2) for block in streams]
    sums = []
    for block in streams:
        kept = jnp.where(odd, block[part:], block[:part])
        kept = kept + swapped(jnp.where(odd, block[:part], block[part:]), 1, "gy")
        if sums:
            kept, outs = lax.optimization_barrier((kept, outs))
        bit = 2
        while bit < slabs:
            kept = kept + swapped(kept, bit, "gy")
            bit *= 2
        sums.append(jnp.concatenate([kept, *around(kept, kept, kept)], axis=0))
    sums += [swapped(block, 1) for block in sums]
    if slabs == 4:
        outs = [fronts[0], outs[0][0], passed[0], outs[0][1], backs[0], outs[0][2], *outs[1:]]
    else:
        outs = [out[slot] for slot in range(2) for out in outs]
    section_out, section_grad = call(
        functools.partial(restore_kernel, (micros, chans, size_x, local_y, width)),
        "restore",
        [((rows, local_z), F32)] * 2,
        outs,
        [pltpu.VMEM((2, micros, local_y, local_z, LANES), F32)],
    )
    weight_total, bias_total = call(
        unpack_kernel,
        "unpack",
        [((2, TAPS, chans, chans), F32), ((2, chans), F32)],
        sums,
        [pltpu.VMEM((BLOCKS * chans, LANES), F32)],
    )
    shape = (1, *inflow.shape)
    return (section_out.reshape(shape), section_grad.reshape(shape), weight_total, bias_total)


def solution(mesh):
    grid = P(None, None, None, "gy", "gz")
    section_grid = P("section", None, None, None, "gy", "gz")
    return jax.shard_map(
        per_device,
        mesh=mesh,
        in_specs=(grid, P("section", None, None, None), P("section", None), grid),
        out_specs=(section_grid, section_grid, P("section", None, None, None), P("section", None)),
        check_vma=False,
    )
```
